32 devices in a mesh: space: 8 (over z, y), head: 4 (over x, core).
Axes of the slice: x: 2, y: 2, z: 4, core: 2. Of those that a mesh axis runs over, the one named last changes fastest.
Arguments:
- frames_in: bfloat16 [16, 2, 256, 1024], P('head', None, 'space'), may hold values from -6 to 6
- action_codes: int32 [16, 2], P('head'), may hold values from 0 to 7
- clip_length: int32 [2], replicated, may hold values from 4 to 16, as said below
- norm_gain: float32 [3, 1024], P(None, ('space', 'head')), may hold values from 0.25 to 1.75
- norm_bias: float32 [3, 1024], P(None, ('space', 'head')), may hold values from -4 to 4
- action_table: float32 [8, 1024], P(None, ('space', 'head')), may hold values from -6 to 6
- spatialin: bfloat16 [1024, 3, 1024], P('space', None, 'head'), may hold values from -0.1875 to 0.1875
- spatialout: bfloat16 [1024, 1024], P('head', 'space'), may hold values from -0.75 to 0.75
- temporalin: bfloat16 [1024, 3, 1024], P('space', None, 'head'), may hold values from -0.1875 to 0.1875
- temporalout: bfloat16 [1024, 1024], P('head', 'space'), may hold values from -0.375 to 0.375
- expand: bfloat16 [1024, 4096], P('space', 'head'), may hold values from -0.1875 to 0.1875
- shrink: bfloat16 [4096, 1024], P('head', 'space'), may hold values from -0.09375 to 0.09375
- out_grad: bfloat16 [16, 2, 256, 1024], P('head', None, 'space'), may hold values from -6 to 6
Outputs:
- frames_out: bfloat16 [16, 2, 256, 1024], P('head', None, 'space')
- frames_grad: float32 [16, 2, 256, 1024], P('head', None, 'space')
- gain_grad: float32 [3, 1024], P(None, ('space', 'head'))
- bias_grad: float32 [3, 1024], P(None, ('space', 'head'))
- table_grad: float32 [8, 1024], P(None, ('space', 'head'))
- spatialin_grad: float32 [1024, 3, 1024], P('space', None, 'head')
- spatialout_grad: float32 [1024, 1024], P('head', 'space')
- temporalin_grad: float32 [1024, 3, 1024], P('space', None, 'head')
- temporalout_grad: float32 [1024, 1024], P('head', 'space')
- expand_grad: float32 [1024, 4096], P('space', 'head')
- shrink_grad: float32 [4096, 1024], P('head', 'space')
The draws below stay inside these ranges and needn't reach their ends.
Inputs may be any that keep to these rules, and one draw needn't show every extreme that they name: `clip_length`: one clip holds exactly 16 frames.
All inputs are finite; a program needn't handle non-finite values.
Results may differ from the reference program's by a relative error of at most 0.02.
Values may be sent and summed in bfloat16 or wider, within the bound.
No kernel may reach another device: no remote copies, remote signals or barrier semaphores. Data moves between devices by JAX's collectives and lax.ppermute only.
A program may use at most 128 MiB of HBM per device.

```python
import jax
import jax.numpy as jnp
from jax import lax

D = 1024
HEADS = 16
HEAD_DIM = 64
FF = 4096
ACTIONS = 8
POS = 256
FRAMES = 16
MIN_FRAMES = 4
CLIPS = 2


def draw_clip_length(key, part):
    key = jax.random.fold_in(key, 11)
    first_key, second_key = jax.random.split(key, 2)
    lengths = jax.random.randint(first_key, (CLIPS,), MIN_FRAMES, FRAMES + 1)
    longest = jax.random.randint(second_key, (), 0, CLIPS)
    positions = jnp.arange(CLIPS)
    lengths = jnp.where(positions == longest, FRAMES, lengths)
    return lengths.astype(jnp.int32)


def set_ends(values, rng, low, high):
    shape = values.shape
    spot = [jax.random.randint(jax.random.fold_in(rng, axis), (), 0, shape[axis]) for axis in range(len(shape))]
    values = values.at[tuple(spot)].set(low)
    longest = shape.index(max(shape))
    spot[longest] = (spot[longest] + 1) % shape[longest]
    return values.at[tuple(spot)].set(high)


def shard_levels(stream_key, shape, cuts, low, high):
    loudness, own = 1.0, jax.random.fold_in(stream_key, 6)
    for position, blocks in cuts:
        draws = jnp.exp(jax.random.uniform(jax.random.fold_in(own, position), (blocks,), jnp.float32, low / len(cuts), high / len(cuts)))
        loudness = loudness * jnp.repeat(draws, shape[position] // blocks).reshape([-1 if axis == position else 1 for axis in range(len(shape))])
    return loudness


def noise(rng, dims, scale, reach, pieces=(), dtype=jnp.bfloat16):
    values = jax.random.normal(rng, dims, jnp.float32) * scale
    if len(pieces) > 0:
        values = shard_levels(rng, dims, pieces, -0.22, 0.18) * values
    return jnp.clip(values, min=-reach, max=reach).astype(dtype)


def setup_inputs(seed: int = 0) -> dict:
    keys = jax.random.split(jax.random.key(seed), 14)
    return {
        "frames_in": noise(keys[0], (FRAMES, CLIPS, POS, D), 1.0, 6.0, ((0, 4), (2, 8))),
        "action_codes": set_ends(jax.random.randint(keys[1], (FRAMES, CLIPS), 0, ACTIONS), jax.random.fold_in(keys[1], 1), 0, ACTIONS - 1).astype(jnp.int32),
        "clip_length": draw_clip_length(jax.random.fold_in(keys[13], 71), 0),
        "norm_gain": jnp.clip(1.0 + 0.15 * jax.random.normal(keys[3], (3, D), jnp.float32), 0.25, 1.75),
        "norm_bias": noise(keys[4], (3, D), 0.3, 4.0, ((1, 32),), jnp.float32),
        "action_table": noise(keys[5], (ACTIONS, D), 0.5, 6.0, ((1, 32),), jnp.float32),
        "spatialin": noise(keys[6], (D, 3, D), D ** -0.5, 0.1875, ((0, 8), (2, 4))),
        "spatialout": noise(keys[7], (D, D), (D // 16) ** -0.5, 0.75, ((0, 4), (1, 8))),
        "temporalin": noise(keys[8], (D, 3, D), D ** -0.5, 0.1875, ((0, 8), (2, 4))),
        "temporalout": noise(keys[9], (D, D), (D // 4) ** -0.5, 0.375, ((0, 4), (1, 8))),
        "expand": noise(keys[10], (D, FF), D ** -0.5, 0.1875, ((0, 8), (1, 4))),
        "shrink": noise(keys[11], (FF, D), FF ** -0.5, 0.09375, ((0, 4), (1, 8))),
        "out_grad": noise(keys[12], (FRAMES, CLIPS, POS, D), 1.0, 6.0, ((0, 4), (2, 8))),
    }


EPSILON = 1e-05
SCORE_SCALE = 0.125
MASKED_SCORE = -1e+30
PRECISE = lax.Precision.HIGHEST
GELU_COEFF = 0.7978845608028654

@jax.custom_vjp
def low(v):
    return lax.optimization_barrier(v.astype(jnp.bfloat16)).astype(jnp.float32)

@jax.custom_vjp
def low_back(v):
    return v

def low_keep(v):
    return (low(v), None)

def low_pass(kept, grad):
    return (grad,)

def back_keep(v):
    return (v, None)

def back_low(kept, grad):
    return (low(grad),)
low.defvjp(low_keep, low_pass)
low_back.defvjp(back_keep, back_low)

def layer_norm(values, gain_row, bias_row):
    row_mean = lax.optimization_barrier(jnp.mean(values, axis=-1, keepdims=True))
    centred = values - row_mean
    row_var = lax.optimization_barrier(jnp.mean(centred * centred, axis=-1, keepdims=True))
    return centred * lax.rsqrt(row_var + EPSILON) * gain_row + bias_row

def gelu_tanh(inputs):
    return 0.5 * inputs * (1.0 + jnp.tanh(GELU_COEFF * (inputs + 0.044715 * inputs * inputs * inputs)))

def softmax_rows(scores):
    row_max = lax.optimization_barrier(jnp.max(scores, axis=-1, keepdims=True))
    raised = jnp.exp(scores - row_max)
    return raised / lax.optimization_barrier(jnp.sum(raised, axis=-1, keepdims=True))

def split_heads(normed, weight):
    stacked = low(low_back(jnp.einsum('fcpd,dke->kfcpe', normed, weight, precision=PRECISE)))
    shape = stacked.shape[1:4] + (HEADS, HEAD_DIM)
    return (stacked[0].reshape(shape), stacked[1].reshape(shape), stacked[2].reshape(shape))

def spatial_frame(block):
    queries, keyset, values = block
    scores = low_back(jnp.einsum('cqhe,ckhe->chqk', queries, keyset, precision=PRECISE) * SCORE_SCALE)
    shares = softmax_rows(scores)
    return jnp.einsum('chqk,ckhe->cqhe', low(shares), values, precision=PRECISE)

def forward(frames_f, gain_all, bias_all, table_all, space_in, space_out, time_in, time_out, expand_f, shrink_f, action_codes, clip_length):
    frame_index = jnp.arange(FRAMES)
    valid = (frame_index[:, None] < clip_length[None, :]).astype(jnp.float32)[:, :, None, None]
    start = valid * (frames_f + table_all[action_codes][:, :, None, :])
    normed = low(layer_norm(start, gain_all[0], bias_all[0]))
    queries, keyset, values = split_heads(normed, space_in)
    attended = lax.map(jax.checkpoint(spatial_frame), (queries, keyset, values))
    attended = low(low_back(attended)).reshape(FRAMES, CLIPS, POS, D)
    first = start + low_back(jnp.einsum('fcpe,ed->fcpd', attended, space_out, precision=PRECISE))
    normed = low(layer_norm(first, gain_all[1], bias_all[1]))
    queries, keyset, values = split_heads(normed, time_in)
    scores = low_back(jnp.einsum('tcphe,ucphe->cphtu', queries, keyset, precision=PRECISE) * SCORE_SCALE)
    allowed = (frame_index[None, :, None] >= frame_index[None, None, :]) & (frame_index[None, None, :] < clip_length[:, None, None])
    scores = jnp.where(allowed[:, None, None], scores, MASKED_SCORE)
    shares = softmax_rows(scores)
    attended = jnp.einsum('cphtu,ucphe->tcphe', low(shares), values, precision=PRECISE)
    attended = low(low_back(attended)).reshape(FRAMES, CLIPS, POS, D)
    second = first + low_back(jnp.einsum('fcpe,ed->fcpd', attended, time_out, precision=PRECISE))
    normed = low(layer_norm(second, gain_all[2], bias_all[2]))
    expanded = low_back(jnp.einsum('fcpd,dh->fcph', normed, expand_f, precision=PRECISE))
    hidden = low(gelu_tanh(expanded))
    third = second + low_back(jnp.einsum('fcph,hd->fcpd', hidden, shrink_f, precision=PRECISE))
    return valid * third

def reference(frames_in, action_codes, clip_length, norm_gain, norm_bias, action_table, spatialin, spatialout, temporalin, temporalout, expand, shrink, out_grad):

    def wrapped(frames_f, gain_all, bias_all, table_all, space_in, space_out, time_in, time_out, expand_f, shrink_f):
        return forward(frames_f, gain_all, bias_all, table_all, space_in, space_out, time_in, time_out, expand_f, shrink_f, action_codes, clip_length)
    result, pullback = jax.vjp(wrapped, frames_in.astype(jnp.float32), norm_gain, norm_bias, action_table, spatialin.astype(jnp.float32), spatialout.astype(jnp.float32), temporalin.astype(jnp.float32), temporalout.astype(jnp.float32), expand.astype(jnp.float32), shrink.astype(jnp.float32))
    grads = pullback(out_grad.astype(jnp.float32))
    return (result.astype(jnp.bfloat16), grads[0], grads[1], grads[2], grads[3], grads[4], grads[5], grads[6], grads[7], grads[8], grads[9])
```

```python
import functools

import jax
import jax.numpy as jnp
from jax import lax
from jax.experimental import pallas as pl
from jax.experimental.pallas import tpu as pltpu
from jax.sharding import PartitionSpec as P

HEAD_DIM = 64


EPSILON = 1e-05
SCORE_SCALE = 0.125
MASKED_SCORE = -1e30
PRECISE = lax.Precision.HIGHEST
GELU_COEFF = 0.7978845608028654


def layer_norm(values, gain_row, bias_row):
    row_mean = jnp.mean(values, axis=-1, keepdims=True)
    centred = values - row_mean
    row_var = jnp.mean(centred * centred, axis=-1, keepdims=True)
    return centred * lax.rsqrt(row_var + EPSILON) * gain_row + bias_row


def gelu_tanh(inputs):
    return (
        0.5 * inputs * (1.0 + jnp.tanh(GELU_COEFF * (inputs + 0.044715 * inputs * inputs * inputs)))
    )


def gather_weights(small, large):
    small_full = (
        lax.all_gather(small[0], ("space", "head"), axis=1, tiled=True),
        lax.all_gather(small[1], ("space", "head"), axis=1, tiled=True),
        lax.all_gather(small[2], ("space", "head"), axis=1, tiled=True),
    )
    large_full = (
        lax.all_gather(large[0], "space", axis=0, tiled=True),
        lax.all_gather(large[1], "space", axis=1, tiled=True),
        lax.all_gather(large[2], "space", axis=0, tiled=True),
        lax.all_gather(large[3], "space", axis=1, tiled=True),
        lax.all_gather(large[4], "space", axis=0, tiled=True),
        lax.all_gather(large[5], "space", axis=1, tiled=True),
    )
    return (small_full, large_full)


def norm_step(inputs, gain_row, bias_row):
    normed, pullback = jax.vjp(layer_norm, inputs, gain_row, bias_row)
    whole = lax.all_gather(normed.astype(jnp.bfloat16), "head", axis=0, tiled=True)
    return (whole, pullback)


def cot_whole(grad_rows):
    return lax.all_gather(grad_rows.astype(jnp.bfloat16), "head", axis=0, tiled=True)


def input_total(partial_value):
    return lax.psum_scatter(
        partial_value.astype(jnp.bfloat16), "head", scatter_dimension=0, tiled=True
    ).astype(jnp.float32)


def heads_total(left, weight):
    return lax.psum_scatter(
        jnp.einsum("fcpe,ed->fcpd", left, weight, preferred_element_type=jnp.float32).astype(
            jnp.bfloat16
        ),
        "head",
        scatter_dimension=0,
        tiled=True,
    ).astype(jnp.float32)


def project_in(whole, weight):
    stacked = jnp.einsum(
        "fcpd,dke->kfcpe", whole, weight, preferred_element_type=jnp.float32
    ).astype(jnp.bfloat16)
    return (stacked[0], stacked[1], stacked[2])


def raw_scores(queries, keyset, form, allowed):
    key_form = form.replace("q", "k")
    scores = (
        jnp.einsum(
            form + "," + key_form + "->bhqk", queries, keyset, preferred_element_type=jnp.float32
        )
        * SCORE_SCALE
    )
    if allowed is not None:
        scores = jnp.where(allowed, scores, MASKED_SCORE)
    return scores


def attend(queries, keyset, values, form, allowed):
    key_form = form.replace("q", "k")
    scores = raw_scores(queries, keyset, form, allowed)
    row_max = jnp.max(scores, axis=-1, keepdims=True)
    log_total = row_max + jnp.log(jnp.sum(jnp.exp(scores - row_max), axis=-1, keepdims=True))
    shares = jnp.exp(scores - log_total).astype(jnp.bfloat16)
    output = jnp.einsum(
        "bhqk," + key_form + "->" + form, shares, values, preferred_element_type=jnp.float32
    )
    return (output.astype(jnp.bfloat16), log_total)


def attend_back(queries, keyset, values, log_total, output_grad, form, allowed):
    key_form = form.replace("q", "k")
    shares = jnp.exp(raw_scores(queries, keyset, form, allowed) - log_total)
    value_grad = jnp.einsum(
        "bhqk," + form + "->" + key_form,
        shares.astype(jnp.bfloat16),
        output_grad,
        preferred_element_type=jnp.float32,
    )
    share_grad = jnp.einsum(
        form + "," + key_form + "->bhqk", output_grad, values, preferred_element_type=jnp.float32
    )
    score_grad = (
        shares * (share_grad - jnp.sum(share_grad * shares, axis=-1, keepdims=True))
    ).astype(jnp.bfloat16)
    query_grad = (
        jnp.einsum(
            "bhqk," + key_form + "->" + form, score_grad, keyset, preferred_element_type=jnp.float32
        )
        * SCORE_SCALE
    )
    key_grad = (
        jnp.einsum(
            "bhqk," + form + "->" + key_form,
            score_grad,
            queries,
            preferred_element_type=jnp.float32,
        )
        * SCORE_SCALE
    )
    return (
        query_grad.astype(jnp.bfloat16),
        key_grad.astype(jnp.bfloat16),
        value_grad.astype(jnp.bfloat16),
    )


def general_shards(
    frames_in,
    action_codes,
    clip_length,
    norm_gain,
    norm_bias,
    action_table,
    spatialin,
    spatialout,
    temporalin,
    temporalout,
    expand,
    shrink,
    out_grad,
):
    head_count = lax.axis_size("head")
    frames_local, clip_count, pos_local, width = frames_in.shape
    frames_total = frames_local * head_count
    local_width = spatialin.shape[2]
    heads_local = local_width // HEAD_DIM
    frame_index = jnp.arange(frames_total)
    local_index = lax.axis_index("head") * frames_local + jnp.arange(frames_local)
    valid_local = (local_index[:, None] < clip_length[None, :]).astype(jnp.float32)[
        :, :, None, None
    ]
    allowed = (frame_index[None, :, None] >= frame_index[None, None, :]) & (
        frame_index[None, None, :] < clip_length[:, None, None]
    )
    allowed = jnp.broadcast_to(
        allowed[:, None, None], (clip_count, pos_local, 1, frames_total, frames_total)
    )
    allowed = allowed.reshape(clip_count * pos_local, 1, frames_total, frames_total)
    small_full, large_full = gather_weights(
        (norm_gain, norm_bias, action_table),
        (spatialin, spatialout, temporalin, temporalout, expand, shrink),
    )
    gain_full, bias_full, table_full = small_full
    space_in, space_out, time_in, time_out, expand_full, shrink_full = large_full
    code_hot = (action_codes[:, :, None] == jnp.arange(table_full.shape[0])[None, None, :]).astype(
        jnp.float32
    )
    embedded = jnp.einsum("fca,ad->fcd", code_hot, table_full, precision=PRECISE)
    start = valid_local * (frames_in.astype(jnp.float32) + embedded[:, :, None, :])
    whole_one, pull_one = norm_step(start, gain_full[0], bias_full[0])
    space_query, space_keys, space_values = project_in(whole_one, space_in)
    flat_shape = (frames_total * clip_count, pos_local, local_width)
    moved = (
        lax.all_to_all(
            space_query.reshape(flat_shape), "space", split_axis=0, concat_axis=1, tiled=True
        ),
        lax.all_to_all(
            space_keys.reshape(flat_shape), "space", split_axis=0, concat_axis=1, tiled=True
        ),
        lax.all_to_all(
            space_values.reshape(flat_shape), "space", split_axis=0, concat_axis=1, tiled=True
        ),
    )
    block_rows = moved[0].shape[0]
    block_cols = moved[0].shape[1]
    frame_shape = (block_rows, block_cols, heads_local, HEAD_DIM)
    frame_query = moved[0].reshape(frame_shape)
    frame_keys = moved[1].reshape(frame_shape)
    frame_values = moved[2].reshape(frame_shape)
    frame_out, frame_total = attend(frame_query, frame_keys, frame_values, "bqhe", None)
    returned = lax.all_to_all(
        frame_out.reshape(block_rows, block_cols, local_width),
        "space",
        split_axis=1,
        concat_axis=0,
        tiled=True,
    )
    space_attended = returned.reshape(frames_total, clip_count, pos_local, local_width)
    first = start + heads_total(space_attended, space_out)
    whole_two, pull_two = norm_step(first, gain_full[1], bias_full[1])
    time_query, time_keys, time_values = project_in(whole_two, time_in)
    time_shape = (frames_total, clip_count * pos_local, heads_local, HEAD_DIM)
    time_query = time_query.reshape(time_shape)
    time_keys = time_keys.reshape(time_shape)
    time_values = time_values.reshape(time_shape)
    time_out_rows, time_total = attend(time_query, time_keys, time_values, "qbhe", allowed)
    time_attended = time_out_rows.reshape(frames_total, clip_count, pos_local, local_width)
    second = first + heads_total(time_attended, time_out)
    whole_three, pull_three = norm_step(second, gain_full[2], bias_full[2])
    expanded = jnp.einsum(
        "fcpd,dh->fcph", whole_three, expand_full, preferred_element_type=jnp.float32
    )
    activated, gelu_pull = jax.vjp(gelu_tanh, expanded)
    activated_low = activated.astype(jnp.bfloat16)
    third = second + heads_total(activated_low, shrink_full)
    frames_out = (valid_local * third).astype(jnp.bfloat16)
    small_full, large_full = gather_weights(
        (norm_gain, norm_bias, action_table),
        (spatialin, spatialout, temporalin, temporalout, expand, shrink),
    )
    space_in, space_out, time_in, time_out, expand_full, shrink_full = large_full
    grad_third = valid_local * out_grad.astype(jnp.float32)
    cot_three = cot_whole(grad_third)
    shrink_part = jnp.einsum(
        "fcph,fcpd->hd", activated_low, cot_three, preferred_element_type=jnp.float32
    )
    act_grad = jnp.einsum(
        "fcpd,hd->fcph", cot_three, shrink_full, preferred_element_type=jnp.float32
    )
    pre_grad = gelu_pull(act_grad)[0].astype(jnp.bfloat16)
    expand_part = jnp.einsum(
        "fcpd,fcph->dh", whole_three, pre_grad, preferred_element_type=jnp.float32
    )
    normed_grad = input_total(
        jnp.einsum("fcph,dh->fcpd", pre_grad, expand_full, preferred_element_type=jnp.float32)
    )
    input_three, gain_three, bias_three = pull_three(normed_grad)
    grad_second = grad_third + input_three
    cot_two = cot_whole(grad_second)
    time_out_part = jnp.einsum(
        "fcpe,fcpd->ed", time_attended, cot_two, preferred_element_type=jnp.float32
    )
    time_grad = jnp.einsum(
        "fcpd,ed->fcpe", cot_two, time_out, preferred_element_type=jnp.float32
    ).astype(jnp.bfloat16)
    time_grads = attend_back(
        time_query,
        time_keys,
        time_values,
        time_total,
        time_grad.reshape(time_shape),
        "qbhe",
        allowed,
    )
    stacked_grad = jnp.stack(
        [member.reshape(frames_total, clip_count, pos_local, local_width) for member in time_grads]
    )
    time_in_part = jnp.einsum(
        "fcpd,kfcpe->dke", whole_two, stacked_grad, preferred_element_type=jnp.float32
    )
    normed_grad = input_total(
        jnp.einsum("kfcpe,dke->fcpd", stacked_grad, time_in, preferred_element_type=jnp.float32)
    )
    input_two, gain_two, bias_two = pull_two(normed_grad)
    grad_first = grad_second + input_two
    cot_one = cot_whole(grad_first)
    space_out_part = jnp.einsum(
        "fcpe,fcpd->ed", space_attended, cot_one, preferred_element_type=jnp.float32
    )
    space_grad = jnp.einsum(
        "fcpd,ed->fcpe", cot_one, space_out, preferred_element_type=jnp.float32
    ).astype(jnp.bfloat16)
    frame_grad = lax.all_to_all(
        space_grad.reshape(flat_shape), "space", split_axis=0, concat_axis=1, tiled=True
    ).reshape(frame_shape)
    query_grad, keys_grad, values_grad = attend_back(
        frame_query, frame_keys, frame_values, frame_total, frame_grad, "bqhe", None
    )
    block_shape = (block_rows, block_cols, local_width)
    back_grads = (
        lax.all_to_all(
            query_grad.reshape(block_shape), "space", split_axis=1, concat_axis=0, tiled=True
        ),
        lax.all_to_all(
            keys_grad.reshape(block_shape), "space", split_axis=1, concat_axis=0, tiled=True
        ),
        lax.all_to_all(
            values_grad.reshape(block_shape), "space", split_axis=1, concat_axis=0, tiled=True
        ),
    )
    stacked_grad = jnp.stack(
        [member.reshape(frames_total, clip_count, pos_local, local_width) for member in back_grads]
    )
    space_in_part = jnp.einsum(
        "fcpd,kfcpe->dke", whole_one, stacked_grad, preferred_element_type=jnp.float32
    )
    normed_grad = input_total(
        jnp.einsum("kfcpe,dke->fcpd", stacked_grad, space_in, preferred_element_type=jnp.float32)
    )
    input_one, gain_one, bias_one = pull_one(normed_grad)
    grad_start = grad_first + input_one
    frames_grad = valid_local * grad_start
    table_part = jnp.einsum(
        "fca,fcd->ad", code_hot, jnp.sum(frames_grad, axis=2), precision=PRECISE
    )
    gain_grad, bias_grad, table_grad = (
        lax.psum_scatter(
            jnp.stack([gain_one, gain_two, gain_three]),
            ("space", "head"),
            scatter_dimension=1,
            tiled=True,
        ),
        lax.psum_scatter(
            jnp.stack([bias_one, bias_two, bias_three]),
            ("space", "head"),
            scatter_dimension=1,
            tiled=True,
        ),
        lax.psum_scatter(table_part, ("space", "head"), scatter_dimension=1, tiled=True),
    )
    weight_grads = (
        lax.psum_scatter(space_in_part, "space", scatter_dimension=0, tiled=True),
        lax.psum_scatter(space_out_part, "space", scatter_dimension=1, tiled=True),
        lax.psum_scatter(time_in_part, "space", scatter_dimension=0, tiled=True),
        lax.psum_scatter(time_out_part, "space", scatter_dimension=1, tiled=True),
        lax.psum_scatter(expand_part, "space", scatter_dimension=0, tiled=True),
        lax.psum_scatter(shrink_part, "space", scatter_dimension=1, tiled=True),
    )
    return (
        frames_out,
        frames_grad,
        gain_grad,
        bias_grad,
        table_grad,
        weight_grads[0],
        weight_grads[1],
        weight_grads[2],
        weight_grads[3],
        weight_grads[4],
        weight_grads[5],
    )


ORDER = (0, 4, 2, 6, 1, 5, 3, 7)
BLOCKS = len(ORDER)
PLACE = tuple(ORDER.index(mask) for mask in range(BLOCKS))
ROUND = 4
ONE_VMEM = pl.BlockSpec(memory_space=pltpu.VMEM)
ONE_SMEM = pl.BlockSpec(memory_space=pltpu.SMEM)
MIB = 1024 * 1024
COST = 1500 * 1024
LOW = jnp.bfloat16
WIDE = jnp.float32


def swap(value, axis, mask):
    return lax.ppermute(value, axis, [(i, i ^ mask) for i in range(lax.axis_size(axis))])


def across(mine):
    return [mine, swap(mine, "head", 2)]


def head_gather(mine):
    _, far = across(mine)
    return [mine, swap(mine, "head", 1), far, swap(far, "head", 1)]


def head_scatter(parts):
    far = parts[2] + swap(parts[3], "head", 1)
    return [parts[0], swap(parts[1], "head", 1), swap(far, "head", 2)]


def after(value, *others):
    return lax.optimization_barrier((value, *others))[0]


def moved(value, axis, mask, begin=(), end=()):
    return after(swap(after(value, *begin), axis, mask), *end)


def doubled(rows, mask, begin=(), end=()):
    return jnp.concatenate([rows, moved(rows, "space", mask, begin, end)], axis=0)


def add_low(first, second):
    return (first.astype(WIDE) + second.astype(WIDE)).astype(LOW)


def halved(line, mask, begin=(), end=()):
    half = line.shape[0] // 2
    return line[:half], moved(line[half:], "space", mask, begin, end)


def to_partners(packed):
    return lax.all_to_all(packed, "space", split_axis=0, concat_axis=0, tiled=True)


WEIGHTS_OF = {"space_forward": 3, "space_back": 5, "time_forward": 8, "time_back": 10, "hidden": 6, "back_third": 3}


def run(body, outs, args, specs, vmem=None):
    single = not isinstance(outs, (list, tuple))
    name = getattr(body, "func", body).__name__.removesuffix("_body")
    return pl.pallas_call(
        body,
        out_shape=outs,
        in_specs=specs,
        out_specs=ONE_VMEM if single else [ONE_VMEM] * len(outs),
        cost_estimate=pl.CostEstimate(
            flops=0, bytes_accessed=COST * WEIGHTS_OF.get(name, 1), transcendentals=0
        ),
        compiler_params=pltpu.CompilerParams(vmem_limit_bytes=vmem or 12 * MIB),
        name=name,
    )(*args)


def shape_of(dims, dtype):
    return jax.ShapeDtypeStruct(tuple(dims), dtype)


def feature_block(place, step):
    return pl.ds(pl.multiple_of(place * step, step), step)


def partner(mask):
    return lax.axis_index("space") ^ mask


def frame_valid(lengths, frames, mask):
    clips = lengths.shape[0]
    frame = lax.axis_index("head") * (frames // clips) + partner(mask) // clips
    return jnp.where(frame < lengths[partner(mask) % clips], 1.0, 0.0).astype(WIDE)


def normed_parts(values):
    centred = values - jnp.mean(values, axis=-1, keepdims=True)
    scale = lax.rsqrt(jnp.mean(centred * centred, axis=-1, keepdims=True) + EPSILON)
    return centred * scale, scale


def norm_back(values, grad, gain_row):
    unit, scale = normed_parts(values)
    scaled = grad * gain_row
    out = scale * (
        scaled
        - jnp.mean(scaled, axis=-1, keepdims=True)
        - unit * jnp.mean(scaled * unit, axis=-1, keepdims=True)
    )
    return (
        out,
        jnp.sum(grad * unit, axis=0, keepdims=True),
        jnp.sum(grad, axis=0, keepdims=True),
    )


def store_for(ref, rows, mask):
    step = rows.shape[-1] // BLOCKS
    for i in range(BLOCKS):
        j = i ^ PLACE[mask]
        ref[partner(mask), :, i * step : (i + 1) * step] = rows[:, j * step : (j + 1) * step]


def pack_frames_body(frames, out):
    step = frames.shape[-1] // BLOCKS
    for mask in range(BLOCKS):
        for i in range(BLOCKS):
            source = partner(ORDER[i ^ PLACE[mask]])
            place = slice(i * step, (i + 1) * step)
            out[partner(mask), :, place] = frames[partner(mask), :, feature_block(source, step)]


def order_inputs_body(lengths, frames, grad, frames_out, grad_out):
    step = frames.shape[-1] // BLOCKS

    def one(mask, carry):
        valid = frame_valid(lengths, BLOCKS, mask)
        for i in range(BLOCKS):
            source = feature_block(partner(ORDER[i]), step)
            place = slice(i * step, (i + 1) * step)
            frames_out[mask, :, place] = frames[partner(mask), :, source]
            kept = grad[partner(mask), :, source].astype(WIDE) * valid
            grad_out[mask, :, place] = kept.astype(LOW)
        return carry

    lax.fori_loop(0, BLOCKS, one, 0)


def start_rows(rows, codes, lengths, small, mask):
    embedded = small[pl.ds(6 + codes[partner(mask)], 1), :]
    return frame_valid(lengths, BLOCKS, mask) * (rows.astype(WIDE) + embedded)


def frame_norm_body(codes, lengths, small, blocks, normed, start):
    rows = blocks.shape[1]
    for b in range(BLOCKS):
        values = start_rows(blocks[partner(b)], codes, lengths, small, 0)
        start[b * rows : (b + 1) * rows, :] = values
        unit, _ = normed_parts(values)
        normed[b * rows : (b + 1) * rows, :] = (unit * small[0:1, :] + small[3:4, :]).astype(LOW)


def spread_body(first, second, out):
    rows = out.shape[1]
    for mask in range(BLOCKS):
        part = slice(mask * rows, (mask + 1) * rows)
        total = first[part, :].astype(WIDE) + second[part, :].astype(WIDE)
        store_for(out, total.astype(LOW), mask)


def join_norm_body(codes, lengths, small, frames, blocks, whole, normed):
    for b in range(BLOCKS):
        values = start_rows(frames[b], codes, lengths, small, b) + blocks[partner(b)].astype(WIDE)
        whole[b] = values
        unit, _ = normed_parts(values)
        normed[b] = (unit * small[1:2, :] + small[4:5, :]).astype(LOW)


def add_norm_body(small, before, first, second, third, whole, normed):
    def one(b, carry):
        values = before[b] + (
            first[b].astype(WIDE) + second[b].astype(WIDE) + third[b].astype(WIDE)
        )
        whole[b] = values
        unit, _ = normed_parts(values)
        normed[b] = (unit * small[2:3, :] + small[5:6, :]).astype(LOW)
        return carry

    lax.fori_loop(0, BLOCKS, one, 0)


def finish_forward_body(lengths, before, first, second, out):
    step = out.shape[-1] // BLOCKS

    def one(b, carry):
        values = before[b] + (first[b].astype(WIDE) + second[b].astype(WIDE))
        values = (frame_valid(lengths, BLOCKS, b) * values).astype(LOW)
        for i in range(BLOCKS):
            place = feature_block(partner(ORDER[i]), step)
            out[partner(b), :, place] = values[:, i * step : (i + 1) * step]
        return carry

    lax.fori_loop(0, BLOCKS, one, 0)


def back_third_body(small, grad, values, first, second, total_out, low_out, sums):
    sums[...] = jnp.zeros_like(sums)

    def one(b, carry):
        normed_grad = first[b].astype(WIDE) + second[b].astype(WIDE)
        out, gain, bias = norm_back(values[b], normed_grad, small[2:3, :])
        total = grad[b].astype(WIDE) + out
        total_out[b] = total
        low_out[b] = total.astype(LOW)
        sums[0:1, :] += gain
        sums[1:2, :] += bias
        return carry

    lax.fori_loop(0, BLOCKS, one, 0)


def back_second_body(codes, lengths, small, grad, values, first, second, third, total_out, sums, table, packed):
    sums[...] = jnp.zeros_like(sums)
    table[...] = jnp.zeros_like(table)
    for b in range(BLOCKS):
        normed_grad = first[b].astype(WIDE) + second[b].astype(WIDE) + third[b].astype(WIDE)
        out, gain, bias = norm_back(values[b], normed_grad, small[1:2, :])
        total = grad[b] + out
        total_out[b] = total
        store_for(packed, total.astype(LOW), b)
        sums[0:1, :] += gain
        sums[1:2, :] += bias
        row = pl.ds(codes[partner(b)], 1)
        table[row, :] += frame_valid(lengths, BLOCKS, b) * jnp.sum(total, axis=0, keepdims=True)


def back_first_body(codes, lengths, small, values, first, second, sums, table, packed):
    sums[...] = jnp.zeros_like(sums)
    table[...] = jnp.zeros_like(table)
    rows = packed.shape[1]
    for b in range(BLOCKS):
        part = slice(b * rows, (b + 1) * rows)
        normed_grad = first[part, :].astype(WIDE) + second[part, :].astype(WIDE)
        out, gain, bias = norm_back(values[part, :], normed_grad, small[0:1, :])
        store_for(packed, out.astype(LOW), b)
        sums[0:1, :] += gain
        sums[1:2, :] += bias
        row = pl.ds(codes[partner(0)], 1)
        table[row, :] += frame_valid(lengths, BLOCKS, 0) * jnp.sum(out, axis=0, keepdims=True)


def collect_body(blocks, out):
    rows = blocks.shape[1]
    for b in range(BLOCKS):
        out[b * rows : (b + 1) * rows, :] = blocks[partner(b)]


def finish_back_body(lengths, grad, blocks, out):
    step = out.shape[-1] // BLOCKS
    for b in range(BLOCKS):
        values = frame_valid(lengths, BLOCKS, b) * (grad[b] + blocks[partner(b)].astype(WIDE))
        for i in range(BLOCKS):
            place = feature_block(partner(ORDER[i]), step)
            out[partner(b), :, place] = values[:, i * step : (i + 1) * step]


def matmul(left, right):
    return lax.dot_general(left, right, (((1,), (0,)), ((), ())), preferred_element_type=WIDE)


def matmul_t(left, right):
    return lax.dot_general(left, right, (((1,), (1,)), ((), ())), preferred_element_type=WIDE)


def matmul_tn(left, right):
    return lax.dot_general(left, right, (((0,), (0,)), ((), ())), preferred_element_type=WIDE)


def head_mask(width, head):
    lane = lax.broadcasted_iota(jnp.int32, (1, width), 1)
    return (lane // HEAD_DIM) == head


def pick(values, mask):
    return jnp.where(mask, values, jnp.zeros_like(values))


def attention_rows(projected, allowed):
    width = projected.shape[1] // 3
    queries = projected[:, :width] * jnp.asarray(SCORE_SCALE, LOW)
    keyset = projected[:, width : 2 * width]
    values = projected[:, 2 * width :]
    lane = lax.broadcasted_iota(jnp.int32, (1, 128), 1)
    output = jnp.zeros((projected.shape[0], width), WIDE)
    totals = jnp.zeros((projected.shape[0], 128), WIDE)
    for head in range(width // HEAD_DIM):
        mask = head_mask(width, head)
        scores = matmul_t(pick(queries, mask), keyset)
        if allowed is not None:
            scores = jnp.where(allowed, scores, MASKED_SCORE)
        row_max = jnp.max(scores, axis=-1, keepdims=True)
        raised = jnp.exp(scores - row_max)
        total = jnp.sum(raised, axis=-1, keepdims=True)
        shares = (raised * (1.0 / total)).astype(LOW)
        output = output + matmul(shares, pick(values, mask))
        totals = jnp.where(lane == head, row_max + jnp.log(total), totals)
    return output.astype(LOW), totals


def attention_rows_back(projected, totals, output_grad, allowed):
    width = projected.shape[1] // 3
    queries = projected[:, :width] * jnp.asarray(SCORE_SCALE, LOW)
    keyset = projected[:, width : 2 * width]
    values = projected[:, 2 * width :]
    scaled_keys = keyset * jnp.asarray(SCORE_SCALE, LOW)
    shape = (projected.shape[0], width)
    query_grad, key_grad, value_grad = (jnp.zeros(shape, WIDE) for _ in range(3))
    for head in range(width // HEAD_DIM):
        mask = head_mask(width, head)
        own_queries = pick(queries, mask)
        own_grad = pick(output_grad, mask)
        scores = matmul_t(own_queries, keyset)
        if allowed is not None:
            scores = jnp.where(allowed, scores, MASKED_SCORE)
        shares = jnp.exp(scores - totals[:, head : head + 1])
        value_grad = value_grad + matmul_tn(shares.astype(LOW), own_grad)
        share_grad = matmul_t(own_grad, values)
        score_grad = shares * (share_grad - jnp.sum(share_grad * shares, axis=-1, keepdims=True))
        score_grad = score_grad.astype(LOW)
        query_grad = query_grad + matmul(score_grad, pick(scaled_keys, mask))
        key_grad = key_grad + matmul_tn(score_grad, own_queries)
    return jnp.concatenate(
        [query_grad.astype(LOW), key_grad.astype(LOW), value_grad.astype(LOW)], axis=1
    )


def enter_rows(rows, parts, columns):
    depth = parts[0].shape[0]
    total = matmul(rows[:, :depth], parts[0][:, columns])
    for i, part in enumerate(parts[1:], 1):
        total = total + matmul(rows[:, i * depth : (i + 1) * depth], part[:, columns])
    return total


def leave_rows(sides, columns, store):
    depth = sides[0][1][0].shape[0]
    for i in range(len(sides[0][1])):
        total = matmul_t(sides[0][0], sides[0][1][i][:, columns])
        for values, parts in sides[1:]:
            total = total + matmul_t(values, parts[i][:, columns])
        store(slice(i * depth, (i + 1) * depth), total.astype(LOW))


def space_forward_body(rows, *refs):
    sides = (refs[0:2], refs[2:4])
    projected_out, output_out, totals_out = refs[4:6], refs[6:8], refs[8:10]
    part_out = refs[10]
    width = output_out[0].shape[1]
    leaving = []
    for side, parts in enumerate(sides):
        projected = enter_rows(rows, parts, slice(0, 3 * width)).astype(LOW)
        projected_out[side][...] = projected
        output, totals = attention_rows(projected, None)
        output_out[side][...] = output
        totals_out[side][...] = totals
        leaving.append((output, parts))

    def store(place, values):
        part_out[:, place] = values

    leave_rows(leaving, slice(3 * width, 4 * width), store)


def space_back_body(rows, *refs):
    sides = (refs[0:2], refs[2:4])
    projected, totals, grads_out = refs[4:6], refs[6:8], refs[8:10]
    part_out = refs[10]
    width = projected[0].shape[1] // 3
    leaving = []
    for side, parts in enumerate(sides):
        output_grad = enter_rows(rows, parts, slice(3 * width, 4 * width)).astype(LOW)
        grads = attention_rows_back(projected[side][...], totals[side][...], output_grad, None)
        grads_out[side][...] = grads
        leaving.append((grads, parts))

    def store(place, values):
        part_out[:, place] = values

    leave_rows(leaving, slice(0, 3 * width), store)


def time_allowed(lengths, clip, frames_local, positions):
    clips = lengths.shape[0]
    count = ROUND * frames_local * positions
    head_at, frame_at = lax.axis_index("head"), partner(0) // clips

    def split(shape, axis):
        row = lax.broadcasted_iota(jnp.int32, shape, axis)
        group = row // (frames_local * positions)
        local = (row // positions) % frames_local
        return (group ^ head_at) * frames_local + (local ^ frame_at), row % positions

    query_frame, query_pos = split((count, 1), 0)
    key_frame, key_pos = split((1, count), 1)
    length = lengths[(partner(0) % clips) ^ clip]
    return (query_pos == key_pos) & (query_frame >= key_frame) & (key_frame < length)


PART = 16


def time_groups(ref):
    return [(c, p) for c in range(ref.shape[1]) for p in range(0, ref.shape[2], PART)]


def join_rows(refs, group):
    c, p = group
    return jnp.concatenate(
        [ref[:, c, p : p + PART, :].reshape(ref.shape[0] * PART, ref.shape[3]) for ref in refs], axis=0
    )


def split_rows(refs, group, values, place=slice(None)):
    c, p = group
    rows = values.shape[0] // len(refs)
    for i, ref in enumerate(refs):
        part = values[i * rows : (i + 1) * rows].reshape(ref.shape[0], PART, values.shape[1])
        ref[:, c, p : p + PART, place] = part


def time_forward_body(lengths, *refs):
    parts, refs = refs[:2], refs[2:]
    rows, projected_out, output_out, totals_out, part_out = (refs[i : i + 4] for i in range(0, 20, 4))
    frames_local, width = rows[0].shape[0], output_out[0].shape[3]
    for group in time_groups(rows[0]):
        joined = join_rows(rows, group)
        projected = enter_rows(joined, parts, slice(0, 3 * width)).astype(LOW)
        split_rows(projected_out, group, projected)
        allowed = time_allowed(lengths, group[0], frames_local, PART)
        output, totals = attention_rows(projected, allowed)
        split_rows(output_out, group, output)
        split_rows(totals_out, group, totals)
        leave_rows(
            [(output, parts)],
            slice(3 * width, 4 * width),
            lambda place, values, group=group: split_rows(part_out, group, values, place),
        )


def time_back_body(lengths, *refs):
    parts, refs = refs[:2], refs[2:]
    rows, projected, totals, grads_out, part_out = (refs[i : i + 4] for i in range(0, 20, 4))
    frames_local, width = rows[0].shape[0], projected[0].shape[3] // 3
    for group in time_groups(rows[0]):
        allowed = time_allowed(lengths, group[0], frames_local, PART)
        joined = join_rows(rows, group)
        output_grad = enter_rows(joined, parts, slice(3 * width, 4 * width)).astype(LOW)
        grads = attention_rows_back(
            join_rows(projected, group), join_rows(totals, group), output_grad, allowed
        )
        split_rows(grads_out, group, grads)
        leave_rows(
            [(grads, parts)],
            slice(0, 3 * width),
            lambda place, values, group=group: split_rows(part_out, group, values, place),
        )


def space_forward(rows, weights):
    count, width = rows.shape
    inner = weights[0].shape[1] // 4
    outs = [shape_of((count, 3 * inner), LOW)] * 2 + [shape_of((count, inner), LOW)] * 2
    outs += [shape_of((count, 128), WIDE)] * 2 + [shape_of((count, width), LOW)]
    results = run(space_forward_body, outs, (rows, *weights), [ONE_VMEM] * 5)
    return results[0:2], results[2:4], results[4:6], results[6]


def space_back(rows, weights, projected, totals):
    count, width = rows.shape
    inner = weights[0].shape[1] // 4
    outs = [shape_of((count, 3 * inner), LOW)] * 2 + [shape_of((count, width), LOW)]
    results = run(space_back_body, outs, (rows, *weights, *projected, *totals), [ONE_VMEM] * 9)
    return results[0:2], results[2]


def time_call(body, lengths, weights, groups, out_widths):
    args, outs = [lengths, *weights], []
    for group in groups:
        args += group
    for features, dtype in out_widths:
        outs += [shape_of((*groups[0][0].shape[:3], features), dtype)] * ROUND
    results = run(body, outs, args, [ONE_SMEM] + [ONE_VMEM] * (len(args) - 1), vmem=16 * MIB)
    return [results[i : i + ROUND] for i in range(0, len(results), ROUND)]


def hidden_body(normed, grad, *refs):
    sides, acts, pres = (refs[0:2], refs[2:4]), refs[4:6], refs[6:8]
    in_part, out_part = refs[8:]
    hidden = acts[0].shape[1]
    tile = 256
    for side, parts in enumerate(sides):
        for start in range(0, hidden, tile):
            enter = slice(start, start + tile)
            leave = slice(hidden + start, hidden + start + tile)
            value = enter_rows(normed, parts, enter)
            square = value * value
            curve = jnp.tanh(GELU_COEFF * (value + 0.044715 * square * value))
            half = 0.5 * (1.0 + curve)
            slope = half + 0.5 * value * (1.0 - curve * curve) * (
                GELU_COEFF * (1.0 + 3.0 * 0.044715 * square)
            )
            acts[side][:, enter] = (value * half).astype(LOW)
            pres[side][:, enter] = (enter_rows(grad, parts, leave) * slope).astype(LOW)
    for values, part, columns in (
        (pres, in_part, slice(0, hidden)),
        (acts, out_part, slice(hidden, 2 * hidden)),
    ):

        def store(place, total, part=part):
            part[:, place] = total

        leave_rows([(values[side][...], parts) for side, parts in enumerate(sides)], columns, store)


def hidden_call(normed, grad, weights):
    count, width = normed.shape
    hidden = weights[0].shape[1] // 2
    outs = [shape_of((count, hidden), LOW)] * 4 + [shape_of((count, width), LOW)] * 2
    results = run(hidden_body, outs, (normed, grad, *weights), [ONE_VMEM] * 6)
    return results[0:2], results[2:4], results[4], results[5]


def weight_grad_tile(counts, refs, start, tile, store):
    at, column = 0, 0
    for count in counts:
        lefts, rights = refs[at : at + count], refs[at + count : at + 2 * count]
        at += 2 * count
        total = matmul_tn(lefts[0][:, start : start + tile], rights[0][...])
        for left, right in zip(lefts[1:], rights[1:]):
            total = total + matmul_tn(left[:, start : start + tile], right[...])
        store(column, total.astype(LOW))
        column += total.shape[1]


def weight_grad_body(counts, half, *refs):
    out, tile = refs[-1], 256
    for row in range(0, out.shape[0], tile):

        def store(column, values, row=row):
            out[row : row + tile, column : column + values.shape[1]] = values

        weight_grad_tile(counts, refs, half * out.shape[0] + row, tile, store)


def weight_grad(pairs, half):
    args, counts = [], []
    for lefts, rights in pairs:
        args += [*lefts, *rights]
        counts.append(len(lefts))
    width = pairs[0][0][0].shape[1]
    columns = sum(rights[0].shape[1] for _, rights in pairs)
    body = functools.partial(weight_grad_body, tuple(counts), half)
    return run(body, shape_of((width // 2, columns), LOW), args, [ONE_VMEM] * len(args))


def small_block(norm_gain, norm_bias, action_table):
    mine = jnp.concatenate([norm_gain, norm_bias, action_table], axis=0)
    mine = jnp.pad(mine, ((0, 2), (0, 0)))
    rows, step = mine.shape
    start = lax.axis_index("head") * step
    block = lax.dynamic_update_slice(jnp.zeros((rows, ROUND * step), WIDE), mine, (0, start))
    return block + swap(block, "head", 1) + swap(block, "head", 2) + swap(block, "head", 3)


def small_line(block):
    block = block[None]
    return jnp.concatenate([block] + [swap(block, "space", mask) for mask in ORDER[1:4]], axis=0)


def small_whole(line):
    whole = doubled(line, 1)
    return jnp.transpose(whole, (1, 0, 2)).reshape(line.shape[1], BLOCKS * line.shape[2])


def small_scatter(sums):
    rows, width = sums.shape
    split = jnp.transpose(sums.reshape(rows, BLOCKS, width // BLOCKS), (1, 0, 2))
    line = split[:4] + swap(split[4:], "space", 1)
    block = line[0]
    for place in (1, 2, 3):
        block = block + swap(line[place], "space", ORDER[place])
    block = block + swap(block, "head", 1) + swap(block, "head", 2) + swap(block, "head", 3)
    step = block.shape[1] // ROUND
    return lax.dynamic_slice(block, (0, lax.axis_index("head") * step), (rows, step))


def shards(
    frames_in,
    action_codes,
    clip_length,
    norm_gain,
    norm_bias,
    action_table,
    spatialin,
    spatialout,
    temporalin,
    temporalout,
    expand,
    shrink,
    out_grad,
):
    frames_local, clips, pos_local, width = frames_in.shape
    local = (frames_local, clips, pos_local, width)
    rel_shape = (BLOCKS, pos_local, width)
    count = BLOCKS * pos_local
    inner = spatialin.shape[2]
    hidden = expand.shape[1]
    codes = action_codes.reshape(BLOCKS)
    scalars = (codes, clip_length)

    packed_shape = shape_of(rel_shape, LOW)
    flat_shape = shape_of((count, width), LOW)
    sums_shape = shape_of((8, width), WIDE)
    frames_flat = frames_in.reshape(rel_shape)

    packed = run(pack_frames_body, packed_shape, (frames_flat,), [ONE_VMEM])
    frame_blocks = to_partners(packed)
    block = small_block(norm_gain, norm_bias, action_table)
    space_rows = jnp.concatenate([spatialin.reshape(-1, 3 * inner), spatialout.T], axis=1)
    time_rows = jnp.concatenate([temporalin.reshape(-1, 3 * inner), temporalout.T], axis=1)
    hidden_rows = jnp.concatenate([expand, shrink.T], axis=1)
    line = small_line(block)
    space_far = doubled(space_rows, 4, (packed,), (line,))
    small = small_whole(line)
    normed, start = run(
        frame_norm_body,
        [flat_shape, shape_of((count, width), WIDE)],
        (*scalars, small, frame_blocks),
        [ONE_SMEM] * 2 + [ONE_VMEM] * 2,
    )
    space_line = doubled(space_far, 2, (), (normed,))
    time_far = moved(time_rows, "space", 4, (normed,))
    frames_rel, grad_low = run(
        order_inputs_body,
        [packed_shape] * 2,
        (clip_length, frames_flat, after(out_grad.reshape(rel_shape), normed)),
        [ONE_SMEM] + [ONE_VMEM] * 2,
    )
    normed_far = moved(normed, "head", 2, (), (time_far,))
    space_other = moved(space_line, "space", 1, (), (normed_far,))
    time_far = jnp.concatenate([time_rows, after(time_far, normed_far)], axis=0)
    time_line = doubled(time_far, 2, (space_line,))
    hidden_far = moved(hidden_rows, "space", 4, (time_far, space_line))
    grad_far = moved(grad_low.reshape(count, width), "head", 2, (normed_far,))
    space_own = [space_line, space_other]
    space_weights = space_own + [moved(part, "head", 1) for part in space_own]
    time_other = moved(time_line, "space", 1, (space_other,))

    far_kept = space_forward(after(normed_far, time_line), space_weights)
    own_kept = space_forward(after(normed, far_kept[3]), space_weights)
    hidden_far = jnp.concatenate([hidden_rows, after(hidden_far, own_kept[3])], axis=0)
    far_part = moved(far_kept[3], "head", 2, (), (own_kept[3],))
    packed = run(spread_body, packed_shape, (own_kept[3], far_part), [ONE_VMEM] * 2)
    spread = to_partners(packed)
    hidden_line = doubled(hidden_far, 2, (), (spread,))
    time_weights = [time_line, after(time_other, spread)]
    hidden_other = moved(hidden_line, "space", 1, (time_weights[1],))
    first, normed_two = run(
        join_norm_body,
        [shape_of(rel_shape, WIDE), packed_shape],
        (*scalars, small, frames_rel, spread),
        [ONE_SMEM] * 2 + [ONE_VMEM] * 3,
    )

    normed_two = head_gather(normed_two.reshape(local))
    normed_two[2] = after(normed_two[2], hidden_line)
    time_projected, time_output, time_totals, time_parts = time_call(
        time_forward_body,
        clip_length,
        time_weights,
        [normed_two],
        [(3 * inner, LOW), (inner, LOW), (128, WIDE), (width, LOW)],
    )
    parts = [part.reshape(rel_shape) for part in head_scatter(time_parts)]
    second, normed_three = run(
        add_norm_body,
        [shape_of(rel_shape, WIDE), packed_shape],
        (small, first, *parts),
        [ONE_VMEM] * 5,
    )

    hidden_own = [hidden_line, after(hidden_other, normed_three)]
    hidden_weights = hidden_own + [moved(part, "head", 1, (normed_three,)) for part in hidden_own]

    normed_three = across(normed_three.reshape(count, width))
    grad_third = [grad_low.reshape(count, width), grad_far]
    own_kept_three = hidden_call(normed_three[0], grad_third[0], hidden_weights)
    far_kept_three = hidden_call(
        after(normed_three[1], own_kept_three[2]), grad_third[1], hidden_weights
    )
    hidden_kept = [own_kept_three, far_kept_three]

    def hidden_part(side, half, *others):
        first = [after(kept[1][side], *others) for kept in hidden_kept]
        second = [kept[0][side] for kept in hidden_kept]
        return weight_grad([(normed_three, first), (grad_third, second)], half)

    beside_send = hidden_part(1, 1)
    own_send = hidden_part(0, 1, beside_send)
    beside_keep = hidden_part(1, 0, own_send)
    own_keep = hidden_part(0, 0, beside_keep)
    hidden_send = add_low(own_send, moved(beside_send, "head", 1, (), (own_keep,)))
    far_part = moved(far_kept_three[2], "head", 2, (), (own_keep,))
    total_second, low_second, sums_third = run(
        back_third_body,
        [shape_of(rel_shape, WIDE), packed_shape, sums_shape],
        (
            small,
            grad_low,
            second,
            *[part.reshape(rel_shape) for part in (own_kept_three[2], after(far_part, hidden_send))],
        ),
        [ONE_VMEM] * 5,
    )

    grad_two = head_gather(low_second.reshape(local))
    hidden_keep = add_low(own_keep, moved(beside_keep, "head", 1, (), (low_second,)))
    grad_two[2] = after(grad_two[2], hidden_keep)
    time_grads, time_parts = time_call(
        time_back_body,
        clip_length,
        time_weights,
        [grad_two, time_projected, time_totals],
        [(3 * inner, LOW), (width, LOW)],
    )
    hidden_got = moved(hidden_send, "space", 1)
    flat = lambda arrays: [a.reshape(count, a.shape[-1]) for a in arrays]
    time_keep, time_send = [
        weight_grad([(flat(normed_two), flat(time_grads)), (flat(grad_two), flat(time_output))], half)
        for half in (0, 1)
    ]
    parts = [part.reshape(rel_shape) for part in head_scatter(time_parts)]
    parts[2] = after(parts[2], time_keep, time_send)
    total_first, sums_second, table_first, packed = run(
        back_second_body,
        [shape_of(rel_shape, WIDE), sums_shape, sums_shape, packed_shape],
        (*scalars, small, total_second, first, *parts),
        [ONE_SMEM] * 2 + [ONE_VMEM] * 6,
    )

    grad_one = run(collect_body, flat_shape, (to_partners(packed),), [ONE_VMEM])
    hidden_sum = halved(add_low(hidden_keep, after(hidden_got, grad_one)), 2)
    grad_one = across(grad_one)
    time_got = moved(time_send, "space", 1, (hidden_sum[0],))
    own_result = space_back(grad_one[0], space_weights, own_kept[0], own_kept[2])
    far_result = space_back(
        after(grad_one[1], hidden_sum[0], own_result[1]), space_weights, far_kept[0], far_kept[2]
    )

    def space_part(side, half, *others):
        first = [after(result[0][side], *others) for result in (own_result, far_result)]
        second = [kept[1][side] for kept in (own_kept, far_kept)]
        return weight_grad([([normed, normed_far], first), (grad_one, second)], half)

    beside_send = space_part(1, 1)
    own_send = space_part(0, 1, beside_send)
    beside_keep = space_part(1, 0, own_send)
    own_keep = space_part(0, 0, beside_keep)
    space_send = add_low(own_send, moved(beside_send, "head", 1, (), (own_keep,)))
    space_got = moved(space_send, "space", 1)
    far_part = moved(far_result[1], "head", 2, (), (space_send, hidden_sum[1], time_got))
    sums_first, table_second, packed = run(
        back_first_body,
        [sums_shape, sums_shape, packed_shape],
        (*scalars, small, start, own_result[1], far_part),
        [ONE_SMEM] * 2 + [ONE_VMEM] * 4,
    )
    last = to_partners(packed)
    space_keep = add_low(own_keep, moved(beside_keep, "head", 1, (), (packed,)))
    sums = small_scatter(
        jnp.concatenate(
            [
                sums_first[0:1],
                sums_second[0:1],
                sums_third[0:1],
                sums_first[1:2],
                sums_second[1:2],
                sums_third[1:2],
                table_first + table_second,
                jnp.zeros((2, width), WIDE),
            ],
            axis=0,
        )
    )
    far_out = moved(far_kept_three[3], "head", 2, (packed,), (space_keep,))
    frames_out = run(
        finish_forward_body,
        packed_shape,
        (clip_length, second, *[part.reshape(rel_shape) for part in (own_kept_three[3], far_out)]),
        [ONE_SMEM] + [ONE_VMEM] * 3,
    )
    hidden_sum = halved(add_low(hidden_sum[0], after(hidden_sum[1], packed)), 4)
    time_sum = halved(add_low(time_keep, after(time_got, packed)), 2)
    space_sum = halved(add_low(space_keep, after(space_got, frames_out, time_sum[0])), 2)
    frames_grad = run(
        finish_back_body,
        shape_of(rel_shape, WIDE),
        (clip_length, total_first, after(last, frames_out, hidden_sum[0], time_sum[0], space_sum[0])),
        [ONE_SMEM] + [ONE_VMEM] * 2,
    )
    time_sum = halved(add_low(time_sum[0], after(time_sum[1], frames_grad)), 4)
    space_sum = halved(add_low(*space_sum), 4)
    hidden_grad, time_grad, space_grad = (
        mine.astype(WIDE) + got.astype(WIDE) for mine, got in (hidden_sum, time_sum, space_sum)
    )
    rows = width // BLOCKS
    return (
        frames_out.reshape(local),
        frames_grad.reshape(local),
        sums[0:3],
        sums[3:6],
        sums[6:14],
        space_grad[:, : 3 * inner].reshape(rows, 3, inner),
        space_grad[:, 3 * inner :].T,
        time_grad[:, : 3 * inner].reshape(rows, 3, inner),
        time_grad[:, 3 * inner :].T,
        hidden_grad[:, :hidden],
        hidden_grad[:, hidden:].T,
    )


def solution(mesh):
    placed = (
        P("head", None, "space", None),
        P("head", None),
        P(),
        P(None, ("space", "head")),
        P(None, ("space", "head")),
        P(None, ("space", "head")),
        P("space", None, "head"),
        P("head", "space"),
        P("space", None, "head"),
        P("head", "space"),
        P("space", "head"),
        P("head", "space"),
        P("head", None, "space", None),
    )
    eight = mesh.shape["space"] == BLOCKS and mesh.shape["head"] == ROUND
    return jax.shard_map(
        shards if eight else general_shards,
        mesh=mesh,
        in_specs=placed,
        out_specs=(
            P("head", None, "space", None),
            P("head", None, "space", None),
            P(None, ("space", "head")),
            P(None, ("space", "head")),
            P(None, ("space", "head")),
            P("space", None, "head"),
            P("head", "space"),
            P("space", None, "head"),
            P("head", "space"),
            P("space", "head"),
            P("head", "space"),
        ),
        check_vma=False,
    )
```

```python
import functools

import jax
import jax.numpy as jnp
from jax import lax
from jax.experimental import pallas as pl
from jax.experimental.pallas import tpu as pltpu
from jax.sharding import PartitionSpec as P

HEAD_DIM = 64


EPSILON = 1e-05
SCORE_SCALE = 0.125
MASKED_SCORE = -1e30
PRECISE = lax.Precision.HIGHEST
GELU_COEFF = 0.7978845608028654


def layer_norm(values, gain_row, bias_row):
    row_mean = jnp.mean(values, axis=-1, keepdims=True)
    centred = values - row_mean
    row_var = jnp.mean(centred * centred, axis=-1, keepdims=True)
    return centred * lax.rsqrt(row_var + EPSILON) * gain_row + bias_row


def gelu_tanh(inputs):
    return (
        0.5 * inputs * (1.0 + jnp.tanh(GELU_COEFF * (inputs + 0.044715 * inputs * inputs * inputs)))
    )


def gather_weights(small, large):
    small_full = (
        lax.all_gather(small[0], ("space", "head"), axis=1, tiled=True),
        lax.all_gather(small[1], ("space", "head"), axis=1, tiled=True),
        lax.all_gather(small[2], ("space", "head"), axis=1, tiled=True),
    )
    large_full = (
        lax.all_gather(large[0], "space", axis=0, tiled=True),
        lax.all_gather(large[1], "space", axis=1, tiled=True),
        lax.all_gather(large[2], "space", axis=0, tiled=True),
        lax.all_gather(large[3], "space", axis=1, tiled=True),
        lax.all_gather(large[4], "space", axis=0, tiled=True),
        lax.all_gather(large[5], "space", axis=1, tiled=True),
    )
    return (small_full, large_full)


def norm_step(inputs, gain_row, bias_row):
    normed, pullback = jax.vjp(layer_norm, inputs, gain_row, bias_row)
    whole = lax.all_gather(normed.astype(jnp.bfloat16), "head", axis=0, tiled=True)
    return (whole, pullback)


def cot_whole(grad_rows):
    return lax.all_gather(grad_rows.astype(jnp.bfloat16), "head", axis=0, tiled=True)


def input_total(partial_value):
    return lax.psum_scatter(
        partial_value.astype(jnp.bfloat16), "head", scatter_dimension=0, tiled=True
    ).astype(jnp.float32)


def heads_total(left, weight):
    return lax.psum_scatter(
        jnp.einsum("fcpe,ed->fcpd", left, weight, preferred_element_type=jnp.float32).astype(
            jnp.bfloat16
        ),
        "head",
        scatter_dimension=0,
        tiled=True,
    ).astype(jnp.float32)


def project_in(whole, weight):
    stacked = jnp.einsum(
        "fcpd,dke->kfcpe", whole, weight, preferred_element_type=jnp.float32
    ).astype(jnp.bfloat16)
    return (stacked[0], stacked[1], stacked[2])


def raw_scores(queries, keyset, form, allowed):
    key_form = form.replace("q", "k")
    scores = (
        jnp.einsum(
            form + "," + key_form + "->bhqk", queries, keyset, preferred_element_type=jnp.float32
        )
        * SCORE_SCALE
    )
    if allowed is not None:
        scores = jnp.where(allowed, scores, MASKED_SCORE)
    return scores


def attend(queries, keyset, values, form, allowed):
    key_form = form.replace("q", "k")
    scores = raw_scores(queries, keyset, form, allowed)
    row_max = jnp.max(scores, axis=-1, keepdims=True)
    log_total = row_max + jnp.log(jnp.sum(jnp.exp(scores - row_max), axis=-1, keepdims=True))
    shares = jnp.exp(scores - log_total).astype(jnp.bfloat16)
    output = jnp.einsum(
        "bhqk," + key_form + "->" + form, shares, values, preferred_element_type=jnp.float32
    )
    return (output.astype(jnp.bfloat16), log_total)


def attend_back(queries, keyset, values, log_total, output_grad, form, allowed):
    key_form = form.replace("q", "k")
    shares = jnp.exp(raw_scores(queries, keyset, form, allowed) - log_total)
    value_grad = jnp.einsum(
        "bhqk," + form + "->" + key_form,
        shares.astype(jnp.bfloat16),
        output_grad,
        preferred_element_type=jnp.float32,
    )
    share_grad = jnp.einsum(
        form + "," + key_form + "->bhqk", output_grad, values, preferred_element_type=jnp.float32
    )
    score_grad = (
        shares * (share_grad - jnp.sum(share_grad * shares, axis=-1, keepdims=True))
    ).astype(jnp.bfloat16)
    query_grad = (
        jnp.einsum(
            "bhqk," + key_form + "->" + form, score_grad, keyset, preferred_element_type=jnp.float32
        )
        * SCORE_SCALE
    )
    key_grad = (
        jnp.einsum(
            "bhqk," + form + "->" + key_form,
            score_grad,
            queries,
            preferred_element_type=jnp.float32,
        )
        * SCORE_SCALE
    )
    return (
        query_grad.astype(jnp.bfloat16),
        key_grad.astype(jnp.bfloat16),
        value_grad.astype(jnp.bfloat16),
    )


def general_shards(
    frames_in,
    action_codes,
    clip_length,
    norm_gain,
    norm_bias,
    action_table,
    spatialin,
    spatialout,
    temporalin,
    temporalout,
    expand,
    shrink,
    out_grad,
):
    head_count = lax.axis_size("head")
    frames_local, clip_count, pos_local, width = frames_in.shape
    frames_total = frames_local * head_count
    local_width = spatialin.shape[2]
    heads_local = local_width // HEAD_DIM
    frame_index = jnp.arange(frames_total)
    local_index = lax.axis_index("head") * frames_local + jnp.arange(frames_local)
    valid_local = (local_index[:, None] < clip_length[None, :]).astype(jnp.float32)[
        :, :, None, None
    ]
    allowed = (frame_index[None, :, None] >= frame_index[None, None, :]) & (
        frame_index[None, None, :] < clip_length[:, None, None]
    )
    allowed = jnp.broadcast_to(
        allowed[:, None, None], (clip_count, pos_local, 1, frames_total, frames_total)
    )
    allowed = allowed.reshape(clip_count * pos_local, 1, frames_total, frames_total)
    small_full, large_full = gather_weights(
        (norm_gain, norm_bias, action_table),
        (spatialin, spatialout, temporalin, temporalout, expand, shrink),
    )
    gain_full, bias_full, table_full = small_full
    space_in, space_out, time_in, time_out, expand_full, shrink_full = large_full
    code_hot = (action_codes[:, :, None] == jnp.arange(table_full.shape[0])[None, None, :]).astype(
        jnp.float32
    )
    embedded = jnp.einsum("fca,ad->fcd", code_hot, table_full, precision=PRECISE)
    start = valid_local * (frames_in.astype(jnp.float32) + embedded[:, :, None, :])
    whole_one, pull_one = norm_step(start, gain_full[0], bias_full[0])
    space_query, space_keys, space_values = project_in(whole_one, space_in)
    flat_shape = (frames_total * clip_count, pos_local, local_width)
    moved = (
        lax.all_to_all(
            space_query.reshape(flat_shape), "space", split_axis=0, concat_axis=1, tiled=True
        ),
        lax.all_to_all(
            space_keys.reshape(flat_shape), "space", split_axis=0, concat_axis=1, tiled=True
        ),
        lax.all_to_all(
            space_values.reshape(flat_shape), "space", split_axis=0, concat_axis=1, tiled=True
        ),
    )
    block_rows = moved[0].shape[0]
    block_cols = moved[0].shape[1]
    frame_shape = (block_rows, block_cols, heads_local, HEAD_DIM)
    frame_query = moved[0].reshape(frame_shape)
    frame_keys = moved[1].reshape(frame_shape)
    frame_values = moved[2].reshape(frame_shape)
    frame_out, frame_total = attend(frame_query, frame_keys, frame_values, "bqhe", None)
    returned = lax.all_to_all(
        frame_out.reshape(block_rows, block_cols, local_width),
        "space",
        split_axis=1,
        concat_axis=0,
        tiled=True,
    )
    space_attended = returned.reshape(frames_total, clip_count, pos_local, local_width)
    first = start + heads_total(space_attended, space_out)
    whole_two, pull_two = norm_step(first, gain_full[1], bias_full[1])
    time_query, time_keys, time_values = project_in(whole_two, time_in)
    time_shape = (frames_total, clip_count * pos_local, heads_local, HEAD_DIM)
    time_query = time_query.reshape(time_shape)
    time_keys = time_keys.reshape(time_shape)
    time_values = time_values.reshape(time_shape)
    time_out_rows, time_total = attend(time_query, time_keys, time_values, "qbhe", allowed)
    time_attended = time_out_rows.reshape(frames_total, clip_count, pos_local, local_width)
    second = first + heads_total(time_attended, time_out)
    whole_three, pull_three = norm_step(second, gain_full[2], bias_full[2])
    expanded = jnp.einsum(
        "fcpd,dh->fcph", whole_three, expand_full, preferred_element_type=jnp.float32
    )
    activated, gelu_pull = jax.vjp(gelu_tanh, expanded)
    activated_low = activated.astype(jnp.bfloat16)
    third = second + heads_total(activated_low, shrink_full)
    frames_out = (valid_local * third).astype(jnp.bfloat16)
    small_full, large_full = gather_weights(
        (norm_gain, norm_bias, action_table),
        (spatialin, spatialout, temporalin, temporalout, expand, shrink),
    )
    space_in, space_out, time_in, time_out, expand_full, shrink_full = large_full
    grad_third = valid_local * out_grad.astype(jnp.float32)
    cot_three = cot_whole(grad_third)
    shrink_part = jnp.einsum(
        "fcph,fcpd->hd", activated_low, cot_three, preferred_element_type=jnp.float32
    )
    act_grad = jnp.einsum(
        "fcpd,hd->fcph", cot_three, shrink_full, preferred_element_type=jnp.float32
    )
    pre_grad = gelu_pull(act_grad)[0].astype(jnp.bfloat16)
    expand_part = jnp.einsum(
        "fcpd,fcph->dh", whole_three, pre_grad, preferred_element_type=jnp.float32
    )
    normed_grad = input_total(
        jnp.einsum("fcph,dh->fcpd", pre_grad, expand_full, preferred_element_type=jnp.float32)
    )
    input_three, gain_three, bias_three = pull_three(normed_grad)
    grad_second = grad_third + input_three
    cot_two = cot_whole(grad_second)
    time_out_part = jnp.einsum(
        "fcpe,fcpd->ed", time_attended, cot_two, preferred_element_type=jnp.float32
    )
    time_grad = jnp.einsum(
        "fcpd,ed->fcpe", cot_two, time_out, preferred_element_type=jnp.float32
    ).astype(jnp.bfloat16)
    time_grads = attend_back(
        time_query,
        time_keys,
        time_values,
        time_total,
        time_grad.reshape(time_shape),
        "qbhe",
        allowed,
    )
    stacked_grad = jnp.stack(
        [member.reshape(frames_total, clip_count, pos_local, local_width) for member in time_grads]
    )
    time_in_part = jnp.einsum(
        "fcpd,kfcpe->dke", whole_two, stacked_grad, preferred_element_type=jnp.float32
    )
    normed_grad = input_total(
        jnp.einsum("kfcpe,dke->fcpd", stacked_grad, time_in, preferred_element_type=jnp.float32)
    )
    input_two, gain_two, bias_two = pull_two(normed_grad)
    grad_first = grad_second + input_two
    cot_one = cot_whole(grad_first)
    space_out_part = jnp.einsum(
        "fcpe,fcpd->ed", space_attended, cot_one, preferred_element_type=jnp.float32
    )
    space_grad = jnp.einsum(
        "fcpd,ed->fcpe", cot_one, space_out, preferred_element_type=jnp.float32
    ).astype(jnp.bfloat16)
    frame_grad = lax.all_to_all(
        space_grad.reshape(flat_shape), "space", split_axis=0, concat_axis=1, tiled=True
    ).reshape(frame_shape)
    query_grad, keys_grad, values_grad = attend_back(
        frame_query, frame_keys, frame_values, frame_total, frame_grad, "bqhe", None
    )
    block_shape = (block_rows, block_cols, local_width)
    back_grads = (
        lax.all_to_all(
            query_grad.reshape(block_shape), "space", split_axis=1, concat_axis=0, tiled=True
        ),
        lax.all_to_all(
            keys_grad.reshape(block_shape), "space", split_axis=1, concat_axis=0, tiled=True
        ),
        lax.all_to_all(
            values_grad.reshape(block_shape), "space", split_axis=1, concat_axis=0, tiled=True
        ),
    )
    stacked_grad = jnp.stack(
        [member.reshape(frames_total, clip_count, pos_local, local_width) for member in back_grads]
    )
    space_in_part = jnp.einsum(
        "fcpd,kfcpe->dke", whole_one, stacked_grad, preferred_element_type=jnp.float32
    )
    normed_grad = input_total(
        jnp.einsum("kfcpe,dke->fcpd", stacked_grad, space_in, preferred_element_type=jnp.float32)
    )
    input_one, gain_one, bias_one = pull_one(normed_grad)
    grad_start = grad_first + input_one
    frames_grad = valid_local * grad_start
    table_part = jnp.einsum(
        "fca,fcd->ad", code_hot, jnp.sum(frames_grad, axis=2), precision=PRECISE
    )
    gain_grad, bias_grad, table_grad = (
        lax.psum_scatter(
            jnp.stack([gain_one, gain_two, gain_three]),
            ("space", "head"),
            scatter_dimension=1,
            tiled=True,
        ),
        lax.psum_scatter(
            jnp.stack([bias_one, bias_two, bias_three]),
            ("space", "head"),
            scatter_dimension=1,
            tiled=True,
        ),
        lax.psum_scatter(table_part, ("space", "head"), scatter_dimension=1, tiled=True),
    )
    weight_grads = (
        lax.psum_scatter(space_in_part, "space", scatter_dimension=0, tiled=True),
        lax.psum_scatter(space_out_part, "space", scatter_dimension=1, tiled=True),
        lax.psum_scatter(time_in_part, "space", scatter_dimension=0, tiled=True),
        lax.psum_scatter(time_out_part, "space", scatter_dimension=1, tiled=True),
        lax.psum_scatter(expand_part, "space", scatter_dimension=0, tiled=True),
        lax.psum_scatter(shrink_part, "space", scatter_dimension=1, tiled=True),
    )
    return (
        frames_out,
        frames_grad,
        gain_grad,
        bias_grad,
        table_grad,
        weight_grads[0],
        weight_grads[1],
        weight_grads[2],
        weight_grads[3],
        weight_grads[4],
        weight_grads[5],
    )


ORDER = (0, 4, 2, 6, 1, 5, 3, 7)
BLOCKS = len(ORDER)
PLACE = tuple(ORDER.index(mask) for mask in range(BLOCKS))
ROUND = 4
ONE_VMEM = pl.BlockSpec(memory_space=pltpu.VMEM)
ONE_SMEM = pl.BlockSpec(memory_space=pltpu.SMEM)
MIB = 1024 * 1024
LOW = jnp.bfloat16
WIDE = jnp.float32


def swap(value, axis, mask):
    return lax.ppermute(value, axis, [(i, i ^ mask) for i in range(lax.axis_size(axis))])


class Order:
    def __init__(self):
        self.last = None

    def tied(self, value):
        if self.last is None:
            return value
        return lax.optimization_barrier((value, self.last))[0]

    def send(self, value, axis, mask):
        return swap(self.tied(value), axis, mask)

    def exchange(self, packed):
        return lax.all_to_all(self.tied(packed), "space", split_axis=0, concat_axis=0, tiled=True)

    def take(self, value):
        self.last = self.tied(value)
        return self.last

    def do(self, step, first, *others):
        result = step(self.tied(first), *others)
        self.last = jax.tree.leaves(result)[0]
        return result


def run(body, outs, args, specs, vmem=None):
    single = not isinstance(outs, (list, tuple))
    name = getattr(body, "func", body).__name__.removesuffix("_body")
    return pl.pallas_call(
        body,
        out_shape=outs,
        in_specs=specs,
        out_specs=ONE_VMEM if single else [ONE_VMEM] * len(outs),
        cost_estimate=pl.CostEstimate(flops=0, bytes_accessed=1024, transcendentals=0),
        compiler_params=pltpu.CompilerParams(vmem_limit_bytes=vmem or 12 * MIB),
        name=name,
    )(*args)


def shape_of(dims, dtype):
    return jax.ShapeDtypeStruct(tuple(dims), dtype)


def feature_block(place, step):
    return pl.ds(pl.multiple_of(place * step, step), step)


def partner(mask):
    return lax.axis_index("space") ^ mask


def frame_valid(lengths, frames, mask):
    clips = lengths.shape[0]
    frame = lax.axis_index("head") * (frames // clips) + partner(mask) // clips
    return jnp.where(frame < lengths[partner(mask) % clips], 1.0, 0.0).astype(WIDE)


def normed_parts(values):
    centred = values - jnp.mean(values, axis=-1, keepdims=True)
    scale = lax.rsqrt(jnp.mean(centred * centred, axis=-1, keepdims=True) + EPSILON)
    return centred * scale, scale


def norm_back(values, grad, gain_row):
    unit, scale = normed_parts(values)
    scaled = grad * gain_row
    out = scale * (
        scaled
        - jnp.mean(scaled, axis=-1, keepdims=True)
        - unit * jnp.mean(scaled * unit, axis=-1, keepdims=True)
    )
    return (
        out,
        jnp.sum(grad * unit, axis=0, keepdims=True),
        jnp.sum(grad, axis=0, keepdims=True),
    )


def store_for(ref, rows, mask):
    step = rows.shape[-1] // BLOCKS
    for i in range(BLOCKS):
        j = i ^ PLACE[mask]
        ref[partner(mask), :, i * step : (i + 1) * step] = rows[:, j * step : (j + 1) * step]


def pack_attention_body(enter, leave, *outs):
    step = leave.shape[0] // len(outs)
    for i, out in enumerate(outs):
        place = slice(i * step, (i + 1) * step)
        for j in range(3):
            out[:, j * step : (j + 1) * step] = enter[j, :, place]
        out[:, 3 * step :] = jnp.transpose(leave[place, :])


def unpack_attention_body(*refs):
    pairs, (enter, leave) = refs[:-2], refs[-2:]
    step = leave.shape[0] // (len(pairs) // 2)
    for i in range(len(pairs) // 2):
        total = pairs[2 * i][...].astype(WIDE) + pairs[2 * i + 1][...].astype(WIDE)
        place = slice(i * step, (i + 1) * step)
        for j in range(3):
            enter[j, :, place] = total[:, j * step : (j + 1) * step]
        leave[place, :] = jnp.transpose(total[:, 3 * step :])


def pack_hidden_body(enter, leave, out):
    hidden = leave.shape[0]
    out[:, :hidden] = enter[...]
    out[:, hidden:] = jnp.transpose(leave[...])


def unpack_hidden_body(mine, got, enter, leave):
    hidden = leave.shape[0]
    total = mine[...].astype(WIDE) + got[...].astype(WIDE)
    enter[...] = total[:, :hidden]
    leave[...] = jnp.transpose(total[:, hidden:])


def pack_frames_body(frames, out):
    step = frames.shape[-1] // BLOCKS
    for mask in range(BLOCKS):
        for i in range(BLOCKS):
            source = partner(ORDER[i ^ PLACE[mask]])
            place = slice(i * step, (i + 1) * step)
            out[partner(mask), :, place] = frames[partner(mask), :, feature_block(source, step)]


def order_inputs_body(lengths, frames, grad, frames_out, grad_out):
    step = frames.shape[-1] // BLOCKS

    def one(mask, carry):
        valid = frame_valid(lengths, BLOCKS, mask)
        for i in range(BLOCKS):
            source = feature_block(partner(ORDER[i]), step)
            place = slice(i * step, (i + 1) * step)
            frames_out[mask, :, place] = frames[partner(mask), :, source]
            kept = grad[partner(mask), :, source].astype(WIDE) * valid
            grad_out[mask, :, place] = kept.astype(LOW)
        return carry

    lax.fori_loop(0, BLOCKS, one, 0)


def start_rows(rows, codes, lengths, small, mask):
    embedded = small[pl.ds(6 + codes[partner(mask)], 1), :]
    return frame_valid(lengths, BLOCKS, mask) * (rows.astype(WIDE) + embedded)


def frame_norm_body(codes, lengths, small, blocks, normed, start):
    rows = blocks.shape[1]
    for b in range(BLOCKS):
        values = start_rows(blocks[partner(b)], codes, lengths, small, 0)
        start[b * rows : (b + 1) * rows, :] = values
        unit, _ = normed_parts(values)
        normed[b * rows : (b + 1) * rows, :] = (unit * small[0:1, :] + small[3:4, :]).astype(LOW)


def spread_body(first, second, out):
    rows = out.shape[1]
    for mask in range(BLOCKS):
        part = slice(mask * rows, (mask + 1) * rows)
        total = first[part, :].astype(WIDE) + second[part, :].astype(WIDE)
        store_for(out, total.astype(LOW), mask)


def join_norm_body(codes, lengths, small, frames, blocks, whole, normed):
    for b in range(BLOCKS):
        values = start_rows(frames[b], codes, lengths, small, b) + blocks[partner(b)].astype(WIDE)
        whole[b] = values
        unit, _ = normed_parts(values)
        normed[b] = (unit * small[1:2, :] + small[4:5, :]).astype(LOW)


def add_norm_body(small, before, first, second, third, whole, normed):
    def one(b, carry):
        values = before[b] + (
            first[b].astype(WIDE) + second[b].astype(WIDE) + third[b].astype(WIDE)
        )
        whole[b] = values
        unit, _ = normed_parts(values)
        normed[b] = (unit * small[2:3, :] + small[5:6, :]).astype(LOW)
        return carry

    lax.fori_loop(0, BLOCKS, one, 0)


def finish_forward_body(lengths, before, first, second, out):
    step = out.shape[-1] // BLOCKS

    def one(b, carry):
        values = before[b] + (first[b].astype(WIDE) + second[b].astype(WIDE))
        values = (frame_valid(lengths, BLOCKS, b) * values).astype(LOW)
        for i in range(BLOCKS):
            place = feature_block(partner(ORDER[i]), step)
            out[partner(b), :, place] = values[:, i * step : (i + 1) * step]
        return carry

    lax.fori_loop(0, BLOCKS, one, 0)


def back_third_body(small, grad, values, first, second, total_out, low_out, sums):
    sums[...] = jnp.zeros_like(sums)

    def one(b, carry):
        normed_grad = first[b].astype(WIDE) + second[b].astype(WIDE)
        out, gain, bias = norm_back(values[b], normed_grad, small[2:3, :])
        total = grad[b].astype(WIDE) + out
        total_out[b] = total
        low_out[b] = total.astype(LOW)
        sums[0:1, :] += gain
        sums[1:2, :] += bias
        return carry

    lax.fori_loop(0, BLOCKS, one, 0)


def back_second_body(codes, lengths, small, grad, values, first, second, third, total_out, sums, table, packed):
    sums[...] = jnp.zeros_like(sums)
    table[...] = jnp.zeros_like(table)
    for b in range(BLOCKS):
        normed_grad = first[b].astype(WIDE) + second[b].astype(WIDE) + third[b].astype(WIDE)
        out, gain, bias = norm_back(values[b], normed_grad, small[1:2, :])
        total = grad[b] + out
        total_out[b] = total
        store_for(packed, total.astype(LOW), b)
        sums[0:1, :] += gain
        sums[1:2, :] += bias
        row = pl.ds(codes[partner(b)], 1)
        table[row, :] += frame_valid(lengths, BLOCKS, b) * jnp.sum(total, axis=0, keepdims=True)


def back_first_body(codes, lengths, small, values, first, second, sums, table, packed):
    sums[...] = jnp.zeros_like(sums)
    table[...] = jnp.zeros_like(table)
    rows = packed.shape[1]
    for b in range(BLOCKS):
        part = slice(b * rows, (b + 1) * rows)
        normed_grad = first[part, :].astype(WIDE) + second[part, :].astype(WIDE)
        out, gain, bias = norm_back(values[part, :], normed_grad, small[0:1, :])
        store_for(packed, out.astype(LOW), b)
        sums[0:1, :] += gain
        sums[1:2, :] += bias
        row = pl.ds(codes[partner(0)], 1)
        table[row, :] += frame_valid(lengths, BLOCKS, 0) * jnp.sum(out, axis=0, keepdims=True)


def collect_body(blocks, out):
    rows = blocks.shape[1]
    for b in range(BLOCKS):
        out[b * rows : (b + 1) * rows, :] = blocks[partner(b)]


def finish_back_body(lengths, grad, blocks, out):
    step = out.shape[-1] // BLOCKS
    for b in range(BLOCKS):
        values = frame_valid(lengths, BLOCKS, b) * (grad[b] + blocks[partner(b)].astype(WIDE))
        for i in range(BLOCKS):
            place = feature_block(partner(ORDER[i]), step)
            out[partner(b), :, place] = values[:, i * step : (i + 1) * step]


def matmul(left, right):
    return lax.dot_general(left, right, (((1,), (0,)), ((), ())), preferred_element_type=WIDE)


def matmul_t(left, right):
    return lax.dot_general(left, right, (((1,), (1,)), ((), ())), preferred_element_type=WIDE)


def matmul_tn(left, right):
    return lax.dot_general(left, right, (((0,), (0,)), ((), ())), preferred_element_type=WIDE)


def head_mask(width, head):
    lane = lax.broadcasted_iota(jnp.int32, (1, width), 1)
    return (lane // HEAD_DIM) == head


def pick(values, mask):
    return jnp.where(mask, values, jnp.zeros_like(values))


def attention_rows(projected, allowed, totals, first):
    width = projected.shape[1] // 3
    queries = projected[:, :width] * jnp.asarray(SCORE_SCALE, LOW)
    keyset = projected[:, width : 2 * width]
    values = projected[:, 2 * width :]
    lane = lax.broadcasted_iota(jnp.int32, (1, 128), 1)
    output = jnp.zeros((projected.shape[0], width), WIDE)
    for head in range(width // HEAD_DIM):
        mask = head_mask(width, head)
        scores = matmul_t(pick(queries, mask), keyset)
        if allowed is not None:
            scores = jnp.where(allowed, scores, MASKED_SCORE)
        row_max = jnp.max(scores, axis=-1, keepdims=True)
        raised = jnp.exp(scores - row_max)
        total = jnp.sum(raised, axis=-1, keepdims=True)
        shares = (raised * (1.0 / total)).astype(LOW)
        output = output + matmul(shares, pick(values, mask))
        totals = jnp.where(lane == first + head, row_max + jnp.log(total), totals)
    return output.astype(LOW), totals


def attention_rows_back(projected, totals, first, output_grad, allowed):
    width = projected.shape[1] // 3
    queries = projected[:, :width] * jnp.asarray(SCORE_SCALE, LOW)
    keyset = projected[:, width : 2 * width]
    values = projected[:, 2 * width :]
    scaled_keys = keyset * jnp.asarray(SCORE_SCALE, LOW)
    shape = (projected.shape[0], width)
    query_grad, key_grad, value_grad = (jnp.zeros(shape, WIDE) for _ in range(3))
    for head in range(width // HEAD_DIM):
        mask = head_mask(width, head)
        own_queries = pick(queries, mask)
        own_grad = pick(output_grad, mask)
        scores = matmul_t(own_queries, keyset)
        if allowed is not None:
            scores = jnp.where(allowed, scores, MASKED_SCORE)
        shares = jnp.exp(scores - totals[:, first + head : first + head + 1])
        value_grad = value_grad + matmul_tn(shares.astype(LOW), own_grad)
        share_grad = matmul_t(own_grad, values)
        score_grad = shares * (share_grad - jnp.sum(share_grad * shares, axis=-1, keepdims=True))
        score_grad = score_grad.astype(LOW)
        query_grad = query_grad + matmul(score_grad, pick(scaled_keys, mask))
        key_grad = key_grad + matmul_tn(score_grad, own_queries)
    return jnp.concatenate(
        [query_grad.astype(LOW), key_grad.astype(LOW), value_grad.astype(LOW)], axis=1
    )


def enter_rows(rows, parts, columns):
    depth = parts[0].shape[0]
    total = matmul(rows[:, :depth], parts[0][:, columns])
    for i, part in enumerate(parts[1:], 1):
        total = total + matmul(rows[:, i * depth : (i + 1) * depth], part[:, columns])
    return total


def leave_rows(sides, columns, store):
    depth = sides[0][1][0].shape[0]
    for i in range(len(sides[0][1])):
        total = matmul_t(sides[0][0], sides[0][1][i][:, columns])
        for values, parts in sides[1:]:
            total = total + matmul_t(values, parts[i][:, columns])
        store(slice(i * depth, (i + 1) * depth), total.astype(LOW))


def space_forward_body(count, rows, *refs):
    sides, refs = [[ref] for ref in refs[:count]], refs[count:]
    projected_out, output_out, (totals_out, part_out) = refs[:count], refs[count : 2 * count], refs[2 * count :]
    width = output_out[0].shape[1]
    totals = jnp.zeros(totals_out.shape, WIDE)
    leaving = []
    for side, parts in enumerate(sides):
        projected = enter_rows(rows, parts, slice(0, 3 * width)).astype(LOW)
        projected_out[side][...] = projected
        output, totals = attention_rows(projected, None, totals, side * (width // HEAD_DIM))
        output_out[side][...] = output
        leaving.append((output, parts))
    totals_out[...] = totals

    def store(place, values):
        part_out[:, place] = values

    leave_rows(leaving, slice(3 * width, 4 * width), store)


def space_back_body(count, rows, *refs):
    sides, refs = [[ref] for ref in refs[:count]], refs[count:]
    projected, totals, grads_out, part_out = refs[:count], refs[count], refs[count + 1 : -1], refs[-1]
    width = projected[0].shape[1] // 3
    leaving = []
    for side, parts in enumerate(sides):
        output_grad = enter_rows(rows, parts, slice(3 * width, 4 * width)).astype(LOW)
        first = side * (width // HEAD_DIM)
        grads = attention_rows_back(projected[side][...], totals[...], first, output_grad, None)
        grads_out[side][...] = grads
        leaving.append((grads, parts))

    def store(place, values):
        part_out[:, place] = values

    leave_rows(leaving, slice(0, 3 * width), store)


def time_allowed(lengths, clip, frames_local, positions):
    clips = lengths.shape[0]
    count = ROUND * frames_local * positions
    head_at, frame_at = lax.axis_index("head"), partner(0) // clips

    def split(shape, axis):
        row = lax.broadcasted_iota(jnp.int32, shape, axis)
        group = row // (frames_local * positions)
        local = (row // positions) % frames_local
        return (group ^ head_at) * frames_local + (local ^ frame_at), row % positions

    query_frame, query_pos = split((count, 1), 0)
    key_frame, key_pos = split((1, count), 1)
    length = lengths[(partner(0) % clips) ^ clip]
    return (query_pos == key_pos) & (query_frame >= key_frame) & (key_frame < length)


PART = 16


def time_groups(ref):
    return [(c, p) for c in range(ref.shape[1]) for p in range(0, ref.shape[2], PART)]


def join_rows(refs, group):
    c, p = group
    return jnp.concatenate(
        [ref[:, c, p : p + PART, :].reshape(ref.shape[0] * PART, ref.shape[3]) for ref in refs], axis=0
    )


def split_rows(refs, group, values, place=slice(None)):
    c, p = group
    rows = values.shape[0] // len(refs)
    for i, ref in enumerate(refs):
        part = values[i * rows : (i + 1) * rows].reshape(ref.shape[0], PART, values.shape[1])
        ref[:, c, p : p + PART, place] = part


def time_forward_body(lengths, *refs):
    parts, refs = refs[:2], refs[2:]
    rows, projected_out, output_out, totals_out, part_out = (refs[i : i + 4] for i in range(0, 20, 4))
    frames_local, width = rows[0].shape[0], output_out[0].shape[3]
    for group in time_groups(rows[0]):
        joined = join_rows(rows, group)
        projected = enter_rows(joined, parts, slice(0, 3 * width)).astype(LOW)
        split_rows(projected_out, group, projected)
        allowed = time_allowed(lengths, group[0], frames_local, PART)
        totals = jnp.zeros((projected.shape[0], 128), WIDE)
        output, totals = attention_rows(projected, allowed, totals, 0)
        split_rows(output_out, group, output)
        split_rows(totals_out, group, totals)
        leave_rows(
            [(output, parts)],
            slice(3 * width, 4 * width),
            lambda place, values, group=group: split_rows(part_out, group, values, place),
        )


def time_back_body(lengths, *refs):
    parts, refs = refs[:2], refs[2:]
    rows, projected, totals, grads_out, part_out = (refs[i : i + 4] for i in range(0, 20, 4))
    frames_local, width = rows[0].shape[0], projected[0].shape[3] // 3
    for group in time_groups(rows[0]):
        allowed = time_allowed(lengths, group[0], frames_local, PART)
        joined = join_rows(rows, group)
        output_grad = enter_rows(joined, parts, slice(3 * width, 4 * width)).astype(LOW)
        grads = attention_rows_back(
            join_rows(projected, group), join_rows(totals, group), 0, output_grad, allowed
        )
        split_rows(grads_out, group, grads)
        leave_rows(
            [(grads, parts)],
            slice(0, 3 * width),
            lambda place, values, group=group: split_rows(part_out, group, values, place),
        )


def space_forward(rows, weights):
    count, width = rows.shape
    sides, inner = len(weights), weights[0].shape[1] // 4
    outs = [shape_of((count, 3 * inner), LOW)] * sides + [shape_of((count, inner), LOW)] * sides
    outs += [shape_of((count, 128), WIDE), shape_of((count, width), LOW)]
    body = functools.partial(space_forward_body, sides)
    results = run(body, outs, (rows, *weights), [ONE_VMEM] * (1 + len(weights)))
    return results[:sides], results[sides : 2 * sides], results[-2], results[-1]


def space_back(rows, weights, projected, totals):
    count, width = rows.shape
    sides, inner = len(weights), weights[0].shape[1] // 4
    outs = [shape_of((count, 3 * inner), LOW)] * sides + [shape_of((count, width), LOW)]
    args = (rows, *weights, *projected, totals)
    results = run(functools.partial(space_back_body, sides), outs, args, [ONE_VMEM] * len(args))
    return results[:sides], results[-1]


def time_call(body, lengths, weights, groups, out_widths):
    args, outs = [lengths, *weights], []
    for group in groups:
        args += group
    for features, dtype in out_widths:
        outs += [shape_of((*groups[0][0].shape[:3], features), dtype)] * ROUND
    results = run(body, outs, args, [ONE_SMEM] + [ONE_VMEM] * (len(args) - 1), vmem=16 * MIB)
    return [results[i : i + ROUND] for i in range(0, len(results), ROUND)]


def hidden_body(normed, grad, *refs):
    sides, acts, pres = (refs[0:2], refs[2:4]), refs[4:6], refs[6:8]
    in_part, out_part = refs[8:]
    hidden = acts[0].shape[1]
    tile = 256
    for side, parts in enumerate(sides):
        for start in range(0, hidden, tile):
            enter = slice(start, start + tile)
            leave = slice(hidden + start, hidden + start + tile)
            value = enter_rows(normed, parts, enter)
            square = value * value
            curve = jnp.tanh(GELU_COEFF * (value + 0.044715 * square * value))
            half = 0.5 * (1.0 + curve)
            slope = half + 0.5 * value * (1.0 - curve * curve) * (
                GELU_COEFF * (1.0 + 3.0 * 0.044715 * square)
            )
            acts[side][:, enter] = (value * half).astype(LOW)
            pres[side][:, enter] = (enter_rows(grad, parts, leave) * slope).astype(LOW)
    for values, part, columns in (
        (pres, in_part, slice(0, hidden)),
        (acts, out_part, slice(hidden, 2 * hidden)),
    ):

        def store(place, total, part=part):
            part[:, place] = total

        leave_rows([(values[side][...], parts) for side, parts in enumerate(sides)], columns, store)


def hidden_call(normed, grad, weights):
    count, width = normed.shape
    hidden = weights[0].shape[1] // 2
    outs = [shape_of((count, hidden), LOW)] * 4 + [shape_of((count, width), LOW)] * 2
    results = run(hidden_body, outs, (normed, grad, *weights), [ONE_VMEM] * 6)
    return results[0:2], results[2:4], results[4], results[5]


def weight_grad_tile(counts, refs, start, tile, store):
    at, column = 0, 0
    for count in counts:
        lefts, rights = refs[at : at + count], refs[at + count : at + 2 * count]
        at += 2 * count
        total = matmul_tn(lefts[0][:, start : start + tile], rights[0][...])
        for left, right in zip(lefts[1:], rights[1:]):
            total = total + matmul_tn(left[:, start : start + tile], right[...])
        store(column, total.astype(LOW))
        column += total.shape[1]


def weight_grad_body(counts, start, *refs):
    out, tile = refs[-1], 256
    for row in range(0, out.shape[0], tile):

        def store(column, values, row=row):
            out[row : row + tile, column : column + values.shape[1]] = values

        weight_grad_tile(counts, refs, start + row, tile, store)


def weight_grad(pairs, half=None):
    args, counts = [], []
    for lefts, rights in pairs:
        args += [*lefts, *rights]
        counts.append(len(lefts))
    width = pairs[0][0][0].shape[1]
    rows = width if half is None else width // 2
    columns = sum(rights[0].shape[1] for _, rights in pairs)
    body = functools.partial(weight_grad_body, tuple(counts), (half or 0) * rows)
    return run(body, shape_of((rows, columns), LOW), args, [ONE_VMEM] * len(args))


def small_mine_body(gain, bias, table, out):
    step = gain.shape[1]
    out[...] = jnp.zeros_like(out)
    row = 0
    for part in (gain, bias, table):
        values = jnp.concatenate([part[...]] * ROUND, axis=1)
        lane = lax.broadcasted_iota(jnp.int32, values.shape, 1)
        out[0, row : row + part.shape[0], :] = pick(values, lane // step == lax.axis_index("head"))
        row += part.shape[0]


def small_rows_body(first, second, out):
    blocks, _, step = first.shape
    for half, part in enumerate((first, second)):
        for i in range(blocks):
            place = (half * blocks + i) * step
            out[:, place : place + step] = part[i]


def small_blocks_body(first, second, third, table_a, table_b, *outs):
    step = outs[0].shape[2]
    for half, out in enumerate(outs):
        for i in range(out.shape[0]):
            place = slice((half * out.shape[0] + i) * step, (half * out.shape[0] + i + 1) * step)
            for row, part in enumerate((first, second, third)):
                out[i, row : row + 1, :] = part[0:1, place]
                out[i, row + 3 : row + 4, :] = part[1:2, place]
            out[i, 6:14, :] = table_a[:, place] + table_b[:, place]
            out[i, 14:16, :] = jnp.zeros((2, step), WIDE)


def stack_body(*refs):
    out, row = refs[-1], 0
    for part in refs[:-1]:
        out[row : row + part.shape[0], ...] = part[...]
        row += part.shape[0]


def sum_body(*refs):
    total = refs[0][...]
    for part in refs[1:-1]:
        total = total + part[...]
    refs[-1][...] = total


def add_split_body(first, second, *outs):
    row = 0
    for out in outs:
        part = slice(row, row + out.shape[0])
        out[...] = (first[part].astype(WIDE) + second[part].astype(WIDE)).astype(out.dtype)
        row += out.shape[0]


def shards(
    frames_in,
    action_codes,
    clip_length,
    norm_gain,
    norm_bias,
    action_table,
    spatialin,
    spatialout,
    temporalin,
    temporalout,
    expand,
    shrink,
    out_grad,
):
    frames_local, clips, pos_local, width = frames_in.shape
    local = (frames_local, clips, pos_local, width)
    rel_shape = (BLOCKS, pos_local, width)
    count = BLOCKS * pos_local
    inner = spatialin.shape[2]
    hidden = expand.shape[1]
    codes = action_codes.reshape(BLOCKS)
    scalars = (codes, clip_length)

    packed_shape = shape_of(rel_shape, LOW)
    flat_shape = shape_of((count, width), LOW)
    sums_shape = shape_of((8, width), WIDE)
    frames_flat = frames_in.reshape(rel_shape)

    order = Order()
    send, take, do = order.send, order.take, order.do
    grad_shapes = [shape_of((3, width // BLOCKS, inner), WIDE), shape_of((inner, width // BLOCKS), WIDE)]
    whole_shape = shape_of(rel_shape, WIDE)

    def kernel(body, outs, first, *others):
        smem = [ONE_SMEM if a.ndim == 1 else ONE_VMEM for a in (first, *others)]
        return do(lambda *args: run(body, outs, args, smem), first, *others)

    def stacked(*parts):
        shape = (sum(part.shape[0] for part in parts), *parts[0].shape[1:])
        return kernel(stack_body, shape_of(shape, parts[0].dtype), *parts)

    def summed(*parts):
        return kernel(sum_body, shape_of(parts[0].shape, parts[0].dtype), *parts)

    def halves(first, second):
        shape = shape_of((first.shape[0] // 2, *first.shape[1:]), first.dtype)
        keep, left = kernel(add_split_body, [shape, shape], first, second)
        order.last = left
        return keep, left

    def added(first, second):
        return kernel(add_split_body, [shape_of(first.shape, first.dtype)], first, second)[0]

    def attention_rows_of(enter, leave, parts):
        outs = [shape_of((enter.shape[0], 4 * inner // parts), LOW)] * parts
        return kernel(pack_attention_body, outs, jnp.transpose(enter, (1, 0, 2)), leave)

    rows_a, rows_b = attention_rows_of(spatialin, spatialout, 2)
    got_a = send(rows_a, "space", 4)
    small_shape = (16, width // BLOCKS)
    block = kernel(small_mine_body, shape_of((1, *small_shape), WIDE), norm_gain, norm_bias, action_table)
    packed = kernel(pack_frames_body, packed_shape, frames_flat)
    far_a = stacked(rows_a, take(got_a))
    got_a = send(far_a, "space", 2)
    got_b = send(rows_b, "space", 4)
    got_small = [send(block, "head", mask) for mask in (1, 2, 3)]
    frame_blocks = order.exchange(packed)
    block = summed(block, *[take(got) for got in got_small])
    got_small = [send(block, "space", mask) for mask in ORDER[1:4]]
    line_a = stacked(far_a, take(got_a))
    far_b = stacked(rows_b, take(got_b))
    got_a = send(line_a, "space", 1)
    got_b = send(far_b, "space", 2)
    (time_rows,) = attention_rows_of(temporalin, temporalout, 1)
    hidden_rows = kernel(pack_hidden_body, shape_of((expand.shape[0], 2 * hidden), LOW), expand, shrink)
    line = stacked(block, *[take(got) for got in got_small])
    got_small = send(line, "space", 1)
    line_b = stacked(far_b, take(got_b))
    got_b = send(line_b, "space", 1)
    small = kernel(small_rows_body, shape_of((16, width), WIDE), line, take(got_small))
    frame_blocks = take(frame_blocks)
    normed, start = kernel(
        frame_norm_body, [flat_shape, shape_of((count, width), WIDE)], *scalars, small, frame_blocks
    )
    normed_far = send(normed, "head", 2)
    got_time = send(time_rows, "space", 4)
    got_a = take(got_a)
    got_b = take(got_b)
    normed_far = take(normed_far)
    space_a = stacked(line_a, got_a)
    time_far = stacked(time_rows, take(got_time))
    beside_a = send(space_a, "head", 1)
    space_b = stacked(line_b, got_b)
    beside_b = send(space_b, "head", 1)
    got_time = send(time_far, "space", 2)
    got_hidden = send(hidden_rows, "space", 4)
    space_weights = [space_a, space_b, take(beside_a), take(beside_b)]

    far_kept = do(space_forward, normed_far, space_weights)
    order.last = far_kept[3]
    far_part = send(far_kept[3], "head", 2)
    own_kept = do(space_forward, normed, space_weights)
    order.last = own_kept[3]
    time_line = stacked(time_far, take(got_time))
    far_part = take(far_part)
    got_time = send(time_line, "space", 1)
    packed = kernel(spread_body, packed_shape, own_kept[3], far_part)
    spread = order.exchange(packed)
    frames_rel, grad_low = kernel(
        order_inputs_body, [packed_shape] * 2, clip_length, frames_flat, out_grad.reshape(rel_shape)
    )
    hidden_far = stacked(hidden_rows, take(got_hidden))
    got_hidden = send(hidden_far, "space", 2)
    grad_far = take(send(grad_low.reshape(count, width), "head", 2))
    time_weights = [time_line, take(got_time)]
    spread = take(spread)
    first, normed_two = kernel(
        join_norm_body, [whole_shape, packed_shape], *scalars, small, frames_rel, spread
    )
    order.last = normed_two

    normed_two = normed_two.reshape(local)
    far = send(normed_two, "head", 2)
    near = send(normed_two, "head", 1)
    hidden_line = stacked(hidden_far, take(got_hidden))
    got_hidden = send(hidden_line, "space", 1)
    far = take(far)
    diagonal = send(far, "head", 1)
    normed_two = [normed_two, take(near), far, take(diagonal)]
    hidden_beside = send(hidden_line, "head", 1)
    time_projected, time_output, time_totals, time_parts = do(
        lambda first, *others: time_call(
            time_forward_body,
            clip_length,
            time_weights,
            [[first, *others]],
            [(3 * inner, LOW), (inner, LOW), (128, WIDE), (width, LOW)],
        ),
        *normed_two,
    )
    order.last = time_parts[3]
    hidden_beside = take(hidden_beside)
    diagonal = send(time_parts[3], "head", 1)
    near = send(time_parts[1], "head", 1)
    far = added(time_parts[2], take(diagonal))
    far = send(far, "head", 2)
    near = take(near)
    parts = [part.reshape(rel_shape) for part in (time_parts[0], near, take(far))]
    second, normed_three = kernel(add_norm_body, [whole_shape, packed_shape], small, first, *parts)
    order.last = normed_three

    normed_three = normed_three.reshape(count, width)
    far = send(normed_three, "head", 2)
    hidden_other = take(got_hidden)
    normed_three = [normed_three, take(far)]
    hidden_last = send(hidden_other, "head", 1)
    hidden_weights = [hidden_line, hidden_other, hidden_beside, take(hidden_last)]
    grad_third = [grad_low.reshape(count, width), grad_far]
    far_kept_three = do(hidden_call, normed_three[1], grad_third[1], hidden_weights)
    order.last = far_kept_three[2]
    far_part = send(far_kept_three[2], "head", 2)
    own_kept_three = do(hidden_call, normed_three[0], grad_third[0], hidden_weights)
    hidden_kept = [own_kept_three, far_kept_three]

    def hidden_part(side, half):
        first = [kept[1][side] for kept in hidden_kept]
        second = [kept[0][side] for kept in hidden_kept]
        return do(
            lambda left, right: weight_grad([([left, right], first), (grad_third, second)], half),
            *normed_three,
        )

    beside_send = hidden_part(1, 1)
    own_send = hidden_part(0, 1)
    far_part = take(far_part)
    beside_send = send(beside_send, "head", 1)
    parts = [part.reshape(rel_shape) for part in (own_kept_three[2], far_part)]
    total_second, low_second, sums_third = kernel(
        back_third_body, [whole_shape, packed_shape, sums_shape], small, grad_low, second, *parts
    )
    order.last = low_second
    low_second = low_second.reshape(local)
    beside_send = take(beside_send)
    far = send(low_second, "head", 2)
    near = send(low_second, "head", 1)
    hidden_send = added(own_send, beside_send)
    hidden_got = send(hidden_send, "space", 1)
    beside_keep = hidden_part(1, 0)
    own_keep = hidden_part(0, 0)
    near = take(near)
    far = take(far)

    diagonal = send(far, "head", 1)
    beside_keep = send(beside_keep, "head", 1)
    grad_two = [low_second, near, far, take(diagonal)]
    time_grads, time_parts = do(
        lambda first, *others: time_call(
            time_back_body,
            clip_length,
            time_weights,
            [[first, *others], time_projected, time_totals],
            [(3 * inner, LOW), (width, LOW)],
        ),
        *grad_two,
    )
    order.last = time_parts[3]
    beside_keep = take(beside_keep)
    diagonal = send(time_parts[3], "head", 1)
    near = send(time_parts[1], "head", 1)
    flat = lambda arrays: [a.reshape(count, a.shape[-1]) for a in arrays]

    def time_part(half):
        lefts, pair = flat(normed_two), (flat(grad_two), flat(time_output))
        return do(lambda *left: weight_grad([(left, flat(time_grads)), pair], half), *lefts)

    far = added(time_parts[2], take(diagonal))
    far = send(far, "head", 2)
    near = take(near)
    time_send = time_part(1)
    time_keep = time_part(0)
    hidden_keep = added(own_keep, beside_keep)
    parts = [part.reshape(rel_shape) for part in (time_parts[0], near, take(far))]
    total_first, sums_second, table_first, packed = kernel(
        back_second_body,
        [whole_shape, sums_shape, sums_shape, packed_shape],
        *scalars,
        small,
        total_second,
        first,
        *parts,
    )
    order.last = packed
    grad_blocks = order.exchange(packed)
    far_out = send(far_kept_three[3], "head", 2)
    hidden_keep, hidden_send = halves(hidden_keep, take(hidden_got))
    hidden_got = send(hidden_send, "space", 2)
    time_got = send(time_send, "space", 1)
    parts = [part.reshape(rel_shape) for part in (own_kept_three[3], take(far_out))]
    frames_out = kernel(finish_forward_body, packed_shape, clip_length, second, *parts)

    grad_blocks = take(grad_blocks)
    grad_one = kernel(collect_body, flat_shape, grad_blocks)
    far = send(grad_one, "head", 2)
    own_result = do(space_back, grad_one, space_weights, own_kept[0], own_kept[2])
    order.last = own_result[1]
    grad_one = [grad_one, take(far)]
    far_result = do(space_back, grad_one[1], space_weights, far_kept[0], far_kept[2])
    order.last = far_result[1]
    far_part = send(far_result[1], "head", 2)

    def space_part(side):
        first = [result[0][side] for result in (own_result, far_result)]
        second = [kept[1][side] for kept in (own_kept, far_kept)]
        return do(
            lambda left, right: weight_grad([([left, right], first), (grad_one, second)]), normed, normed_far
        )

    beside_a = space_part(2)
    space_a = space_part(0)
    hidden_keep, hidden_send = halves(hidden_keep, take(hidden_got))
    hidden_got = send(hidden_send, "space", 4)
    time_keep, time_send = halves(time_keep, take(time_got))
    time_got = send(time_send, "space", 2)
    beside_b = space_part(3)
    space_b = space_part(1)
    far_part = take(far_part)
    beside_a = send(beside_a, "head", 1)
    sums_first, table_second, packed = kernel(
        back_first_body, [sums_shape, sums_shape, packed_shape], *scalars, small, start, own_result[1], far_part
    )
    order.last = packed
    last = order.exchange(packed)
    keep_a, send_a = halves(space_a, take(beside_a))
    got_a = send(send_a, "space", 1)
    beside_b = send(beside_b, "head", 1)
    half_shape = shape_of((BLOCKS // 2, *small_shape), WIDE)
    sums, small_send = kernel(
        small_blocks_body, [half_shape] * 2, sums_first, sums_second, sums_third, table_first, table_second
    )
    order.last = small_send
    got_small = send(small_send, "space", 1)
    keep_b, send_b = halves(space_b, take(beside_b))
    sums, small_send = halves(sums, take(got_small))
    got_small = send(small_send, "space", 2)
    keep_a, send_a = halves(keep_a, take(got_a))
    got_a = send(send_a, "space", 2)
    got_b = send(send_b, "space", 1)
    time_keep, time_send = halves(time_keep, take(time_got))
    keep_a, send_a = halves(keep_a, take(got_a))
    got_a = send(send_a, "space", 4)
    time_got = send(time_send, "space", 4)
    sums, small_send = halves(sums, take(got_small))
    got_small = send(small_send, "space", 4)
    keep_b, send_b = halves(keep_b, take(got_b))
    got_b = send(send_b, "space", 2)
    last = take(last)
    frames_grad = kernel(finish_back_body, whole_shape, clip_length, total_first, last)
    sums = summed(sums, take(got_small))
    got_small = send(sums, "head", 1)
    hidden_grads = kernel(
        unpack_hidden_body,
        [shape_of((width // BLOCKS, hidden), WIDE), shape_of((hidden, width // BLOCKS), WIDE)],
        hidden_keep,
        take(hidden_got),
    )
    time_grads = kernel(unpack_attention_body, grad_shapes, time_keep, take(time_got))
    sums = summed(sums, take(got_small))
    got_small = send(sums, "head", 2)
    got_a = take(got_a)
    keep_b, send_b = halves(keep_b, take(got_b))
    got_b = send(send_b, "space", 4)
    sums = summed(sums, take(got_small))[0]
    step = sums.shape[1] // ROUND
    sums = lax.dynamic_slice(sums, (0, lax.axis_index("head") * step), (sums.shape[0], step))
    space_grads = kernel(unpack_attention_body, grad_shapes, keep_a, got_a, keep_b, take(got_b))
    return (
        frames_out.reshape(local),
        frames_grad.reshape(local),
        sums[0:3],
        sums[3:6],
        sums[6:14],
        jnp.transpose(space_grads[0], (1, 0, 2)),
        space_grads[1],
        jnp.transpose(time_grads[0], (1, 0, 2)),
        time_grads[1],
        *hidden_grads,
    )


def solution(mesh):
    placed = (
        P("head", None, "space", None),
        P("head", None),
        P(),
        P(None, ("space", "head")),
        P(None, ("space", "head")),
        P(None, ("space", "head")),
        P("space", None, "head"),
        P("head", "space"),
        P("space", None, "head"),
        P("head", "space"),
        P("space", "head"),
        P("head", "space"),
        P("head", None, "space", None),
    )
    eight = mesh.shape["space"] == BLOCKS and mesh.shape["head"] == ROUND
    return jax.shard_map(
        shards if eight else general_shards,
        mesh=mesh,
        in_specs=placed,
        out_specs=(
            P("head", None, "space", None),
            P("head", None, "space", None),
            P(None, ("space", "head")),
            P(None, ("space", "head")),
            P(None, ("space", "head")),
            P("space", None, "head"),
            P("head", "space"),
            P("space", None, "head"),
            P("head", "space"),
            P("space", "head"),
            P("head", "space"),
        ),
        check_vma=False,
    )
```

```python
import functools

import jax
import jax.numpy as jnp
from jax import lax
from jax.experimental import pallas as pl
from jax.experimental.pallas import tpu as pltpu
from jax.sharding import PartitionSpec as P

HEAD_DIM = 64


EPSILON = 1e-05
SCORE_SCALE = 0.125
MASKED_SCORE = -1e30
PRECISE = lax.Precision.HIGHEST
GELU_COEFF = 0.7978845608028654


def layer_norm(values, gain_row, bias_row):
    row_mean = jnp.mean(values, axis=-1, keepdims=True)
    centred = values - row_mean
    row_var = jnp.mean(centred * centred, axis=-1, keepdims=True)
    return centred * lax.rsqrt(row_var + EPSILON) * gain_row + bias_row


def gelu_tanh(inputs):
    return (
        0.5 * inputs * (1.0 + jnp.tanh(GELU_COEFF * (inputs + 0.044715 * inputs * inputs * inputs)))
    )


def gather_weights(small, large):
    small_full = (
        lax.all_gather(small[0], ("space", "head"), axis=1, tiled=True),
        lax.all_gather(small[1], ("space", "head"), axis=1, tiled=True),
        lax.all_gather(small[2], ("space", "head"), axis=1, tiled=True),
    )
    large_full = (
        lax.all_gather(large[0], "space", axis=0, tiled=True),
        lax.all_gather(large[1], "space", axis=1, tiled=True),
        lax.all_gather(large[2], "space", axis=0, tiled=True),
        lax.all_gather(large[3], "space", axis=1, tiled=True),
        lax.all_gather(large[4], "space", axis=0, tiled=True),
        lax.all_gather(large[5], "space", axis=1, tiled=True),
    )
    return (small_full, large_full)


def norm_step(inputs, gain_row, bias_row):
    normed, pullback = jax.vjp(layer_norm, inputs, gain_row, bias_row)
    whole = lax.all_gather(normed.astype(jnp.bfloat16), "head", axis=0, tiled=True)
    return (whole, pullback)


def cot_whole(grad_rows):
    return lax.all_gather(grad_rows.astype(jnp.bfloat16), "head", axis=0, tiled=True)


def input_total(partial_value):
    return lax.psum_scatter(
        partial_value.astype(jnp.bfloat16), "head", scatter_dimension=0, tiled=True
    ).astype(jnp.float32)


def heads_total(left, weight):
    return lax.psum_scatter(
        jnp.einsum("fcpe,ed->fcpd", left, weight, preferred_element_type=jnp.float32).astype(
            jnp.bfloat16
        ),
        "head",
        scatter_dimension=0,
        tiled=True,
    ).astype(jnp.float32)


def project_in(whole, weight):
    stacked = jnp.einsum(
        "fcpd,dke->kfcpe", whole, weight, preferred_element_type=jnp.float32
    ).astype(jnp.bfloat16)
    return (stacked[0], stacked[1], stacked[2])


def raw_scores(queries, keyset, form, allowed):
    key_form = form.replace("q", "k")
    scores = (
        jnp.einsum(
            form + "," + key_form + "->bhqk", queries, keyset, preferred_element_type=jnp.float32
        )
        * SCORE_SCALE
    )
    if allowed is not None:
        scores = jnp.where(allowed, scores, MASKED_SCORE)
    return scores


def attend(queries, keyset, values, form, allowed):
    key_form = form.replace("q", "k")
    scores = raw_scores(queries, keyset, form, allowed)
    row_max = jnp.max(scores, axis=-1, keepdims=True)
    log_total = row_max + jnp.log(jnp.sum(jnp.exp(scores - row_max), axis=-1, keepdims=True))
    shares = jnp.exp(scores - log_total).astype(jnp.bfloat16)
    output = jnp.einsum(
        "bhqk," + key_form + "->" + form, shares, values, preferred_element_type=jnp.float32
    )
    return (output.astype(jnp.bfloat16), log_total)


def attend_back(queries, keyset, values, log_total, output_grad, form, allowed):
    key_form = form.replace("q", "k")
    shares = jnp.exp(raw_scores(queries, keyset, form, allowed) - log_total)
    value_grad = jnp.einsum(
        "bhqk," + form + "->" + key_form,
        shares.astype(jnp.bfloat16),
        output_grad,
        preferred_element_type=jnp.float32,
    )
    share_grad = jnp.einsum(
        form + "," + key_form + "->bhqk", output_grad, values, preferred_element_type=jnp.float32
    )
    score_grad = (
        shares * (share_grad - jnp.sum(share_grad * shares, axis=-1, keepdims=True))
    ).astype(jnp.bfloat16)
    query_grad = (
        jnp.einsum(
            "bhqk," + key_form + "->" + form, score_grad, keyset, preferred_element_type=jnp.float32
        )
        * SCORE_SCALE
    )
    key_grad = (
        jnp.einsum(
            "bhqk," + form + "->" + key_form,
            score_grad,
            queries,
            preferred_element_type=jnp.float32,
        )
        * SCORE_SCALE
    )
    return (
        query_grad.astype(jnp.bfloat16),
        key_grad.astype(jnp.bfloat16),
        value_grad.astype(jnp.bfloat16),
    )


def general_shards(
    frames_in,
    action_codes,
    clip_length,
    norm_gain,
    norm_bias,
    action_table,
    spatialin,
    spatialout,
    temporalin,
    temporalout,
    expand,
    shrink,
    out_grad,
):
    head_count = lax.axis_size("head")
    frames_local, clip_count, pos_local, width = frames_in.shape
    frames_total = frames_local * head_count
    local_width = spatialin.shape[2]
    heads_local = local_width // HEAD_DIM
    frame_index = jnp.arange(frames_total)
    local_index = lax.axis_index("head") * frames_local + jnp.arange(frames_local)
    valid_local = (local_index[:, None] < clip_length[None, :]).astype(jnp.float32)[
        :, :, None, None
    ]
    allowed = (frame_index[None, :, None] >= frame_index[None, None, :]) & (
        frame_index[None, None, :] < clip_length[:, None, None]
    )
    allowed = jnp.broadcast_to(
        allowed[:, None, None], (clip_count, pos_local, 1, frames_total, frames_total)
    )
    allowed = allowed.reshape(clip_count * pos_local, 1, frames_total, frames_total)
    small_full, large_full = gather_weights(
        (norm_gain, norm_bias, action_table),
        (spatialin, spatialout, temporalin, temporalout, expand, shrink),
    )
    gain_full, bias_full, table_full = small_full
    space_in, space_out, time_in, time_out, expand_full, shrink_full = large_full
    code_hot = (action_codes[:, :, None] == jnp.arange(table_full.shape[0])[None, None, :]).astype(
        jnp.float32
    )
    embedded = jnp.einsum("fca,ad->fcd", code_hot, table_full, precision=PRECISE)
    start = valid_local * (frames_in.astype(jnp.float32) + embedded[:, :, None, :])
    whole_one, pull_one = norm_step(start, gain_full[0], bias_full[0])
    space_query, space_keys, space_values = project_in(whole_one, space_in)
    flat_shape = (frames_total * clip_count, pos_local, local_width)
    moved = (
        lax.all_to_all(
            space_query.reshape(flat_shape), "space", split_axis=0, concat_axis=1, tiled=True
        ),
        lax.all_to_all(
            space_keys.reshape(flat_shape), "space", split_axis=0, concat_axis=1, tiled=True
        ),
        lax.all_to_all(
            space_values.reshape(flat_shape), "space", split_axis=0, concat_axis=1, tiled=True
        ),
    )
    block_rows = moved[0].shape[0]
    block_cols = moved[0].shape[1]
    frame_shape = (block_rows, block_cols, heads_local, HEAD_DIM)
    frame_query = moved[0].reshape(frame_shape)
    frame_keys = moved[1].reshape(frame_shape)
    frame_values = moved[2].reshape(frame_shape)
    frame_out, frame_total = attend(frame_query, frame_keys, frame_values, "bqhe", None)
    returned = lax.all_to_all(
        frame_out.reshape(block_rows, block_cols, local_width),
        "space",
        split_axis=1,
        concat_axis=0,
        tiled=True,
    )
    space_attended = returned.reshape(frames_total, clip_count, pos_local, local_width)
    first = start + heads_total(space_attended, space_out)
    whole_two, pull_two = norm_step(first, gain_full[1], bias_full[1])
    time_query, time_keys, time_values = project_in(whole_two, time_in)
    time_shape = (frames_total, clip_count * pos_local, heads_local, HEAD_DIM)
    time_query = time_query.reshape(time_shape)
    time_keys = time_keys.reshape(time_shape)
    time_values = time_values.reshape(time_shape)
    time_out_rows, time_total = attend(time_query, time_keys, time_values, "qbhe", allowed)
    time_attended = time_out_rows.reshape(frames_total, clip_count, pos_local, local_width)
    second = first + heads_total(time_attended, time_out)
    whole_three, pull_three = norm_step(second, gain_full[2], bias_full[2])
    expanded = jnp.einsum(
        "fcpd,dh->fcph", whole_three, expand_full, preferred_element_type=jnp.float32
    )
    activated, gelu_pull = jax.vjp(gelu_tanh, expanded)
    activated_low = activated.astype(jnp.bfloat16)
    third = second + heads_total(activated_low, shrink_full)
    frames_out = (valid_local * third).astype(jnp.bfloat16)
    small_full, large_full = gather_weights(
        (norm_gain, norm_bias, action_table),
        (spatialin, spatialout, temporalin, temporalout, expand, shrink),
    )
    space_in, space_out, time_in, time_out, expand_full, shrink_full = large_full
    grad_third = valid_local * out_grad.astype(jnp.float32)
    cot_three = cot_whole(grad_third)
    shrink_part = jnp.einsum(
        "fcph,fcpd->hd", activated_low, cot_three, preferred_element_type=jnp.float32
    )
    act_grad = jnp.einsum(
        "fcpd,hd->fcph", cot_three, shrink_full, preferred_element_type=jnp.float32
    )
    pre_grad = gelu_pull(act_grad)[0].astype(jnp.bfloat16)
    expand_part = jnp.einsum(
        "fcpd,fcph->dh", whole_three, pre_grad, preferred_element_type=jnp.float32
    )
    normed_grad = input_total(
        jnp.einsum("fcph,dh->fcpd", pre_grad, expand_full, preferred_element_type=jnp.float32)
    )
    input_three, gain_three, bias_three = pull_three(normed_grad)
    grad_second = grad_third + input_three
    cot_two = cot_whole(grad_second)
    time_out_part = jnp.einsum(
        "fcpe,fcpd->ed", time_attended, cot_two, preferred_element_type=jnp.float32
    )
    time_grad = jnp.einsum(
        "fcpd,ed->fcpe", cot_two, time_out, preferred_element_type=jnp.float32
    ).astype(jnp.bfloat16)
    time_grads = attend_back(
        time_query,
        time_keys,
        time_values,
        time_total,
        time_grad.reshape(time_shape),
        "qbhe",
        allowed,
    )
    stacked_grad = jnp.stack(
        [member.reshape(frames_total, clip_count, pos_local, local_width) for member in time_grads]
    )
    time_in_part = jnp.einsum(
        "fcpd,kfcpe->dke", whole_two, stacked_grad, preferred_element_type=jnp.float32
    )
    normed_grad = input_total(
        jnp.einsum("kfcpe,dke->fcpd", stacked_grad, time_in, preferred_element_type=jnp.float32)
    )
    input_two, gain_two, bias_two = pull_two(normed_grad)
    grad_first = grad_second + input_two
    cot_one = cot_whole(grad_first)
    space_out_part = jnp.einsum(
        "fcpe,fcpd->ed", space_attended, cot_one, preferred_element_type=jnp.float32
    )
    space_grad = jnp.einsum(
        "fcpd,ed->fcpe", cot_one, space_out, preferred_element_type=jnp.float32
    ).astype(jnp.bfloat16)
    frame_grad = lax.all_to_all(
        space_grad.reshape(flat_shape), "space", split_axis=0, concat_axis=1, tiled=True
    ).reshape(frame_shape)
    query_grad, keys_grad, values_grad = attend_back(
        frame_query, frame_keys, frame_values, frame_total, frame_grad, "bqhe", None
    )
    block_shape = (block_rows, block_cols, local_width)
    back_grads = (
        lax.all_to_all(
            query_grad.reshape(block_shape), "space", split_axis=1, concat_axis=0, tiled=True
        ),
        lax.all_to_all(
            keys_grad.reshape(block_shape), "space", split_axis=1, concat_axis=0, tiled=True
        ),
        lax.all_to_all(
            values_grad.reshape(block_shape), "space", split_axis=1, concat_axis=0, tiled=True
        ),
    )
    stacked_grad = jnp.stack(
        [member.reshape(frames_total, clip_count, pos_local, local_width) for member in back_grads]
    )
    space_in_part = jnp.einsum(
        "fcpd,kfcpe->dke", whole_one, stacked_grad, preferred_element_type=jnp.float32
    )
    normed_grad = input_total(
        jnp.einsum("kfcpe,dke->fcpd", stacked_grad, space_in, preferred_element_type=jnp.float32)
    )
    input_one, gain_one, bias_one = pull_one(normed_grad)
    grad_start = grad_first + input_one
    frames_grad = valid_local * grad_start
    table_part = jnp.einsum(
        "fca,fcd->ad", code_hot, jnp.sum(frames_grad, axis=2), precision=PRECISE
    )
    gain_grad, bias_grad, table_grad = (
        lax.psum_scatter(
            jnp.stack([gain_one, gain_two, gain_three]),
            ("space", "head"),
            scatter_dimension=1,
            tiled=True,
        ),
        lax.psum_scatter(
            jnp.stack([bias_one, bias_two, bias_three]),
            ("space", "head"),
            scatter_dimension=1,
            tiled=True,
        ),
        lax.psum_scatter(table_part, ("space", "head"), scatter_dimension=1, tiled=True),
    )
    weight_grads = (
        lax.psum_scatter(space_in_part, "space", scatter_dimension=0, tiled=True),
        lax.psum_scatter(space_out_part, "space", scatter_dimension=1, tiled=True),
        lax.psum_scatter(time_in_part, "space", scatter_dimension=0, tiled=True),
        lax.psum_scatter(time_out_part, "space", scatter_dimension=1, tiled=True),
        lax.psum_scatter(expand_part, "space", scatter_dimension=0, tiled=True),
        lax.psum_scatter(shrink_part, "space", scatter_dimension=1, tiled=True),
    )
    return (
        frames_out,
        frames_grad,
        gain_grad,
        bias_grad,
        table_grad,
        weight_grads[0],
        weight_grads[1],
        weight_grads[2],
        weight_grads[3],
        weight_grads[4],
        weight_grads[5],
    )


ORDER = (0, 4, 2, 6, 1, 5, 3, 7)
BLOCKS = len(ORDER)
PLACE = tuple(ORDER.index(mask) for mask in range(BLOCKS))
ROUND = 4
ONE_VMEM = pl.BlockSpec(memory_space=pltpu.VMEM)
ONE_SMEM = pl.BlockSpec(memory_space=pltpu.SMEM)
MIB = 1024 * 1024
LOW = jnp.bfloat16
WIDE = jnp.float32


def swap(value, axis, mask):
    return lax.ppermute(value, axis, [(i, i ^ mask) for i in range(lax.axis_size(axis))])


class Order:
    def __init__(self):
        self.last = None

    def tied(self, value):
        if self.last is None:
            return value
        return lax.optimization_barrier((value, self.last))[0]

    def send(self, value, axis, mask):
        return swap(self.tied(value), axis, mask)

    def exchange(self, packed):
        return lax.all_to_all(self.tied(packed), "space", split_axis=0, concat_axis=0, tiled=True)

    def take(self, value):
        self.last = self.tied(value)
        return self.last

    def do(self, step, first, *others):
        result = step(self.tied(first), *others)
        self.last = jax.tree.leaves(result)[0]
        return result


def run(body, outs, args, specs, vmem=None, stored=()):
    single = not isinstance(outs, (list, tuple))
    name = getattr(body, "func", body).__name__.removesuffix("_body")
    args, specs, scratch, whole = list(args), list(specs), [], body
    if stored:
        for place in stored:
            args[place] = pltpu.with_memory_space_constraint(args[place], pltpu.HBM)
            specs[place] = pl.BlockSpec(memory_space=pltpu.HBM)
            scratch.append(pltpu.VMEM(args[place].shape, args[place].dtype))
        scratch.append(pltpu.SemaphoreType.DMA((len(stored),)))

        def whole(*refs):
            refs, held, sem = list(refs[: -len(scratch)]), refs[-len(scratch) : -1], refs[-1]
            copies = [
                pltpu.make_async_copy(refs[place], held[i], sem.at[i]) for i, place in enumerate(stored)
            ]
            for copy in copies:
                copy.start()
            for i, place in enumerate(stored):
                copies[i].wait()
                refs[place] = held[i]
            body(*refs)

    return pl.pallas_call(
        whole,
        out_shape=outs,
        in_specs=specs,
        out_specs=ONE_VMEM if single else [ONE_VMEM] * len(outs),
        scratch_shapes=scratch,
        cost_estimate=pl.CostEstimate(flops=0, bytes_accessed=1024, transcendentals=0),
        compiler_params=pltpu.CompilerParams(vmem_limit_bytes=vmem or 12 * MIB),
        name=name,
    )(*args)


def kept_of(dims, dtype):
    return pltpu.HBM(tuple(dims), dtype)


def shape_of(dims, dtype):
    return jax.ShapeDtypeStruct(tuple(dims), dtype)


def feature_block(place, step):
    return pl.ds(pl.multiple_of(place * step, step), step)


def partner(mask):
    return lax.axis_index("space") ^ mask


def frame_valid(lengths, frames, mask):
    clips = lengths.shape[0]
    frame = lax.axis_index("head") * (frames // clips) + partner(mask) // clips
    return jnp.where(frame < lengths[partner(mask) % clips], 1.0, 0.0).astype(WIDE)


def normed_parts(values):
    centred = values - jnp.mean(values, axis=-1, keepdims=True)
    scale = lax.rsqrt(jnp.mean(centred * centred, axis=-1, keepdims=True) + EPSILON)
    return centred * scale, scale


def norm_back(values, grad, gain_row):
    unit, scale = normed_parts(values)
    scaled = grad * gain_row
    out = scale * (
        scaled
        - jnp.mean(scaled, axis=-1, keepdims=True)
        - unit * jnp.mean(scaled * unit, axis=-1, keepdims=True)
    )
    return (
        out,
        jnp.sum(grad * unit, axis=0, keepdims=True),
        jnp.sum(grad, axis=0, keepdims=True),
    )


def store_for(ref, rows, mask):
    step = rows.shape[-1] // BLOCKS
    for i in range(BLOCKS):
        j = i ^ PLACE[mask]
        ref[partner(mask), :, i * step : (i + 1) * step] = rows[:, j * step : (j + 1) * step]


def pack_attention_body(enter, leave, *outs):
    step = leave.shape[0] // len(outs)
    for i, out in enumerate(outs):
        place = slice(i * step, (i + 1) * step)
        for j in range(3):
            out[:, j * step : (j + 1) * step] = enter[j, :, place]
        out[:, 3 * step :] = jnp.transpose(leave[place, :])


def unpack_attention_body(*refs):
    pairs, (enter, leave) = refs[:-2], refs[-2:]
    step = leave.shape[0] // (len(pairs) // 2)
    for i in range(len(pairs) // 2):
        total = pairs[2 * i][...].astype(WIDE) + pairs[2 * i + 1][...].astype(WIDE)
        place = slice(i * step, (i + 1) * step)
        for j in range(3):
            enter[j, :, place] = total[:, j * step : (j + 1) * step]
        leave[place, :] = jnp.transpose(total[:, 3 * step :])


def pack_hidden_body(enter, leave, out):
    hidden = leave.shape[0]
    out[:, :hidden] = enter[...]
    out[:, hidden:] = jnp.transpose(leave[...])


def unpack_hidden_body(total, enter, leave):
    hidden = leave.shape[0]
    enter[...] = total[:, :hidden].astype(WIDE)
    leave[...] = jnp.transpose(total[:, hidden:].astype(WIDE))


def pack_frames_body(frames, out):
    step = frames.shape[-1] // BLOCKS
    for mask in range(BLOCKS):
        for i in range(BLOCKS):
            source = partner(ORDER[i ^ PLACE[mask]])
            place = slice(i * step, (i + 1) * step)
            out[partner(mask), :, place] = frames[partner(mask), :, feature_block(source, step)]


def order_inputs_body(lengths, frames, grad, frames_out, grad_out):
    step = frames.shape[-1] // BLOCKS

    def one(mask, carry):
        valid = frame_valid(lengths, BLOCKS, mask)
        for i in range(BLOCKS):
            source = feature_block(partner(ORDER[i]), step)
            place = slice(i * step, (i + 1) * step)
            frames_out[mask, :, place] = frames[partner(mask), :, source]
            kept = grad[partner(mask), :, source].astype(WIDE) * valid
            grad_out[mask, :, place] = kept.astype(LOW)
        return carry

    lax.fori_loop(0, BLOCKS, one, 0)


def start_rows(rows, codes, lengths, small, mask):
    embedded = small[pl.ds(6 + codes[partner(mask)], 1), :]
    return frame_valid(lengths, BLOCKS, mask) * (rows.astype(WIDE) + embedded)


def frame_norm_body(codes, lengths, small, blocks, normed, start):
    rows = blocks.shape[1]
    for b in range(BLOCKS):
        values = start_rows(blocks[partner(b)], codes, lengths, small, 0)
        start[b * rows : (b + 1) * rows, :] = values
        unit, _ = normed_parts(values)
        normed[b * rows : (b + 1) * rows, :] = (unit * small[0:1, :] + small[3:4, :]).astype(LOW)


def spread_body(first, second, out):
    rows = out.shape[1]
    for mask in range(BLOCKS):
        part = slice(mask * rows, (mask + 1) * rows)
        total = first[part, :].astype(WIDE) + second[part, :].astype(WIDE)
        store_for(out, total.astype(LOW), mask)


def join_norm_body(codes, lengths, small, frames, blocks, whole, normed):
    for b in range(BLOCKS):
        values = start_rows(frames[b], codes, lengths, small, b) + blocks[partner(b)].astype(WIDE)
        whole[b] = values
        unit, _ = normed_parts(values)
        normed[b] = (unit * small[1:2, :] + small[4:5, :]).astype(LOW)


def add_norm_body(small, before, first, second, third, whole, normed):
    def one(b, carry):
        values = before[b] + (
            first[b].astype(WIDE) + second[b].astype(WIDE) + third[b].astype(WIDE)
        )
        whole[b] = values
        unit, _ = normed_parts(values)
        normed[b] = (unit * small[2:3, :] + small[5:6, :]).astype(LOW)
        return carry

    lax.fori_loop(0, BLOCKS, one, 0)


def finish_forward_body(lengths, before, first, second, out):
    step = out.shape[-1] // BLOCKS

    def one(b, carry):
        values = before[b] + (first[b].astype(WIDE) + second[b].astype(WIDE))
        values = (frame_valid(lengths, BLOCKS, b) * values).astype(LOW)
        for i in range(BLOCKS):
            place = feature_block(partner(ORDER[i]), step)
            out[partner(b), :, place] = values[:, i * step : (i + 1) * step]
        return carry

    lax.fori_loop(0, BLOCKS, one, 0)


def back_third_body(small, grad, values, first, second, total_out, low_out, sums):
    sums[...] = jnp.zeros_like(sums)

    def one(b, carry):
        normed_grad = first[b].astype(WIDE) + second[b].astype(WIDE)
        out, gain, bias = norm_back(values[b], normed_grad, small[2:3, :])
        total = grad[b].astype(WIDE) + out
        total_out[b] = total
        low_out[b] = total.astype(LOW)
        sums[0:1, :] += gain
        sums[1:2, :] += bias
        return carry

    lax.fori_loop(0, BLOCKS, one, 0)


def back_second_body(codes, lengths, small, grad, values, first, second, third, total_out, sums, table, packed):
    sums[...] = jnp.zeros_like(sums)
    table[...] = jnp.zeros_like(table)
    for b in range(BLOCKS):
        normed_grad = first[b].astype(WIDE) + second[b].astype(WIDE) + third[b].astype(WIDE)
        out, gain, bias = norm_back(values[b], normed_grad, small[1:2, :])
        total = grad[b] + out
        total_out[b] = total
        store_for(packed, total.astype(LOW), b)
        sums[0:1, :] += gain
        sums[1:2, :] += bias
        row = pl.ds(codes[partner(b)], 1)
        table[row, :] += frame_valid(lengths, BLOCKS, b) * jnp.sum(total, axis=0, keepdims=True)


def back_first_body(codes, lengths, small, values, first, second, sums, table, packed):
    sums[...] = jnp.zeros_like(sums)
    table[...] = jnp.zeros_like(table)
    rows = packed.shape[1]
    for b in range(BLOCKS):
        part = slice(b * rows, (b + 1) * rows)
        normed_grad = first[part, :].astype(WIDE) + second[part, :].astype(WIDE)
        out, gain, bias = norm_back(values[part, :], normed_grad, small[0:1, :])
        store_for(packed, out.astype(LOW), b)
        sums[0:1, :] += gain
        sums[1:2, :] += bias
        row = pl.ds(codes[partner(0)], 1)
        table[row, :] += frame_valid(lengths, BLOCKS, 0) * jnp.sum(out, axis=0, keepdims=True)


def collect_body(blocks, out):
    rows = blocks.shape[1]
    for b in range(BLOCKS):
        out[b * rows : (b + 1) * rows, :] = blocks[partner(b)]


def finish_back_body(lengths, grad, blocks, out):
    step = out.shape[-1] // BLOCKS
    for b in range(BLOCKS):
        values = frame_valid(lengths, BLOCKS, b) * (grad[b] + blocks[partner(b)].astype(WIDE))
        for i in range(BLOCKS):
            place = feature_block(partner(ORDER[i]), step)
            out[partner(b), :, place] = values[:, i * step : (i + 1) * step]


def matmul(left, right):
    return lax.dot_general(left, right, (((1,), (0,)), ((), ())), preferred_element_type=WIDE)


def matmul_t(left, right):
    return lax.dot_general(left, right, (((1,), (1,)), ((), ())), preferred_element_type=WIDE)


def matmul_tn(left, right):
    return lax.dot_general(left, right, (((0,), (0,)), ((), ())), preferred_element_type=WIDE)


def head_mask(width, head):
    lane = lax.broadcasted_iota(jnp.int32, (1, width), 1)
    return (lane // HEAD_DIM) == head


def pick(values, mask):
    return jnp.where(mask, values, jnp.zeros_like(values))


def attention_rows(projected, allowed, totals, first):
    width = projected.shape[1] // 3
    queries = projected[:, :width] * jnp.asarray(SCORE_SCALE, LOW)
    keyset = projected[:, width : 2 * width]
    values = projected[:, 2 * width :]
    lane = lax.broadcasted_iota(jnp.int32, (1, 128), 1)
    output = jnp.zeros((projected.shape[0], width), WIDE)
    for head in range(width // HEAD_DIM):
        mask = head_mask(width, head)
        scores = matmul_t(pick(queries, mask), keyset)
        if allowed is not None:
            scores = jnp.where(allowed, scores, MASKED_SCORE)
        row_max = jnp.max(scores, axis=-1, keepdims=True)
        raised = jnp.exp(scores - row_max)
        total = jnp.sum(raised, axis=-1, keepdims=True)
        shares = (raised * (1.0 / total)).astype(LOW)
        output = output + matmul(shares, pick(values, mask))
        totals = jnp.where(lane == first + head, row_max + jnp.log(total), totals)
    return output.astype(LOW), totals


def attention_rows_back(projected, totals, first, output_grad, allowed):
    width = projected.shape[1] // 3
    queries = projected[:, :width] * jnp.asarray(SCORE_SCALE, LOW)
    keyset = projected[:, width : 2 * width]
    values = projected[:, 2 * width :]
    scaled_keys = keyset * jnp.asarray(SCORE_SCALE, LOW)
    shape = (projected.shape[0], width)
    query_grad, key_grad, value_grad = (jnp.zeros(shape, WIDE) for _ in range(3))
    for head in range(width // HEAD_DIM):
        mask = head_mask(width, head)
        own_queries = pick(queries, mask)
        own_grad = pick(output_grad, mask)
        scores = matmul_t(own_queries, keyset)
        if allowed is not None:
            scores = jnp.where(allowed, scores, MASKED_SCORE)
        shares = jnp.exp(scores - totals[:, first + head : first + head + 1])
        value_grad = value_grad + matmul_tn(shares.astype(LOW), own_grad)
        share_grad = matmul_t(own_grad, values)
        score_grad = shares * (share_grad - jnp.sum(share_grad * shares, axis=-1, keepdims=True))
        score_grad = score_grad.astype(LOW)
        query_grad = query_grad + matmul(score_grad, pick(scaled_keys, mask))
        key_grad = key_grad + matmul_tn(score_grad, own_queries)
    return jnp.concatenate(
        [query_grad.astype(LOW), key_grad.astype(LOW), value_grad.astype(LOW)], axis=1
    )


def enter_rows(rows, parts, columns):
    depth = parts[0].shape[0]
    total = matmul(rows[:, :depth], parts[0][:, columns])
    for i, part in enumerate(parts[1:], 1):
        total = total + matmul(rows[:, i * depth : (i + 1) * depth], part[:, columns])
    return total


def leave_rows(sides, columns, store):
    depth = sides[0][1][0].shape[0]
    for i in range(len(sides[0][1])):
        total = matmul_t(sides[0][0], sides[0][1][i][:, columns])
        for values, parts in sides[1:]:
            total = total + matmul_t(values, parts[i][:, columns])
        store(slice(i * depth, (i + 1) * depth), total.astype(LOW))


def side_columns(side, width):
    return slice(side * width, (side + 1) * width)


def space_forward_body(count, rows, *refs):
    sides = [[ref] for ref in refs[:count]]
    projected_out, output_out, totals_out, part_out = refs[count:]
    width = output_out.shape[1] // count
    totals = jnp.zeros(totals_out.shape, WIDE)
    leaving = []
    for side, parts in enumerate(sides):
        projected = enter_rows(rows, parts, slice(0, 3 * width)).astype(LOW)
        projected_out[:, side_columns(side, 3 * width)] = projected
        output, totals = attention_rows(projected, None, totals, side * (width // HEAD_DIM))
        output_out[:, side_columns(side, width)] = output
        leaving.append((output, parts))
    totals_out[...] = totals

    def store(place, values):
        part_out[:, place] = values

    leave_rows(leaving, slice(3 * width, 4 * width), store)


def space_back_body(count, rows, *refs):
    sides = [[ref] for ref in refs[:count]]
    projected, totals, grads_out, part_out = refs[count:]
    width = projected.shape[1] // (3 * count)
    leaving = []
    for side, parts in enumerate(sides):
        output_grad = enter_rows(rows, parts, slice(3 * width, 4 * width)).astype(LOW)
        first, columns = side * (width // HEAD_DIM), side_columns(side, 3 * width)
        grads = attention_rows_back(projected[:, columns], totals[...], first, output_grad, None)
        grads_out[:, columns] = grads
        leaving.append((grads, parts))

    def store(place, values):
        part_out[:, place] = values

    leave_rows(leaving, slice(0, 3 * width), store)


def time_allowed(lengths, clip, frames_local, positions):
    clips = lengths.shape[0]
    count = ROUND * frames_local * positions
    head_at, frame_at = lax.axis_index("head"), partner(0) // clips

    def split(shape, axis):
        row = lax.broadcasted_iota(jnp.int32, shape, axis)
        group = row // (frames_local * positions)
        local = (row // positions) % frames_local
        return (group ^ head_at) * frames_local + (local ^ frame_at), row % positions

    query_frame, query_pos = split((count, 1), 0)
    key_frame, key_pos = split((1, count), 1)
    length = lengths[(partner(0) % clips) ^ clip]
    return (query_pos == key_pos) & (query_frame >= key_frame) & (key_frame < length)


PART = 16


def time_groups(ref):
    return [(c, p) for c in range(ref.shape[1]) for p in range(0, ref.shape[2], PART)]


def join_rows(refs, group):
    c, p = group
    return jnp.concatenate(
        [ref[:, c, p : p + PART, :].reshape(ref.shape[0] * PART, ref.shape[3]) for ref in refs], axis=0
    )


def split_rows(refs, group, values, place=slice(None)):
    c, p = group
    rows = values.shape[0] // len(refs)
    for i, ref in enumerate(refs):
        part = values[i * rows : (i + 1) * rows].reshape(ref.shape[0], PART, values.shape[1])
        ref[:, c, p : p + PART, place] = part


def time_forward_body(lengths, *refs):
    parts, refs = refs[:2], refs[2:]
    rows, projected_out, output_out, totals_out, part_out = (refs[i : i + 4] for i in range(0, 20, 4))
    frames_local, width = rows[0].shape[0], output_out[0].shape[3]
    for group in time_groups(rows[0]):
        joined = join_rows(rows, group)
        projected = enter_rows(joined, parts, slice(0, 3 * width)).astype(LOW)
        split_rows(projected_out, group, projected)
        allowed = time_allowed(lengths, group[0], frames_local, PART)
        totals = jnp.zeros((projected.shape[0], 128), WIDE)
        output, totals = attention_rows(projected, allowed, totals, 0)
        split_rows(output_out, group, output)
        split_rows(totals_out, group, totals)
        leave_rows(
            [(output, parts)],
            slice(3 * width, 4 * width),
            lambda place, values, group=group: split_rows(part_out, group, values, place),
        )


def time_back_body(lengths, *refs):
    parts, refs = refs[:2], refs[2:]
    rows, projected, totals, grads_out, part_out = (refs[i : i + 4] for i in range(0, 20, 4))
    frames_local, width = rows[0].shape[0], projected[0].shape[3] // 3
    for group in time_groups(rows[0]):
        allowed = time_allowed(lengths, group[0], frames_local, PART)
        joined = join_rows(rows, group)
        output_grad = enter_rows(joined, parts, slice(3 * width, 4 * width)).astype(LOW)
        grads = attention_rows_back(
            join_rows(projected, group), join_rows(totals, group), 0, output_grad, allowed
        )
        split_rows(grads_out, group, grads)
        leave_rows(
            [(grads, parts)],
            slice(0, 3 * width),
            lambda place, values, group=group: split_rows(part_out, group, values, place),
        )


def space_forward(rows, weights):
    count, width = rows.shape
    sides, inner = len(weights), weights[0].shape[1] // 4
    outs = [
        kept_of((count, 3 * inner * sides), LOW),
        kept_of((count, inner * sides), LOW),
        kept_of((count, 128), WIDE),
        shape_of((count, width), LOW),
    ]
    body = functools.partial(space_forward_body, sides)
    return run(body, outs, (rows, *weights), [ONE_VMEM] * (1 + sides))


def space_back(rows, weights, projected, totals):
    count, width = rows.shape
    sides = len(weights)
    outs = [shape_of(projected.shape, LOW), shape_of((count, width), LOW)]
    args = (rows, *weights, projected, totals)
    body = functools.partial(space_back_body, sides)
    return run(body, outs, args, [ONE_VMEM] * len(args), stored=(sides + 1, sides + 2))


def time_call(body, lengths, weights, groups, out_widths):
    args, outs = [lengths, *weights], []
    for group in groups:
        args += group
    for features, dtype, shape in out_widths:
        outs += [shape((*groups[0][0].shape[:3], features), dtype)] * ROUND
    stored = range(1 + len(weights) + ROUND, len(args))
    results = run(body, outs, args, [ONE_SMEM] + [ONE_VMEM] * (len(args) - 1), vmem=16 * MIB, stored=stored)
    return [results[i : i + ROUND] for i in range(0, len(results), ROUND)]


def reorder_body(blocks, out, sem):
    rows = blocks.shape[1]
    copies = [
        pltpu.make_async_copy(blocks.at[partner(ORDER[i])], out.at[pl.ds(i * rows, rows), :], sem.at[i])
        for i in range(BLOCKS)
    ]
    for copy in copies:
        copy.start()
    for copy in copies:
        copy.wait()


def reorder(blocks):
    count, rows, columns = blocks.shape
    return pl.pallas_call(
        reorder_body,
        out_shape=shape_of((count * rows, columns), blocks.dtype),
        in_specs=[pl.BlockSpec(memory_space=pltpu.HBM)],
        out_specs=ONE_VMEM,
        scratch_shapes=[pltpu.SemaphoreType.DMA((count,))],
        cost_estimate=pl.CostEstimate(flops=0, bytes_accessed=1024, transcendentals=0),
        compiler_params=pltpu.CompilerParams(vmem_limit_bytes=12 * MIB),
        name="reorder",
    )(pltpu.with_memory_space_constraint(blocks, pltpu.HBM))


def add_order_body(first, second, out):
    rows = out.shape[1]
    for i in range(BLOCKS):
        part = slice(i * rows, (i + 1) * rows)
        out[partner(ORDER[i])] = (first[part].astype(WIDE) + second[part].astype(WIDE)).astype(out.dtype)


def hidden_body(normed, grad, *refs):
    sides, acts, pres = ([refs[0]], [refs[1]]), refs[2:4], refs[4:6]
    in_part, out_part = refs[6:]
    hidden = acts[0].shape[1]
    tile = 256
    for side, parts in enumerate(sides):
        for start in range(0, hidden, tile):
            enter = slice(start, start + tile)
            leave = slice(hidden + start, hidden + start + tile)
            value = enter_rows(normed, parts, enter)
            square = value * value
            curve = jnp.tanh(GELU_COEFF * (value + 0.044715 * square * value))
            half = 0.5 * (1.0 + curve)
            slope = half + 0.5 * value * (1.0 - curve * curve) * (
                GELU_COEFF * (1.0 + 3.0 * 0.044715 * square)
            )
            acts[side][:, enter] = (value * half).astype(LOW)
            pres[side][:, enter] = (enter_rows(grad, parts, leave) * slope).astype(LOW)
    for values, part, columns in (
        (pres, in_part, slice(0, hidden)),
        (acts, out_part, slice(hidden, 2 * hidden)),
    ):

        def store(place, total, part=part):
            part[:, place] = total

        leave_rows([(values[side][...], parts) for side, parts in enumerate(sides)], columns, store)


def hidden_call(normed, grad, weights):
    count, width = normed.shape
    hidden = weights[0].shape[1] // 2
    outs = [shape_of((count, hidden), LOW)] * 4 + [shape_of((count, width), LOW)] * 2
    results = run(hidden_body, outs, (normed, grad, *weights), [ONE_VMEM] * 4)
    return results[0:2], results[2:4], results[4], results[5]


def weight_grad_tile(counts, ranges, refs, start, tile, store):
    at, column = 0, 0
    for count, columns in zip(counts, ranges):
        lefts, rights = refs[at : at + count], refs[at + count : at + 2 * count]
        at += 2 * count
        total = matmul_tn(lefts[0][:, start : start + tile], rights[0][:, columns])
        for left, right in zip(lefts[1:], rights[1:]):
            total = total + matmul_tn(left[:, start : start + tile], right[:, columns])
        store(column, total.astype(LOW))
        column += total.shape[1]


def weight_grad_body(counts, ranges, start, *refs):
    out, tile = refs[-1], 256
    for row in range(0, out.shape[0], tile):

        def store(column, values, row=row):
            out[row : row + tile, column : column + values.shape[1]] = values

        weight_grad_tile(counts, ranges, refs, start + row, tile, store)


def weight_grad(pairs, half=None, ranges=None, stored=()):
    args, counts = [], []
    for lefts, rights in pairs:
        args += [*lefts, *rights]
        counts.append(len(lefts))
    width = pairs[0][0][0].shape[1]
    rows = width if half is None else width // 2
    ranges = ranges or [slice(0, rights[0].shape[1]) for _, rights in pairs]
    columns = sum(part.stop - part.start for part in ranges)
    body = functools.partial(weight_grad_body, tuple(counts), ranges, (half or 0) * rows)
    return run(body, shape_of((rows, columns), LOW), args, [ONE_VMEM] * len(args), stored=stored)


def small_mine_body(gain, bias, table, out):
    step = gain.shape[1]
    out[...] = jnp.zeros_like(out)
    row = 0
    for part in (gain, bias, table):
        values = jnp.concatenate([part[...]] * ROUND, axis=1)
        lane = lax.broadcasted_iota(jnp.int32, values.shape, 1)
        out[0, row : row + part.shape[0], :] = pick(values, lane // step == lax.axis_index("head"))
        row += part.shape[0]


def small_rows_body(first, second, out):
    blocks, _, step = first.shape
    for half, part in enumerate((first, second)):
        for i in range(blocks):
            place = (half * blocks + i) * step
            out[:, place : place + step] = part[i]


def small_blocks_body(first, second, third, table_a, table_b, *outs):
    step = outs[0].shape[2]
    for half, out in enumerate(outs):
        for i in range(out.shape[0]):
            place = slice((half * out.shape[0] + i) * step, (half * out.shape[0] + i + 1) * step)
            for row, part in enumerate((first, second, third)):
                out[i, row : row + 1, :] = part[0:1, place]
                out[i, row + 3 : row + 4, :] = part[1:2, place]
            out[i, 6:14, :] = table_a[:, place] + table_b[:, place]
            out[i, 14:16, :] = jnp.zeros((2, step), WIDE)


def stack_body(*refs):
    out, row = refs[-1], 0
    for part in refs[:-1]:
        out[row : row + part.shape[0], ...] = part[...]
        row += part.shape[0]


def sum_body(*refs):
    total = refs[0][...]
    for part in refs[1:-1]:
        total = total + part[...]
    refs[-1][...] = total


def add_split_body(first, second, *outs):
    row = 0
    for out in outs:
        part = slice(row, row + out.shape[0])
        out[...] = (first[part].astype(WIDE) + second[part].astype(WIDE)).astype(out.dtype)
        row += out.shape[0]


def shards(
    frames_in,
    action_codes,
    clip_length,
    norm_gain,
    norm_bias,
    action_table,
    spatialin,
    spatialout,
    temporalin,
    temporalout,
    expand,
    shrink,
    out_grad,
):
    frames_local, clips, pos_local, width = frames_in.shape
    local = (frames_local, clips, pos_local, width)
    rel_shape = (BLOCKS, pos_local, width)
    count = BLOCKS * pos_local
    inner = spatialin.shape[2]
    hidden = expand.shape[1]
    codes = action_codes.reshape(BLOCKS)
    scalars = (codes, clip_length)

    packed_shape = shape_of(rel_shape, LOW)
    flat_shape = shape_of((count, width), LOW)
    sums_shape = shape_of((8, width), WIDE)
    frames_flat = frames_in.reshape(rel_shape)

    order = Order()
    send, take, do = order.send, order.take, order.do
    grad_shapes = [shape_of((3, width // BLOCKS, inner), WIDE), shape_of((inner, width // BLOCKS), WIDE)]
    whole_shape = shape_of(rel_shape, WIDE)

    def kernel(body, outs, first, *others, stored=()):
        smem = [ONE_SMEM if a.ndim == 1 else ONE_VMEM for a in (first, *others)]
        return do(lambda *args: run(body, outs, args, smem, stored=stored), first, *others)

    def stacked(*parts):
        shape = (sum(part.shape[0] for part in parts), *parts[0].shape[1:])
        return kernel(stack_body, shape_of(shape, parts[0].dtype), *parts)

    def summed(*parts):
        return kernel(sum_body, shape_of(parts[0].shape, parts[0].dtype), *parts)

    def halves(first, second):
        shape = shape_of((first.shape[0] // 2, *first.shape[1:]), first.dtype)
        keep, left = kernel(add_split_body, [shape, shape], first, second)
        order.last = left
        return keep, left

    def added(first, second):
        return kernel(add_split_body, [shape_of(first.shape, first.dtype)], first, second)[0]

    def attention_rows_of(enter, leave, parts):
        outs = [shape_of((enter.shape[0], 4 * inner // parts), LOW)] * parts
        return kernel(pack_attention_body, outs, jnp.transpose(enter, (1, 0, 2)), leave, stored=(0, 1))

    packed = kernel(pack_frames_body, packed_shape, frames_flat, stored=(0,))
    frame_blocks = order.exchange(packed)
    rows_a, rows_b = attention_rows_of(spatialin, spatialout, 2)
    got_a = send(rows_a, "space", 4)
    small_shape = (16, width // BLOCKS)
    block = kernel(
        small_mine_body,
        shape_of((1, *small_shape), WIDE),
        norm_gain,
        norm_bias,
        action_table,
        stored=(0, 1, 2),
    )
    got_small = [send(block, "head", mask) for mask in (1, 2, 3)]
    far_a = stacked(rows_a, take(got_a))
    got_a = send(far_a, "space", 2)
    got_b = send(rows_b, "space", 4)
    block = summed(block, *[take(got) for got in got_small])
    got_small = [send(block, "space", mask) for mask in ORDER[1:4]]
    line_a = stacked(far_a, take(got_a))
    far_b = stacked(rows_b, take(got_b))
    got_a = send(line_a, "space", 1)
    got_b = send(far_b, "space", 2)
    (time_rows,) = attention_rows_of(temporalin, temporalout, 1)
    hidden_rows = kernel(pack_hidden_body, kept_of((expand.shape[0], 2 * hidden), LOW), expand, shrink, stored=(0, 1))
    line = stacked(block, *[take(got) for got in got_small])
    got_small = send(line, "space", 1)
    line_b = stacked(far_b, take(got_b))
    got_b = send(line_b, "space", 1)
    small = kernel(small_rows_body, shape_of((16, width), WIDE), line, take(got_small))
    frame_blocks = take(frame_blocks)
    normed, start = kernel(
        frame_norm_body, [flat_shape, kept_of((count, width), WIDE)], *scalars, small, frame_blocks
    )
    normed_far = send(normed, "head", 2)
    got_time = send(time_rows, "space", 4)
    got_a = take(got_a)
    got_b = take(got_b)
    normed_far = take(normed_far)
    space_a = stacked(line_a, got_a)
    time_far = stacked(time_rows, take(got_time))
    beside_a = send(space_a, "head", 1)
    space_b = stacked(line_b, got_b)
    beside_b = send(space_b, "head", 1)
    got_time = send(time_far, "space", 2)
    hidden_blocks = lax.all_gather(order.tied(hidden_rows), "space", axis=0)
    space_weights = [space_a, space_b, take(beside_a), take(beside_b)]

    far_kept = do(space_forward, normed_far, space_weights)
    order.last = far_kept[3]
    far_part = send(far_kept[3], "head", 2)
    own_kept = do(space_forward, normed, space_weights)
    order.last = own_kept[3]
    time_line = stacked(time_far, take(got_time))
    far_part = take(far_part)
    got_time = send(time_line, "space", 1)
    packed = kernel(spread_body, packed_shape, own_kept[3], far_part)
    spread = order.exchange(packed)
    frames_rel, grad_low = kernel(
        order_inputs_body, [packed_shape] * 2, clip_length, frames_flat, out_grad.reshape(rel_shape), stored=(1, 2)
    )
    grad_far = take(send(grad_low.reshape(count, width), "head", 2))
    time_weights = [time_line, take(got_time)]
    spread = take(spread)
    first, normed_two = kernel(
        join_norm_body, [whole_shape, packed_shape], *scalars, small, frames_rel, spread
    )
    order.last = normed_two

    normed_two = normed_two.reshape(local)
    far = send(normed_two, "head", 2)
    near = send(normed_two, "head", 1)
    far = take(far)
    diagonal = send(far, "head", 1)
    normed_two = [normed_two, take(near), far, take(diagonal)]
    time_projected, time_output, time_totals, time_parts = do(
        lambda first, *others: time_call(
            time_forward_body,
            clip_length,
            time_weights,
            [[first, *others]],
            [(3 * inner, LOW, kept_of), (inner, LOW, kept_of), (128, WIDE, kept_of), (width, LOW, shape_of)],
        ),
        *normed_two,
    )
    order.last = time_parts[3]
    diagonal = send(time_parts[3], "head", 1)
    near = send(time_parts[1], "head", 1)
    far = added(time_parts[2], take(diagonal))
    far = send(far, "head", 2)
    near = take(near)
    hidden_own = do(reorder, take(hidden_blocks))
    parts = [part.reshape(rel_shape) for part in (time_parts[0], near, take(far))]
    second, normed_three = kernel(add_norm_body, [whole_shape, packed_shape], small, first, *parts)
    order.last = normed_three

    normed_three = normed_three.reshape(count, width)
    far = send(normed_three, "head", 2)
    hidden_beside = send(hidden_own, "head", 1)
    normed_three = [normed_three, take(far)]
    hidden_weights = [hidden_own, take(hidden_beside)]
    grad_third = [grad_low.reshape(count, width), grad_far]
    far_kept_three = do(hidden_call, normed_three[1], grad_third[1], hidden_weights)
    order.last = far_kept_three[2]
    far_part = send(far_kept_three[2], "head", 2)
    own_kept_three = do(hidden_call, normed_three[0], grad_third[0], hidden_weights)
    hidden_kept = [own_kept_three, far_kept_three]

    def hidden_part(side):
        first = [kept[1][side] for kept in hidden_kept]
        second = [kept[0][side] for kept in hidden_kept]
        return do(
            lambda left, right: weight_grad([([left, right], first), (grad_third, second)]), *normed_three
        )

    hidden_sent = hidden_part(1)
    far_part = take(far_part)
    hidden_sent = send(hidden_sent, "head", 1)
    parts = [part.reshape(rel_shape) for part in (own_kept_three[2], far_part)]
    total_second, low_second, sums_third = kernel(
        back_third_body, [whole_shape, packed_shape, sums_shape], small, grad_low, second, *parts
    )
    order.last = low_second
    low_second = low_second.reshape(local)
    far = send(low_second, "head", 2)
    near = send(low_second, "head", 1)
    hidden_grad = hidden_part(0)
    near = take(near)
    far = take(far)

    diagonal = send(far, "head", 1)
    grad_two = [low_second, near, far, take(diagonal)]
    time_grads, time_parts = do(
        lambda first, *others: time_call(
            time_back_body,
            clip_length,
            time_weights,
            [[first, *others], time_projected, time_totals],
            [(3 * inner, LOW, shape_of), (width, LOW, shape_of)],
        ),
        *grad_two,
    )
    order.last = time_parts[3]
    diagonal = send(time_parts[3], "head", 1)
    near = send(time_parts[1], "head", 1)
    flat = lambda arrays: [a.reshape(count, a.shape[-1]) for a in arrays]

    def time_part(half):
        lefts, pair = flat(normed_two), (flat(grad_two), flat(time_output))
        return do(
            lambda *left: weight_grad([(left, flat(time_grads)), pair], half, stored=range(12, 16)), *lefts
        )

    far = added(time_parts[2], take(diagonal))
    far = send(far, "head", 2)
    near = take(near)
    time_send = time_part(1)
    time_keep = time_part(0)
    hidden_grad = kernel(
        add_order_body,
        kept_of((BLOCKS, width // BLOCKS, 2 * hidden), LOW),
        hidden_grad,
        take(hidden_sent),
    )
    hidden_grad = lax.psum_scatter(hidden_grad, "space", scatter_dimension=0)
    parts = [part.reshape(rel_shape) for part in (time_parts[0], near, take(far))]
    total_first, sums_second, table_first, packed = kernel(
        back_second_body,
        [whole_shape, sums_shape, sums_shape, packed_shape],
        *scalars,
        small,
        total_second,
        first,
        *parts,
    )
    order.last = packed
    grad_blocks = order.exchange(packed)
    time_got = send(time_send, "space", 1)
    far_out = send(far_kept_three[3], "head", 2)
    parts = [part.reshape(rel_shape) for part in (own_kept_three[3], take(far_out))]
    frames_out = kernel(finish_forward_body, packed_shape, clip_length, second, *parts)

    grad_blocks = take(grad_blocks)
    grad_one = kernel(collect_body, flat_shape, grad_blocks)
    far = send(grad_one, "head", 2)
    own_result = do(space_back, grad_one, space_weights, own_kept[0], own_kept[2])
    order.last = own_result[1]
    grad_one = [grad_one, take(far)]
    time_got = take(time_got)
    far_result = do(space_back, grad_one[1], space_weights, far_kept[0], far_kept[2])
    order.last = far_result[1]
    far_part = send(far_result[1], "head", 2)

    def space_part(side):
        firsts = [own_result[0], far_result[0]]
        seconds = [own_kept[1], far_kept[1]]
        step = inner // 2
        return do(
            lambda left, right: weight_grad(
                [([left, right], firsts), (grad_one, seconds)],
                ranges=[side_columns(side, 3 * step), side_columns(side, step)],
                stored=(6, 7),
            ),
            normed,
            normed_far,
        )

    beside_a = space_part(2)
    space_a = space_part(0)
    time_keep, time_send = halves(time_keep, time_got)
    time_got = send(time_send, "space", 2)
    beside_b = space_part(3)
    space_b = space_part(1)
    far_part = take(far_part)
    beside_a = send(beside_a, "head", 1)
    sums_first, table_second, packed = kernel(
        back_first_body,
        [sums_shape, sums_shape, packed_shape],
        *scalars,
        small,
        start,
        own_result[1],
        far_part,
        stored=(3,),
    )
    order.last = packed
    last = order.exchange(packed)
    keep_a, send_a = halves(space_a, take(beside_a))
    got_a = send(send_a, "space", 1)
    beside_b = send(beside_b, "head", 1)
    half_shape = shape_of((BLOCKS // 2, *small_shape), WIDE)
    sums, small_send = kernel(
        small_blocks_body, [half_shape] * 2, sums_first, sums_second, sums_third, table_first, table_second
    )
    order.last = small_send
    got_small = send(small_send, "space", 1)
    keep_b, send_b = halves(space_b, take(beside_b))
    sums, small_send = halves(sums, take(got_small))
    got_small = send(small_send, "space", 2)
    keep_a, send_a = halves(keep_a, take(got_a))
    got_a = send(send_a, "space", 2)
    got_b = send(send_b, "space", 1)
    time_keep, time_send = halves(time_keep, take(time_got))
    keep_a, send_a = halves(keep_a, take(got_a))
    got_a = send(send_a, "space", 4)
    time_got = send(time_send, "space", 4)
    sums, small_send = halves(sums, take(got_small))
    got_small = send(small_send, "space", 4)
    keep_b, send_b = halves(keep_b, take(got_b))
    got_b = send(send_b, "space", 2)
    last = take(last)
    frames_grad = kernel(finish_back_body, whole_shape, clip_length, total_first, last)
    sums = summed(sums, take(got_small))
    got_small = send(sums, "head", 1)
    hidden_grads = kernel(
        unpack_hidden_body,
        [shape_of((width // BLOCKS, hidden), WIDE), shape_of((hidden, width // BLOCKS), WIDE)],
        take(hidden_grad),
    )
    time_grads = kernel(unpack_attention_body, grad_shapes, time_keep, take(time_got))
    sums = summed(sums, take(got_small))
    got_small = send(sums, "head", 2)
    got_a = take(got_a)
    keep_b, send_b = halves(keep_b, take(got_b))
    got_b = send(send_b, "space", 4)
    sums = summed(sums, take(got_small))[0]
    step = sums.shape[1] // ROUND
    sums = lax.dynamic_slice(sums, (0, lax.axis_index("head") * step), (sums.shape[0], step))
    space_grads = kernel(unpack_attention_body, grad_shapes, keep_a, got_a, keep_b, take(got_b))
    return (
        frames_out.reshape(local),
        frames_grad.reshape(local),
        sums[0:3],
        sums[3:6],
        sums[6:14],
        jnp.transpose(space_grads[0], (1, 0, 2)),
        space_grads[1],
        jnp.transpose(time_grads[0], (1, 0, 2)),
        time_grads[1],
        *hidden_grads,
    )


def solution(mesh):
    placed = (
        P("head", None, "space", None),
        P("head", None),
        P(),
        P(None, ("space", "head")),
        P(None, ("space", "head")),
        P(None, ("space", "head")),
        P("space", None, "head"),
        P("head", "space"),
        P("space", None, "head"),
        P("head", "space"),
        P("space", "head"),
        P("head", "space"),
        P("head", None, "space", None),
    )
    eight = mesh.shape["space"] == BLOCKS and mesh.shape["head"] == ROUND
    return jax.shard_map(
        shards if eight else general_shards,
        mesh=mesh,
        in_specs=placed,
        out_specs=(
            P("head", None, "space", None),
            P("head", None, "space", None),
            P(None, ("space", "head")),
            P(None, ("space", "head")),
            P(None, ("space", "head")),
            P("space", None, "head"),
            P("head", "space"),
            P("space", None, "head"),
            P("head", "space"),
            P("space", "head"),
            P("head", "space"),
        ),
        check_vma=False,
    )
```

```python
import functools

import jax
import jax.numpy as jnp
from jax import lax
from jax.experimental import pallas as pl
from jax.experimental.pallas import tpu as pltpu
from jax.sharding import PartitionSpec as P

HEAD_DIM = 64


EPSILON = 1e-05
SCORE_SCALE = 0.125
MASKED_SCORE = -1e30
PRECISE = lax.Precision.HIGHEST
GELU_COEFF = 0.7978845608028654


def layer_norm(values, gain_row, bias_row):
    row_mean = jnp.mean(values, axis=-1, keepdims=True)
    centred = values - row_mean
    row_var = jnp.mean(centred * centred, axis=-1, keepdims=True)
    return centred * lax.rsqrt(row_var + EPSILON) * gain_row + bias_row


def gelu_tanh(inputs):
    return (
        0.5 * inputs * (1.0 + jnp.tanh(GELU_COEFF * (inputs + 0.044715 * inputs * inputs * inputs)))
    )


def gather_weights(small, large):
    small_full = (
        lax.all_gather(small[0], ("space", "head"), axis=1, tiled=True),
        lax.all_gather(small[1], ("space", "head"), axis=1, tiled=True),
        lax.all_gather(small[2], ("space", "head"), axis=1, tiled=True),
    )
    large_full = (
        lax.all_gather(large[0], "space", axis=0, tiled=True),
        lax.all_gather(large[1], "space", axis=1, tiled=True),
        lax.all_gather(large[2], "space", axis=0, tiled=True),
        lax.all_gather(large[3], "space", axis=1, tiled=True),
        lax.all_gather(large[4], "space", axis=0, tiled=True),
        lax.all_gather(large[5], "space", axis=1, tiled=True),
    )
    return (small_full, large_full)


def norm_step(inputs, gain_row, bias_row):
    normed, pullback = jax.vjp(layer_norm, inputs, gain_row, bias_row)
    whole = lax.all_gather(normed.astype(jnp.bfloat16), "head", axis=0, tiled=True)
    return (whole, pullback)


def cot_whole(grad_rows):
    return lax.all_gather(grad_rows.astype(jnp.bfloat16), "head", axis=0, tiled=True)


def input_total(partial_value):
    return lax.psum_scatter(
        partial_value.astype(jnp.bfloat16), "head", scatter_dimension=0, tiled=True
    ).astype(jnp.float32)


def heads_total(left, weight):
    return lax.psum_scatter(
        jnp.einsum("fcpe,ed->fcpd", left, weight, preferred_element_type=jnp.float32).astype(
            jnp.bfloat16
        ),
        "head",
        scatter_dimension=0,
        tiled=True,
    ).astype(jnp.float32)


def project_in(whole, weight):
    stacked = jnp.einsum(
        "fcpd,dke->kfcpe", whole, weight, preferred_element_type=jnp.float32
    ).astype(jnp.bfloat16)
    return (stacked[0], stacked[1], stacked[2])


def raw_scores(queries, keyset, form, allowed):
    key_form = form.replace("q", "k")
    scores = (
        jnp.einsum(
            form + "," + key_form + "->bhqk", queries, keyset, preferred_element_type=jnp.float32
        )
        * SCORE_SCALE
    )
    if allowed is not None:
        scores = jnp.where(allowed, scores, MASKED_SCORE)
    return scores


def attend(queries, keyset, values, form, allowed):
    key_form = form.replace("q", "k")
    scores = raw_scores(queries, keyset, form, allowed)
    row_max = jnp.max(scores, axis=-1, keepdims=True)
    log_total = row_max + jnp.log(jnp.sum(jnp.exp(scores - row_max), axis=-1, keepdims=True))
    shares = jnp.exp(scores - log_total).astype(jnp.bfloat16)
    output = jnp.einsum(
        "bhqk," + key_form + "->" + form, shares, values, preferred_element_type=jnp.float32
    )
    return (output.astype(jnp.bfloat16), log_total)


def attend_back(queries, keyset, values, log_total, output_grad, form, allowed):
    key_form = form.replace("q", "k")
    shares = jnp.exp(raw_scores(queries, keyset, form, allowed) - log_total)
    value_grad = jnp.einsum(
        "bhqk," + form + "->" + key_form,
        shares.astype(jnp.bfloat16),
        output_grad,
        preferred_element_type=jnp.float32,
    )
    share_grad = jnp.einsum(
        form + "," + key_form + "->bhqk", output_grad, values, preferred_element_type=jnp.float32
    )
    score_grad = (
        shares * (share_grad - jnp.sum(share_grad * shares, axis=-1, keepdims=True))
    ).astype(jnp.bfloat16)
    query_grad = (
        jnp.einsum(
            "bhqk," + key_form + "->" + form, score_grad, keyset, preferred_element_type=jnp.float32
        )
        * SCORE_SCALE
    )
    key_grad = (
        jnp.einsum(
            "bhqk," + form + "->" + key_form,
            score_grad,
            queries,
            preferred_element_type=jnp.float32,
        )
        * SCORE_SCALE
    )
    return (
        query_grad.astype(jnp.bfloat16),
        key_grad.astype(jnp.bfloat16),
        value_grad.astype(jnp.bfloat16),
    )


def general_shards(
    frames_in,
    action_codes,
    clip_length,
    norm_gain,
    norm_bias,
    action_table,
    spatialin,
    spatialout,
    temporalin,
    temporalout,
    expand,
    shrink,
    out_grad,
):
    head_count = lax.axis_size("head")
    frames_local, clip_count, pos_local, width = frames_in.shape
    frames_total = frames_local * head_count
    local_width = spatialin.shape[2]
    heads_local = local_width // HEAD_DIM
    frame_index = jnp.arange(frames_total)
    local_index = lax.axis_index("head") * frames_local + jnp.arange(frames_local)
    valid_local = (local_index[:, None] < clip_length[None, :]).astype(jnp.float32)[
        :, :, None, None
    ]
    allowed = (frame_index[None, :, None] >= frame_index[None, None, :]) & (
        frame_index[None, None, :] < clip_length[:, None, None]
    )
    allowed = jnp.broadcast_to(
        allowed[:, None, None], (clip_count, pos_local, 1, frames_total, frames_total)
    )
    allowed = allowed.reshape(clip_count * pos_local, 1, frames_total, frames_total)
    small_full, large_full = gather_weights(
        (norm_gain, norm_bias, action_table),
        (spatialin, spatialout, temporalin, temporalout, expand, shrink),
    )
    gain_full, bias_full, table_full = small_full
    space_in, space_out, time_in, time_out, expand_full, shrink_full = large_full
    code_hot = (action_codes[:, :, None] == jnp.arange(table_full.shape[0])[None, None, :]).astype(
        jnp.float32
    )
    embedded = jnp.einsum("fca,ad->fcd", code_hot, table_full, precision=PRECISE)
    start = valid_local * (frames_in.astype(jnp.float32) + embedded[:, :, None, :])
    whole_one, pull_one = norm_step(start, gain_full[0], bias_full[0])
    space_query, space_keys, space_values = project_in(whole_one, space_in)
    flat_shape = (frames_total * clip_count, pos_local, local_width)
    moved = (
        lax.all_to_all(
            space_query.reshape(flat_shape), "space", split_axis=0, concat_axis=1, tiled=True
        ),
        lax.all_to_all(
            space_keys.reshape(flat_shape), "space", split_axis=0, concat_axis=1, tiled=True
        ),
        lax.all_to_all(
            space_values.reshape(flat_shape), "space", split_axis=0, concat_axis=1, tiled=True
        ),
    )
    block_rows = moved[0].shape[0]
    block_cols = moved[0].shape[1]
    frame_shape = (block_rows, block_cols, heads_local, HEAD_DIM)
    frame_query = moved[0].reshape(frame_shape)
    frame_keys = moved[1].reshape(frame_shape)
    frame_values = moved[2].reshape(frame_shape)
    frame_out, frame_total = attend(frame_query, frame_keys, frame_values, "bqhe", None)
    returned = lax.all_to_all(
        frame_out.reshape(block_rows, block_cols, local_width),
        "space",
        split_axis=1,
        concat_axis=0,
        tiled=True,
    )
    space_attended = returned.reshape(frames_total, clip_count, pos_local, local_width)
    first = start + heads_total(space_attended, space_out)
    whole_two, pull_two = norm_step(first, gain_full[1], bias_full[1])
    time_query, time_keys, time_values = project_in(whole_two, time_in)
    time_shape = (frames_total, clip_count * pos_local, heads_local, HEAD_DIM)
    time_query = time_query.reshape(time_shape)
    time_keys = time_keys.reshape(time_shape)
    time_values = time_values.reshape(time_shape)
    time_out_rows, time_total = attend(time_query, time_keys, time_values, "qbhe", allowed)
    time_attended = time_out_rows.reshape(frames_total, clip_count, pos_local, local_width)
    second = first + heads_total(time_attended, time_out)
    whole_three, pull_three = norm_step(second, gain_full[2], bias_full[2])
    expanded = jnp.einsum(
        "fcpd,dh->fcph", whole_three, expand_full, preferred_element_type=jnp.float32
    )
    activated, gelu_pull = jax.vjp(gelu_tanh, expanded)
    activated_low = activated.astype(jnp.bfloat16)
    third = second + heads_total(activated_low, shrink_full)
    frames_out = (valid_local * third).astype(jnp.bfloat16)
    small_full, large_full = gather_weights(
        (norm_gain, norm_bias, action_table),
        (spatialin, spatialout, temporalin, temporalout, expand, shrink),
    )
    space_in, space_out, time_in, time_out, expand_full, shrink_full = large_full
    grad_third = valid_local * out_grad.astype(jnp.float32)
    cot_three = cot_whole(grad_third)
    shrink_part = jnp.einsum(
        "fcph,fcpd->hd", activated_low, cot_three, preferred_element_type=jnp.float32
    )
    act_grad = jnp.einsum(
        "fcpd,hd->fcph", cot_three, shrink_full, preferred_element_type=jnp.float32
    )
    pre_grad = gelu_pull(act_grad)[0].astype(jnp.bfloat16)
    expand_part = jnp.einsum(
        "fcpd,fcph->dh", whole_three, pre_grad, preferred_element_type=jnp.float32
    )
    normed_grad = input_total(
        jnp.einsum("fcph,dh->fcpd", pre_grad, expand_full, preferred_element_type=jnp.float32)
    )
    input_three, gain_three, bias_three = pull_three(normed_grad)
    grad_second = grad_third + input_three
    cot_two = cot_whole(grad_second)
    time_out_part = jnp.einsum(
        "fcpe,fcpd->ed", time_attended, cot_two, preferred_element_type=jnp.float32
    )
    time_grad = jnp.einsum(
        "fcpd,ed->fcpe", cot_two, time_out, preferred_element_type=jnp.float32
    ).astype(jnp.bfloat16)
    time_grads = attend_back(
        time_query,
        time_keys,
        time_values,
        time_total,
        time_grad.reshape(time_shape),
        "qbhe",
        allowed,
    )
    stacked_grad = jnp.stack(
        [member.reshape(frames_total, clip_count, pos_local, local_width) for member in time_grads]
    )
    time_in_part = jnp.einsum(
        "fcpd,kfcpe->dke", whole_two, stacked_grad, preferred_element_type=jnp.float32
    )
    normed_grad = input_total(
        jnp.einsum("kfcpe,dke->fcpd", stacked_grad, time_in, preferred_element_type=jnp.float32)
    )
    input_two, gain_two, bias_two = pull_two(normed_grad)
    grad_first = grad_second + input_two
    cot_one = cot_whole(grad_first)
    space_out_part = jnp.einsum(
        "fcpe,fcpd->ed", space_attended, cot_one, preferred_element_type=jnp.float32
    )
    space_grad = jnp.einsum(
        "fcpd,ed->fcpe", cot_one, space_out, preferred_element_type=jnp.float32
    ).astype(jnp.bfloat16)
    frame_grad = lax.all_to_all(
        space_grad.reshape(flat_shape), "space", split_axis=0, concat_axis=1, tiled=True
    ).reshape(frame_shape)
    query_grad, keys_grad, values_grad = attend_back(
        frame_query, frame_keys, frame_values, frame_total, frame_grad, "bqhe", None
    )
    block_shape = (block_rows, block_cols, local_width)
    back_grads = (
        lax.all_to_all(
            query_grad.reshape(block_shape), "space", split_axis=1, concat_axis=0, tiled=True
        ),
        lax.all_to_all(
            keys_grad.reshape(block_shape), "space", split_axis=1, concat_axis=0, tiled=True
        ),
        lax.all_to_all(
            values_grad.reshape(block_shape), "space", split_axis=1, concat_axis=0, tiled=True
        ),
    )
    stacked_grad = jnp.stack(
        [member.reshape(frames_total, clip_count, pos_local, local_width) for member in back_grads]
    )
    space_in_part = jnp.einsum(
        "fcpd,kfcpe->dke", whole_one, stacked_grad, preferred_element_type=jnp.float32
    )
    normed_grad = input_total(
        jnp.einsum("kfcpe,dke->fcpd", stacked_grad, space_in, preferred_element_type=jnp.float32)
    )
    input_one, gain_one, bias_one = pull_one(normed_grad)
    grad_start = grad_first + input_one
    frames_grad = valid_local * grad_start
    table_part = jnp.einsum(
        "fca,fcd->ad", code_hot, jnp.sum(frames_grad, axis=2), precision=PRECISE
    )
    gain_grad, bias_grad, table_grad = (
        lax.psum_scatter(
            jnp.stack([gain_one, gain_two, gain_three]),
            ("space", "head"),
            scatter_dimension=1,
            tiled=True,
        ),
        lax.psum_scatter(
            jnp.stack([bias_one, bias_two, bias_three]),
            ("space", "head"),
            scatter_dimension=1,
            tiled=True,
        ),
        lax.psum_scatter(table_part, ("space", "head"), scatter_dimension=1, tiled=True),
    )
    weight_grads = (
        lax.psum_scatter(space_in_part, "space", scatter_dimension=0, tiled=True),
        lax.psum_scatter(space_out_part, "space", scatter_dimension=1, tiled=True),
        lax.psum_scatter(time_in_part, "space", scatter_dimension=0, tiled=True),
        lax.psum_scatter(time_out_part, "space", scatter_dimension=1, tiled=True),
        lax.psum_scatter(expand_part, "space", scatter_dimension=0, tiled=True),
        lax.psum_scatter(shrink_part, "space", scatter_dimension=1, tiled=True),
    )
    return (
        frames_out,
        frames_grad,
        gain_grad,
        bias_grad,
        table_grad,
        weight_grads[0],
        weight_grads[1],
        weight_grads[2],
        weight_grads[3],
        weight_grads[4],
        weight_grads[5],
    )


ORDER = (0, 4, 2, 6, 1, 5, 3, 7)
BLOCKS = len(ORDER)
PLACE = tuple(ORDER.index(mask) for mask in range(BLOCKS))
ROUND = 4
ONE_VMEM = pl.BlockSpec(memory_space=pltpu.VMEM)
ONE_SMEM = pl.BlockSpec(memory_space=pltpu.SMEM)
MIB = 1024 * 1024
LOW = jnp.bfloat16
WIDE = jnp.float32


def swap(value, axis, mask):
    return lax.ppermute(value, axis, [(i, i ^ mask) for i in range(lax.axis_size(axis))])


class Order:
    def __init__(self):
        self.last = None

    def tied(self, value):
        if self.last is None:
            return value
        return lax.optimization_barrier((value, self.last))[0]

    def send(self, value, axis, mask):
        return swap(self.tied(value), axis, mask)

    def exchange(self, packed):
        return lax.all_to_all(self.tied(packed), "space", split_axis=0, concat_axis=0, tiled=True)

    def take(self, value):
        self.last = self.tied(value)
        return self.last

    def do(self, step, first, *others):
        result = step(self.tied(first), *others)
        self.last = jax.tree.leaves(result)[0]
        return result


def run(body, outs, args, specs, vmem=None, stored=()):
    single = not isinstance(outs, (list, tuple))
    name = getattr(body, "func", body).__name__.removesuffix("_body")
    args, specs, scratch, whole = list(args), list(specs), [], body
    if stored:
        for place in stored:
            args[place] = pltpu.with_memory_space_constraint(args[place], pltpu.HBM)
            specs[place] = pl.BlockSpec(memory_space=pltpu.HBM)
            scratch.append(pltpu.VMEM(args[place].shape, args[place].dtype))
        scratch.append(pltpu.SemaphoreType.DMA((len(stored),)))

        def whole(*refs):
            refs, held, sem = list(refs[: -len(scratch)]), refs[-len(scratch) : -1], refs[-1]
            copies = [
                pltpu.make_async_copy(refs[place], held[i], sem.at[i]) for i, place in enumerate(stored)
            ]
            for copy in copies:
                copy.start()
            for i, place in enumerate(stored):
                copies[i].wait()
                refs[place] = held[i]
            body(*refs)

    return pl.pallas_call(
        whole,
        out_shape=outs,
        in_specs=specs,
        out_specs=ONE_VMEM if single else [ONE_VMEM] * len(outs),
        scratch_shapes=scratch,
        cost_estimate=pl.CostEstimate(flops=0, bytes_accessed=1024, transcendentals=0),
        compiler_params=pltpu.CompilerParams(vmem_limit_bytes=vmem or 12 * MIB),
        name=name,
    )(*args)


def kept_of(dims, dtype):
    return pltpu.HBM(tuple(dims), dtype)


def shape_of(dims, dtype):
    return jax.ShapeDtypeStruct(tuple(dims), dtype)


def feature_block(place, step):
    return pl.ds(pl.multiple_of(place * step, step), step)


def partner(mask):
    return lax.axis_index("space") ^ mask


def frame_valid(lengths, frames, mask):
    clips = lengths.shape[0]
    frame = lax.axis_index("head") * (frames // clips) + partner(mask) // clips
    return jnp.where(frame < lengths[partner(mask) % clips], 1.0, 0.0).astype(WIDE)


def normed_parts(values):
    centred = values - jnp.mean(values, axis=-1, keepdims=True)
    scale = lax.rsqrt(jnp.mean(centred * centred, axis=-1, keepdims=True) + EPSILON)
    return centred * scale, scale


def norm_back(values, grad, gain_row):
    unit, scale = normed_parts(values)
    scaled = grad * gain_row
    out = scale * (
        scaled
        - jnp.mean(scaled, axis=-1, keepdims=True)
        - unit * jnp.mean(scaled * unit, axis=-1, keepdims=True)
    )
    return (
        out,
        jnp.sum(grad * unit, axis=0, keepdims=True),
        jnp.sum(grad, axis=0, keepdims=True),
    )


def store_for(ref, rows, mask):
    step = rows.shape[-1] // BLOCKS
    for i in range(BLOCKS):
        j = i ^ PLACE[mask]
        ref[partner(mask), :, i * step : (i + 1) * step] = rows[:, j * step : (j + 1) * step]


def pack_attention_body(enter, leave, out):
    step = leave.shape[0] // 2
    for i in range(2):
        place, column = slice(i * step, (i + 1) * step), 4 * i * step
        for j in range(3):
            out[:, column + j * step : column + (j + 1) * step] = enter[j, :, place]
        out[:, column + 3 * step : column + 4 * step] = jnp.transpose(leave[place, :])


def unpack_attention_body(mine, got, enter, leave):
    step = leave.shape[0] // 2
    for i in range(2):
        columns = side_columns(i, 4 * step)
        total = mine[:, columns].astype(WIDE) + got[:, columns].astype(WIDE)
        place = slice(i * step, (i + 1) * step)
        for j in range(3):
            enter[j, :, place] = total[:, j * step : (j + 1) * step]
        leave[place, :] = jnp.transpose(total[:, 3 * step :])


def pack_hidden_body(enter, leave, out):
    hidden = leave.shape[0]
    out[:, :hidden] = enter[...]
    out[:, hidden:] = jnp.transpose(leave[...])


def unpack_hidden_body(mine, got, enter, leave):
    hidden = leave.shape[0]
    total = mine[...].astype(WIDE) + got[...].astype(WIDE)
    enter[...] = total[:, :hidden]
    leave[...] = jnp.transpose(total[:, hidden:])


def stack_split_body(first, second, *outs):
    rows, column = first.shape[0], 0
    for out in outs:
        place = slice(column, column + out.shape[1])
        out[:rows, :] = first[:, place]
        out[rows:, :] = second[:, place]
        column += out.shape[1]


def stack_cross_body(first, second, out):
    tile = first.shape[0] // 2
    for i, (part, place) in enumerate(((first, 0), (second, 0), (first, 1), (second, 1))):
        out[i * tile : (i + 1) * tile, :] = part[place * tile : (place + 1) * tile, :]


def add_join_body(first_a, second_a, first_b, second_b, *outs):
    row, half = 0, first_a.shape[1]
    for out in outs:
        part = slice(row, row + out.shape[0])
        out[:, :half] = (first_a[part].astype(WIDE) + second_a[part].astype(WIDE)).astype(out.dtype)
        out[:, half:] = (first_b[part].astype(WIDE) + second_b[part].astype(WIDE)).astype(out.dtype)
        row += out.shape[0]


def pack_frames_body(frames, out):
    step = frames.shape[-1] // BLOCKS
    for mask in range(BLOCKS):
        for i in range(BLOCKS):
            source = partner(ORDER[i ^ PLACE[mask]])
            place = slice(i * step, (i + 1) * step)
            out[partner(mask), :, place] = frames[partner(mask), :, feature_block(source, step)]


def order_inputs_body(lengths, frames, grad, frames_out, grad_out):
    step = frames.shape[-1] // BLOCKS

    def one(mask, carry):
        valid = frame_valid(lengths, BLOCKS, mask)
        for i in range(BLOCKS):
            source = feature_block(partner(ORDER[i]), step)
            place = slice(i * step, (i + 1) * step)
            frames_out[mask, :, place] = frames[partner(mask), :, source]
            kept = grad[partner(mask), :, source].astype(WIDE) * valid
            grad_out[mask, :, place] = kept.astype(LOW)
        return carry

    lax.fori_loop(0, BLOCKS, one, 0)


def start_rows(rows, codes, lengths, small, mask):
    embedded = small[pl.ds(6 + codes[partner(mask)], 1), :]
    return frame_valid(lengths, BLOCKS, mask) * (rows.astype(WIDE) + embedded)


def frame_norm_body(codes, lengths, small, blocks, normed, start):
    rows = blocks.shape[1]
    for b in range(BLOCKS):
        values = start_rows(blocks[partner(b)], codes, lengths, small, 0)
        start[b * rows : (b + 1) * rows, :] = values
        unit, _ = normed_parts(values)
        normed[b * rows : (b + 1) * rows, :] = (unit * small[0:1, :] + small[3:4, :]).astype(LOW)


def spread_body(first, second, out):
    rows = out.shape[1]
    for mask in range(BLOCKS):
        part = slice(mask * rows, (mask + 1) * rows)
        total = first[part, :].astype(WIDE) + second[part, :].astype(WIDE)
        store_for(out, total.astype(LOW), mask)


def join_norm_body(codes, lengths, small, frames, blocks, whole, normed):
    for b in range(BLOCKS):
        values = start_rows(frames[b], codes, lengths, small, b) + blocks[partner(b)].astype(WIDE)
        whole[b] = values
        unit, _ = normed_parts(values)
        normed[b] = (unit * small[1:2, :] + small[4:5, :]).astype(LOW)


def add_norm_body(small, before, first, second, third, whole, normed):
    def one(b, carry):
        values = before[b] + (
            first[b].astype(WIDE) + second[b].astype(WIDE) + third[b].astype(WIDE)
        )
        whole[b] = values
        unit, _ = normed_parts(values)
        normed[b] = (unit * small[2:3, :] + small[5:6, :]).astype(LOW)
        return carry

    lax.fori_loop(0, BLOCKS, one, 0)


def finish_forward_body(lengths, before, first, second, out):
    step = out.shape[-1] // BLOCKS

    def one(b, carry):
        values = before[b] + (first[b].astype(WIDE) + second[b].astype(WIDE))
        values = (frame_valid(lengths, BLOCKS, b) * values).astype(LOW)
        for i in range(BLOCKS):
            place = feature_block(partner(ORDER[i]), step)
            out[partner(b), :, place] = values[:, i * step : (i + 1) * step]
        return carry

    lax.fori_loop(0, BLOCKS, one, 0)


def back_third_body(small, grad, values, first, second, total_out, low_out, sums):
    sums[...] = jnp.zeros_like(sums)

    def one(b, carry):
        normed_grad = first[b].astype(WIDE) + second[b].astype(WIDE)
        out, gain, bias = norm_back(values[b], normed_grad, small[2:3, :])
        total = grad[b].astype(WIDE) + out
        total_out[b] = total
        low_out[b] = total.astype(LOW)
        sums[0:1, :] += gain
        sums[1:2, :] += bias
        return carry

    lax.fori_loop(0, BLOCKS, one, 0)


def back_second_body(codes, lengths, small, grad, values, first, second, third, total_out, sums, table, packed):
    sums[...] = jnp.zeros_like(sums)
    table[...] = jnp.zeros_like(table)
    for b in range(BLOCKS):
        normed_grad = first[b].astype(WIDE) + second[b].astype(WIDE) + third[b].astype(WIDE)
        out, gain, bias = norm_back(values[b], normed_grad, small[1:2, :])
        total = grad[b] + out
        total_out[b] = total
        store_for(packed, total.astype(LOW), b)
        sums[0:1, :] += gain
        sums[1:2, :] += bias
        row = pl.ds(codes[partner(b)], 1)
        table[row, :] += frame_valid(lengths, BLOCKS, b) * jnp.sum(total, axis=0, keepdims=True)


def back_first_body(codes, lengths, small, values, first, second, sums, table, packed):
    sums[...] = jnp.zeros_like(sums)
    table[...] = jnp.zeros_like(table)
    rows = packed.shape[1]
    for b in range(BLOCKS):
        part = slice(b * rows, (b + 1) * rows)
        normed_grad = first[part, :].astype(WIDE) + second[part, :].astype(WIDE)
        out, gain, bias = norm_back(values[part, :], normed_grad, small[0:1, :])
        store_for(packed, out.astype(LOW), b)
        sums[0:1, :] += gain
        sums[1:2, :] += bias
        row = pl.ds(codes[partner(0)], 1)
        table[row, :] += frame_valid(lengths, BLOCKS, 0) * jnp.sum(out, axis=0, keepdims=True)


def collect_body(blocks, out):
    rows = blocks.shape[1]
    for b in range(BLOCKS):
        out[b * rows : (b + 1) * rows, :] = blocks[partner(b)]


def finish_back_body(lengths, grad, blocks, out):
    step = out.shape[-1] // BLOCKS
    for b in range(BLOCKS):
        values = frame_valid(lengths, BLOCKS, b) * (grad[b] + blocks[partner(b)].astype(WIDE))
        for i in range(BLOCKS):
            place = feature_block(partner(ORDER[i]), step)
            out[partner(b), :, place] = values[:, i * step : (i + 1) * step]


def matmul(left, right):
    return lax.dot_general(left, right, (((1,), (0,)), ((), ())), preferred_element_type=WIDE)


def matmul_t(left, right):
    return lax.dot_general(left, right, (((1,), (1,)), ((), ())), preferred_element_type=WIDE)


def matmul_tn(left, right):
    return lax.dot_general(left, right, (((0,), (0,)), ((), ())), preferred_element_type=WIDE)


def head_mask(width, head):
    lane = lax.broadcasted_iota(jnp.int32, (1, width), 1)
    return (lane // HEAD_DIM) == head


def pick(values, mask):
    return jnp.where(mask, values, jnp.zeros_like(values))


def attention_rows(projected, allowed, totals, first):
    width = projected.shape[1] // 3
    queries = projected[:, :width] * jnp.asarray(SCORE_SCALE, LOW)
    keyset = projected[:, width : 2 * width]
    values = projected[:, 2 * width :]
    lane = lax.broadcasted_iota(jnp.int32, (1, 128), 1)
    output = jnp.zeros((projected.shape[0], width), WIDE)
    for head in range(width // HEAD_DIM):
        mask = head_mask(width, head)
        scores = matmul_t(pick(queries, mask), keyset)
        if allowed is not None:
            scores = jnp.where(allowed, scores, MASKED_SCORE)
        row_max = jnp.max(scores, axis=-1, keepdims=True)
        raised = jnp.exp(scores - row_max)
        total = jnp.sum(raised, axis=-1, keepdims=True)
        shares = (raised * (1.0 / total)).astype(LOW)
        output = output + matmul(shares, pick(values, mask))
        totals = jnp.where(lane == first + head, row_max + jnp.log(total), totals)
    return output.astype(LOW), totals


def attention_rows_back(projected, totals, first, output_grad, allowed):
    width = projected.shape[1] // 3
    queries = projected[:, :width] * jnp.asarray(SCORE_SCALE, LOW)
    keyset = projected[:, width : 2 * width]
    values = projected[:, 2 * width :]
    scaled_keys = keyset * jnp.asarray(SCORE_SCALE, LOW)
    shape = (projected.shape[0], width)
    query_grad, key_grad, value_grad = (jnp.zeros(shape, WIDE) for _ in range(3))
    for head in range(width // HEAD_DIM):
        mask = head_mask(width, head)
        own_queries = pick(queries, mask)
        own_grad = pick(output_grad, mask)
        scores = matmul_t(own_queries, keyset)
        if allowed is not None:
            scores = jnp.where(allowed, scores, MASKED_SCORE)
        shares = jnp.exp(scores - totals[:, first + head : first + head + 1])
        value_grad = value_grad + matmul_tn(shares.astype(LOW), own_grad)
        share_grad = matmul_t(own_grad, values)
        score_grad = shares * (share_grad - jnp.sum(share_grad * shares, axis=-1, keepdims=True))
        score_grad = score_grad.astype(LOW)
        query_grad = query_grad + matmul(score_grad, pick(scaled_keys, mask))
        key_grad = key_grad + matmul_tn(score_grad, own_queries)
    return jnp.concatenate(
        [query_grad.astype(LOW), key_grad.astype(LOW), value_grad.astype(LOW)], axis=1
    )


def enter_rows(rows, parts, columns):
    depth = parts[0].shape[0]
    total = matmul(rows[:, :depth], parts[0][:, columns])
    for i, part in enumerate(parts[1:], 1):
        total = total + matmul(rows[:, i * depth : (i + 1) * depth], part[:, columns])
    return total


def leave_rows(sides, columns, store):
    depth = sides[0][1][0].shape[0]
    for i in range(len(sides[0][1])):
        total = matmul_t(sides[0][0], sides[0][1][i][:, columns])
        for values, parts in sides[1:]:
            total = total + matmul_t(values, parts[i][:, columns])
        store(slice(i * depth, (i + 1) * depth), total.astype(LOW))


def side_columns(side, width):
    return slice(side * width, (side + 1) * width)


def space_forward_body(count, rows, *refs):
    sides = [[ref] for ref in refs[:count]]
    projected_out, output_out, totals_out, part_out = refs[count:]
    width = output_out.shape[1] // count
    totals = jnp.zeros(totals_out.shape, WIDE)
    leaving = []
    for side, parts in enumerate(sides):
        projected = enter_rows(rows, parts, slice(0, 3 * width)).astype(LOW)
        projected_out[:, side_columns(side, 3 * width)] = projected
        output, totals = attention_rows(projected, None, totals, side * (width // HEAD_DIM))
        output_out[:, side_columns(side, width)] = output
        leaving.append((output, parts))
    totals_out[...] = totals

    def store(place, values):
        part_out[:, place] = values

    leave_rows(leaving, slice(3 * width, 4 * width), store)


def space_back_body(count, rows, *refs):
    sides = [[ref] for ref in refs[:count]]
    projected, totals, grads_out, part_out = refs[count:]
    width = projected.shape[1] // (3 * count)
    leaving = []
    for side, parts in enumerate(sides):
        output_grad = enter_rows(rows, parts, slice(3 * width, 4 * width)).astype(LOW)
        first, columns = side * (width // HEAD_DIM), side_columns(side, 3 * width)
        grads = attention_rows_back(projected[:, columns], totals[...], first, output_grad, None)
        grads_out[:, columns] = grads
        leaving.append((grads, parts))

    def store(place, values):
        part_out[:, place] = values

    leave_rows(leaving, slice(0, 3 * width), store)


def time_allowed(lengths, clip, frames_local, positions):
    clips = lengths.shape[0]
    count = ROUND * frames_local * positions
    head_at, frame_at = lax.axis_index("head"), partner(0) // clips

    def split(shape, axis):
        row = lax.broadcasted_iota(jnp.int32, shape, axis)
        group = row // (frames_local * positions)
        local = (row // positions) % frames_local
        return (group ^ head_at) * frames_local + (local ^ frame_at), row % positions

    query_frame, query_pos = split((count, 1), 0)
    key_frame, key_pos = split((1, count), 1)
    length = lengths[(partner(0) % clips) ^ clip]
    return (query_pos == key_pos) & (query_frame >= key_frame) & (key_frame < length)


PART = 16


def time_groups(ref):
    return [(c, p) for c in range(ref.shape[1]) for p in range(0, ref.shape[2], PART)]


def join_rows(refs, group):
    c, p = group
    return jnp.concatenate(
        [ref[:, c, p : p + PART, :].reshape(ref.shape[0] * PART, ref.shape[3]) for ref in refs], axis=0
    )


def split_rows(refs, group, values, place=slice(None)):
    c, p = group
    rows = values.shape[0] // len(refs)
    for i, ref in enumerate(refs):
        part = values[i * rows : (i + 1) * rows].reshape(ref.shape[0], PART, values.shape[1])
        ref[:, c, p : p + PART, place] = part


def time_forward_body(lengths, *refs):
    sides, refs = refs[:2], refs[2:]
    rows, projected_out, output_out, totals_out, part_out = (refs[i : i + 4] for i in range(0, 20, 4))
    frames_local, width = rows[0].shape[0], output_out[0].shape[3]
    side_width = width // len(sides)
    for group in time_groups(rows[0]):
        joined = join_rows(rows, group)
        allowed = time_allowed(lengths, group[0], frames_local, PART)
        totals = jnp.zeros((joined.shape[0], 128), WIDE)
        leaving = []
        for side, weights in enumerate(sides):
            projected = matmul(joined, weights[:, : 3 * side_width]).astype(LOW)
            split_rows(projected_out, group, projected, side_columns(side, 3 * side_width))
            output, totals = attention_rows(projected, allowed, totals, side * (side_width // HEAD_DIM))
            split_rows(output_out, group, output, side_columns(side, side_width))
            leaving.append((output, [weights]))
        split_rows(totals_out, group, totals)
        leave_rows(
            leaving,
            slice(3 * side_width, 4 * side_width),
            lambda place, values, group=group: split_rows(part_out, group, values, place),
        )


def time_back_body(lengths, *refs):
    sides, refs = refs[:2], refs[2:]
    rows, projected, totals, grads_out, part_out = (refs[i : i + 4] for i in range(0, 20, 4))
    frames_local, width = rows[0].shape[0], projected[0].shape[3] // 3
    side_width = width // len(sides)
    for group in time_groups(rows[0]):
        allowed = time_allowed(lengths, group[0], frames_local, PART)
        joined = join_rows(rows, group)
        kept, sums = join_rows(projected, group), join_rows(totals, group)
        leaving = []
        for side, weights in enumerate(sides):
            output_grad = matmul(joined, weights[:, 3 * side_width :]).astype(LOW)
            first, columns = side * (side_width // HEAD_DIM), side_columns(side, 3 * side_width)
            grads = attention_rows_back(kept[:, columns], sums, first, output_grad, allowed)
            split_rows(grads_out, group, grads, columns)
            leaving.append((grads, [weights]))
        leave_rows(
            leaving,
            slice(0, 3 * side_width),
            lambda place, values, group=group: split_rows(part_out, group, values, place),
        )


def space_forward(rows, weights):
    count, width = rows.shape
    sides, inner = len(weights), weights[0].shape[1] // 4
    outs = [
        kept_of((count, 3 * inner * sides), LOW),
        kept_of((count, inner * sides), LOW),
        kept_of((count, 128), WIDE),
        shape_of((count, width), LOW),
    ]
    body = functools.partial(space_forward_body, sides)
    return run(body, outs, (rows, *weights), [ONE_VMEM] * (1 + sides))


def space_back(rows, weights, projected, totals):
    count, width = rows.shape
    sides = len(weights)
    outs = [shape_of(projected.shape, LOW), shape_of((count, width), LOW)]
    args = (rows, *weights, projected, totals)
    body = functools.partial(space_back_body, sides)
    return run(body, outs, args, [ONE_VMEM] * len(args), stored=(sides + 1, sides + 2))


def time_call(body, lengths, weights, groups, out_widths):
    args, outs = [lengths, *weights], []
    for group in groups:
        args += group
    for features, dtype, shape in out_widths:
        outs += [shape((*groups[0][0].shape[:3], features), dtype)] * ROUND
    stored = range(1 + len(weights) + ROUND, len(args))
    results = run(body, outs, args, [ONE_SMEM] + [ONE_VMEM] * (len(args) - 1), vmem=16 * MIB, stored=stored)
    return [results[i : i + ROUND] for i in range(0, len(results), ROUND)]


def hidden_body(normed, grad, *refs):
    enters, leaves, acts, pres = (refs[0], refs[2]), (refs[1], refs[3]), refs[4:6], refs[6:8]
    in_part, out_part = refs[8:]
    hidden = acts[0].shape[1]
    tile = 256
    for side in range(2):
        for start in range(0, hidden, tile):
            place = slice(start, start + tile)
            value = matmul(normed[...], enters[side][:, place])
            square = value * value
            curve = jnp.tanh(GELU_COEFF * (value + 0.044715 * square * value))
            half = 0.5 * (1.0 + curve)
            slope = half + 0.5 * value * (1.0 - curve * curve) * (
                GELU_COEFF * (1.0 + 3.0 * 0.044715 * square)
            )
            acts[side][:, place] = (value * half).astype(LOW)
            pres[side][:, place] = (matmul(grad[...], leaves[side][:, place]) * slope).astype(LOW)
    for values, part, weights in ((pres, in_part, enters), (acts, out_part, leaves)):
        total = matmul_t(values[0][...], weights[0][...]) + matmul_t(values[1][...], weights[1][...])
        part[...] = total.astype(LOW)


def hidden_call(normed, grad, weights):
    count, width = normed.shape
    hidden = weights[0].shape[1]
    outs = [shape_of((count, hidden), LOW)] * 4 + [shape_of((count, width), LOW)] * 2
    results = run(hidden_body, outs, (normed, grad, *weights), [ONE_VMEM] * 6)
    return results[0:2], results[2:4], results[4], results[5]


def weight_grad_tile(counts, ranges, refs, start, tile, store):
    at, column = 0, 0
    for count, columns in zip(counts, ranges):
        lefts, rights = refs[at : at + count], refs[at + count : at + 2 * count]
        at += 2 * count
        total = matmul_tn(lefts[0][:, start : start + tile], rights[0][:, columns])
        for left, right in zip(lefts[1:], rights[1:]):
            total = total + matmul_tn(left[:, start : start + tile], right[:, columns])
        store(column, total.astype(LOW))
        column += total.shape[1]


def weight_grad_body(counts, ranges, near_first, *refs):
    out = refs[-1]
    tile = out.shape[0] // 4
    for place, start in enumerate((0, 2, 1, 3) if near_first else range(4)):

        def store(column, values, place=place):
            out[place * tile : (place + 1) * tile, column : column + values.shape[1]] = values

        weight_grad_tile(counts, ranges, refs, start * tile, tile, store)


def weight_grad(pairs, near_first=False, ranges=None, stored=()):
    args, counts = [], []
    for lefts, rights in pairs:
        args += [*lefts, *rights]
        counts.append(len(lefts))
    width = pairs[0][0][0].shape[1]
    ranges = ranges or [slice(0, rights[0].shape[1]) for _, rights in pairs]
    columns = sum(part.stop - part.start for part in ranges)
    body = functools.partial(weight_grad_body, tuple(counts), ranges, near_first)
    return run(body, shape_of((width, columns), LOW), args, [ONE_VMEM] * len(args), stored=stored)


def small_mine_body(gain, bias, table, out):
    step = gain.shape[1]
    out[...] = jnp.zeros_like(out)
    row = 0
    for part in (gain, bias, table):
        values = jnp.concatenate([part[...]] * ROUND, axis=1)
        lane = lax.broadcasted_iota(jnp.int32, values.shape, 1)
        out[0, row : row + part.shape[0], :] = pick(values, lane // step == lax.axis_index("head"))
        row += part.shape[0]


def small_rows_body(first, second, out):
    blocks, _, step = first.shape
    for half, part in enumerate((first, second)):
        for i in range(blocks):
            place = (half * blocks + i) * step
            out[:, place : place + step] = part[i]


def small_blocks_body(first, second, third, table_a, table_b, *outs):
    step = outs[0].shape[2]
    for half, out in enumerate(outs):
        for i in range(out.shape[0]):
            place = slice((half * out.shape[0] + i) * step, (half * out.shape[0] + i + 1) * step)
            for row, part in enumerate((first, second, third)):
                out[i, row : row + 1, :] = part[0:1, place]
                out[i, row + 3 : row + 4, :] = part[1:2, place]
            out[i, 6:14, :] = table_a[:, place] + table_b[:, place]
            out[i, 14:16, :] = jnp.zeros((2, step), WIDE)


def stack_body(*refs):
    out, row = refs[-1], 0
    for part in refs[:-1]:
        out[row : row + part.shape[0], ...] = part[...]
        row += part.shape[0]


def sum_body(*refs):
    total = refs[0][...]
    for part in refs[1:-1]:
        total = total + part[...]
    refs[-1][...] = total


def add_split_body(first, second, *outs):
    row = 0
    for out in outs:
        part = slice(row, row + out.shape[0])
        out[...] = (first[part].astype(WIDE) + second[part].astype(WIDE)).astype(out.dtype)
        row += out.shape[0]


def shards(
    frames_in,
    action_codes,
    clip_length,
    norm_gain,
    norm_bias,
    action_table,
    spatialin,
    spatialout,
    temporalin,
    temporalout,
    expand,
    shrink,
    out_grad,
):
    frames_local, clips, pos_local, width = frames_in.shape
    local = (frames_local, clips, pos_local, width)
    rel_shape = (BLOCKS, pos_local, width)
    count = BLOCKS * pos_local
    inner = spatialin.shape[2]
    hidden = expand.shape[1]
    codes = action_codes.reshape(BLOCKS)
    scalars = (codes, clip_length)

    packed_shape = shape_of(rel_shape, LOW)
    flat_shape = shape_of((count, width), LOW)
    sums_shape = shape_of((8, width), WIDE)
    frames_flat = frames_in.reshape(rel_shape)

    order = Order()
    send, take, do = order.send, order.take, order.do
    grad_shapes = [shape_of((3, width // BLOCKS, inner), WIDE), shape_of((inner, width // BLOCKS), WIDE)]
    whole_shape = shape_of(rel_shape, WIDE)

    def kernel(body, outs, first, *others, stored=()):
        smem = [ONE_SMEM if a.ndim == 1 else ONE_VMEM for a in (first, *others)]
        return do(lambda *args: run(body, outs, args, smem, stored=stored), first, *others)

    def stacked(*parts):
        shape = (sum(part.shape[0] for part in parts), *parts[0].shape[1:])
        return kernel(stack_body, shape_of(shape, parts[0].dtype), *parts)

    def summed(*parts):
        return kernel(sum_body, shape_of(parts[0].shape, parts[0].dtype), *parts)

    def halves(first, second):
        shape = shape_of((first.shape[0] // 2, *first.shape[1:]), first.dtype)
        keep, left = kernel(add_split_body, [shape, shape], first, second)
        order.last = left
        return keep, left

    def added(first, second):
        return kernel(add_split_body, [shape_of(first.shape, first.dtype)], first, second)[0]

    def attention_rows_of(enter, leave):
        out = shape_of((enter.shape[0], 4 * inner), LOW)
        return kernel(pack_attention_body, out, jnp.transpose(enter, (1, 0, 2)), leave, stored=(0, 1))

    def split_columns(rows, far):
        outs = [shape_of((2 * rows.shape[0], rows.shape[1] // 2), LOW)] * 2
        a, b = kernel(stack_split_body, outs, rows, far)
        order.last = b
        return a, b

    def crossed(first, second):
        out = shape_of((2 * first.shape[0], first.shape[1]), LOW)
        return kernel(stack_cross_body, out, first, second)

    def joined(a, b):
        outs = [shape_of((a[0].shape[0] // 2, 2 * a[0].shape[1]), LOW)] * 2
        keep, left = kernel(add_join_body, outs, *a, *b)
        order.last = left
        return keep, left

    space_rows = attention_rows_of(spatialin, spatialout)
    got = send(space_rows, "space", 4)
    packed = kernel(pack_frames_body, packed_shape, frames_flat, stored=(0,))
    frame_blocks = order.exchange(packed)
    small_shape = (16, width // BLOCKS)
    block = kernel(
        small_mine_body,
        shape_of((1, *small_shape), WIDE),
        norm_gain,
        norm_bias,
        action_table,
        stored=(0, 1, 2),
    )
    got_small = [send(block, "space", mask) for mask in ORDER[1:4]]
    space_a, space_b = split_columns(space_rows, take(got))
    got_a, got_b = send(space_a, "space", 2), send(space_b, "space", 1)
    line = stacked(block, *[take(got) for got in got_small])
    got_small = send(line, "space", 1)
    time_rows = attention_rows_of(temporalin, temporalout)
    space_a = stacked(space_a, take(got_a))
    space_b = stacked(space_b, take(got_b))
    got_a, got_b = send(space_a, "space", 1), send(space_b, "space", 2)
    small = kernel(small_rows_body, shape_of((16, width), WIDE), line, take(got_small))
    got_small = [send(small, "head", mask) for mask in (1, 2, 3)]
    hidden_rows = kernel(
        pack_hidden_body, shape_of((expand.shape[0], 2 * hidden), LOW), expand, shrink, stored=(0, 1)
    )
    small = summed(small, *[take(got) for got in got_small])
    frame_blocks = take(frame_blocks)
    normed, start = kernel(
        frame_norm_body, [flat_shape, kept_of((count, width), WIDE)], *scalars, small, frame_blocks
    )
    normed_far = send(normed, "head", 2)
    got_time = send(time_rows, "space", 4)
    got_a, got_b = take(got_a), take(got_b)
    space_a = stacked(space_a, got_a)
    space_b = crossed(space_b, got_b)
    beside_a, beside_b = send(space_a, "head", 1), send(space_b, "head", 1)
    got_hidden = send(hidden_rows, "space", 4)
    normed_far = take(normed_far)
    time_a, time_b = split_columns(time_rows, take(got_time))
    space_weights = [space_a, space_b, take(beside_a), take(beside_b)]
    got_a, got_b = send(time_a, "space", 2), send(time_b, "space", 1)

    far_kept = do(space_forward, normed_far, space_weights)
    order.last = far_kept[3]
    far_part = send(far_kept[3], "head", 2)
    own_kept = do(space_forward, normed, space_weights)
    order.last = own_kept[3]
    time_a = stacked(time_a, take(got_a))
    time_b = stacked(time_b, take(got_b))
    got_a, got_b = send(time_a, "space", 1), send(time_b, "space", 2)
    far_part = take(far_part)
    packed = kernel(spread_body, packed_shape, own_kept[3], far_part)
    spread = order.exchange(packed)
    hidden_a, hidden_b = split_columns(hidden_rows, take(got_hidden))
    hidden_got = send(hidden_a, "space", 2), send(hidden_b, "space", 1)
    frames_rel, grad_low = kernel(
        order_inputs_body, [packed_shape] * 2, clip_length, frames_flat, out_grad.reshape(rel_shape), stored=(1, 2)
    )
    grad_far = send(grad_low.reshape(count, width), "head", 2)
    grad_far = take(grad_far)
    spread = take(spread)
    first, normed_two = kernel(
        join_norm_body, [whole_shape, packed_shape], *scalars, small, frames_rel, spread
    )
    order.last = normed_two

    normed_two = normed_two.reshape(local)
    far = send(normed_two, "head", 2)
    near = send(normed_two, "head", 1)
    hidden_a = stacked(hidden_a, take(hidden_got[0]))
    hidden_b = stacked(hidden_b, take(hidden_got[1]))
    hidden_got = send(hidden_a, "space", 1), send(hidden_b, "space", 2)
    near = take(near)
    time_a = stacked(time_a, take(got_a))
    time_b = crossed(time_b, take(got_b))
    far = take(far)
    diagonal = send(far, "head", 1)
    normed_two = [normed_two, near, far, take(diagonal)]
    time_projected, time_output, time_totals, time_parts = do(
        lambda first, *others: time_call(
            time_forward_body,
            clip_length,
            [time_a, time_b],
            [[first, *others]],
            [(3 * inner, LOW, kept_of), (inner, LOW, kept_of), (128, WIDE, kept_of), (width, LOW, shape_of)],
        ),
        *normed_two,
    )
    order.last = time_parts[3]
    diagonal = send(time_parts[3], "head", 1)
    near = send(time_parts[1], "head", 1)
    far = added(time_parts[2], take(diagonal))
    far = send(far, "head", 2)
    near = take(near)
    parts = [part.reshape(rel_shape) for part in (time_parts[0], near, take(far))]
    second, normed_three = kernel(add_norm_body, [whole_shape, packed_shape], small, first, *parts)
    order.last = normed_three

    normed_three = normed_three.reshape(count, width)
    grad_low_flat = grad_low.reshape(count, width)
    far = send(normed_three, "head", 2)
    hidden_a = stacked(hidden_a, take(hidden_got[0]))
    hidden_b = crossed(hidden_b, take(hidden_got[1]))
    beside_a, beside_b = send(hidden_a, "head", 1), send(hidden_b, "head", 1)
    normed_three = [normed_three, take(far)]
    hidden_weights = [hidden_a, hidden_b, take(beside_a), take(beside_b)]
    grad_third = [grad_low_flat, grad_far]
    far_kept_three = do(hidden_call, normed_three[1], grad_third[1], hidden_weights)
    order.last = far_kept_three[2]
    far_part = send(far_kept_three[2], "head", 2)
    own_kept_three = do(hidden_call, normed_three[0], grad_third[0], hidden_weights)
    hidden_kept = [own_kept_three, far_kept_three]

    def hidden_part(side, leave):
        lefts = grad_third if leave else normed_three
        rights = [kept[0 if leave else 1][side] for kept in hidden_kept]
        return do(lambda *left: weight_grad([(left, rights)], near_first=leave), *lefts)

    beside_a = hidden_part(1, False)
    beside_b = hidden_part(1, True)
    far_part = take(far_part)
    beside_a, beside_b = send(beside_a, "head", 1), send(beside_b, "head", 1)
    parts = [part.reshape(rel_shape) for part in (own_kept_three[2], far_part)]
    total_second, low_second, sums_third = kernel(
        back_third_body, [whole_shape, packed_shape, sums_shape], small, grad_low, second, *parts
    )
    order.last = low_second
    low_second = low_second.reshape(local)
    far = send(low_second, "head", 2)
    near = send(low_second, "head", 1)
    hidden_a = hidden_part(0, False)
    hidden_b = hidden_part(0, True)
    near = take(near)
    far = take(far)
    diagonal = send(far, "head", 1)
    hidden_a, send_a = halves(hidden_a, take(beside_a))
    got_a = send(send_a, "space", 1)
    hidden_b, send_b = halves(hidden_b, take(beside_b))
    got_b = send(send_b, "space", 2)

    grad_two = [low_second, near, far, take(diagonal)]
    time_grads, time_parts = do(
        lambda first, *others: time_call(
            time_back_body,
            clip_length,
            [time_a, time_b],
            [[first, *others], time_projected, time_totals],
            [(3 * inner, LOW, shape_of), (width, LOW, shape_of)],
        ),
        *grad_two,
    )
    order.last = time_parts[3]
    diagonal = send(time_parts[3], "head", 1)
    near = send(time_parts[1], "head", 1)
    flat = lambda arrays: [a.reshape(count, a.shape[-1]) for a in arrays]
    far = added(time_parts[2], take(diagonal))
    far = send(far, "head", 2)
    near = take(near)

    def attention_part(side, lefts, grads, backs, outputs, stored):
        step = inner // 2
        return do(
            lambda *left: weight_grad(
                [(left, grads), (backs, outputs)],
                near_first=side % 2 == 1,
                ranges=[side_columns(side, 3 * step), side_columns(side, step)],
                stored=stored,
            ),
            *lefts,
        )

    time_args = flat(normed_two), flat(time_grads), flat(grad_two), flat(time_output), range(12, 16)
    time_a = attention_part(0, *time_args)
    time_b = attention_part(1, *time_args)
    hidden_a, send_a = halves(hidden_a, take(got_a))
    hidden_b, send_b = halves(hidden_b, take(got_b))
    hidden_got = send(send_a, "space", 2), send(send_b, "space", 1)
    parts = [part.reshape(rel_shape) for part in (time_parts[0], near, take(far))]
    total_first, sums_second, table_first, packed = kernel(
        back_second_body,
        [whole_shape, sums_shape, sums_shape, packed_shape],
        *scalars,
        small,
        total_second,
        first,
        *parts,
    )
    order.last = packed
    grad_blocks = order.exchange(packed)
    hidden_keep, hidden_send = joined((hidden_a, take(hidden_got[0])), (hidden_b, take(hidden_got[1])))
    (time_a, send_a), (time_b, send_b) = [jnp.split(part, 2) for part in (time_a, time_b)]
    got_a, got_b = send(send_a, "space", 1), send(send_b, "space", 2)
    got_hidden = send(hidden_send, "space", 4)
    far_out = send(far_kept_three[3], "head", 2)
    parts = [part.reshape(rel_shape) for part in (own_kept_three[3], take(far_out))]
    frames_out = kernel(finish_forward_body, packed_shape, clip_length, second, *parts)

    grad_blocks = take(grad_blocks)
    grad_one = kernel(collect_body, flat_shape, grad_blocks)
    far = send(grad_one, "head", 2)
    own_result = do(space_back, grad_one, space_weights, own_kept[0], own_kept[2])
    order.last = own_result[1]
    got_hidden = take(got_hidden)
    time_a, send_a = halves(time_a, take(got_a))
    time_b, send_b = halves(time_b, take(got_b))
    grad_one = [grad_one, take(far)]
    got_a, got_b = send(send_a, "space", 2), send(send_b, "space", 1)
    far_result = do(space_back, grad_one[1], space_weights, far_kept[0], far_kept[2])
    order.last = far_result[1]
    far_part = send(far_result[1], "head", 2)
    space_args = [normed, normed_far], [own_result[0], far_result[0]], grad_one, [own_kept[1], far_kept[1]], (6, 7)
    beside_a = attention_part(2, *space_args)
    beside_b = attention_part(3, *space_args)
    time_keep, time_send = joined((time_a, take(got_a)), (time_b, take(got_b)))
    got_time = send(time_send, "space", 4)
    space_a = attention_part(0, *space_args)
    space_b = attention_part(1, *space_args)
    far_part = take(far_part)
    beside_a, beside_b = send(beside_a, "head", 1), send(beside_b, "head", 1)
    sums_first, table_second, packed = kernel(
        back_first_body,
        [sums_shape, sums_shape, packed_shape],
        *scalars,
        small,
        start,
        own_result[1],
        far_part,
        stored=(3,),
    )
    order.last = packed
    space_a, send_a = halves(space_a, take(beside_a))
    space_b, send_b = halves(space_b, take(beside_b))
    got_a, got_b = send(send_a, "space", 1), send(send_b, "space", 2)
    last = order.exchange(packed)
    half_shape = shape_of((BLOCKS // 2, *small_shape), WIDE)
    sums, small_send = kernel(
        small_blocks_body, [half_shape] * 2, sums_first, sums_second, sums_third, table_first, table_second
    )
    order.last = small_send
    got_small = send(small_send, "space", 1)
    hidden_grads = kernel(
        unpack_hidden_body,
        [shape_of((width // BLOCKS, hidden), WIDE), shape_of((hidden, width // BLOCKS), WIDE)],
        hidden_keep,
        got_hidden,
    )
    sums, small_send = halves(sums, take(got_small))
    got_small = send(small_send, "space", 2)
    space_a, send_a = halves(space_a, take(got_a))
    space_b, send_b = halves(space_b, take(got_b))
    got_a, got_b = send(send_a, "space", 2), send(send_b, "space", 1)
    sums, small_send = halves(sums, take(got_small))
    got_small = send(small_send, "space", 4)
    space_keep, space_send = joined((space_a, take(got_a)), (space_b, take(got_b)))
    sums = summed(sums, take(got_small))
    got_small = send(sums, "head", 1)
    got = send(space_send, "space", 4)
    last = take(last)
    frames_grad = kernel(finish_back_body, whole_shape, clip_length, total_first, last)
    sums = summed(sums, take(got_small))
    got_small = send(sums, "head", 2)
    time_grads = kernel(unpack_attention_body, grad_shapes, time_keep, take(got_time))
    sums = summed(sums, take(got_small))[0]
    step = sums.shape[1] // ROUND
    sums = lax.dynamic_slice(sums, (0, lax.axis_index("head") * step), (sums.shape[0], step))
    space_grads = kernel(unpack_attention_body, grad_shapes, space_keep, take(got))
    return (
        frames_out.reshape(local),
        frames_grad.reshape(local),
        sums[0:3],
        sums[3:6],
        sums[6:14],
        jnp.transpose(space_grads[0], (1, 0, 2)),
        space_grads[1],
        jnp.transpose(time_grads[0], (1, 0, 2)),
        time_grads[1],
        *hidden_grads,
    )


def solution(mesh):
    placed = (
        P("head", None, "space", None),
        P("head", None),
        P(),
        P(None, ("space", "head")),
        P(None, ("space", "head")),
        P(None, ("space", "head")),
        P("space", None, "head"),
        P("head", "space"),
        P("space", None, "head"),
        P("head", "space"),
        P("space", "head"),
        P("head", "space"),
        P("head", None, "space", None),
    )
    eight = mesh.shape["space"] == BLOCKS and mesh.shape["head"] == ROUND
    return jax.shard_map(
        shards if eight else general_shards,
        mesh=mesh,
        in_specs=placed,
        out_specs=(
            P("head", None, "space", None),
            P("head", None, "space", None),
            P(None, ("space", "head")),
            P(None, ("space", "head")),
            P(None, ("space", "head")),
            P("space", None, "head"),
            P("head", "space"),
            P("space", None, "head"),
            P("head", "space"),
            P("space", "head"),
            P("head", "space"),
        ),
        check_vma=False,
    )
```

```python
import functools

import jax
import jax.numpy as jnp
from jax import lax
from jax.experimental import pallas as pl
from jax.experimental.pallas import tpu as pltpu
from jax.sharding import PartitionSpec as P

HEAD_DIM = 64


EPSILON = 1e-05
SCORE_SCALE = 0.125
MASKED_SCORE = -1e30
PRECISE = lax.Precision.HIGHEST
GELU_COEFF = 0.7978845608028654


def layer_norm(values, gain_row, bias_row):
    row_mean = jnp.mean(values, axis=-1, keepdims=True)
    centred = values - row_mean
    row_var = jnp.mean(centred * centred, axis=-1, keepdims=True)
    return centred * lax.rsqrt(row_var + EPSILON) * gain_row + bias_row


def gelu_tanh(inputs):
    return (
        0.5 * inputs * (1.0 + jnp.tanh(GELU_COEFF * (inputs + 0.044715 * inputs * inputs * inputs)))
    )


def gather_weights(small, large):
    small_full = (
        lax.all_gather(small[0], ("space", "head"), axis=1, tiled=True),
        lax.all_gather(small[1], ("space", "head"), axis=1, tiled=True),
        lax.all_gather(small[2], ("space", "head"), axis=1, tiled=True),
    )
    large_full = (
        lax.all_gather(large[0], "space", axis=0, tiled=True),
        lax.all_gather(large[1], "space", axis=1, tiled=True),
        lax.all_gather(large[2], "space", axis=0, tiled=True),
        lax.all_gather(large[3], "space", axis=1, tiled=True),
        lax.all_gather(large[4], "space", axis=0, tiled=True),
        lax.all_gather(large[5], "space", axis=1, tiled=True),
    )
    return (small_full, large_full)


def norm_step(inputs, gain_row, bias_row):
    normed, pullback = jax.vjp(layer_norm, inputs, gain_row, bias_row)
    whole = lax.all_gather(normed.astype(jnp.bfloat16), "head", axis=0, tiled=True)
    return (whole, pullback)


def cot_whole(grad_rows):
    return lax.all_gather(grad_rows.astype(jnp.bfloat16), "head", axis=0, tiled=True)


def input_total(partial_value):
    return lax.psum_scatter(
        partial_value.astype(jnp.bfloat16), "head", scatter_dimension=0, tiled=True
    ).astype(jnp.float32)


def heads_total(left, weight):
    return lax.psum_scatter(
        jnp.einsum("fcpe,ed->fcpd", left, weight, preferred_element_type=jnp.float32).astype(
            jnp.bfloat16
        ),
        "head",
        scatter_dimension=0,
        tiled=True,
    ).astype(jnp.float32)


def project_in(whole, weight):
    stacked = jnp.einsum(
        "fcpd,dke->kfcpe", whole, weight, preferred_element_type=jnp.float32
    ).astype(jnp.bfloat16)
    return (stacked[0], stacked[1], stacked[2])


def raw_scores(queries, keyset, form, allowed):
    key_form = form.replace("q", "k")
    scores = (
        jnp.einsum(
            form + "," + key_form + "->bhqk", queries, keyset, preferred_element_type=jnp.float32
        )
        * SCORE_SCALE
    )
    if allowed is not None:
        scores = jnp.where(allowed, scores, MASKED_SCORE)
    return scores


def attend(queries, keyset, values, form, allowed):
    key_form = form.replace("q", "k")
    scores = raw_scores(queries, keyset, form, allowed)
    row_max = jnp.max(scores, axis=-1, keepdims=True)
    log_total = row_max + jnp.log(jnp.sum(jnp.exp(scores - row_max), axis=-1, keepdims=True))
    shares = jnp.exp(scores - log_total).astype(jnp.bfloat16)
    output = jnp.einsum(
        "bhqk," + key_form + "->" + form, shares, values, preferred_element_type=jnp.float32
    )
    return (output.astype(jnp.bfloat16), log_total)


def attend_back(queries, keyset, values, log_total, output_grad, form, allowed):
    key_form = form.replace("q", "k")
    shares = jnp.exp(raw_scores(queries, keyset, form, allowed) - log_total)
    value_grad = jnp.einsum(
        "bhqk," + form + "->" + key_form,
        shares.astype(jnp.bfloat16),
        output_grad,
        preferred_element_type=jnp.float32,
    )
    share_grad = jnp.einsum(
        form + "," + key_form + "->bhqk", output_grad, values, preferred_element_type=jnp.float32
    )
    score_grad = (
        shares * (share_grad - jnp.sum(share_grad * shares, axis=-1, keepdims=True))
    ).astype(jnp.bfloat16)
    query_grad = (
        jnp.einsum(
            "bhqk," + key_form + "->" + form, score_grad, keyset, preferred_element_type=jnp.float32
        )
        * SCORE_SCALE
    )
    key_grad = (
        jnp.einsum(
            "bhqk," + form + "->" + key_form,
            score_grad,
            queries,
            preferred_element_type=jnp.float32,
        )
        * SCORE_SCALE
    )
    return (
        query_grad.astype(jnp.bfloat16),
        key_grad.astype(jnp.bfloat16),
        value_grad.astype(jnp.bfloat16),
    )


def general_shards(
    frames_in,
    action_codes,
    clip_length,
    norm_gain,
    norm_bias,
    action_table,
    spatialin,
    spatialout,
    temporalin,
    temporalout,
    expand,
    shrink,
    out_grad,
):
    head_count = lax.axis_size("head")
    frames_local, clip_count, pos_local, width = frames_in.shape
    frames_total = frames_local * head_count
    local_width = spatialin.shape[2]
    heads_local = local_width // HEAD_DIM
    frame_index = jnp.arange(frames_total)
    local_index = lax.axis_index("head") * frames_local + jnp.arange(frames_local)
    valid_local = (local_index[:, None] < clip_length[None, :]).astype(jnp.float32)[
        :, :, None, None
    ]
    allowed = (frame_index[None, :, None] >= frame_index[None, None, :]) & (
        frame_index[None, None, :] < clip_length[:, None, None]
    )
    allowed = jnp.broadcast_to(
        allowed[:, None, None], (clip_count, pos_local, 1, frames_total, frames_total)
    )
    allowed = allowed.reshape(clip_count * pos_local, 1, frames_total, frames_total)
    small_full, large_full = gather_weights(
        (norm_gain, norm_bias, action_table),
        (spatialin, spatialout, temporalin, temporalout, expand, shrink),
    )
    gain_full, bias_full, table_full = small_full
    space_in, space_out, time_in, time_out, expand_full, shrink_full = large_full
    code_hot = (action_codes[:, :, None] == jnp.arange(table_full.shape[0])[None, None, :]).astype(
        jnp.float32
    )
    embedded = jnp.einsum("fca,ad->fcd", code_hot, table_full, precision=PRECISE)
    start = valid_local * (frames_in.astype(jnp.float32) + embedded[:, :, None, :])
    whole_one, pull_one = norm_step(start, gain_full[0], bias_full[0])
    space_query, space_keys, space_values = project_in(whole_one, space_in)
    flat_shape = (frames_total * clip_count, pos_local, local_width)
    moved = (
        lax.all_to_all(
            space_query.reshape(flat_shape), "space", split_axis=0, concat_axis=1, tiled=True
        ),
        lax.all_to_all(
            space_keys.reshape(flat_shape), "space", split_axis=0, concat_axis=1, tiled=True
        ),
        lax.all_to_all(
            space_values.reshape(flat_shape), "space", split_axis=0, concat_axis=1, tiled=True
        ),
    )
    block_rows = moved[0].shape[0]
    block_cols = moved[0].shape[1]
    frame_shape = (block_rows, block_cols, heads_local, HEAD_DIM)
    frame_query = moved[0].reshape(frame_shape)
    frame_keys = moved[1].reshape(frame_shape)
    frame_values = moved[2].reshape(frame_shape)
    frame_out, frame_total = attend(frame_query, frame_keys, frame_values, "bqhe", None)
    returned = lax.all_to_all(
        frame_out.reshape(block_rows, block_cols, local_width),
        "space",
        split_axis=1,
        concat_axis=0,
        tiled=True,
    )
    space_attended = returned.reshape(frames_total, clip_count, pos_local, local_width)
    first = start + heads_total(space_attended, space_out)
    whole_two, pull_two = norm_step(first, gain_full[1], bias_full[1])
    time_query, time_keys, time_values = project_in(whole_two, time_in)
    time_shape = (frames_total, clip_count * pos_local, heads_local, HEAD_DIM)
    time_query = time_query.reshape(time_shape)
    time_keys = time_keys.reshape(time_shape)
    time_values = time_values.reshape(time_shape)
    time_out_rows, time_total = attend(time_query, time_keys, time_values, "qbhe", allowed)
    time_attended = time_out_rows.reshape(frames_total, clip_count, pos_local, local_width)
    second = first + heads_total(time_attended, time_out)
    whole_three, pull_three = norm_step(second, gain_full[2], bias_full[2])
    expanded = jnp.einsum(
        "fcpd,dh->fcph", whole_three, expand_full, preferred_element_type=jnp.float32
    )
    activated, gelu_pull = jax.vjp(gelu_tanh, expanded)
    activated_low = activated.astype(jnp.bfloat16)
    third = second + heads_total(activated_low, shrink_full)
    frames_out = (valid_local * third).astype(jnp.bfloat16)
    small_full, large_full = gather_weights(
        (norm_gain, norm_bias, action_table),
        (spatialin, spatialout, temporalin, temporalout, expand, shrink),
    )
    space_in, space_out, time_in, time_out, expand_full, shrink_full = large_full
    grad_third = valid_local * out_grad.astype(jnp.float32)
    cot_three = cot_whole(grad_third)
    shrink_part = jnp.einsum(
        "fcph,fcpd->hd", activated_low, cot_three, preferred_element_type=jnp.float32
    )
    act_grad = jnp.einsum(
        "fcpd,hd->fcph", cot_three, shrink_full, preferred_element_type=jnp.float32
    )
    pre_grad = gelu_pull(act_grad)[0].astype(jnp.bfloat16)
    expand_part = jnp.einsum(
        "fcpd,fcph->dh", whole_three, pre_grad, preferred_element_type=jnp.float32
    )
    normed_grad = input_total(
        jnp.einsum("fcph,dh->fcpd", pre_grad, expand_full, preferred_element_type=jnp.float32)
    )
    input_three, gain_three, bias_three = pull_three(normed_grad)
    grad_second = grad_third + input_three
    cot_two = cot_whole(grad_second)
    time_out_part = jnp.einsum(
        "fcpe,fcpd->ed", time_attended, cot_two, preferred_element_type=jnp.float32
    )
    time_grad = jnp.einsum(
        "fcpd,ed->fcpe", cot_two, time_out, preferred_element_type=jnp.float32
    ).astype(jnp.bfloat16)
    time_grads = attend_back(
        time_query,
        time_keys,
        time_values,
        time_total,
        time_grad.reshape(time_shape),
        "qbhe",
        allowed,
    )
    stacked_grad = jnp.stack(
        [member.reshape(frames_total, clip_count, pos_local, local_width) for member in time_grads]
    )
    time_in_part = jnp.einsum(
        "fcpd,kfcpe->dke", whole_two, stacked_grad, preferred_element_type=jnp.float32
    )
    normed_grad = input_total(
        jnp.einsum("kfcpe,dke->fcpd", stacked_grad, time_in, preferred_element_type=jnp.float32)
    )
    input_two, gain_two, bias_two = pull_two(normed_grad)
    grad_first = grad_second + input_two
    cot_one = cot_whole(grad_first)
    space_out_part = jnp.einsum(
        "fcpe,fcpd->ed", space_attended, cot_one, preferred_element_type=jnp.float32
    )
    space_grad = jnp.einsum(
        "fcpd,ed->fcpe", cot_one, space_out, preferred_element_type=jnp.float32
    ).astype(jnp.bfloat16)
    frame_grad = lax.all_to_all(
        space_grad.reshape(flat_shape), "space", split_axis=0, concat_axis=1, tiled=True
    ).reshape(frame_shape)
    query_grad, keys_grad, values_grad = attend_back(
        frame_query, frame_keys, frame_values, frame_total, frame_grad, "bqhe", None
    )
    block_shape = (block_rows, block_cols, local_width)
    back_grads = (
        lax.all_to_all(
            query_grad.reshape(block_shape), "space", split_axis=1, concat_axis=0, tiled=True
        ),
        lax.all_to_all(
            keys_grad.reshape(block_shape), "space", split_axis=1, concat_axis=0, tiled=True
        ),
        lax.all_to_all(
            values_grad.reshape(block_shape), "space", split_axis=1, concat_axis=0, tiled=True
        ),
    )
    stacked_grad = jnp.stack(
        [member.reshape(frames_total, clip_count, pos_local, local_width) for member in back_grads]
    )
    space_in_part = jnp.einsum(
        "fcpd,kfcpe->dke", whole_one, stacked_grad, preferred_element_type=jnp.float32
    )
    normed_grad = input_total(
        jnp.einsum("kfcpe,dke->fcpd", stacked_grad, space_in, preferred_element_type=jnp.float32)
    )
    input_one, gain_one, bias_one = pull_one(normed_grad)
    grad_start = grad_first + input_one
    frames_grad = valid_local * grad_start
    table_part = jnp.einsum(
        "fca,fcd->ad", code_hot, jnp.sum(frames_grad, axis=2), precision=PRECISE
    )
    gain_grad, bias_grad, table_grad = (
        lax.psum_scatter(
            jnp.stack([gain_one, gain_two, gain_three]),
            ("space", "head"),
            scatter_dimension=1,
            tiled=True,
        ),
        lax.psum_scatter(
            jnp.stack([bias_one, bias_two, bias_three]),
            ("space", "head"),
            scatter_dimension=1,
            tiled=True,
        ),
        lax.psum_scatter(table_part, ("space", "head"), scatter_dimension=1, tiled=True),
    )
    weight_grads = (
        lax.psum_scatter(space_in_part, "space", scatter_dimension=0, tiled=True),
        lax.psum_scatter(space_out_part, "space", scatter_dimension=1, tiled=True),
        lax.psum_scatter(time_in_part, "space", scatter_dimension=0, tiled=True),
        lax.psum_scatter(time_out_part, "space", scatter_dimension=1, tiled=True),
        lax.psum_scatter(expand_part, "space", scatter_dimension=0, tiled=True),
        lax.psum_scatter(shrink_part, "space", scatter_dimension=1, tiled=True),
    )
    return (
        frames_out,
        frames_grad,
        gain_grad,
        bias_grad,
        table_grad,
        weight_grads[0],
        weight_grads[1],
        weight_grads[2],
        weight_grads[3],
        weight_grads[4],
        weight_grads[5],
    )


ORDER = (0, 4, 2, 6, 1, 5, 3, 7)
BLOCKS = len(ORDER)
PLACE = tuple(ORDER.index(mask) for mask in range(BLOCKS))
ROUND = 4
ONE_VMEM = pl.BlockSpec(memory_space=pltpu.VMEM)
ONE_SMEM = pl.BlockSpec(memory_space=pltpu.SMEM)
MIB = 1024 * 1024
LOW = jnp.bfloat16
WIDE = jnp.float32


def swap(value, axis, mask):
    return lax.ppermute(value, axis, [(i, i ^ mask) for i in range(lax.axis_size(axis))])


class Order:
    def __init__(self):
        self.last = None

    def tied(self, value):
        if self.last is None:
            return value
        return lax.optimization_barrier((value, self.last))[0]

    def send(self, value, axis, mask):
        return swap(self.tied(value), axis, mask)

    def exchange(self, packed):
        return lax.all_to_all(self.tied(packed), "space", split_axis=0, concat_axis=0, tiled=True)

    def take(self, value):
        self.last = self.tied(value)
        return self.last

    def do(self, step, first, *others):
        result = step(self.tied(first), *others)
        self.last = jax.tree.leaves(result)[0]
        return result


def run(body, outs, args, specs, vmem=None, stored=()):
    single = not isinstance(outs, (list, tuple))
    name = getattr(body, "func", body).__name__.removesuffix("_body")
    args, specs, scratch, whole = list(args), list(specs), [], body
    if stored:
        for place in stored:
            args[place] = pltpu.with_memory_space_constraint(args[place], pltpu.HBM)
            specs[place] = pl.BlockSpec(memory_space=pltpu.HBM)
            scratch.append(pltpu.VMEM(args[place].shape, args[place].dtype))
        scratch.append(pltpu.SemaphoreType.DMA((len(stored),)))

        def whole(*refs):
            refs, held, sem = list(refs[: -len(scratch)]), refs[-len(scratch) : -1], refs[-1]
            copies = [
                pltpu.make_async_copy(refs[place], held[i], sem.at[i]) for i, place in enumerate(stored)
            ]
            for copy in copies:
                copy.start()
            for i, place in enumerate(stored):
                copies[i].wait()
                refs[place] = held[i]
            body(*refs)

    return pl.pallas_call(
        whole,
        out_shape=outs,
        in_specs=specs,
        out_specs=ONE_VMEM if single else [ONE_VMEM] * len(outs),
        scratch_shapes=scratch,
        cost_estimate=pl.CostEstimate(flops=0, bytes_accessed=1024, transcendentals=0),
        compiler_params=pltpu.CompilerParams(vmem_limit_bytes=vmem or 12 * MIB),
        name=name,
    )(*args)


def kept_of(dims, dtype):
    return pltpu.HBM(tuple(dims), dtype)


def shape_of(dims, dtype):
    return jax.ShapeDtypeStruct(tuple(dims), dtype)


def feature_block(place, step):
    return pl.ds(pl.multiple_of(place * step, step), step)


def partner(mask):
    return lax.axis_index("space") ^ mask


def frame_valid(lengths, frames, mask):
    clips = lengths.shape[0]
    frame = lax.axis_index("head") * (frames // clips) + partner(mask) // clips
    return jnp.where(frame < lengths[partner(mask) % clips], 1.0, 0.0).astype(WIDE)


def normed_parts(values):
    centred = values - jnp.mean(values, axis=-1, keepdims=True)
    scale = lax.rsqrt(jnp.mean(centred * centred, axis=-1, keepdims=True) + EPSILON)
    return centred * scale, scale


def norm_back(values, grad, gain_row):
    unit, scale = normed_parts(values)
    scaled = grad * gain_row
    out = scale * (
        scaled
        - jnp.mean(scaled, axis=-1, keepdims=True)
        - unit * jnp.mean(scaled * unit, axis=-1, keepdims=True)
    )
    return (
        out,
        jnp.sum(grad * unit, axis=0, keepdims=True),
        jnp.sum(grad, axis=0, keepdims=True),
    )


def store_for(ref, rows, mask):
    step = rows.shape[-1] // BLOCKS
    for i in range(BLOCKS):
        j = i ^ PLACE[mask]
        ref[partner(mask), :, i * step : (i + 1) * step] = rows[:, j * step : (j + 1) * step]


def pack_attention_body(enter, leave, out):
    step = leave.shape[0] // 2
    for i in range(2):
        place, column = slice(i * step, (i + 1) * step), 4 * i * step
        for j in range(3):
            out[:, column + j * step : column + (j + 1) * step] = enter[j, :, place]
        out[:, column + 3 * step : column + 4 * step] = jnp.transpose(leave[place, :])


def unpack_attention_body(mine, got, enter, leave):
    step = leave.shape[0] // 2
    for i in range(2):
        columns = side_columns(i, 4 * step)
        total = mine[:, columns].astype(WIDE) + got[:, columns].astype(WIDE)
        place = slice(i * step, (i + 1) * step)
        for j in range(3):
            enter[j, :, place] = total[:, j * step : (j + 1) * step]
        leave[place, :] = jnp.transpose(total[:, 3 * step :])


def pack_hidden_body(enter, leave, out):
    hidden = leave.shape[0]
    out[:, :hidden] = enter[...]
    out[:, hidden:] = jnp.transpose(leave[...])


def unpack_hidden_body(mine, got, enter, leave):
    hidden = leave.shape[0]
    total = mine[...].astype(WIDE) + got[...].astype(WIDE)
    enter[...] = total[:, :hidden]
    leave[...] = jnp.transpose(total[:, hidden:])


def stack_split_body(first, second, *outs):
    rows, column = first.shape[0], 0
    for out in outs:
        place = slice(column, column + out.shape[1])
        out[:rows, :] = first[:, place]
        out[rows:, :] = second[:, place]
        column += out.shape[1]


def stack_cross_body(first, second, out):
    tile = first.shape[0] // 2
    for i, (part, place) in enumerate(((first, 0), (second, 0), (first, 1), (second, 1))):
        out[i * tile : (i + 1) * tile, :] = part[place * tile : (place + 1) * tile, :]


def add_join_body(first_a, second_a, first_b, second_b, *outs):
    row, half = 0, first_a.shape[1]
    for out in outs:
        part = slice(row, row + out.shape[0])
        out[:, :half] = (first_a[part].astype(WIDE) + second_a[part].astype(WIDE)).astype(out.dtype)
        out[:, half:] = (first_b[part].astype(WIDE) + second_b[part].astype(WIDE)).astype(out.dtype)
        row += out.shape[0]


def pack_frames_body(frames, out):
    step = frames.shape[-1] // BLOCKS
    for mask in range(BLOCKS):
        for i in range(BLOCKS):
            source = partner(ORDER[i ^ PLACE[mask]])
            place = slice(i * step, (i + 1) * step)
            out[partner(mask), :, place] = frames[partner(mask), :, feature_block(source, step)]


def order_inputs_body(lengths, frames, grad, frames_out, grad_out):
    step = frames.shape[-1] // BLOCKS

    def one(mask, carry):
        valid = frame_valid(lengths, BLOCKS, mask)
        for i in range(BLOCKS):
            source = feature_block(partner(ORDER[i]), step)
            place = slice(i * step, (i + 1) * step)
            frames_out[mask, :, place] = frames[partner(mask), :, source]
            kept = grad[partner(mask), :, source].astype(WIDE) * valid
            grad_out[mask, :, place] = kept.astype(LOW)
        return carry

    lax.fori_loop(0, BLOCKS, one, 0)


def start_rows(rows, codes, lengths, small, mask):
    embedded = small[pl.ds(6 + codes[partner(mask)], 1), :]
    return frame_valid(lengths, BLOCKS, mask) * (rows.astype(WIDE) + embedded)


def frame_norm_body(codes, lengths, small, blocks, normed, start):
    rows = blocks.shape[1]
    for b in range(BLOCKS):
        values = start_rows(blocks[partner(b)], codes, lengths, small, 0)
        start[b * rows : (b + 1) * rows, :] = values
        unit, _ = normed_parts(values)
        normed[b * rows : (b + 1) * rows, :] = (unit * small[0:1, :] + small[3:4, :]).astype(LOW)


def spread_body(first, second, out):
    rows = out.shape[1]
    for mask in range(BLOCKS):
        part = slice(mask * rows, (mask + 1) * rows)
        total = first[part, :].astype(WIDE) + second[part, :].astype(WIDE)
        store_for(out, total.astype(LOW), mask)


def join_norm_body(codes, lengths, small, frames, blocks, whole, normed):
    for b in range(BLOCKS):
        values = start_rows(frames[b], codes, lengths, small, b) + blocks[partner(b)].astype(WIDE)
        whole[b] = values
        unit, _ = normed_parts(values)
        normed[b] = (unit * small[1:2, :] + small[4:5, :]).astype(LOW)


def add_norm_body(small, before, first, second, third, whole, normed):
    def one(b, carry):
        values = before[b] + (
            first[b].astype(WIDE) + second[b].astype(WIDE) + third[b].astype(WIDE)
        )
        whole[b] = values
        unit, _ = normed_parts(values)
        normed[b] = (unit * small[2:3, :] + small[5:6, :]).astype(LOW)
        return carry

    lax.fori_loop(0, BLOCKS, one, 0)


def finish_forward_body(lengths, before, first, second, out):
    step = out.shape[-1] // BLOCKS

    def one(b, carry):
        values = before[b] + (first[b].astype(WIDE) + second[b].astype(WIDE))
        values = (frame_valid(lengths, BLOCKS, b) * values).astype(LOW)
        for i in range(BLOCKS):
            place = feature_block(partner(ORDER[i]), step)
            out[partner(b), :, place] = values[:, i * step : (i + 1) * step]
        return carry

    lax.fori_loop(0, BLOCKS, one, 0)


def back_third_body(small, grad, values, first, second, total_out, low_out, sums):
    sums[...] = jnp.zeros_like(sums)

    def one(b, carry):
        normed_grad = first[b].astype(WIDE) + second[b].astype(WIDE)
        out, gain, bias = norm_back(values[b], normed_grad, small[2:3, :])
        total = grad[b].astype(WIDE) + out
        total_out[b] = total
        low_out[b] = total.astype(LOW)
        sums[0:1, :] += gain
        sums[1:2, :] += bias
        return carry

    lax.fori_loop(0, BLOCKS, one, 0)


def back_second_body(codes, lengths, small, grad, values, first, second, third, total_out, sums, table, packed):
    sums[...] = jnp.zeros_like(sums)
    table[...] = jnp.zeros_like(table)
    for b in range(BLOCKS):
        normed_grad = first[b].astype(WIDE) + second[b].astype(WIDE) + third[b].astype(WIDE)
        out, gain, bias = norm_back(values[b], normed_grad, small[1:2, :])
        total = grad[b] + out
        total_out[b] = total
        store_for(packed, total.astype(LOW), b)
        sums[0:1, :] += gain
        sums[1:2, :] += bias
        row = pl.ds(codes[partner(b)], 1)
        table[row, :] += frame_valid(lengths, BLOCKS, b) * jnp.sum(total, axis=0, keepdims=True)


def back_first_body(codes, lengths, small, values, first, second, sums, table, packed):
    sums[...] = jnp.zeros_like(sums)
    table[...] = jnp.zeros_like(table)
    rows = packed.shape[1]
    for b in range(BLOCKS):
        part = slice(b * rows, (b + 1) * rows)
        normed_grad = first[part, :].astype(WIDE) + second[part, :].astype(WIDE)
        out, gain, bias = norm_back(values[part, :], normed_grad, small[0:1, :])
        store_for(packed, out.astype(LOW), b)
        sums[0:1, :] += gain
        sums[1:2, :] += bias
        row = pl.ds(codes[partner(0)], 1)
        table[row, :] += frame_valid(lengths, BLOCKS, 0) * jnp.sum(out, axis=0, keepdims=True)


def collect_body(blocks, out):
    rows = blocks.shape[1]
    for b in range(BLOCKS):
        out[b * rows : (b + 1) * rows, :] = blocks[partner(b)]


def finish_back_body(lengths, grad, blocks, out):
    step = out.shape[-1] // BLOCKS
    for b in range(BLOCKS):
        values = frame_valid(lengths, BLOCKS, b) * (grad[b] + blocks[partner(b)].astype(WIDE))
        for i in range(BLOCKS):
            place = feature_block(partner(ORDER[i]), step)
            out[partner(b), :, place] = values[:, i * step : (i + 1) * step]


def matmul(left, right):
    return lax.dot_general(left, right, (((1,), (0,)), ((), ())), preferred_element_type=WIDE)


def matmul_t(left, right):
    return lax.dot_general(left, right, (((1,), (1,)), ((), ())), preferred_element_type=WIDE)


def matmul_tn(left, right):
    return lax.dot_general(left, right, (((0,), (0,)), ((), ())), preferred_element_type=WIDE)


def head_mask(width, head):
    lane = lax.broadcasted_iota(jnp.int32, (1, width), 1)
    return (lane // HEAD_DIM) == head


def pick(values, mask):
    return jnp.where(mask, values, jnp.zeros_like(values))


def attention_rows(projected, allowed, totals, first):
    width = projected.shape[1] // 3
    queries = projected[:, :width] * jnp.asarray(SCORE_SCALE, LOW)
    keyset = projected[:, width : 2 * width]
    values = projected[:, 2 * width :]
    lane = lax.broadcasted_iota(jnp.int32, (1, 128), 1)
    output = jnp.zeros((projected.shape[0], width), WIDE)
    for head in range(width // HEAD_DIM):
        mask = head_mask(width, head)
        scores = matmul_t(pick(queries, mask), keyset)
        if allowed is not None:
            scores = jnp.where(allowed, scores, MASKED_SCORE)
        row_max = jnp.max(scores, axis=-1, keepdims=True)
        raised = jnp.exp(scores - row_max)
        total = jnp.sum(raised, axis=-1, keepdims=True)
        shares = (raised * (1.0 / total)).astype(LOW)
        output = output + matmul(shares, pick(values, mask))
        totals = jnp.where(lane == first + head, row_max + jnp.log(total), totals)
    return output.astype(LOW), totals


def attention_rows_back(projected, totals, first, output_grad, allowed):
    width = projected.shape[1] // 3
    queries = projected[:, :width] * jnp.asarray(SCORE_SCALE, LOW)
    keyset = projected[:, width : 2 * width]
    values = projected[:, 2 * width :]
    scaled_keys = keyset * jnp.asarray(SCORE_SCALE, LOW)
    shape = (projected.shape[0], width)
    query_grad, key_grad, value_grad = (jnp.zeros(shape, WIDE) for _ in range(3))
    for head in range(width // HEAD_DIM):
        mask = head_mask(width, head)
        own_queries = pick(queries, mask)
        own_grad = pick(output_grad, mask)
        scores = matmul_t(own_queries, keyset)
        if allowed is not None:
            scores = jnp.where(allowed, scores, MASKED_SCORE)
        shares = jnp.exp(scores - totals[:, first + head : first + head + 1])
        value_grad = value_grad + matmul_tn(shares.astype(LOW), own_grad)
        share_grad = matmul_t(own_grad, values)
        score_grad = shares * (share_grad - jnp.sum(share_grad * shares, axis=-1, keepdims=True))
        score_grad = score_grad.astype(LOW)
        query_grad = query_grad + matmul(score_grad, pick(scaled_keys, mask))
        key_grad = key_grad + matmul_tn(score_grad, own_queries)
    return jnp.concatenate(
        [query_grad.astype(LOW), key_grad.astype(LOW), value_grad.astype(LOW)], axis=1
    )


def enter_rows(rows, parts, columns):
    depth = parts[0].shape[0]
    total = matmul(rows[:, :depth], parts[0][:, columns])
    for i, part in enumerate(parts[1:], 1):
        total = total + matmul(rows[:, i * depth : (i + 1) * depth], part[:, columns])
    return total


def leave_rows(sides, columns, store):
    depth = sides[0][1][0].shape[0]
    for i in range(len(sides[0][1])):
        total = matmul_t(sides[0][0], sides[0][1][i][:, columns])
        for values, parts in sides[1:]:
            total = total + matmul_t(values, parts[i][:, columns])
        store(slice(i * depth, (i + 1) * depth), total.astype(LOW))


def side_columns(side, width):
    return slice(side * width, (side + 1) * width)


def space_forward_body(count, rows, *refs):
    sides = [[ref] for ref in refs[:count]]
    projected_out, output_out, totals_out, part_out = refs[count:]
    width = output_out.shape[1] // count
    totals = jnp.zeros(totals_out.shape, WIDE)
    leaving = []
    for side, parts in enumerate(sides):
        projected = enter_rows(rows, parts, slice(0, 3 * width)).astype(LOW)
        projected_out[:, side_columns(side, 3 * width)] = projected
        output, totals = attention_rows(projected, None, totals, side * (width // HEAD_DIM))
        output_out[:, side_columns(side, width)] = output
        leaving.append((output, parts))
    totals_out[...] = totals

    def store(place, values):
        part_out[:, place] = values

    leave_rows(leaving, slice(3 * width, 4 * width), store)


def space_back_body(count, rows, *refs):
    sides = [[ref] for ref in refs[:count]]
    projected, totals, grads_out, part_out = refs[count:]
    width = projected.shape[1] // (3 * count)
    leaving = []
    for side, parts in enumerate(sides):
        output_grad = enter_rows(rows, parts, slice(3 * width, 4 * width)).astype(LOW)
        first, columns = side * (width // HEAD_DIM), side_columns(side, 3 * width)
        grads = attention_rows_back(projected[:, columns], totals[...], first, output_grad, None)
        grads_out[:, columns] = grads
        leaving.append((grads, parts))

    def store(place, values):
        part_out[:, place] = values

    leave_rows(leaving, slice(0, 3 * width), store)


def time_allowed(lengths, clip, frames_local, positions):
    clips = lengths.shape[0]
    count = ROUND * frames_local * positions
    head_at, frame_at = lax.axis_index("head"), partner(0) // clips

    def split(shape, axis):
        row = lax.broadcasted_iota(jnp.int32, shape, axis)
        group = row // (frames_local * positions)
        local = (row // positions) % frames_local
        return (group ^ head_at) * frames_local + (local ^ frame_at), row % positions

    query_frame, query_pos = split((count, 1), 0)
    key_frame, key_pos = split((1, count), 1)
    length = lengths[(partner(0) % clips) ^ clip]
    return (query_pos == key_pos) & (query_frame >= key_frame) & (key_frame < length)


PART = 16


def time_groups(ref):
    return [(c, p) for c in range(ref.shape[1]) for p in range(0, ref.shape[2], PART)]


def join_rows(refs, group):
    c, p = group
    return jnp.concatenate(
        [ref[:, c, p : p + PART, :].reshape(ref.shape[0] * PART, ref.shape[3]) for ref in refs], axis=0
    )


def split_rows(refs, group, values, place=slice(None)):
    c, p = group
    rows = values.shape[0] // len(refs)
    for i, ref in enumerate(refs):
        part = values[i * rows : (i + 1) * rows].reshape(ref.shape[0], PART, values.shape[1])
        ref[:, c, p : p + PART, place] = part


def time_forward_body(lengths, *refs):
    sides, refs = refs[:2], refs[2:]
    rows, projected_out, output_out, totals_out, part_out = (refs[i : i + 4] for i in range(0, 20, 4))
    frames_local, width = rows[0].shape[0], output_out[0].shape[3]
    side_width = width // len(sides)
    for group in time_groups(rows[0]):
        joined = join_rows(rows, group)
        allowed = time_allowed(lengths, group[0], frames_local, PART)
        totals = jnp.zeros((joined.shape[0], 128), WIDE)
        leaving = []
        for side, weights in enumerate(sides):
            projected = matmul(joined, weights[:, : 3 * side_width]).astype(LOW)
            split_rows(projected_out, group, projected, side_columns(side, 3 * side_width))
            output, totals = attention_rows(projected, allowed, totals, side * (side_width // HEAD_DIM))
            split_rows(output_out, group, output, side_columns(side, side_width))
            leaving.append((output, [weights]))
        split_rows(totals_out, group, totals)
        leave_rows(
            leaving,
            slice(3 * side_width, 4 * side_width),
            lambda place, values, group=group: split_rows(part_out, group, values, place),
        )


def time_back_body(lengths, *refs):
    sides, refs = refs[:2], refs[2:]
    rows, projected, totals, grads_out, part_out = (refs[i : i + 4] for i in range(0, 20, 4))
    frames_local, width = rows[0].shape[0], projected[0].shape[3] // 3
    side_width = width // len(sides)
    for group in time_groups(rows[0]):
        allowed = time_allowed(lengths, group[0], frames_local, PART)
        joined = join_rows(rows, group)
        kept, sums = join_rows(projected, group), join_rows(totals, group)
        leaving = []
        for side, weights in enumerate(sides):
            output_grad = matmul(joined, weights[:, 3 * side_width :]).astype(LOW)
            first, columns = side * (side_width // HEAD_DIM), side_columns(side, 3 * side_width)
            grads = attention_rows_back(kept[:, columns], sums, first, output_grad, allowed)
            split_rows(grads_out, group, grads, columns)
            leaving.append((grads, [weights]))
        leave_rows(
            leaving,
            slice(0, 3 * side_width),
            lambda place, values, group=group: split_rows(part_out, group, values, place),
        )


def space_forward(rows, weights):
    count, width = rows.shape
    sides, inner = len(weights), weights[0].shape[1] // 4
    outs = [
        kept_of((count, 3 * inner * sides), LOW),
        shape_of((count, inner * sides), LOW),
        kept_of((count, 128), WIDE),
        shape_of((count, width), LOW),
    ]
    body = functools.partial(space_forward_body, sides)
    return run(body, outs, (rows, *weights), [ONE_VMEM] * (1 + sides))


def space_back(rows, weights, projected, totals):
    count, width = rows.shape
    sides = len(weights)
    outs = [shape_of(projected.shape, LOW), shape_of((count, width), LOW)]
    args = (rows, *weights, projected, totals)
    body = functools.partial(space_back_body, sides)
    return run(body, outs, args, [ONE_VMEM] * len(args), stored=(sides + 1, sides + 2))


def time_call(body, lengths, weights, groups, out_widths):
    args, outs = [lengths, *weights], []
    for group in groups:
        args += group
    for features, dtype in out_widths:
        outs += [shape_of((*groups[0][0].shape[:3], features), dtype)] * ROUND
    results = run(body, outs, args, [ONE_SMEM] + [ONE_VMEM] * (len(args) - 1), vmem=16 * MIB)
    return [results[i : i + ROUND] for i in range(0, len(results), ROUND)]


def hidden_body(normed, grad, *refs):
    enters, leaves, acts, pres = (refs[0], refs[2]), (refs[1], refs[3]), refs[4:6], refs[6:8]
    in_part, out_part = refs[8:]
    hidden = acts[0].shape[1]
    tile = 256
    for side in range(2):
        for start in range(0, hidden, tile):
            place = slice(start, start + tile)
            value = matmul(normed[...], enters[side][:, place])
            square = value * value
            curve = jnp.tanh(GELU_COEFF * (value + 0.044715 * square * value))
            half = 0.5 * (1.0 + curve)
            slope = half + 0.5 * value * (1.0 - curve * curve) * (
                GELU_COEFF * (1.0 + 3.0 * 0.044715 * square)
            )
            acts[side][:, place] = (value * half).astype(LOW)
            pres[side][:, place] = (matmul(grad[...], leaves[side][:, place]) * slope).astype(LOW)
    for values, part, weights in ((pres, in_part, enters), (acts, out_part, leaves)):
        total = matmul_t(values[0][...], weights[0][...]) + matmul_t(values[1][...], weights[1][...])
        part[...] = total.astype(LOW)


def hidden_call(normed, grad, weights):
    count, width = normed.shape
    hidden = weights[0].shape[1]
    outs = [shape_of((count, hidden), LOW)] * 4 + [shape_of((count, width), LOW)] * 2
    results = run(hidden_body, outs, (normed, grad, *weights), [ONE_VMEM] * 6)
    return results[0:2], results[2:4], results[4], results[5]


def weight_grad_tile(counts, ranges, refs, start, tile, store):
    at, column = 0, 0
    for count, columns in zip(counts, ranges):
        lefts, rights = refs[at : at + count], refs[at + count : at + 2 * count]
        at += 2 * count
        total = matmul_tn(lefts[0][:, start : start + tile], rights[0][:, columns])
        for left, right in zip(lefts[1:], rights[1:]):
            total = total + matmul_tn(left[:, start : start + tile], right[:, columns])
        store(column, total.astype(LOW))
        column += total.shape[1]


def weight_grad_body(counts, ranges, near_first, *refs):
    out = refs[-1]
    tile = out.shape[0] // 4
    for place, start in enumerate((0, 2, 1, 3) if near_first else range(4)):

        def store(column, values, place=place):
            out[place * tile : (place + 1) * tile, column : column + values.shape[1]] = values

        weight_grad_tile(counts, ranges, refs, start * tile, tile, store)


def weight_grad(pairs, near_first=False, ranges=None, stored=()):
    args, counts = [], []
    for lefts, rights in pairs:
        args += [*lefts, *rights]
        counts.append(len(lefts))
    width = pairs[0][0][0].shape[1]
    ranges = ranges or [slice(0, rights[0].shape[1]) for _, rights in pairs]
    columns = sum(part.stop - part.start for part in ranges)
    body = functools.partial(weight_grad_body, tuple(counts), ranges, near_first)
    return run(body, shape_of((width, columns), LOW), args, [ONE_VMEM] * len(args), stored=stored)


def small_mine_body(gain, bias, table, out):
    step = gain.shape[1]
    out[...] = jnp.zeros_like(out)
    row = 0
    for part in (gain, bias, table):
        values = jnp.concatenate([part[...]] * ROUND, axis=1)
        lane = lax.broadcasted_iota(jnp.int32, values.shape, 1)
        out[0, row : row + part.shape[0], :] = pick(values, lane // step == lax.axis_index("head"))
        row += part.shape[0]


def small_rows_body(*refs):
    pairs, out = refs[:-1], refs[-1]
    step = pairs[0].shape[2]
    for i, pair in enumerate(pairs):
        for half in range(2):
            place = (half * len(pairs) + i) * step
            out[:, place : place + step] = pair[half]


def small_blocks_body(first, second, third, table_a, table_b, *outs):
    step = outs[0].shape[2]
    for half, out in enumerate(outs):
        for i in range(out.shape[0]):
            place = slice((half * out.shape[0] + i) * step, (half * out.shape[0] + i + 1) * step)
            for row, part in enumerate((first, second, third)):
                out[i, row : row + 1, :] = part[0:1, place]
                out[i, row + 3 : row + 4, :] = part[1:2, place]
            out[i, 6:14, :] = table_a[:, place] + table_b[:, place]
            out[i, 14:16, :] = jnp.zeros((2, step), WIDE)


def stack_body(*refs):
    out, row = refs[-1], 0
    for part in refs[:-1]:
        out[row : row + part.shape[0], ...] = part[...]
        row += part.shape[0]


def sum_body(*refs):
    total = refs[0][...]
    for part in refs[1:-1]:
        total = total + part[...]
    refs[-1][...] = total


def add_split_body(first, second, *outs):
    row = 0
    for out in outs:
        part = slice(row, row + out.shape[0])
        out[...] = (first[part].astype(WIDE) + second[part].astype(WIDE)).astype(out.dtype)
        row += out.shape[0]


def shards(
    frames_in,
    action_codes,
    clip_length,
    norm_gain,
    norm_bias,
    action_table,
    spatialin,
    spatialout,
    temporalin,
    temporalout,
    expand,
    shrink,
    out_grad,
):
    frames_local, clips, pos_local, width = frames_in.shape
    local = (frames_local, clips, pos_local, width)
    rel_shape = (BLOCKS, pos_local, width)
    count = BLOCKS * pos_local
    inner = spatialin.shape[2]
    hidden = expand.shape[1]
    codes = action_codes.reshape(BLOCKS)
    scalars = (codes, clip_length)

    packed_shape = shape_of(rel_shape, LOW)
    flat_shape = shape_of((count, width), LOW)
    sums_shape = shape_of((8, width), WIDE)
    frames_flat = frames_in.reshape(rel_shape)

    order = Order()
    send, take, do = order.send, order.take, order.do
    grad_shapes = [shape_of((3, width // BLOCKS, inner), WIDE), shape_of((inner, width // BLOCKS), WIDE)]
    whole_shape = shape_of(rel_shape, WIDE)

    def kernel(body, outs, first, *others, stored=()):
        smem = [ONE_SMEM if a.ndim == 1 else ONE_VMEM for a in (first, *others)]
        return do(lambda *args: run(body, outs, args, smem, stored=stored), first, *others)

    def stacked(*parts):
        shape = (sum(part.shape[0] for part in parts), *parts[0].shape[1:])
        return kernel(stack_body, shape_of(shape, parts[0].dtype), *parts)

    def summed(*parts):
        return kernel(sum_body, shape_of(parts[0].shape, parts[0].dtype), *parts)

    def halves(first, second):
        shape = shape_of((first.shape[0] // 2, *first.shape[1:]), first.dtype)
        keep, left = kernel(add_split_body, [shape, shape], first, second)
        order.last = left
        return keep, left

    def added(first, second):
        return kernel(add_split_body, [shape_of(first.shape, first.dtype)], first, second)[0]

    def attention_rows_of(enter, leave):
        out = shape_of((enter.shape[0], 4 * inner), LOW)
        return kernel(pack_attention_body, out, jnp.transpose(enter, (1, 0, 2)), leave, stored=(0, 1))

    def split_columns(rows, far):
        outs = [shape_of((2 * rows.shape[0], rows.shape[1] // 2), LOW)] * 2
        a, b = kernel(stack_split_body, outs, rows, far)
        order.last = b
        return a, b

    def crossed(first, second):
        out = shape_of((2 * first.shape[0], first.shape[1]), LOW)
        return kernel(stack_cross_body, out, first, second)

    def joined(a, b):
        outs = [shape_of((a[0].shape[0] // 2, 2 * a[0].shape[1]), LOW)] * 2
        keep, left = kernel(add_join_body, outs, *a, *b)
        order.last = left
        return keep, left

    space_rows = attention_rows_of(spatialin, spatialout)
    got = send(space_rows, "space", 4)
    packed = kernel(pack_frames_body, packed_shape, frames_flat, stored=(0,))
    frame_blocks = order.exchange(packed)
    small_shape = (16, width // BLOCKS)
    block = kernel(
        small_mine_body,
        shape_of((1, *small_shape), WIDE),
        norm_gain,
        norm_bias,
        action_table,
        stored=(0, 1, 2),
    )
    got_small = take(send(block, "space", 1))
    pair = stacked(block, got_small)
    got_small = [send(pair, "space", mask) for mask in ORDER[1:4]]
    space_a, space_b = split_columns(space_rows, take(got))
    got_a, got_b = send(space_a, "space", 2), send(space_b, "space", 1)
    time_rows = attention_rows_of(temporalin, temporalout)
    got_small = [take(got) for got in got_small]
    small = kernel(small_rows_body, shape_of((16, width), WIDE), pair, *got_small)
    got_small = send(small, "head", 1)
    space_a = stacked(space_a, take(got_a))
    space_b = stacked(space_b, take(got_b))
    small = summed(small, take(got_small))
    got_small = send(small, "head", 2)
    got_a, got_b = send(space_a, "space", 1), send(space_b, "space", 2)
    hidden_rows = kernel(pack_hidden_body, shape_of((expand.shape[0], 2 * hidden), LOW), expand, shrink)
    small = summed(small, take(got_small))
    frame_blocks = take(frame_blocks)
    normed, start = kernel(
        frame_norm_body, [flat_shape, shape_of((count, width), WIDE)], *scalars, small, frame_blocks
    )
    normed_far = send(normed, "head", 2)
    got_time = send(time_rows, "space", 4)
    got_a, got_b = take(got_a), take(got_b)
    space_a = stacked(space_a, got_a)
    space_b = crossed(space_b, got_b)
    beside_a, beside_b = send(space_a, "head", 1), send(space_b, "head", 1)
    got_hidden = send(hidden_rows, "space", 4)
    normed_far = take(normed_far)
    space_weights = [space_a, space_b, take(beside_a), take(beside_b)]

    far_kept = do(space_forward, normed_far, space_weights)
    order.last = far_kept[3]
    far_part = send(far_kept[3], "head", 2)
    time_a, time_b = split_columns(time_rows, take(got_time))
    got_a, got_b = send(time_a, "space", 2), send(time_b, "space", 1)
    own_kept = do(space_forward, normed, space_weights)
    order.last = own_kept[3]
    time_a = stacked(time_a, take(got_a))
    time_b = stacked(time_b, take(got_b))
    got_a, got_b = send(time_a, "space", 1), send(time_b, "space", 2)
    far_part = take(far_part)
    packed = kernel(spread_body, packed_shape, own_kept[3], far_part)
    spread = order.exchange(packed)
    hidden_a, hidden_b = split_columns(hidden_rows, take(got_hidden))
    frames_rel, grad_low = kernel(
        order_inputs_body, [packed_shape] * 2, clip_length, frames_flat, out_grad.reshape(rel_shape)
    )
    order.last = grad_low
    grad_far = send(grad_low.reshape(count, width), "head", 2)
    hidden_got = send(hidden_a, "space", 2), send(hidden_b, "space", 1)
    time_a = stacked(time_a, take(got_a))
    time_b = crossed(time_b, take(got_b))
    grad_far = take(grad_far)
    spread = take(spread)
    first, normed_two = kernel(
        join_norm_body, [whole_shape, packed_shape], *scalars, small, frames_rel, spread
    )
    order.last = normed_two

    normed_two = normed_two.reshape(local)
    far = send(normed_two, "head", 2)
    near = send(normed_two, "head", 1)
    hidden_a = stacked(hidden_a, take(hidden_got[0]))
    hidden_b = stacked(hidden_b, take(hidden_got[1]))
    hidden_got = send(hidden_a, "space", 1), send(hidden_b, "space", 2)
    near = take(near)
    far = take(far)
    diagonal = send(far, "head", 1)
    normed_two = [normed_two, near, far, take(diagonal)]
    time_projected, time_output, time_totals, time_parts = do(
        lambda first, *others: time_call(
            time_forward_body,
            clip_length,
            [time_a, time_b],
            [[first, *others]],
            [(3 * inner, LOW), (inner, LOW), (128, WIDE), (width, LOW)],
        ),
        *normed_two,
    )
    order.last = time_parts[3]
    hidden_got = [take(got) for got in hidden_got]
    diagonal = send(time_parts[3], "head", 1)
    near = send(time_parts[1], "head", 1)
    far = added(time_parts[2], take(diagonal))
    far = send(far, "head", 2)
    near = take(near)
    hidden_a = stacked(hidden_a, hidden_got[0])
    hidden_b = crossed(hidden_b, hidden_got[1])
    parts = [part.reshape(rel_shape) for part in (time_parts[0], near, take(far))]
    second, normed_three = kernel(add_norm_body, [whole_shape, packed_shape], small, first, *parts)
    order.last = normed_three

    normed_three = normed_three.reshape(count, width)
    grad_low_flat = grad_low.reshape(count, width)
    far = send(normed_three, "head", 2)
    beside_a, beside_b = send(hidden_a, "head", 1), send(hidden_b, "head", 1)
    normed_three = [normed_three, take(far)]
    hidden_weights = [hidden_a, hidden_b, take(beside_a), take(beside_b)]
    grad_third = [grad_low_flat, grad_far]
    far_kept_three = do(hidden_call, normed_three[1], grad_third[1], hidden_weights)
    order.last = far_kept_three[2]
    far_part = send(far_kept_three[2], "head", 2)
    own_kept_three = do(hidden_call, normed_three[0], grad_third[0], hidden_weights)
    hidden_kept = [own_kept_three, far_kept_three]

    def hidden_part(side, leave):
        lefts = grad_third if leave else normed_three
        rights = [kept[0 if leave else 1][side] for kept in hidden_kept]
        return do(lambda *left: weight_grad([(left, rights)], near_first=leave), *lefts)

    beside_a = hidden_part(1, False)
    beside_b = hidden_part(1, True)
    far_part = take(far_part)
    beside_a, beside_b = send(beside_a, "head", 1), send(beside_b, "head", 1)
    parts = [part.reshape(rel_shape) for part in (own_kept_three[2], far_part)]
    total_second, low_second, sums_third = kernel(
        back_third_body, [whole_shape, packed_shape, sums_shape], small, grad_low, second, *parts
    )
    order.last = low_second
    low_second = low_second.reshape(local)
    far = send(low_second, "head", 2)
    near = send(low_second, "head", 1)
    hidden_a = hidden_part(0, False)
    hidden_b = hidden_part(0, True)
    near = take(near)
    far = take(far)
    diagonal = send(far, "head", 1)
    hidden_a, send_a = halves(hidden_a, take(beside_a))
    got_a = send(send_a, "space", 1)
    hidden_b, send_b = halves(hidden_b, take(beside_b))
    got_b = send(send_b, "space", 2)

    grad_two = [low_second, near, far, take(diagonal)]
    time_grads, time_parts = do(
        lambda first, *others: time_call(
            time_back_body,
            clip_length,
            [time_a, time_b],
            [[first, *others], time_projected, time_totals],
            [(3 * inner, LOW), (width, LOW)],
        ),
        *grad_two,
    )
    order.last = time_parts[3]
    diagonal = send(time_parts[3], "head", 1)
    near = send(time_parts[1], "head", 1)
    flat = lambda arrays: [a.reshape(count, a.shape[-1]) for a in arrays]
    far = added(time_parts[2], take(diagonal))
    far = send(far, "head", 2)
    near = take(near)

    def attention_part(side, lefts, grads, backs, outputs):
        step = inner // 2
        return do(
            lambda *left: weight_grad(
                [(left, grads), (backs, outputs)],
                near_first=side % 2 == 1,
                ranges=[side_columns(side, 3 * step), side_columns(side, step)],
            ),
            *lefts,
        )

    time_args = flat(normed_two), flat(time_grads), flat(grad_two), flat(time_output)
    time_a = attention_part(0, *time_args)
    time_b = attention_part(1, *time_args)
    hidden_a, send_a = halves(hidden_a, take(got_a))
    hidden_b, send_b = halves(hidden_b, take(got_b))
    hidden_got = send(send_a, "space", 2), send(send_b, "space", 1)
    parts = [part.reshape(rel_shape) for part in (time_parts[0], near, take(far))]
    total_first, sums_second, table_first, packed = kernel(
        back_second_body,
        [whole_shape, sums_shape, sums_shape, packed_shape],
        *scalars,
        small,
        total_second,
        first,
        *parts,
    )
    order.last = packed
    grad_blocks = order.exchange(packed)
    hidden_keep, hidden_send = joined((hidden_a, take(hidden_got[0])), (hidden_b, take(hidden_got[1])))
    (time_a, send_a), (time_b, send_b) = [jnp.split(part, 2) for part in (time_a, time_b)]
    got_a, got_b = send(send_a, "space", 1), send(send_b, "space", 2)
    got_hidden = send(hidden_send, "space", 4)
    far_out = send(far_kept_three[3], "head", 2)
    parts = [part.reshape(rel_shape) for part in (own_kept_three[3], take(far_out))]
    frames_out = kernel(finish_forward_body, packed_shape, clip_length, second, *parts)

    grad_blocks = take(grad_blocks)
    grad_one = kernel(collect_body, flat_shape, grad_blocks)
    far = send(grad_one, "head", 2)
    own_result = do(space_back, grad_one, space_weights, own_kept[0], own_kept[2])
    order.last = own_result[1]
    got_hidden = take(got_hidden)
    time_a, send_a = halves(time_a, take(got_a))
    time_b, send_b = halves(time_b, take(got_b))
    grad_one = [grad_one, take(far)]
    got_a, got_b = send(send_a, "space", 2), send(send_b, "space", 1)
    far_result = do(space_back, grad_one[1], space_weights, far_kept[0], far_kept[2])
    order.last = far_result[1]
    far_part = send(far_result[1], "head", 2)
    space_args = [normed, normed_far], [own_result[0], far_result[0]], grad_one, [own_kept[1], far_kept[1]]
    beside_a = attention_part(2, *space_args)
    beside_b = attention_part(3, *space_args)
    time_keep, time_send = joined((time_a, take(got_a)), (time_b, take(got_b)))
    got_time = send(time_send, "space", 4)
    space_a = attention_part(0, *space_args)
    space_b = attention_part(1, *space_args)
    far_part = take(far_part)
    beside_a, beside_b = send(beside_a, "head", 1), send(beside_b, "head", 1)
    sums_first, table_second, packed = kernel(
        back_first_body,
        [sums_shape, sums_shape, packed_shape],
        *scalars,
        small,
        start,
        own_result[1],
        far_part,
    )
    order.last = packed
    last = order.exchange(packed)
    half_shape = shape_of((BLOCKS // 2, *small_shape), WIDE)
    sums, small_send = kernel(
        small_blocks_body, [half_shape] * 2, sums_first, sums_second, sums_third, table_first, table_second
    )
    order.last = small_send
    got_small = send(small_send, "space", 1)
    space_a, send_a = halves(space_a, take(beside_a))
    space_b, send_b = halves(space_b, take(beside_b))
    sums, small_send = halves(sums, take(got_small))
    got_a, got_b = send(send_a, "space", 1), send(send_b, "space", 2)
    got_small = send(small_send, "space", 2)
    hidden_grads = kernel(
        unpack_hidden_body,
        [shape_of((width // BLOCKS, hidden), WIDE), shape_of((hidden, width // BLOCKS), WIDE)],
        hidden_keep,
        got_hidden,
    )
    sums, small_send = halves(sums, take(got_small))
    got_small = send(small_send, "space", 4)
    space_a, send_a = halves(space_a, take(got_a))
    space_b, send_b = halves(space_b, take(got_b))
    got_a, got_b = send(send_a, "space", 2), send(send_b, "space", 1)
    space_keep, space_send = joined((space_a, take(got_a)), (space_b, take(got_b)))
    sums = summed(sums, take(got_small))
    got_small = send(sums, "head", 1)
    got = send(space_send, "space", 4)
    last = take(last)
    frames_grad = kernel(finish_back_body, whole_shape, clip_length, total_first, last)
    sums = summed(sums, take(got_small))
    got_small = send(sums, "head", 2)
    time_grads = kernel(unpack_attention_body, grad_shapes, time_keep, take(got_time))
    sums = summed(sums, take(got_small))[0]
    step = sums.shape[1] // ROUND
    sums = lax.dynamic_slice(sums, (0, lax.axis_index("head") * step), (sums.shape[0], step))
    space_grads = kernel(unpack_attention_body, grad_shapes, space_keep, take(got))
    return (
        frames_out.reshape(local),
        frames_grad.reshape(local),
        sums[0:3],
        sums[3:6],
        sums[6:14],
        jnp.transpose(space_grads[0], (1, 0, 2)),
        space_grads[1],
        jnp.transpose(time_grads[0], (1, 0, 2)),
        time_grads[1],
        *hidden_grads,
    )


def solution(mesh):
    placed = (
        P("head", None, "space", None),
        P("head", None),
        P(),
        P(None, ("space", "head")),
        P(None, ("space", "head")),
        P(None, ("space", "head")),
        P("space", None, "head"),
        P("head", "space"),
        P("space", None, "head"),
        P("head", "space"),
        P("space", "head"),
        P("head", "space"),
        P("head", None, "space", None),
    )
    eight = mesh.shape["space"] == BLOCKS and mesh.shape["head"] == ROUND
    return jax.shard_map(
        shards if eight else general_shards,
        mesh=mesh,
        in_specs=placed,
        out_specs=(
            P("head", None, "space", None),
            P("head", None, "space", None),
            P(None, ("space", "head")),
            P(None, ("space", "head")),
            P(None, ("space", "head")),
            P("space", None, "head"),
            P("head", "space"),
            P("space", None, "head"),
            P("head", "space"),
            P("space", "head"),
            P("head", "space"),
        ),
        check_vma=False,
    )
```

```python
import functools

import jax
import jax.numpy as jnp
from jax import lax
from jax.experimental import pallas as pl
from jax.experimental.pallas import tpu as pltpu
from jax.sharding import PartitionSpec as P

HEAD_DIM = 64


EPSILON = 1e-05
SCORE_SCALE = 0.125
MASKED_SCORE = -1e30
PRECISE = lax.Precision.HIGHEST
GELU_COEFF = 0.7978845608028654


def layer_norm(values, gain_row, bias_row):
    row_mean = jnp.mean(values, axis=-1, keepdims=True)
    centred = values - row_mean
    row_var = jnp.mean(centred * centred, axis=-1, keepdims=True)
    return centred * lax.rsqrt(row_var + EPSILON) * gain_row + bias_row


def gelu_tanh(inputs):
    return (
        0.5 * inputs * (1.0 + jnp.tanh(GELU_COEFF * (inputs + 0.044715 * inputs * inputs * inputs)))
    )


def gather_weights(small, large):
    small_full = (
        lax.all_gather(small[0], ("space", "head"), axis=1, tiled=True),
        lax.all_gather(small[1], ("space", "head"), axis=1, tiled=True),
        lax.all_gather(small[2], ("space", "head"), axis=1, tiled=True),
    )
    large_full = (
        lax.all_gather(large[0], "space", axis=0, tiled=True),
        lax.all_gather(large[1], "space", axis=1, tiled=True),
        lax.all_gather(large[2], "space", axis=0, tiled=True),
        lax.all_gather(large[3], "space", axis=1, tiled=True),
        lax.all_gather(large[4], "space", axis=0, tiled=True),
        lax.all_gather(large[5], "space", axis=1, tiled=True),
    )
    return (small_full, large_full)


def norm_step(inputs, gain_row, bias_row):
    normed, pullback = jax.vjp(layer_norm, inputs, gain_row, bias_row)
    whole = lax.all_gather(normed.astype(jnp.bfloat16), "head", axis=0, tiled=True)
    return (whole, pullback)


def cot_whole(grad_rows):
    return lax.all_gather(grad_rows.astype(jnp.bfloat16), "head", axis=0, tiled=True)


def input_total(partial_value):
    return lax.psum_scatter(
        partial_value.astype(jnp.bfloat16), "head", scatter_dimension=0, tiled=True
    ).astype(jnp.float32)


def heads_total(left, weight):
    return lax.psum_scatter(
        jnp.einsum("fcpe,ed->fcpd", left, weight, preferred_element_type=jnp.float32).astype(
            jnp.bfloat16
        ),
        "head",
        scatter_dimension=0,
        tiled=True,
    ).astype(jnp.float32)


def project_in(whole, weight):
    stacked = jnp.einsum(
        "fcpd,dke->kfcpe", whole, weight, preferred_element_type=jnp.float32
    ).astype(jnp.bfloat16)
    return (stacked[0], stacked[1], stacked[2])


def raw_scores(queries, keyset, form, allowed):
    key_form = form.replace("q", "k")
    scores = (
        jnp.einsum(
            form + "," + key_form + "->bhqk", queries, keyset, preferred_element_type=jnp.float32
        )
        * SCORE_SCALE
    )
    if allowed is not None:
        scores = jnp.where(allowed, scores, MASKED_SCORE)
    return scores


def attend(queries, keyset, values, form, allowed):
    key_form = form.replace("q", "k")
    scores = raw_scores(queries, keyset, form, allowed)
    row_max = jnp.max(scores, axis=-1, keepdims=True)
    log_total = row_max + jnp.log(jnp.sum(jnp.exp(scores - row_max), axis=-1, keepdims=True))
    shares = jnp.exp(scores - log_total).astype(jnp.bfloat16)
    output = jnp.einsum(
        "bhqk," + key_form + "->" + form, shares, values, preferred_element_type=jnp.float32
    )
    return (output.astype(jnp.bfloat16), log_total)


def attend_back(queries, keyset, values, log_total, output_grad, form, allowed):
    key_form = form.replace("q", "k")
    shares = jnp.exp(raw_scores(queries, keyset, form, allowed) - log_total)
    value_grad = jnp.einsum(
        "bhqk," + form + "->" + key_form,
        shares.astype(jnp.bfloat16),
        output_grad,
        preferred_element_type=jnp.float32,
    )
    share_grad = jnp.einsum(
        form + "," + key_form + "->bhqk", output_grad, values, preferred_element_type=jnp.float32
    )
    score_grad = (
        shares * (share_grad - jnp.sum(share_grad * shares, axis=-1, keepdims=True))
    ).astype(jnp.bfloat16)
    query_grad = (
        jnp.einsum(
            "bhqk," + key_form + "->" + form, score_grad, keyset, preferred_element_type=jnp.float32
        )
        * SCORE_SCALE
    )
    key_grad = (
        jnp.einsum(
            "bhqk," + form + "->" + key_form,
            score_grad,
            queries,
            preferred_element_type=jnp.float32,
        )
        * SCORE_SCALE
    )
    return (
        query_grad.astype(jnp.bfloat16),
        key_grad.astype(jnp.bfloat16),
        value_grad.astype(jnp.bfloat16),
    )


def general_shards(
    frames_in,
    action_codes,
    clip_length,
    norm_gain,
    norm_bias,
    action_table,
    spatialin,
    spatialout,
    temporalin,
    temporalout,
    expand,
    shrink,
    out_grad,
):
    head_count = lax.axis_size("head")
    frames_local, clip_count, pos_local, width = frames_in.shape
    frames_total = frames_local * head_count
    local_width = spatialin.shape[2]
    heads_local = local_width // HEAD_DIM
    frame_index = jnp.arange(frames_total)
    local_index = lax.axis_index("head") * frames_local + jnp.arange(frames_local)
    valid_local = (local_index[:, None] < clip_length[None, :]).astype(jnp.float32)[
        :, :, None, None
    ]
    allowed = (frame_index[None, :, None] >= frame_index[None, None, :]) & (
        frame_index[None, None, :] < clip_length[:, None, None]
    )
    allowed = jnp.broadcast_to(
        allowed[:, None, None], (clip_count, pos_local, 1, frames_total, frames_total)
    )
    allowed = allowed.reshape(clip_count * pos_local, 1, frames_total, frames_total)
    small_full, large_full = gather_weights(
        (norm_gain, norm_bias, action_table),
        (spatialin, spatialout, temporalin, temporalout, expand, shrink),
    )
    gain_full, bias_full, table_full = small_full
    space_in, space_out, time_in, time_out, expand_full, shrink_full = large_full
    code_hot = (action_codes[:, :, None] == jnp.arange(table_full.shape[0])[None, None, :]).astype(
        jnp.float32
    )
    embedded = jnp.einsum("fca,ad->fcd", code_hot, table_full, precision=PRECISE)
    start = valid_local * (frames_in.astype(jnp.float32) + embedded[:, :, None, :])
    whole_one, pull_one = norm_step(start, gain_full[0], bias_full[0])
    space_query, space_keys, space_values = project_in(whole_one, space_in)
    flat_shape = (frames_total * clip_count, pos_local, local_width)
    moved = (
        lax.all_to_all(
            space_query.reshape(flat_shape), "space", split_axis=0, concat_axis=1, tiled=True
        ),
        lax.all_to_all(
            space_keys.reshape(flat_shape), "space", split_axis=0, concat_axis=1, tiled=True
        ),
        lax.all_to_all(
            space_values.reshape(flat_shape), "space", split_axis=0, concat_axis=1, tiled=True
        ),
    )
    block_rows = moved[0].shape[0]
    block_cols = moved[0].shape[1]
    frame_shape = (block_rows, block_cols, heads_local, HEAD_DIM)
    frame_query = moved[0].reshape(frame_shape)
    frame_keys = moved[1].reshape(frame_shape)
    frame_values = moved[2].reshape(frame_shape)
    frame_out, frame_total = attend(frame_query, frame_keys, frame_values, "bqhe", None)
    returned = lax.all_to_all(
        frame_out.reshape(block_rows, block_cols, local_width),
        "space",
        split_axis=1,
        concat_axis=0,
        tiled=True,
    )
    space_attended = returned.reshape(frames_total, clip_count, pos_local, local_width)
    first = start + heads_total(space_attended, space_out)
    whole_two, pull_two = norm_step(first, gain_full[1], bias_full[1])
    time_query, time_keys, time_values = project_in(whole_two, time_in)
    time_shape = (frames_total, clip_count * pos_local, heads_local, HEAD_DIM)
    time_query = time_query.reshape(time_shape)
    time_keys = time_keys.reshape(time_shape)
    time_values = time_values.reshape(time_shape)
    time_out_rows, time_total = attend(time_query, time_keys, time_values, "qbhe", allowed)
    time_attended = time_out_rows.reshape(frames_total, clip_count, pos_local, local_width)
    second = first + heads_total(time_attended, time_out)
    whole_three, pull_three = norm_step(second, gain_full[2], bias_full[2])
    expanded = jnp.einsum(
        "fcpd,dh->fcph", whole_three, expand_full, preferred_element_type=jnp.float32
    )
    activated, gelu_pull = jax.vjp(gelu_tanh, expanded)
    activated_low = activated.astype(jnp.bfloat16)
    third = second + heads_total(activated_low, shrink_full)
    frames_out = (valid_local * third).astype(jnp.bfloat16)
    small_full, large_full = gather_weights(
        (norm_gain, norm_bias, action_table),
        (spatialin, spatialout, temporalin, temporalout, expand, shrink),
    )
    space_in, space_out, time_in, time_out, expand_full, shrink_full = large_full
    grad_third = valid_local * out_grad.astype(jnp.float32)
    cot_three = cot_whole(grad_third)
    shrink_part = jnp.einsum(
        "fcph,fcpd->hd", activated_low, cot_three, preferred_element_type=jnp.float32
    )
    act_grad = jnp.einsum(
        "fcpd,hd->fcph", cot_three, shrink_full, preferred_element_type=jnp.float32
    )
    pre_grad = gelu_pull(act_grad)[0].astype(jnp.bfloat16)
    expand_part = jnp.einsum(
        "fcpd,fcph->dh", whole_three, pre_grad, preferred_element_type=jnp.float32
    )
    normed_grad = input_total(
        jnp.einsum("fcph,dh->fcpd", pre_grad, expand_full, preferred_element_type=jnp.float32)
    )
    input_three, gain_three, bias_three = pull_three(normed_grad)
    grad_second = grad_third + input_three
    cot_two = cot_whole(grad_second)
    time_out_part = jnp.einsum(
        "fcpe,fcpd->ed", time_attended, cot_two, preferred_element_type=jnp.float32
    )
    time_grad = jnp.einsum(
        "fcpd,ed->fcpe", cot_two, time_out, preferred_element_type=jnp.float32
    ).astype(jnp.bfloat16)
    time_grads = attend_back(
        time_query,
        time_keys,
        time_values,
        time_total,
        time_grad.reshape(time_shape),
        "qbhe",
        allowed,
    )
    stacked_grad = jnp.stack(
        [member.reshape(frames_total, clip_count, pos_local, local_width) for member in time_grads]
    )
    time_in_part = jnp.einsum(
        "fcpd,kfcpe->dke", whole_two, stacked_grad, preferred_element_type=jnp.float32
    )
    normed_grad = input_total(
        jnp.einsum("kfcpe,dke->fcpd", stacked_grad, time_in, preferred_element_type=jnp.float32)
    )
    input_two, gain_two, bias_two = pull_two(normed_grad)
    grad_first = grad_second + input_two
    cot_one = cot_whole(grad_first)
    space_out_part = jnp.einsum(
        "fcpe,fcpd->ed", space_attended, cot_one, preferred_element_type=jnp.float32
    )
    space_grad = jnp.einsum(
        "fcpd,ed->fcpe", cot_one, space_out, preferred_element_type=jnp.float32
    ).astype(jnp.bfloat16)
    frame_grad = lax.all_to_all(
        space_grad.reshape(flat_shape), "space", split_axis=0, concat_axis=1, tiled=True
    ).reshape(frame_shape)
    query_grad, keys_grad, values_grad = attend_back(
        frame_query, frame_keys, frame_values, frame_total, frame_grad, "bqhe", None
    )
    block_shape = (block_rows, block_cols, local_width)
    back_grads = (
        lax.all_to_all(
            query_grad.reshape(block_shape), "space", split_axis=1, concat_axis=0, tiled=True
        ),
        lax.all_to_all(
            keys_grad.reshape(block_shape), "space", split_axis=1, concat_axis=0, tiled=True
        ),
        lax.all_to_all(
            values_grad.reshape(block_shape), "space", split_axis=1, concat_axis=0, tiled=True
        ),
    )
    stacked_grad = jnp.stack(
        [member.reshape(frames_total, clip_count, pos_local, local_width) for member in back_grads]
    )
    space_in_part = jnp.einsum(
        "fcpd,kfcpe->dke", whole_one, stacked_grad, preferred_element_type=jnp.float32
    )
    normed_grad = input_total(
        jnp.einsum("kfcpe,dke->fcpd", stacked_grad, space_in, preferred_element_type=jnp.float32)
    )
    input_one, gain_one, bias_one = pull_one(normed_grad)
    grad_start = grad_first + input_one
    frames_grad = valid_local * grad_start
    table_part = jnp.einsum(
        "fca,fcd->ad", code_hot, jnp.sum(frames_grad, axis=2), precision=PRECISE
    )
    gain_grad, bias_grad, table_grad = (
        lax.psum_scatter(
            jnp.stack([gain_one, gain_two, gain_three]),
            ("space", "head"),
            scatter_dimension=1,
            tiled=True,
        ),
        lax.psum_scatter(
            jnp.stack([bias_one, bias_two, bias_three]),
            ("space", "head"),
            scatter_dimension=1,
            tiled=True,
        ),
        lax.psum_scatter(table_part, ("space", "head"), scatter_dimension=1, tiled=True),
    )
    weight_grads = (
        lax.psum_scatter(space_in_part, "space", scatter_dimension=0, tiled=True),
        lax.psum_scatter(space_out_part, "space", scatter_dimension=1, tiled=True),
        lax.psum_scatter(time_in_part, "space", scatter_dimension=0, tiled=True),
        lax.psum_scatter(time_out_part, "space", scatter_dimension=1, tiled=True),
        lax.psum_scatter(expand_part, "space", scatter_dimension=0, tiled=True),
        lax.psum_scatter(shrink_part, "space", scatter_dimension=1, tiled=True),
    )
    return (
        frames_out,
        frames_grad,
        gain_grad,
        bias_grad,
        table_grad,
        weight_grads[0],
        weight_grads[1],
        weight_grads[2],
        weight_grads[3],
        weight_grads[4],
        weight_grads[5],
    )


ORDER = (0, 4, 2, 6, 1, 5, 3, 7)
BLOCKS = len(ORDER)
PLACE = tuple(ORDER.index(mask) for mask in range(BLOCKS))
ROUND = 4
ONE_VMEM = pl.BlockSpec(memory_space=pltpu.VMEM)
ONE_SMEM = pl.BlockSpec(memory_space=pltpu.SMEM)
MIB = 1024 * 1024
LOW = jnp.bfloat16
WIDE = jnp.float32


def swap(value, axis, mask):
    return lax.ppermute(value, axis, [(i, i ^ mask) for i in range(lax.axis_size(axis))])


class Order:
    def __init__(self):
        self.last = None

    def tied(self, value):
        if self.last is None:
            return value
        return lax.optimization_barrier((value, self.last))[0]

    def send(self, value, axis, mask):
        return swap(self.tied(value), axis, mask)

    def exchange(self, packed):
        return lax.all_to_all(self.tied(packed), "space", split_axis=0, concat_axis=0, tiled=True)

    def take(self, value):
        self.last = self.tied(value)
        return self.last

    def do(self, step, first, *others):
        result = step(self.tied(first), *others)
        self.last = jax.tree.leaves(result)[0]
        return result


def run(body, outs, args, specs, vmem=None, stored=()):
    single = not isinstance(outs, (list, tuple))
    name = getattr(body, "func", body).__name__.removesuffix("_body")
    args, specs, scratch, whole = list(args), list(specs), [], body
    if stored:
        for place in stored:
            args[place] = pltpu.with_memory_space_constraint(args[place], pltpu.HBM)
            specs[place] = pl.BlockSpec(memory_space=pltpu.HBM)
            scratch.append(pltpu.VMEM(args[place].shape, args[place].dtype))
        scratch.append(pltpu.SemaphoreType.DMA((len(stored),)))

        def whole(*refs):
            refs, held, sem = list(refs[: -len(scratch)]), refs[-len(scratch) : -1], refs[-1]
            copies = [
                pltpu.make_async_copy(refs[place], held[i], sem.at[i]) for i, place in enumerate(stored)
            ]
            for copy in copies:
                copy.start()
            for i, place in enumerate(stored):
                copies[i].wait()
                refs[place] = held[i]
            body(*refs)

    return pl.pallas_call(
        whole,
        out_shape=outs,
        in_specs=specs,
        out_specs=ONE_VMEM if single else [ONE_VMEM] * len(outs),
        scratch_shapes=scratch,
        cost_estimate=pl.CostEstimate(flops=0, bytes_accessed=1024, transcendentals=0),
        compiler_params=pltpu.CompilerParams(vmem_limit_bytes=vmem or 12 * MIB),
        name=name,
    )(*args)


def kept_of(dims, dtype):
    return pltpu.HBM(tuple(dims), dtype)


def shape_of(dims, dtype):
    return jax.ShapeDtypeStruct(tuple(dims), dtype)


def feature_block(place, step):
    return pl.ds(pl.multiple_of(place * step, step), step)


def partner(mask):
    return lax.axis_index("space") ^ mask


def frame_valid(lengths, frames, mask):
    clips = lengths.shape[0]
    frame = lax.axis_index("head") * (frames // clips) + partner(mask) // clips
    return jnp.where(frame < lengths[partner(mask) % clips], 1.0, 0.0).astype(WIDE)


def normed_parts(values):
    centred = values - jnp.mean(values, axis=-1, keepdims=True)
    scale = lax.rsqrt(jnp.mean(centred * centred, axis=-1, keepdims=True) + EPSILON)
    return centred * scale, scale


def norm_back(values, grad, gain_row):
    unit, scale = normed_parts(values)
    scaled = grad * gain_row
    out = scale * (
        scaled
        - jnp.mean(scaled, axis=-1, keepdims=True)
        - unit * jnp.mean(scaled * unit, axis=-1, keepdims=True)
    )
    return (
        out,
        jnp.sum(grad * unit, axis=0, keepdims=True),
        jnp.sum(grad, axis=0, keepdims=True),
    )


def store_for(ref, rows, mask):
    step = rows.shape[-1] // BLOCKS
    for i in range(BLOCKS):
        j = i ^ PLACE[mask]
        ref[partner(mask), :, i * step : (i + 1) * step] = rows[:, j * step : (j + 1) * step]


def pack_attention_body(enter, leave, out):
    step = leave.shape[0] // 2
    for i in range(2):
        place, column = slice(i * step, (i + 1) * step), 4 * i * step
        for j in range(3):
            out[:, column + j * step : column + (j + 1) * step] = enter[j, :, place]
        out[:, column + 3 * step : column + 4 * step] = jnp.transpose(leave[place, :])


def unpack_attention_body(mine, got, enter, leave):
    step = leave.shape[0] // 2
    for i in range(2):
        columns = side_columns(i, 4 * step)
        total = mine[:, columns].astype(WIDE) + got[:, columns].astype(WIDE)
        place = slice(i * step, (i + 1) * step)
        for j in range(3):
            enter[j, :, place] = total[:, j * step : (j + 1) * step]
        leave[place, :] = jnp.transpose(total[:, 3 * step :])


def pack_hidden_body(enter, leave, out):
    hidden = leave.shape[0]
    out[:, :hidden] = enter[...]
    out[:, hidden:] = jnp.transpose(leave[...])


def unpack_hidden_body(mine, got, enter, leave):
    hidden = leave.shape[0]
    total = mine[...].astype(WIDE) + got[...].astype(WIDE)
    enter[...] = total[:, :hidden]
    leave[...] = jnp.transpose(total[:, hidden:])


def stack_split_body(first, second, *outs):
    rows, column = first.shape[0], 0
    for out in outs:
        place = slice(column, column + out.shape[1])
        out[:rows, :] = first[:, place]
        out[rows:, :] = second[:, place]
        column += out.shape[1]


def stack_cross_body(first, second, out):
    tile = first.shape[0] // 2
    for i, (part, place) in enumerate(((first, 0), (second, 0), (first, 1), (second, 1))):
        out[i * tile : (i + 1) * tile, :] = part[place * tile : (place + 1) * tile, :]


def add_join_body(first_a, second_a, first_b, second_b, *outs):
    row, half = 0, first_a.shape[1]
    for out in outs:
        part = slice(row, row + out.shape[0])
        out[:, :half] = (first_a[part].astype(WIDE) + second_a[part].astype(WIDE)).astype(out.dtype)
        out[:, half:] = (first_b[part].astype(WIDE) + second_b[part].astype(WIDE)).astype(out.dtype)
        row += out.shape[0]


def pack_frames_body(frames, out):
    step = frames.shape[-1] // BLOCKS
    for mask in range(BLOCKS):
        for i in range(BLOCKS):
            source = partner(ORDER[i ^ PLACE[mask]])
            place = slice(i * step, (i + 1) * step)
            out[partner(mask), :, place] = frames[partner(mask), :, feature_block(source, step)]


def order_inputs_body(lengths, frames, grad, frames_out, grad_out):
    step = frames.shape[-1] // BLOCKS

    def one(mask, carry):
        valid = frame_valid(lengths, BLOCKS, mask)
        for i in range(BLOCKS):
            source = feature_block(partner(ORDER[i]), step)
            place = slice(i * step, (i + 1) * step)
            frames_out[mask, :, place] = frames[partner(mask), :, source]
            kept = grad[partner(mask), :, source].astype(WIDE) * valid
            grad_out[mask, :, place] = kept.astype(LOW)
        return carry

    lax.fori_loop(0, BLOCKS, one, 0)


def start_rows(rows, codes, lengths, small, mask):
    embedded = small[pl.ds(6 + codes[partner(mask)], 1), :]
    return frame_valid(lengths, BLOCKS, mask) * (rows.astype(WIDE) + embedded)


def frame_norm_body(codes, lengths, small, blocks, normed, start):
    rows = blocks.shape[1]
    for b in range(BLOCKS):
        values = start_rows(blocks[partner(b)], codes, lengths, small, 0)
        start[b * rows : (b + 1) * rows, :] = values
        unit, _ = normed_parts(values)
        normed[b * rows : (b + 1) * rows, :] = (unit * small[0:1, :] + small[3:4, :]).astype(LOW)


def spread_body(first, second, out):
    rows = out.shape[1]
    for mask in range(BLOCKS):
        part = slice(mask * rows, (mask + 1) * rows)
        total = first[part, :].astype(WIDE) + second[part, :].astype(WIDE)
        store_for(out, total.astype(LOW), mask)


def join_norm_body(codes, lengths, small, frames, blocks, whole, normed):
    for b in range(BLOCKS):
        values = start_rows(frames[b], codes, lengths, small, b) + blocks[partner(b)].astype(WIDE)
        whole[b] = values
        unit, _ = normed_parts(values)
        normed[b] = (unit * small[1:2, :] + small[4:5, :]).astype(LOW)


def add_norm_body(small, before, first, second, third, whole, normed):
    def one(b, carry):
        values = before[b] + (
            first[b].astype(WIDE) + second[b].astype(WIDE) + third[b].astype(WIDE)
        )
        whole[b] = values
        unit, _ = normed_parts(values)
        normed[b] = (unit * small[2:3, :] + small[5:6, :]).astype(LOW)
        return carry

    lax.fori_loop(0, BLOCKS, one, 0)


def finish_forward_body(lengths, before, first, second, out):
    step = out.shape[-1] // BLOCKS

    def one(b, carry):
        values = before[b] + (first[b].astype(WIDE) + second[b].astype(WIDE))
        values = (frame_valid(lengths, BLOCKS, b) * values).astype(LOW)
        for i in range(BLOCKS):
            place = feature_block(partner(ORDER[i]), step)
            out[partner(b), :, place] = values[:, i * step : (i + 1) * step]
        return carry

    lax.fori_loop(0, BLOCKS, one, 0)


def back_third_body(small, grad, values, first, second, total_out, low_out, sums):
    sums[...] = jnp.zeros_like(sums)

    def one(b, carry):
        normed_grad = first[b].astype(WIDE) + second[b].astype(WIDE)
        out, gain, bias = norm_back(values[b], normed_grad, small[2:3, :])
        total = grad[b].astype(WIDE) + out
        total_out[b] = total
        low_out[b] = total.astype(LOW)
        sums[0:1, :] += gain
        sums[1:2, :] += bias
        return carry

    lax.fori_loop(0, BLOCKS, one, 0)


def back_second_body(codes, lengths, small, grad, values, first, second, third, total_out, sums, table, packed):
    sums[...] = jnp.zeros_like(sums)
    table[...] = jnp.zeros_like(table)
    for b in range(BLOCKS):
        normed_grad = first[b].astype(WIDE) + second[b].astype(WIDE) + third[b].astype(WIDE)
        out, gain, bias = norm_back(values[b], normed_grad, small[1:2, :])
        total = grad[b] + out
        total_out[b] = total
        store_for(packed, total.astype(LOW), b)
        sums[0:1, :] += gain
        sums[1:2, :] += bias
        row = pl.ds(codes[partner(b)], 1)
        table[row, :] += frame_valid(lengths, BLOCKS, b) * jnp.sum(total, axis=0, keepdims=True)


def back_first_body(codes, lengths, small, values, first, second, sums, table, packed):
    sums[...] = jnp.zeros_like(sums)
    table[...] = jnp.zeros_like(table)
    rows = packed.shape[1]
    for b in range(BLOCKS):
        part = slice(b * rows, (b + 1) * rows)
        normed_grad = first[part, :].astype(WIDE) + second[part, :].astype(WIDE)
        out, gain, bias = norm_back(values[part, :], normed_grad, small[0:1, :])
        store_for(packed, out.astype(LOW), b)
        sums[0:1, :] += gain
        sums[1:2, :] += bias
        row = pl.ds(codes[partner(0)], 1)
        table[row, :] += frame_valid(lengths, BLOCKS, 0) * jnp.sum(out, axis=0, keepdims=True)


def collect_body(blocks, out):
    rows = blocks.shape[1]
    for b in range(BLOCKS):
        out[b * rows : (b + 1) * rows, :] = blocks[partner(b)]


def finish_back_body(lengths, grad, blocks, out):
    step = out.shape[-1] // BLOCKS
    for b in range(BLOCKS):
        values = frame_valid(lengths, BLOCKS, b) * (grad[b] + blocks[partner(b)].astype(WIDE))
        for i in range(BLOCKS):
            place = feature_block(partner(ORDER[i]), step)
            out[partner(b), :, place] = values[:, i * step : (i + 1) * step]


def matmul(left, right):
    return lax.dot_general(left, right, (((1,), (0,)), ((), ())), preferred_element_type=WIDE)


def matmul_t(left, right):
    return lax.dot_general(left, right, (((1,), (1,)), ((), ())), preferred_element_type=WIDE)


def matmul_tn(left, right):
    return lax.dot_general(left, right, (((0,), (0,)), ((), ())), preferred_element_type=WIDE)


def head_mask(width, head):
    lane = lax.broadcasted_iota(jnp.int32, (1, width), 1)
    return (lane // HEAD_DIM) == head


def pick(values, mask):
    return jnp.where(mask, values, jnp.zeros_like(values))


def attention_rows(projected, allowed, totals, first):
    width = projected.shape[1] // 3
    queries = projected[:, :width] * jnp.asarray(SCORE_SCALE, LOW)
    keyset = projected[:, width : 2 * width]
    values = projected[:, 2 * width :]
    lane = lax.broadcasted_iota(jnp.int32, (1, 128), 1)
    output = jnp.zeros((projected.shape[0], width), WIDE)
    for head in range(width // HEAD_DIM):
        mask = head_mask(width, head)
        scores = matmul_t(pick(queries, mask), keyset)
        if allowed is not None:
            scores = jnp.where(allowed, scores, MASKED_SCORE)
        row_max = jnp.max(scores, axis=-1, keepdims=True)
        raised = jnp.exp(scores - row_max)
        total = jnp.sum(raised, axis=-1, keepdims=True)
        shares = (raised * (1.0 / total)).astype(LOW)
        output = output + matmul(shares, pick(values, mask))
        totals = jnp.where(lane == first + head, row_max + jnp.log(total), totals)
    return output.astype(LOW), totals


def attention_rows_back(projected, totals, first, output_grad, allowed):
    width = projected.shape[1] // 3
    queries = projected[:, :width] * jnp.asarray(SCORE_SCALE, LOW)
    keyset = projected[:, width : 2 * width]
    values = projected[:, 2 * width :]
    scaled_keys = keyset * jnp.asarray(SCORE_SCALE, LOW)
    shape = (projected.shape[0], width)
    query_grad, key_grad, value_grad = (jnp.zeros(shape, WIDE) for _ in range(3))
    for head in range(width // HEAD_DIM):
        mask = head_mask(width, head)
        own_queries = pick(queries, mask)
        own_grad = pick(output_grad, mask)
        scores = matmul_t(own_queries, keyset)
        if allowed is not None:
            scores = jnp.where(allowed, scores, MASKED_SCORE)
        shares = jnp.exp(scores - totals[:, first + head : first + head + 1])
        value_grad = value_grad + matmul_tn(shares.astype(LOW), own_grad)
        share_grad = matmul_t(own_grad, values)
        score_grad = shares * (share_grad - jnp.sum(share_grad * shares, axis=-1, keepdims=True))
        score_grad = score_grad.astype(LOW)
        query_grad = query_grad + matmul(score_grad, pick(scaled_keys, mask))
        key_grad = key_grad + matmul_tn(score_grad, own_queries)
    return jnp.concatenate(
        [query_grad.astype(LOW), key_grad.astype(LOW), value_grad.astype(LOW)], axis=1
    )


def enter_rows(rows, parts, columns):
    depth = parts[0].shape[0]
    total = matmul(rows[:, :depth], parts[0][:, columns])
    for i, part in enumerate(parts[1:], 1):
        total = total + matmul(rows[:, i * depth : (i + 1) * depth], part[:, columns])
    return total


def leave_rows(sides, columns, store):
    depth = sides[0][1][0].shape[0]
    for i in range(len(sides[0][1])):
        total = matmul_t(sides[0][0], sides[0][1][i][:, columns])
        for values, parts in sides[1:]:
            total = total + matmul_t(values, parts[i][:, columns])
        store(slice(i * depth, (i + 1) * depth), total.astype(LOW))


def side_columns(side, width):
    return slice(side * width, (side + 1) * width)


def space_forward_body(count, rows, *refs):
    sides = [[ref] for ref in refs[:count]]
    projected_out, output_out, totals_out, part_out = refs[count:]
    width = output_out.shape[1] // count
    totals = jnp.zeros(totals_out.shape, WIDE)
    leaving = []
    for side, parts in enumerate(sides):
        projected = enter_rows(rows, parts, slice(0, 3 * width)).astype(LOW)
        projected_out[:, side_columns(side, 3 * width)] = projected
        output, totals = attention_rows(projected, None, totals, side * (width // HEAD_DIM))
        output_out[:, side_columns(side, width)] = output
        leaving.append((output, parts))
    totals_out[...] = totals

    def store(place, values):
        part_out[:, place] = values

    leave_rows(leaving, slice(3 * width, 4 * width), store)


def space_back_body(count, rows, *refs):
    sides = [[ref] for ref in refs[:count]]
    projected, totals, grads_out, part_out = refs[count:]
    width = projected.shape[1] // (3 * count)
    leaving = []
    for side, parts in enumerate(sides):
        output_grad = enter_rows(rows, parts, slice(3 * width, 4 * width)).astype(LOW)
        first, columns = side * (width // HEAD_DIM), side_columns(side, 3 * width)
        grads = attention_rows_back(projected[:, columns], totals[...], first, output_grad, None)
        grads_out[:, columns] = grads
        leaving.append((grads, parts))

    def store(place, values):
        part_out[:, place] = values

    leave_rows(leaving, slice(0, 3 * width), store)


def time_allowed(lengths, clip, frames_local, positions):
    clips = lengths.shape[0]
    count = ROUND * frames_local * positions
    head_at, frame_at = lax.axis_index("head"), partner(0) // clips

    def split(shape, axis):
        row = lax.broadcasted_iota(jnp.int32, shape, axis)
        group = row // (frames_local * positions)
        local = (row // positions) % frames_local
        return (group ^ head_at) * frames_local + (local ^ frame_at), row % positions

    query_frame, query_pos = split((count, 1), 0)
    key_frame, key_pos = split((1, count), 1)
    length = lengths[(partner(0) % clips) ^ clip]
    return (query_pos == key_pos) & (query_frame >= key_frame) & (key_frame < length)


PART = 16


def time_groups(ref):
    return [(c, p) for c in range(ref.shape[1]) for p in range(0, ref.shape[2], PART)]


def join_rows(refs, group):
    c, p = group
    return jnp.concatenate(
        [ref[:, c, p : p + PART, :].reshape(ref.shape[0] * PART, ref.shape[3]) for ref in refs], axis=0
    )


def split_rows(refs, group, values, place=slice(None)):
    c, p = group
    rows = values.shape[0] // len(refs)
    for i, ref in enumerate(refs):
        part = values[i * rows : (i + 1) * rows].reshape(ref.shape[0], PART, values.shape[1])
        ref[:, c, p : p + PART, place] = part


def time_forward_body(lengths, *refs):
    sides, refs = refs[:2], refs[2:]
    rows, projected_out, output_out, totals_out, part_out = (refs[i : i + 4] for i in range(0, 20, 4))
    frames_local, width = rows[0].shape[0], output_out[0].shape[3]
    side_width = width // len(sides)
    for group in time_groups(rows[0]):
        joined = join_rows(rows, group)
        allowed = time_allowed(lengths, group[0], frames_local, PART)
        totals = jnp.zeros((joined.shape[0], 128), WIDE)
        leaving = []
        for side, weights in enumerate(sides):
            projected = matmul(joined, weights[:, : 3 * side_width]).astype(LOW)
            split_rows(projected_out, group, projected, side_columns(side, 3 * side_width))
            output, totals = attention_rows(projected, allowed, totals, side * (side_width // HEAD_DIM))
            split_rows(output_out, group, output, side_columns(side, side_width))
            leaving.append((output, [weights]))
        split_rows(totals_out, group, totals)
        leave_rows(
            leaving,
            slice(3 * side_width, 4 * side_width),
            lambda place, values, group=group: split_rows(part_out, group, values, place),
        )


def time_back_body(lengths, *refs):
    sides, refs = refs[:2], refs[2:]
    rows, projected, totals, grads_out, part_out = (refs[i : i + 4] for i in range(0, 20, 4))
    frames_local, width = rows[0].shape[0], projected[0].shape[3] // 3
    side_width = width // len(sides)
    for group in time_groups(rows[0]):
        allowed = time_allowed(lengths, group[0], frames_local, PART)
        joined = join_rows(rows, group)
        kept, sums = join_rows(projected, group), join_rows(totals, group)
        leaving = []
        for side, weights in enumerate(sides):
            output_grad = matmul(joined, weights[:, 3 * side_width :]).astype(LOW)
            first, columns = side * (side_width // HEAD_DIM), side_columns(side, 3 * side_width)
            grads = attention_rows_back(kept[:, columns], sums, first, output_grad, allowed)
            split_rows(grads_out, group, grads, columns)
            leaving.append((grads, [weights]))
        leave_rows(
            leaving,
            slice(0, 3 * side_width),
            lambda place, values, group=group: split_rows(part_out, group, values, place),
        )


def space_forward(rows, weights):
    count, width = rows.shape
    sides, inner = len(weights), weights[0].shape[1] // 4
    outs = [
        kept_of((count, 3 * inner * sides), LOW),
        shape_of((count, inner * sides), LOW),
        kept_of((count, 128), WIDE),
        shape_of((count, width), LOW),
    ]
    body = functools.partial(space_forward_body, sides)
    return run(body, outs, (rows, *weights), [ONE_VMEM] * (1 + sides))


def space_back(rows, weights, projected, totals):
    count, width = rows.shape
    sides = len(weights)
    outs = [shape_of(projected.shape, LOW), shape_of((count, width), LOW)]
    args = (rows, *weights, projected, totals)
    body = functools.partial(space_back_body, sides)
    return run(body, outs, args, [ONE_VMEM] * len(args), stored=(sides + 1, sides + 2))


def time_call(body, lengths, weights, groups, out_widths):
    args, outs = [lengths, *weights], []
    for group in groups:
        args += group
    for features, dtype in out_widths:
        outs += [shape_of((*groups[0][0].shape[:3], features), dtype)] * ROUND
    results = run(body, outs, args, [ONE_SMEM] + [ONE_VMEM] * (len(args) - 1), vmem=16 * MIB)
    return [results[i : i + ROUND] for i in range(0, len(results), ROUND)]


def hidden_body(normed, grad, *refs):
    enters, leaves, acts, pres = (refs[0], refs[2]), (refs[1], refs[3]), refs[4:6], refs[6:8]
    in_part, out_part = refs[8:]
    hidden = acts[0].shape[1]
    tile = 256
    for side in range(2):
        for start in range(0, hidden, tile):
            place = slice(start, start + tile)
            value = matmul(normed[...], enters[side][:, place])
            square = value * value
            curve = jnp.tanh(GELU_COEFF * (value + 0.044715 * square * value))
            half = 0.5 * (1.0 + curve)
            slope = half + 0.5 * value * (1.0 - curve * curve) * (
                GELU_COEFF * (1.0 + 3.0 * 0.044715 * square)
            )
            acts[side][:, place] = (value * half).astype(LOW)
            pres[side][:, place] = (matmul(grad[...], leaves[side][:, place]) * slope).astype(LOW)
    for values, part, weights in ((pres, in_part, enters), (acts, out_part, leaves)):
        total = matmul_t(values[0][...], weights[0][...]) + matmul_t(values[1][...], weights[1][...])
        part[...] = total.astype(LOW)


def hidden_call(normed, grad, weights):
    count, width = normed.shape
    hidden = weights[0].shape[1]
    outs = [shape_of((count, hidden), LOW)] * 4 + [shape_of((count, width), LOW)] * 2
    results = run(hidden_body, outs, (normed, grad, *weights), [ONE_VMEM] * 6)
    return results[0:2], results[2:4], results[4], results[5]


def weight_grad_tile(counts, ranges, refs, start, tile, store):
    at, column = 0, 0
    for count, columns in zip(counts, ranges):
        lefts, rights = refs[at : at + count], refs[at + count : at + 2 * count]
        at += 2 * count
        total = matmul_tn(lefts[0][:, start : start + tile], rights[0][:, columns])
        for left, right in zip(lefts[1:], rights[1:]):
            total = total + matmul_tn(left[:, start : start + tile], right[:, columns])
        store(column, total.astype(LOW))
        column += total.shape[1]


def weight_grad_body(counts, ranges, near_first, *refs):
    out = refs[-1]
    tile = out.shape[0] // 4
    for place, start in enumerate((0, 2, 1, 3) if near_first else range(4)):

        def store(column, values, place=place):
            out[place * tile : (place + 1) * tile, column : column + values.shape[1]] = values

        weight_grad_tile(counts, ranges, refs, start * tile, tile, store)


def weight_grad(pairs, near_first=False, ranges=None, stored=()):
    args, counts = [], []
    for lefts, rights in pairs:
        args += [*lefts, *rights]
        counts.append(len(lefts))
    width = pairs[0][0][0].shape[1]
    ranges = ranges or [slice(0, rights[0].shape[1]) for _, rights in pairs]
    columns = sum(part.stop - part.start for part in ranges)
    body = functools.partial(weight_grad_body, tuple(counts), ranges, near_first)
    return run(body, shape_of((width, columns), LOW), args, [ONE_VMEM] * len(args), stored=stored)


def small_mine_body(gain, bias, table, out):
    step = gain.shape[1]
    out[...] = jnp.zeros_like(out)
    row = 0
    for part in (gain, bias, table):
        values = jnp.concatenate([part[...]] * ROUND, axis=1)
        lane = lax.broadcasted_iota(jnp.int32, values.shape, 1)
        out[0, row : row + part.shape[0], :] = pick(values, lane // step == lax.axis_index("head"))
        row += part.shape[0]


def small_rows_body(*refs):
    pairs, out = refs[:-1], refs[-1]
    step = pairs[0].shape[2]
    for i, pair in enumerate(pairs):
        for half in range(2):
            place = (half * len(pairs) + i) * step
            out[:, place : place + step] = pair[half]


def small_blocks_body(first, second, third, table_a, table_b, *outs):
    step = outs[0].shape[2]
    for half, out in enumerate(outs):
        for i in range(out.shape[0]):
            place = slice((half * out.shape[0] + i) * step, (half * out.shape[0] + i + 1) * step)
            for row, part in enumerate((first, second, third)):
                out[i, row : row + 1, :] = part[0:1, place]
                out[i, row + 3 : row + 4, :] = part[1:2, place]
            out[i, 6:14, :] = table_a[:, place] + table_b[:, place]
            out[i, 14:16, :] = jnp.zeros((2, step), WIDE)


def stack_body(*refs):
    out, row = refs[-1], 0
    for part in refs[:-1]:
        out[row : row + part.shape[0], ...] = part[...]
        row += part.shape[0]


def sum_body(*refs):
    total = refs[0][...]
    for part in refs[1:-1]:
        total = total + part[...]
    refs[-1][...] = total


def add_split_body(first, second, *outs):
    row = 0
    for out in outs:
        part = slice(row, row + out.shape[0])
        out[...] = (first[part].astype(WIDE) + second[part].astype(WIDE)).astype(out.dtype)
        row += out.shape[0]


def shards(
    frames_in,
    action_codes,
    clip_length,
    norm_gain,
    norm_bias,
    action_table,
    spatialin,
    spatialout,
    temporalin,
    temporalout,
    expand,
    shrink,
    out_grad,
):
    frames_local, clips, pos_local, width = frames_in.shape
    local = (frames_local, clips, pos_local, width)
    rel_shape = (BLOCKS, pos_local, width)
    count = BLOCKS * pos_local
    inner = spatialin.shape[2]
    hidden = expand.shape[1]
    codes = action_codes.reshape(BLOCKS)
    scalars = (codes, clip_length)

    packed_shape = shape_of(rel_shape, LOW)
    flat_shape = shape_of((count, width), LOW)
    sums_shape = shape_of((8, width), WIDE)
    frames_flat = frames_in.reshape(rel_shape)

    order = Order()
    send, take, do = order.send, order.take, order.do
    grad_shapes = [shape_of((3, width // BLOCKS, inner), WIDE), shape_of((inner, width // BLOCKS), WIDE)]
    whole_shape = shape_of(rel_shape, WIDE)

    def kernel(body, outs, first, *others, stored=()):
        smem = [ONE_SMEM if a.ndim == 1 else ONE_VMEM for a in (first, *others)]
        return do(lambda *args: run(body, outs, args, smem, stored=stored), first, *others)

    def stacked(*parts):
        shape = (sum(part.shape[0] for part in parts), *parts[0].shape[1:])
        return kernel(stack_body, shape_of(shape, parts[0].dtype), *parts)

    def summed(*parts):
        return kernel(sum_body, shape_of(parts[0].shape, parts[0].dtype), *parts)

    def halves(first, second):
        shape = shape_of((first.shape[0] // 2, *first.shape[1:]), first.dtype)
        keep, left = kernel(add_split_body, [shape, shape], first, second)
        order.last = left
        return keep, left

    def added(first, second):
        return kernel(add_split_body, [shape_of(first.shape, first.dtype)], first, second)[0]

    def attention_rows_of(enter, leave):
        out = shape_of((enter.shape[0], 4 * inner), LOW)
        return kernel(pack_attention_body, out, jnp.transpose(enter, (1, 0, 2)), leave, stored=(0, 1))

    def split_columns(rows, far):
        outs = [shape_of((2 * rows.shape[0], rows.shape[1] // 2), LOW)] * 2
        a, b = kernel(stack_split_body, outs, rows, far)
        order.last = b
        return a, b

    def crossed(first, second):
        out = shape_of((2 * first.shape[0], first.shape[1]), LOW)
        return kernel(stack_cross_body, out, first, second)

    def joined(a, b):
        outs = [shape_of((a[0].shape[0] // 2, 2 * a[0].shape[1]), LOW)] * 2
        keep, left = kernel(add_join_body, outs, *a, *b)
        order.last = left
        return keep, left

    space_rows = attention_rows_of(spatialin, spatialout)
    got = send(space_rows, "space", 4)
    packed = kernel(pack_frames_body, packed_shape, frames_flat, stored=(0,))
    small_shape = (16, width // BLOCKS)
    block = kernel(
        small_mine_body,
        shape_of((1, *small_shape), WIDE),
        norm_gain,
        norm_bias,
        action_table,
        stored=(0, 1, 2),
    )
    got_small = take(send(block, "space", 1))
    pair = stacked(block, got_small)
    got_small = [send(pair, "space", mask) for mask in ORDER[1:4]]
    got = take(got)
    got_small = [take(part) for part in got_small]
    space_a, space_b = split_columns(space_rows, got)
    got_a, got_b = send(space_a, "space", 2), send(space_b, "space", 1)
    frame_blocks = order.exchange(packed)
    small = kernel(small_rows_body, shape_of((16, width), WIDE), pair, *got_small)
    small = summed(small, take(send(small, "head", 1)))
    got_small = send(small, "head", 2)
    time_rows = attention_rows_of(temporalin, temporalout)
    hidden_rows = kernel(pack_hidden_body, shape_of((expand.shape[0], 2 * hidden), LOW), expand, shrink)
    small = summed(small, take(got_small))
    space_b = stacked(space_b, take(got_b))
    space_a = stacked(space_a, take(got_a))
    got_a, got_b = send(space_a, "space", 1), send(space_b, "space", 2)
    frame_blocks = take(frame_blocks)
    normed, start = kernel(
        frame_norm_body, [flat_shape, shape_of((count, width), WIDE)], *scalars, small, frame_blocks
    )
    normed_far = send(normed, "head", 2)
    got_a, got_b = take(got_a), take(got_b)
    got_time = send(time_rows, "space", 4)
    space_a = stacked(space_a, got_a)
    space_b = crossed(space_b, got_b)
    normed_far = take(normed_far)
    beside_a, beside_b = send(space_a, "head", 1), send(space_b, "head", 1)
    space_weights = [space_a, space_b, take(beside_a), take(beside_b)]
    got_hidden = send(hidden_rows, "space", 4)
    far_kept = do(space_forward, normed_far, space_weights)
    order.last = far_kept[3]
    far_part = send(far_kept[3], "head", 2)
    time_a, time_b = split_columns(time_rows, take(got_time))
    got_a, got_b = send(time_a, "space", 2), send(time_b, "space", 1)
    own_kept = do(space_forward, normed, space_weights)
    order.last = own_kept[3]
    time_a = stacked(time_a, take(got_a))
    time_b = stacked(time_b, take(got_b))
    got_a, got_b = send(time_a, "space", 1), send(time_b, "space", 2)
    far_part = take(far_part)
    packed = kernel(spread_body, packed_shape, own_kept[3], far_part)
    spread = order.exchange(packed)
    hidden_a, hidden_b = split_columns(hidden_rows, take(got_hidden))
    frames_rel, grad_low = kernel(
        order_inputs_body, [packed_shape] * 2, clip_length, frames_flat, out_grad.reshape(rel_shape)
    )
    order.last = grad_low
    grad_far = send(grad_low.reshape(count, width), "head", 2)
    hidden_got = send(hidden_a, "space", 2), send(hidden_b, "space", 1)
    grad_far = take(grad_far)
    spread = take(spread)
    first, normed_two = kernel(
        join_norm_body, [whole_shape, packed_shape], *scalars, small, frames_rel, spread
    )
    order.last = normed_two
    normed_two = normed_two.reshape(local)
    far = send(normed_two, "head", 2)
    near = send(normed_two, "head", 1)
    hidden_b = stacked(hidden_b, take(hidden_got[1]))
    hidden_a = stacked(hidden_a, take(hidden_got[0]))
    hidden_got = send(hidden_a, "space", 1), send(hidden_b, "space", 2)
    time_a = stacked(time_a, take(got_a))
    time_b = crossed(time_b, take(got_b))
    far = take(far)
    diagonal = send(far, "head", 1)
    near = take(near)
    normed_two = [normed_two, near, far, take(diagonal)]
    time_projected, time_output, time_totals, time_parts = do(
        lambda first, *others: time_call(
            time_forward_body,
            clip_length,
            [time_a, time_b],
            [[first, *others]],
            [(3 * inner, LOW), (inner, LOW), (128, WIDE), (width, LOW)],
        ),
        *normed_two,
    )
    order.last = time_parts[3]
    diagonal = send(time_parts[3], "head", 1)
    near = send(time_parts[1], "head", 1)
    far = added(time_parts[2], take(diagonal))
    far = send(far, "head", 2)
    hidden_got = [take(got) for got in hidden_got]
    near = take(near)
    hidden_a = stacked(hidden_a, hidden_got[0])
    hidden_b = crossed(hidden_b, hidden_got[1])
    parts = [part.reshape(rel_shape) for part in (time_parts[0], near, take(far))]
    second, normed_three = kernel(add_norm_body, [whole_shape, packed_shape], small, first, *parts)
    order.last = normed_three
    normed_three = normed_three.reshape(count, width)
    grad_low_flat = grad_low.reshape(count, width)
    far = send(normed_three, "head", 2)
    beside_a, beside_b = send(hidden_a, "head", 1), send(hidden_b, "head", 1)
    hidden_weights = [hidden_a, hidden_b, take(beside_a), take(beside_b)]
    normed_three = [normed_three, take(far)]
    grad_third = [grad_low_flat, grad_far]
    far_kept_three = do(hidden_call, normed_three[1], grad_third[1], hidden_weights)
    order.last = far_kept_three[2]
    far_part = send(far_kept_three[2], "head", 2)
    own_kept_three = do(hidden_call, normed_three[0], grad_third[0], hidden_weights)
    hidden_kept = [own_kept_three, far_kept_three]
    def hidden_part(side, leave):
        lefts = grad_third if leave else normed_three
        rights = [kept[0 if leave else 1][side] for kept in hidden_kept]
        return do(lambda *left: weight_grad([(left, rights)], near_first=leave), *lefts)
    beside_a = hidden_part(1, False)
    beside_b = hidden_part(1, True)
    far_part = take(far_part)
    beside_a, beside_b = send(beside_a, "head", 1), send(beside_b, "head", 1)
    parts = [part.reshape(rel_shape) for part in (own_kept_three[2], far_part)]
    total_second, low_second, sums_third = kernel(
        back_third_body, [whole_shape, packed_shape, sums_shape], small, grad_low, second, *parts
    )
    order.last = low_second
    low_second = low_second.reshape(local)
    far = send(low_second, "head", 2)
    near = send(low_second, "head", 1)
    hidden_a = hidden_part(0, False)
    hidden_b = hidden_part(0, True)
    near = take(near)
    far = take(far)
    diagonal = send(far, "head", 1)
    hidden_a, send_a = halves(hidden_a, take(beside_a))
    got_a = send(send_a, "space", 1)
    hidden_b, send_b = halves(hidden_b, take(beside_b))
    got_b = send(send_b, "space", 2)
    grad_two = [low_second, near, far, take(diagonal)]
    time_grads, time_parts = do(
        lambda first, *others: time_call(
            time_back_body,
            clip_length,
            [time_a, time_b],
            [[first, *others], time_projected, time_totals],
            [(3 * inner, LOW), (width, LOW)],
        ),
        *grad_two,
    )
    order.last = time_parts[3]
    diagonal = send(time_parts[3], "head", 1)
    near = send(time_parts[1], "head", 1)
    flat = lambda arrays: [a.reshape(count, a.shape[-1]) for a in arrays]
    far = added(time_parts[2], take(diagonal))
    far = send(far, "head", 2)
    near = take(near)
    def attention_part(side, lefts, grads, backs, outputs):
        step = inner // 2
        return do(
            lambda *left: weight_grad(
                [(left, grads), (backs, outputs)],
                near_first=side % 2 == 1,
                ranges=[side_columns(side, 3 * step), side_columns(side, step)],
            ),
            *lefts,
        )
    time_args = flat(normed_two), flat(time_grads), flat(grad_two), flat(time_output)
    time_a = attention_part(0, *time_args)
    time_b = attention_part(1, *time_args)
    hidden_a, send_a = halves(hidden_a, take(got_a))
    hidden_b, send_b = halves(hidden_b, take(got_b))
    hidden_got = send(send_a, "space", 2), send(send_b, "space", 1)
    parts = [part.reshape(rel_shape) for part in (time_parts[0], near, take(far))]
    total_first, sums_second, table_first, packed = kernel(
        back_second_body,
        [whole_shape, sums_shape, sums_shape, packed_shape],
        *scalars,
        small,
        total_second,
        first,
        *parts,
    )
    order.last = packed
    grad_blocks = order.exchange(packed)
    hidden_keep, hidden_send = joined((hidden_a, take(hidden_got[0])), (hidden_b, take(hidden_got[1])))
    (time_a, send_a), (time_b, send_b) = [jnp.split(part, 2) for part in (time_a, time_b)]
    got_a, got_b = send(send_a, "space", 1), send(send_b, "space", 2)
    got_hidden = send(hidden_send, "space", 4)
    far_out = take(send(far_kept_three[3], "head", 2))
    grad_blocks = take(grad_blocks)
    grad_one = kernel(collect_body, flat_shape, grad_blocks)
    far = send(grad_one, "head", 2)
    own_result = do(space_back, grad_one, space_weights, own_kept[0], own_kept[2])
    order.last = own_result[1]
    got_hidden = take(got_hidden)
    got_a, got_b = take(got_a), take(got_b)
    grad_one = [grad_one, take(far)]
    far_result = do(space_back, grad_one[1], space_weights, far_kept[0], far_kept[2])
    order.last = far_result[1]
    time_a, send_a = halves(time_a, got_a)
    far_part = send(far_result[1], "head", 2)
    time_b, send_b = halves(time_b, got_b)
    got_a, got_b = send(send_a, "space", 2), send(send_b, "space", 1)
    space_args = [normed, normed_far], [own_result[0], far_result[0]], grad_one, [own_kept[1], far_kept[1]]
    beside_a = attention_part(2, *space_args)
    beside_b = attention_part(3, *space_args)
    time_keep, time_send = joined((time_a, take(got_a)), (time_b, take(got_b)))
    got_time = send(time_send, "space", 4)
    space_a = attention_part(0, *space_args)
    space_b = attention_part(1, *space_args)
    far_part = take(far_part)
    beside_a, beside_b = send(beside_a, "head", 1), send(beside_b, "head", 1)
    sums_first, table_second, packed = kernel(
        back_first_body,
        [sums_shape, sums_shape, packed_shape],
        *scalars,
        small,
        start,
        own_result[1],
        far_part,
    )
    order.last = packed
    last = order.exchange(packed)
    half_shape = shape_of((BLOCKS // 2, *small_shape), WIDE)
    sums, small_send = kernel(
        small_blocks_body, [half_shape] * 2, sums_first, sums_second, sums_third, table_first, table_second
    )
    order.last = small_send
    got_small = send(small_send, "space", 1)
    space_a, send_a = halves(space_a, take(beside_a))
    space_b, send_b = halves(space_b, take(beside_b))
    sums, small_send = halves(sums, take(got_small))
    got_small = send(small_send, "space", 2)
    got_a, got_b = send(send_a, "space", 1), send(send_b, "space", 2)
    parts = [part.reshape(rel_shape) for part in (own_kept_three[3], far_out)]
    frames_out = kernel(finish_forward_body, packed_shape, clip_length, second, *parts)
    hidden_grads = kernel(
        unpack_hidden_body,
        [shape_of((width // BLOCKS, hidden), WIDE), shape_of((hidden, width // BLOCKS), WIDE)],
        hidden_keep,
        got_hidden,
    )
    sums, small_send = halves(sums, take(got_small))
    got_small = send(small_send, "space", 4)
    space_a, send_a = halves(space_a, take(got_a))
    space_b, send_b = halves(space_b, take(got_b))
    got_a, got_b = send(send_a, "space", 2), send(send_b, "space", 1)
    space_keep, space_send = joined((space_a, take(got_a)), (space_b, take(got_b)))
    sums = summed(sums, take(got_small))
    got = send(space_send, "space", 4)
    got_small = send(sums, "head", 1)
    last = take(last)
    frames_grad = kernel(finish_back_body, whole_shape, clip_length, total_first, last)
    sums = summed(sums, take(got_small))
    got_small = send(sums, "head", 2)
    sums = summed(sums, take(got_small))[0]
    step = sums.shape[1] // ROUND
    sums = lax.dynamic_slice(sums, (0, lax.axis_index("head") * step), (sums.shape[0], step))
    time_grads = kernel(unpack_attention_body, grad_shapes, time_keep, take(got_time))
    space_grads = kernel(unpack_attention_body, grad_shapes, space_keep, take(got))
    return (
        frames_out.reshape(local),
        frames_grad.reshape(local),
        sums[0:3],
        sums[3:6],
        sums[6:14],
        jnp.transpose(space_grads[0], (1, 0, 2)),
        space_grads[1],
        jnp.transpose(time_grads[0], (1, 0, 2)),
        time_grads[1],
        *hidden_grads,
    )


def solution(mesh):
    placed = (
        P("head", None, "space", None),
        P("head", None),
        P(),
        P(None, ("space", "head")),
        P(None, ("space", "head")),
        P(None, ("space", "head")),
        P("space", None, "head"),
        P("head", "space"),
        P("space", None, "head"),
        P("head", "space"),
        P("space", "head"),
        P("head", "space"),
        P("head", None, "space", None),
    )
    eight = mesh.shape["space"] == BLOCKS and mesh.shape["head"] == ROUND
    return jax.shard_map(
        shards if eight else general_shards,
        mesh=mesh,
        in_specs=placed,
        out_specs=(
            P("head", None, "space", None),
            P("head", None, "space", None),
            P(None, ("space", "head")),
            P(None, ("space", "head")),
            P(None, ("space", "head")),
            P("space", None, "head"),
            P("head", "space"),
            P("space", None, "head"),
            P("head", "space"),
            P("space", "head"),
            P("head", "space"),
        ),
        check_vma=False,
    )
```

```python
import functools

import jax
import jax.numpy as jnp
from jax import lax
from jax.experimental import pallas as pl
from jax.experimental.pallas import tpu as pltpu
from jax.sharding import PartitionSpec as P

HEAD_DIM = 64


EPSILON = 1e-05
SCORE_SCALE = 0.125
MASKED_SCORE = -1e30
PRECISE = lax.Precision.HIGHEST
GELU_COEFF = 0.7978845608028654


def layer_norm(values, gain_row, bias_row):
    row_mean = jnp.mean(values, axis=-1, keepdims=True)
    centred = values - row_mean
    row_var = jnp.mean(centred * centred, axis=-1, keepdims=True)
    return centred * lax.rsqrt(row_var + EPSILON) * gain_row + bias_row


def gelu_tanh(inputs):
    return (
        0.5 * inputs * (1.0 + jnp.tanh(GELU_COEFF * (inputs + 0.044715 * inputs * inputs * inputs)))
    )


def gather_weights(small, large):
    small_full = (
        lax.all_gather(small[0], ("space", "head"), axis=1, tiled=True),
        lax.all_gather(small[1], ("space", "head"), axis=1, tiled=True),
        lax.all_gather(small[2], ("space", "head"), axis=1, tiled=True),
    )
    large_full = (
        lax.all_gather(large[0], "space", axis=0, tiled=True),
        lax.all_gather(large[1], "space", axis=1, tiled=True),
        lax.all_gather(large[2], "space", axis=0, tiled=True),
        lax.all_gather(large[3], "space", axis=1, tiled=True),
        lax.all_gather(large[4], "space", axis=0, tiled=True),
        lax.all_gather(large[5], "space", axis=1, tiled=True),
    )
    return (small_full, large_full)


def norm_step(inputs, gain_row, bias_row):
    normed, pullback = jax.vjp(layer_norm, inputs, gain_row, bias_row)
    whole = lax.all_gather(normed.astype(jnp.bfloat16), "head", axis=0, tiled=True)
    return (whole, pullback)


def cot_whole(grad_rows):
    return lax.all_gather(grad_rows.astype(jnp.bfloat16), "head", axis=0, tiled=True)


def input_total(partial_value):
    return lax.psum_scatter(
        partial_value.astype(jnp.bfloat16), "head", scatter_dimension=0, tiled=True
    ).astype(jnp.float32)


def heads_total(left, weight):
    return lax.psum_scatter(
        jnp.einsum("fcpe,ed->fcpd", left, weight, preferred_element_type=jnp.float32).astype(
            jnp.bfloat16
        ),
        "head",
        scatter_dimension=0,
        tiled=True,
    ).astype(jnp.float32)


def project_in(whole, weight):
    stacked = jnp.einsum(
        "fcpd,dke->kfcpe", whole, weight, preferred_element_type=jnp.float32
    ).astype(jnp.bfloat16)
    return (stacked[0], stacked[1], stacked[2])


def raw_scores(queries, keyset, form, allowed):
    key_form = form.replace("q", "k")
    scores = (
        jnp.einsum(
            form + "," + key_form + "->bhqk", queries, keyset, preferred_element_type=jnp.float32
        )
        * SCORE_SCALE
    )
    if allowed is not None:
        scores = jnp.where(allowed, scores, MASKED_SCORE)
    return scores


def attend(queries, keyset, values, form, allowed):
    key_form = form.replace("q", "k")
    scores = raw_scores(queries, keyset, form, allowed)
    row_max = jnp.max(scores, axis=-1, keepdims=True)
    log_total = row_max + jnp.log(jnp.sum(jnp.exp(scores - row_max), axis=-1, keepdims=True))
    shares = jnp.exp(scores - log_total).astype(jnp.bfloat16)
    output = jnp.einsum(
        "bhqk," + key_form + "->" + form, shares, values, preferred_element_type=jnp.float32
    )
    return (output.astype(jnp.bfloat16), log_total)


def attend_back(queries, keyset, values, log_total, output_grad, form, allowed):
    key_form = form.replace("q", "k")
    shares = jnp.exp(raw_scores(queries, keyset, form, allowed) - log_total)
    value_grad = jnp.einsum(
        "bhqk," + form + "->" + key_form,
        shares.astype(jnp.bfloat16),
        output_grad,
        preferred_element_type=jnp.float32,
    )
    share_grad = jnp.einsum(
        form + "," + key_form + "->bhqk", output_grad, values, preferred_element_type=jnp.float32
    )
    score_grad = (
        shares * (share_grad - jnp.sum(share_grad * shares, axis=-1, keepdims=True))
    ).astype(jnp.bfloat16)
    query_grad = (
        jnp.einsum(
            "bhqk," + key_form + "->" + form, score_grad, keyset, preferred_element_type=jnp.float32
        )
        * SCORE_SCALE
    )
    key_grad = (
        jnp.einsum(
            "bhqk," + form + "->" + key_form,
            score_grad,
            queries,
            preferred_element_type=jnp.float32,
        )
        * SCORE_SCALE
    )
    return (
        query_grad.astype(jnp.bfloat16),
        key_grad.astype(jnp.bfloat16),
        value_grad.astype(jnp.bfloat16),
    )


def general_shards(
    frames_in,
    action_codes,
    clip_length,
    norm_gain,
    norm_bias,
    action_table,
    spatialin,
    spatialout,
    temporalin,
    temporalout,
    expand,
    shrink,
    out_grad,
):
    head_count = lax.axis_size("head")
    frames_local, clip_count, pos_local, width = frames_in.shape
    frames_total = frames_local * head_count
    local_width = spatialin.shape[2]
    heads_local = local_width // HEAD_DIM
    frame_index = jnp.arange(frames_total)
    local_index = lax.axis_index("head") * frames_local + jnp.arange(frames_local)
    valid_local = (local_index[:, None] < clip_length[None, :]).astype(jnp.float32)[
        :, :, None, None
    ]
    allowed = (frame_index[None, :, None] >= frame_index[None, None, :]) & (
        frame_index[None, None, :] < clip_length[:, None, None]
    )
    allowed = jnp.broadcast_to(
        allowed[:, None, None], (clip_count, pos_local, 1, frames_total, frames_total)
    )
    allowed = allowed.reshape(clip_count * pos_local, 1, frames_total, frames_total)
    small_full, large_full = gather_weights(
        (norm_gain, norm_bias, action_table),
        (spatialin, spatialout, temporalin, temporalout, expand, shrink),
    )
    gain_full, bias_full, table_full = small_full
    space_in, space_out, time_in, time_out, expand_full, shrink_full = large_full
    code_hot = (action_codes[:, :, None] == jnp.arange(table_full.shape[0])[None, None, :]).astype(
        jnp.float32
    )
    embedded = jnp.einsum("fca,ad->fcd", code_hot, table_full, precision=PRECISE)
    start = valid_local * (frames_in.astype(jnp.float32) + embedded[:, :, None, :])
    whole_one, pull_one = norm_step(start, gain_full[0], bias_full[0])
    space_query, space_keys, space_values = project_in(whole_one, space_in)
    flat_shape = (frames_total * clip_count, pos_local, local_width)
    moved = (
        lax.all_to_all(
            space_query.reshape(flat_shape), "space", split_axis=0, concat_axis=1, tiled=True
        ),
        lax.all_to_all(
            space_keys.reshape(flat_shape), "space", split_axis=0, concat_axis=1, tiled=True
        ),
        lax.all_to_all(
            space_values.reshape(flat_shape), "space", split_axis=0, concat_axis=1, tiled=True
        ),
    )
    block_rows = moved[0].shape[0]
    block_cols = moved[0].shape[1]
    frame_shape = (block_rows, block_cols, heads_local, HEAD_DIM)
    frame_query = moved[0].reshape(frame_shape)
    frame_keys = moved[1].reshape(frame_shape)
    frame_values = moved[2].reshape(frame_shape)
    frame_out, frame_total = attend(frame_query, frame_keys, frame_values, "bqhe", None)
    returned = lax.all_to_all(
        frame_out.reshape(block_rows, block_cols, local_width),
        "space",
        split_axis=1,
        concat_axis=0,
        tiled=True,
    )
    space_attended = returned.reshape(frames_total, clip_count, pos_local, local_width)
    first = start + heads_total(space_attended, space_out)
    whole_two, pull_two = norm_step(first, gain_full[1], bias_full[1])
    time_query, time_keys, time_values = project_in(whole_two, time_in)
    time_shape = (frames_total, clip_count * pos_local, heads_local, HEAD_DIM)
    time_query = time_query.reshape(time_shape)
    time_keys = time_keys.reshape(time_shape)
    time_values = time_values.reshape(time_shape)
    time_out_rows, time_total = attend(time_query, time_keys, time_values, "qbhe", allowed)
    time_attended = time_out_rows.reshape(frames_total, clip_count, pos_local, local_width)
    second = first + heads_total(time_attended, time_out)
    whole_three, pull_three = norm_step(second, gain_full[2], bias_full[2])
    expanded = jnp.einsum(
        "fcpd,dh->fcph", whole_three, expand_full, preferred_element_type=jnp.float32
    )
    activated, gelu_pull = jax.vjp(gelu_tanh, expanded)
    activated_low = activated.astype(jnp.bfloat16)
    third = second + heads_total(activated_low, shrink_full)
    frames_out = (valid_local * third).astype(jnp.bfloat16)
    small_full, large_full = gather_weights(
        (norm_gain, norm_bias, action_table),
        (spatialin, spatialout, temporalin, temporalout, expand, shrink),
    )
    space_in, space_out, time_in, time_out, expand_full, shrink_full = large_full
    grad_third = valid_local * out_grad.astype(jnp.float32)
    cot_three = cot_whole(grad_third)
    shrink_part = jnp.einsum(
        "fcph,fcpd->hd", activated_low, cot_three, preferred_element_type=jnp.float32
    )
    act_grad = jnp.einsum(
        "fcpd,hd->fcph", cot_three, shrink_full, preferred_element_type=jnp.float32
    )
    pre_grad = gelu_pull(act_grad)[0].astype(jnp.bfloat16)
    expand_part = jnp.einsum(
        "fcpd,fcph->dh", whole_three, pre_grad, preferred_element_type=jnp.float32
    )
    normed_grad = input_total(
        jnp.einsum("fcph,dh->fcpd", pre_grad, expand_full, preferred_element_type=jnp.float32)
    )
    input_three, gain_three, bias_three = pull_three(normed_grad)
    grad_second = grad_third + input_three
    cot_two = cot_whole(grad_second)
    time_out_part = jnp.einsum(
        "fcpe,fcpd->ed", time_attended, cot_two, preferred_element_type=jnp.float32
    )
    time_grad = jnp.einsum(
        "fcpd,ed->fcpe", cot_two, time_out, preferred_element_type=jnp.float32
    ).astype(jnp.bfloat16)
    time_grads = attend_back(
        time_query,
        time_keys,
        time_values,
        time_total,
        time_grad.reshape(time_shape),
        "qbhe",
        allowed,
    )
    stacked_grad = jnp.stack(
        [member.reshape(frames_total, clip_count, pos_local, local_width) for member in time_grads]
    )
    time_in_part = jnp.einsum(
        "fcpd,kfcpe->dke", whole_two, stacked_grad, preferred_element_type=jnp.float32
    )
    normed_grad = input_total(
        jnp.einsum("kfcpe,dke->fcpd", stacked_grad, time_in, preferred_element_type=jnp.float32)
    )
    input_two, gain_two, bias_two = pull_two(normed_grad)
    grad_first = grad_second + input_two
    cot_one = cot_whole(grad_first)
    space_out_part = jnp.einsum(
        "fcpe,fcpd->ed", space_attended, cot_one, preferred_element_type=jnp.float32
    )
    space_grad = jnp.einsum(
        "fcpd,ed->fcpe", cot_one, space_out, preferred_element_type=jnp.float32
    ).astype(jnp.bfloat16)
    frame_grad = lax.all_to_all(
        space_grad.reshape(flat_shape), "space", split_axis=0, concat_axis=1, tiled=True
    ).reshape(frame_shape)
    query_grad, keys_grad, values_grad = attend_back(
        frame_query, frame_keys, frame_values, frame_total, frame_grad, "bqhe", None
    )
    block_shape = (block_rows, block_cols, local_width)
    back_grads = (
        lax.all_to_all(
            query_grad.reshape(block_shape), "space", split_axis=1, concat_axis=0, tiled=True
        ),
        lax.all_to_all(
            keys_grad.reshape(block_shape), "space", split_axis=1, concat_axis=0, tiled=True
        ),
        lax.all_to_all(
            values_grad.reshape(block_shape), "space", split_axis=1, concat_axis=0, tiled=True
        ),
    )
    stacked_grad = jnp.stack(
        [member.reshape(frames_total, clip_count, pos_local, local_width) for member in back_grads]
    )
    space_in_part = jnp.einsum(
        "fcpd,kfcpe->dke", whole_one, stacked_grad, preferred_element_type=jnp.float32
    )
    normed_grad = input_total(
        jnp.einsum("kfcpe,dke->fcpd", stacked_grad, space_in, preferred_element_type=jnp.float32)
    )
    input_one, gain_one, bias_one = pull_one(normed_grad)
    grad_start = grad_first + input_one
    frames_grad = valid_local * grad_start
    table_part = jnp.einsum(
        "fca,fcd->ad", code_hot, jnp.sum(frames_grad, axis=2), precision=PRECISE
    )
    gain_grad, bias_grad, table_grad = (
        lax.psum_scatter(
            jnp.stack([gain_one, gain_two, gain_three]),
            ("space", "head"),
            scatter_dimension=1,
            tiled=True,
        ),
        lax.psum_scatter(
            jnp.stack([bias_one, bias_two, bias_three]),
            ("space", "head"),
            scatter_dimension=1,
            tiled=True,
        ),
        lax.psum_scatter(table_part, ("space", "head"), scatter_dimension=1, tiled=True),
    )
    weight_grads = (
        lax.psum_scatter(space_in_part, "space", scatter_dimension=0, tiled=True),
        lax.psum_scatter(space_out_part, "space", scatter_dimension=1, tiled=True),
        lax.psum_scatter(time_in_part, "space", scatter_dimension=0, tiled=True),
        lax.psum_scatter(time_out_part, "space", scatter_dimension=1, tiled=True),
        lax.psum_scatter(expand_part, "space", scatter_dimension=0, tiled=True),
        lax.psum_scatter(shrink_part, "space", scatter_dimension=1, tiled=True),
    )
    return (
        frames_out,
        frames_grad,
        gain_grad,
        bias_grad,
        table_grad,
        weight_grads[0],
        weight_grads[1],
        weight_grads[2],
        weight_grads[3],
        weight_grads[4],
        weight_grads[5],
    )


ORDER = (0, 4, 2, 6, 1, 5, 3, 7)
BLOCKS = len(ORDER)
PLACE = tuple(ORDER.index(mask) for mask in range(BLOCKS))
ROUND = 4
ONE_VMEM = pl.BlockSpec(memory_space=pltpu.VMEM)
ONE_SMEM = pl.BlockSpec(memory_space=pltpu.SMEM)
MIB = 1024 * 1024
LOW = jnp.bfloat16
WIDE = jnp.float32


def swap(value, axis, mask):
    return lax.ppermute(value, axis, [(i, i ^ mask) for i in range(lax.axis_size(axis))])


class Order:
    def __init__(self):
        self.last = None

    def tied(self, value):
        if self.last is None:
            return value
        return lax.optimization_barrier((value, self.last))[0]

    def send(self, value, axis, mask):
        return swap(self.tied(value), axis, mask)

    def exchange(self, packed):
        return lax.all_to_all(self.tied(packed), "space", split_axis=0, concat_axis=0, tiled=True)

    def take(self, value):
        self.last = self.tied(value)
        return self.last

    def do(self, step, first, *others):
        result = step(self.tied(first), *others)
        self.last = jax.tree.leaves(result)[0]
        return result


def run(body, outs, args, specs, vmem=None, stored=()):
    single = not isinstance(outs, (list, tuple))
    name = getattr(body, "func", body).__name__.removesuffix("_body")
    args, specs, scratch, whole = list(args), list(specs), [], body
    if stored:
        for place in stored:
            args[place] = pltpu.with_memory_space_constraint(args[place], pltpu.HBM)
            specs[place] = pl.BlockSpec(memory_space=pltpu.HBM)
            scratch.append(pltpu.VMEM(args[place].shape, args[place].dtype))
        scratch.append(pltpu.SemaphoreType.DMA((len(stored),)))

        def whole(*refs):
            refs, held, sem = list(refs[: -len(scratch)]), refs[-len(scratch) : -1], refs[-1]
            copies = [
                pltpu.make_async_copy(refs[place], held[i], sem.at[i]) for i, place in enumerate(stored)
            ]
            for copy in copies:
                copy.start()
            for i, place in enumerate(stored):
                copies[i].wait()
                refs[place] = held[i]
            body(*refs)

    return pl.pallas_call(
        whole,
        out_shape=outs,
        in_specs=specs,
        out_specs=ONE_VMEM if single else [ONE_VMEM] * len(outs),
        scratch_shapes=scratch,
        cost_estimate=pl.CostEstimate(flops=0, bytes_accessed=1024, transcendentals=0),
        compiler_params=pltpu.CompilerParams(vmem_limit_bytes=vmem or 12 * MIB),
        name=name,
    )(*args)


def kept_of(dims, dtype):
    return pltpu.HBM(tuple(dims), dtype)


def shape_of(dims, dtype):
    return jax.ShapeDtypeStruct(tuple(dims), dtype)


def feature_block(place, step):
    return pl.ds(pl.multiple_of(place * step, step), step)


def partner(mask):
    return lax.axis_index("space") ^ mask


def frame_valid(lengths, frames, mask):
    clips = lengths.shape[0]
    frame = lax.axis_index("head") * (frames // clips) + partner(mask) // clips
    return jnp.where(frame < lengths[partner(mask) % clips], 1.0, 0.0).astype(WIDE)


def normed_parts(values):
    centred = values - jnp.mean(values, axis=-1, keepdims=True)
    scale = lax.rsqrt(jnp.mean(centred * centred, axis=-1, keepdims=True) + EPSILON)
    return centred * scale, scale


def norm_back(values, grad, gain_row):
    unit, scale = normed_parts(values)
    scaled = grad * gain_row
    out = scale * (
        scaled
        - jnp.mean(scaled, axis=-1, keepdims=True)
        - unit * jnp.mean(scaled * unit, axis=-1, keepdims=True)
    )
    return (
        out,
        jnp.sum(grad * unit, axis=0, keepdims=True),
        jnp.sum(grad, axis=0, keepdims=True),
    )


def store_for(ref, rows, mask):
    step = rows.shape[-1] // BLOCKS
    for i in range(BLOCKS):
        j = i ^ PLACE[mask]
        ref[partner(mask), :, i * step : (i + 1) * step] = rows[:, j * step : (j + 1) * step]


def pack_attention_body(enter, leave, out):
    step = leave.shape[0] // 2
    for i in range(2):
        place, column = slice(i * step, (i + 1) * step), 4 * i * step
        for j in range(3):
            out[:, column + j * step : column + (j + 1) * step] = enter[j, :, place]
        out[:, column + 3 * step : column + 4 * step] = jnp.transpose(leave[place, :])


def unpack_attention_body(mine, got, enter, leave):
    step = leave.shape[0] // 2
    for i in range(2):
        columns = side_columns(i, 4 * step)
        total = mine[:, columns].astype(WIDE) + got[:, columns].astype(WIDE)
        place = slice(i * step, (i + 1) * step)
        for j in range(3):
            enter[j, :, place] = total[:, j * step : (j + 1) * step]
        leave[place, :] = jnp.transpose(total[:, 3 * step :])


def pack_hidden_body(enter, leave, out):
    hidden = leave.shape[0]
    out[:, :hidden] = enter[...]
    out[:, hidden:] = jnp.transpose(leave[...])


def unpack_hidden_body(mine, got, enter, leave):
    hidden = leave.shape[0]
    total = mine[...].astype(WIDE) + got[...].astype(WIDE)
    enter[...] = total[:, :hidden]
    leave[...] = jnp.transpose(total[:, hidden:])


def stack_split_body(first, second, *outs):
    rows, column = first.shape[0], 0
    for out in outs:
        place = slice(column, column + out.shape[1])
        out[:rows, :] = first[:, place]
        out[rows:, :] = second[:, place]
        column += out.shape[1]


def stack_cross_body(first, second, out):
    tile = first.shape[0] // 2
    for i, (part, place) in enumerate(((first, 0), (second, 0), (first, 1), (second, 1))):
        out[i * tile : (i + 1) * tile, :] = part[place * tile : (place + 1) * tile, :]


def add_join_body(first_a, second_a, first_b, second_b, *outs):
    row, half = 0, first_a.shape[1]
    for out in outs:
        part = slice(row, row + out.shape[0])
        out[:, :half] = (first_a[part].astype(WIDE) + second_a[part].astype(WIDE)).astype(out.dtype)
        out[:, half:] = (first_b[part].astype(WIDE) + second_b[part].astype(WIDE)).astype(out.dtype)
        row += out.shape[0]


def pack_frames_body(frames, out):
    step = frames.shape[-1] // BLOCKS
    for mask in range(BLOCKS):
        for i in range(BLOCKS):
            source = partner(ORDER[i ^ PLACE[mask]])
            place = slice(i * step, (i + 1) * step)
            out[partner(mask), :, place] = frames[partner(mask), :, feature_block(source, step)]


def order_inputs_body(lengths, frames, grad, frames_out, grad_out):
    step = frames.shape[-1] // BLOCKS

    def one(mask, carry):
        valid = frame_valid(lengths, BLOCKS, mask)
        for i in range(BLOCKS):
            source = feature_block(partner(ORDER[i]), step)
            place = slice(i * step, (i + 1) * step)
            frames_out[mask, :, place] = frames[partner(mask), :, source]
            kept = grad[partner(mask), :, source].astype(WIDE) * valid
            grad_out[mask, :, place] = kept.astype(LOW)
        return carry

    lax.fori_loop(0, BLOCKS, one, 0)


def start_rows(rows, codes, lengths, small, mask):
    embedded = small[pl.ds(6 + codes[partner(mask)], 1), :]
    return frame_valid(lengths, BLOCKS, mask) * (rows.astype(WIDE) + embedded)


def frame_norm_body(codes, lengths, small, blocks, normed, start):
    rows = blocks.shape[1]
    for b in range(BLOCKS):
        values = start_rows(blocks[partner(b)], codes, lengths, small, 0)
        start[b * rows : (b + 1) * rows, :] = values
        unit, _ = normed_parts(values)
        normed[b * rows : (b + 1) * rows, :] = (unit * small[0:1, :] + small[3:4, :]).astype(LOW)


def spread_body(first, second, out):
    rows = out.shape[1]
    for mask in range(BLOCKS):
        part = slice(mask * rows, (mask + 1) * rows)
        total = first[part, :].astype(WIDE) + second[part, :].astype(WIDE)
        store_for(out, total.astype(LOW), mask)


def join_norm_body(codes, lengths, small, frames, blocks, whole, normed):
    for b in range(BLOCKS):
        values = start_rows(frames[b], codes, lengths, small, b) + blocks[partner(b)].astype(WIDE)
        whole[b] = values
        unit, _ = normed_parts(values)
        normed[b] = (unit * small[1:2, :] + small[4:5, :]).astype(LOW)


def add_norm_body(small, before, first, second, third, whole, normed):
    def one(b, carry):
        values = before[b] + (
            first[b].astype(WIDE) + second[b].astype(WIDE) + third[b].astype(WIDE)
        )
        whole[b] = values
        unit, _ = normed_parts(values)
        normed[b] = (unit * small[2:3, :] + small[5:6, :]).astype(LOW)
        return carry

    lax.fori_loop(0, BLOCKS, one, 0)


def finish_forward_body(lengths, before, first, second, out):
    step = out.shape[-1] // BLOCKS

    def one(b, carry):
        values = before[b] + (first[b].astype(WIDE) + second[b].astype(WIDE))
        values = (frame_valid(lengths, BLOCKS, b) * values).astype(LOW)
        for i in range(BLOCKS):
            place = feature_block(partner(ORDER[i]), step)
            out[partner(b), :, place] = values[:, i * step : (i + 1) * step]
        return carry

    lax.fori_loop(0, BLOCKS, one, 0)


def back_third_body(small, grad, values, first, second, total_out, low_out, sums):
    sums[...] = jnp.zeros_like(sums)

    def one(b, carry):
        normed_grad = first[b].astype(WIDE) + second[b].astype(WIDE)
        out, gain, bias = norm_back(values[b], normed_grad, small[2:3, :])
        total = grad[b].astype(WIDE) + out
        total_out[b] = total
        low_out[b] = total.astype(LOW)
        sums[0:1, :] += gain
        sums[1:2, :] += bias
        return carry

    lax.fori_loop(0, BLOCKS, one, 0)


def back_second_body(codes, lengths, small, grad, values, first, second, third, total_out, sums, table, packed):
    sums[...] = jnp.zeros_like(sums)
    table[...] = jnp.zeros_like(table)
    for b in range(BLOCKS):
        normed_grad = first[b].astype(WIDE) + second[b].astype(WIDE) + third[b].astype(WIDE)
        out, gain, bias = norm_back(values[b], normed_grad, small[1:2, :])
        total = grad[b] + out
        total_out[b] = total
        store_for(packed, total.astype(LOW), b)
        sums[0:1, :] += gain
        sums[1:2, :] += bias
        row = pl.ds(codes[partner(b)], 1)
        table[row, :] += frame_valid(lengths, BLOCKS, b) * jnp.sum(total, axis=0, keepdims=True)


def back_first_body(codes, lengths, small, values, first, second, sums, table, packed):
    sums[...] = jnp.zeros_like(sums)
    table[...] = jnp.zeros_like(table)
    rows = packed.shape[1]
    for b in range(BLOCKS):
        part = slice(b * rows, (b + 1) * rows)
        normed_grad = first[part, :].astype(WIDE) + second[part, :].astype(WIDE)
        out, gain, bias = norm_back(values[part, :], normed_grad, small[0:1, :])
        store_for(packed, out.astype(LOW), b)
        sums[0:1, :] += gain
        sums[1:2, :] += bias
        row = pl.ds(codes[partner(0)], 1)
        table[row, :] += frame_valid(lengths, BLOCKS, 0) * jnp.sum(out, axis=0, keepdims=True)


def collect_body(blocks, out):
    rows = blocks.shape[1]
    for b in range(BLOCKS):
        out[b * rows : (b + 1) * rows, :] = blocks[partner(b)]


def finish_back_body(lengths, grad, blocks, out):
    step = out.shape[-1] // BLOCKS
    for b in range(BLOCKS):
        values = frame_valid(lengths, BLOCKS, b) * (grad[b] + blocks[partner(b)].astype(WIDE))
        for i in range(BLOCKS):
            place = feature_block(partner(ORDER[i]), step)
            out[partner(b), :, place] = values[:, i * step : (i + 1) * step]


def matmul(left, right):
    return lax.dot_general(left, right, (((1,), (0,)), ((), ())), preferred_element_type=WIDE)


def matmul_t(left, right):
    return lax.dot_general(left, right, (((1,), (1,)), ((), ())), preferred_element_type=WIDE)


def matmul_tn(left, right):
    return lax.dot_general(left, right, (((0,), (0,)), ((), ())), preferred_element_type=WIDE)


def head_mask(width, head):
    lane = lax.broadcasted_iota(jnp.int32, (1, width), 1)
    return (lane // HEAD_DIM) == head


def pick(values, mask):
    return jnp.where(mask, values, jnp.zeros_like(values))


def attention_rows(projected, allowed, totals, first):
    width = projected.shape[1] // 3
    queries = projected[:, :width] * jnp.asarray(SCORE_SCALE, LOW)
    keyset = projected[:, width : 2 * width]
    values = projected[:, 2 * width :]
    lane = lax.broadcasted_iota(jnp.int32, (1, 128), 1)
    output = jnp.zeros((projected.shape[0], width), WIDE)
    for head in range(width // HEAD_DIM):
        mask = head_mask(width, head)
        scores = matmul_t(pick(queries, mask), keyset)
        if allowed is not None:
            scores = jnp.where(allowed, scores, MASKED_SCORE)
        row_max = jnp.max(scores, axis=-1, keepdims=True)
        raised = jnp.exp(scores - row_max)
        total = jnp.sum(raised, axis=-1, keepdims=True)
        shares = (raised * (1.0 / total)).astype(LOW)
        output = output + matmul(shares, pick(values, mask))
        totals = jnp.where(lane == first + head, row_max + jnp.log(total), totals)
    return output.astype(LOW), totals


def attention_rows_back(projected, totals, first, output_grad, allowed):
    width = projected.shape[1] // 3
    queries = projected[:, :width] * jnp.asarray(SCORE_SCALE, LOW)
    keyset = projected[:, width : 2 * width]
    values = projected[:, 2 * width :]
    scaled_keys = keyset * jnp.asarray(SCORE_SCALE, LOW)
    shape = (projected.shape[0], width)
    query_grad, key_grad, value_grad = (jnp.zeros(shape, WIDE) for _ in range(3))
    for head in range(width // HEAD_DIM):
        mask = head_mask(width, head)
        own_queries = pick(queries, mask)
        own_grad = pick(output_grad, mask)
        scores = matmul_t(own_queries, keyset)
        if allowed is not None:
            scores = jnp.where(allowed, scores, MASKED_SCORE)
        shares = jnp.exp(scores - totals[:, first + head : first + head + 1])
        value_grad = value_grad + matmul_tn(shares.astype(LOW), own_grad)
        share_grad = matmul_t(own_grad, values)
        score_grad = shares * (share_grad - jnp.sum(share_grad * shares, axis=-1, keepdims=True))
        score_grad = score_grad.astype(LOW)
        query_grad = query_grad + matmul(score_grad, pick(scaled_keys, mask))
        key_grad = key_grad + matmul_tn(score_grad, own_queries)
    return jnp.concatenate(
        [query_grad.astype(LOW), key_grad.astype(LOW), value_grad.astype(LOW)], axis=1
    )


def enter_rows(rows, parts, columns):
    depth = parts[0].shape[0]
    total = matmul(rows[:, :depth], parts[0][:, columns])
    for i, part in enumerate(parts[1:], 1):
        total = total + matmul(rows[:, i * depth : (i + 1) * depth], part[:, columns])
    return total


def leave_rows(sides, columns, store):
    depth = sides[0][1][0].shape[0]
    for i in range(len(sides[0][1])):
        total = matmul_t(sides[0][0], sides[0][1][i][:, columns])
        for values, parts in sides[1:]:
            total = total + matmul_t(values, parts[i][:, columns])
        store(slice(i * depth, (i + 1) * depth), total.astype(LOW))


def side_columns(side, width):
    return slice(side * width, (side + 1) * width)


def space_forward_body(count, rows, *refs):
    sides = [[ref] for ref in refs[:count]]
    projected_out, output_out, totals_out, part_out = refs[count:]
    width = output_out.shape[1] // count
    totals = jnp.zeros(totals_out.shape, WIDE)
    leaving = []
    for side, parts in enumerate(sides):
        projected = enter_rows(rows, parts, slice(0, 3 * width)).astype(LOW)
        projected_out[:, side_columns(side, 3 * width)] = projected
        output, totals = attention_rows(projected, None, totals, side * (width // HEAD_DIM))
        output_out[:, side_columns(side, width)] = output
        leaving.append((output, parts))
    totals_out[...] = totals

    def store(place, values):
        part_out[:, place] = values

    leave_rows(leaving, slice(3 * width, 4 * width), store)


def space_back_body(count, rows, *refs):
    sides = [[ref] for ref in refs[:count]]
    projected, totals, grads_out, part_out = refs[count:]
    width = projected.shape[1] // (3 * count)
    leaving = []
    for side, parts in enumerate(sides):
        output_grad = enter_rows(rows, parts, slice(3 * width, 4 * width)).astype(LOW)
        first, columns = side * (width // HEAD_DIM), side_columns(side, 3 * width)
        grads = attention_rows_back(projected[:, columns], totals[...], first, output_grad, None)
        grads_out[:, columns] = grads
        leaving.append((grads, parts))

    def store(place, values):
        part_out[:, place] = values

    leave_rows(leaving, slice(0, 3 * width), store)


def time_allowed(lengths, clip, frames_local, positions):
    clips = lengths.shape[0]
    count = ROUND * frames_local * positions
    head_at, frame_at = lax.axis_index("head"), partner(0) // clips

    def split(shape, axis):
        row = lax.broadcasted_iota(jnp.int32, shape, axis)
        group = row // (frames_local * positions)
        local = (row // positions) % frames_local
        return (group ^ head_at) * frames_local + (local ^ frame_at), row % positions

    query_frame, query_pos = split((count, 1), 0)
    key_frame, key_pos = split((1, count), 1)
    length = lengths[(partner(0) % clips) ^ clip]
    return (query_pos == key_pos) & (query_frame >= key_frame) & (key_frame < length)


PART = 16


def time_groups(ref):
    return [(c, p) for c in range(ref.shape[1]) for p in range(0, ref.shape[2], PART)]


def join_rows(refs, group):
    c, p = group
    return jnp.concatenate(
        [ref[:, c, p : p + PART, :].reshape(ref.shape[0] * PART, ref.shape[3]) for ref in refs], axis=0
    )


def split_rows(refs, group, values, place=slice(None)):
    c, p = group
    rows = values.shape[0] // len(refs)
    for i, ref in enumerate(refs):
        part = values[i * rows : (i + 1) * rows].reshape(ref.shape[0], PART, values.shape[1])
        ref[:, c, p : p + PART, place] = part


def time_forward_body(lengths, *refs):
    sides, refs = refs[:2], refs[2:]
    rows, projected_out, output_out, totals_out, part_out = (refs[i : i + 4] for i in range(0, 20, 4))
    frames_local, width = rows[0].shape[0], output_out[0].shape[3]
    side_width = width // len(sides)
    for group in time_groups(rows[0]):
        joined = join_rows(rows, group)
        allowed = time_allowed(lengths, group[0], frames_local, PART)
        totals = jnp.zeros((joined.shape[0], 128), WIDE)
        leaving = []
        for side, weights in enumerate(sides):
            projected = matmul(joined, weights[:, : 3 * side_width]).astype(LOW)
            split_rows(projected_out, group, projected, side_columns(side, 3 * side_width))
            output, totals = attention_rows(projected, allowed, totals, side * (side_width // HEAD_DIM))
            split_rows(output_out, group, output, side_columns(side, side_width))
            leaving.append((output, [weights]))
        split_rows(totals_out, group, totals)
        leave_rows(
            leaving,
            slice(3 * side_width, 4 * side_width),
            lambda place, values, group=group: split_rows(part_out, group, values, place),
        )


def time_back_body(lengths, *refs):
    sides, refs = refs[:2], refs[2:]
    rows, projected, totals, grads_out, part_out = (refs[i : i + 4] for i in range(0, 20, 4))
    frames_local, width = rows[0].shape[0], projected[0].shape[3] // 3
    side_width = width // len(sides)
    for group in time_groups(rows[0]):
        allowed = time_allowed(lengths, group[0], frames_local, PART)
        joined = join_rows(rows, group)
        kept, sums = join_rows(projected, group), join_rows(totals, group)
        leaving = []
        for side, weights in enumerate(sides):
            output_grad = matmul(joined, weights[:, 3 * side_width :]).astype(LOW)
            first, columns = side * (side_width // HEAD_DIM), side_columns(side, 3 * side_width)
            grads = attention_rows_back(kept[:, columns], sums, first, output_grad, allowed)
            split_rows(grads_out, group, grads, columns)
            leaving.append((grads, [weights]))
        leave_rows(
            leaving,
            slice(0, 3 * side_width),
            lambda place, values, group=group: split_rows(part_out, group, values, place),
        )


def space_forward(rows, weights):
    count, width = rows.shape
    sides, inner = len(weights), weights[0].shape[1] // 4
    outs = [
        kept_of((count, 3 * inner * sides), LOW),
        shape_of((count, inner * sides), LOW),
        kept_of((count, 128), WIDE),
        shape_of((count, width), LOW),
    ]
    body = functools.partial(space_forward_body, sides)
    return run(body, outs, (rows, *weights), [ONE_VMEM] * (1 + sides))


def space_back(rows, weights, projected, totals):
    count, width = rows.shape
    sides = len(weights)
    outs = [shape_of(projected.shape, LOW), shape_of((count, width), LOW)]
    args = (rows, *weights, projected, totals)
    body = functools.partial(space_back_body, sides)
    return run(body, outs, args, [ONE_VMEM] * len(args), stored=(sides + 1, sides + 2))


def time_call(body, lengths, weights, groups, out_widths):
    args, outs = [lengths, *weights], []
    for group in groups:
        args += group
    for features, dtype in out_widths:
        outs += [shape_of((*groups[0][0].shape[:3], features), dtype)] * ROUND
    results = run(body, outs, args, [ONE_SMEM] + [ONE_VMEM] * (len(args) - 1), vmem=16 * MIB)
    return [results[i : i + ROUND] for i in range(0, len(results), ROUND)]


def hidden_body(normed, grad, *refs):
    enters, leaves, acts, pres = (refs[0], refs[2]), (refs[1], refs[3]), refs[4:6], refs[6:8]
    in_part, out_part = refs[8:]
    hidden = acts[0].shape[1]
    tile = 256
    for side in range(2):
        for start in range(0, hidden, tile):
            place = slice(start, start + tile)
            value = matmul(normed[...], enters[side][:, place])
            square = value * value
            curve = jnp.tanh(GELU_COEFF * (value + 0.044715 * square * value))
            half = 0.5 * (1.0 + curve)
            slope = half + 0.5 * value * (1.0 - curve * curve) * (
                GELU_COEFF * (1.0 + 3.0 * 0.044715 * square)
            )
            acts[side][:, place] = (value * half).astype(LOW)
            pres[side][:, place] = (matmul(grad[...], leaves[side][:, place]) * slope).astype(LOW)
    for values, part, weights in ((pres, in_part, enters), (acts, out_part, leaves)):
        total = matmul_t(values[0][...], weights[0][...]) + matmul_t(values[1][...], weights[1][...])
        part[...] = total.astype(LOW)


def hidden_call(normed, grad, weights):
    count, width = normed.shape
    hidden = weights[0].shape[1]
    outs = [shape_of((count, hidden), LOW)] * 4 + [shape_of((count, width), LOW)] * 2
    results = run(hidden_body, outs, (normed, grad, *weights), [ONE_VMEM] * 6)
    return results[0:2], results[2:4], results[4], results[5]


def weight_grad_tile(counts, ranges, refs, start, tile, store):
    at, column = 0, 0
    for count, columns in zip(counts, ranges):
        lefts, rights = refs[at : at + count], refs[at + count : at + 2 * count]
        at += 2 * count
        total = matmul_tn(lefts[0][:, start : start + tile], rights[0][:, columns])
        for left, right in zip(lefts[1:], rights[1:]):
            total = total + matmul_tn(left[:, start : start + tile], right[:, columns])
        store(column, total.astype(LOW))
        column += total.shape[1]


def weight_grad_body(counts, ranges, near_first, *refs):
    out = refs[-1]
    tile = out.shape[0] // 4
    for place, start in enumerate((0, 2, 1, 3) if near_first else range(4)):

        def store(column, values, place=place):
            out[place * tile : (place + 1) * tile, column : column + values.shape[1]] = values

        weight_grad_tile(counts, ranges, refs, start * tile, tile, store)


def weight_grad(pairs, near_first=False, ranges=None, stored=()):
    args, counts = [], []
    for lefts, rights in pairs:
        args += [*lefts, *rights]
        counts.append(len(lefts))
    width = pairs[0][0][0].shape[1]
    ranges = ranges or [slice(0, rights[0].shape[1]) for _, rights in pairs]
    columns = sum(part.stop - part.start for part in ranges)
    body = functools.partial(weight_grad_body, tuple(counts), ranges, near_first)
    return run(body, shape_of((width, columns), LOW), args, [ONE_VMEM] * len(args), stored=stored)


def small_mine_body(gain, bias, table, out):
    step = gain.shape[1]
    out[...] = jnp.zeros_like(out)
    row = 0
    for part in (gain, bias, table):
        values = jnp.concatenate([part[...]] * ROUND, axis=1)
        lane = lax.broadcasted_iota(jnp.int32, values.shape, 1)
        out[0, row : row + part.shape[0], :] = pick(values, lane // step == lax.axis_index("head"))
        row += part.shape[0]


def small_rows_body(*refs):
    pairs, out = refs[:-1], refs[-1]
    step = pairs[0].shape[2]
    for i, pair in enumerate(pairs):
        for half in range(2):
            place = (half * len(pairs) + i) * step
            out[:, place : place + step] = pair[half]


def small_blocks_body(first, second, third, table_a, table_b, *outs):
    step = outs[0].shape[2]
    for half, out in enumerate(outs):
        for i in range(out.shape[0]):
            place = slice((half * out.shape[0] + i) * step, (half * out.shape[0] + i + 1) * step)
            for row, part in enumerate((first, second, third)):
                out[i, row : row + 1, :] = part[0:1, place]
                out[i, row + 3 : row + 4, :] = part[1:2, place]
            out[i, 6:14, :] = table_a[:, place] + table_b[:, place]
            out[i, 14:16, :] = jnp.zeros((2, step), WIDE)


def stack_body(*refs):
    out, row = refs[-1], 0
    for part in refs[:-1]:
        out[row : row + part.shape[0], ...] = part[...]
        row += part.shape[0]


def sum_body(*refs):
    total = refs[0][...]
    for part in refs[1:-1]:
        total = total + part[...]
    refs[-1][...] = total


def add_split_body(first, second, *outs):
    row = 0
    for out in outs:
        part = slice(row, row + out.shape[0])
        out[...] = (first[part].astype(WIDE) + second[part].astype(WIDE)).astype(out.dtype)
        row += out.shape[0]


def shards(
    frames_in,
    action_codes,
    clip_length,
    norm_gain,
    norm_bias,
    action_table,
    spatialin,
    spatialout,
    temporalin,
    temporalout,
    expand,
    shrink,
    out_grad,
):
    frames_local, clips, pos_local, width = frames_in.shape
    local = (frames_local, clips, pos_local, width)
    rel_shape = (BLOCKS, pos_local, width)
    count = BLOCKS * pos_local
    inner = spatialin.shape[2]
    hidden = expand.shape[1]
    codes = action_codes.reshape(BLOCKS)
    scalars = (codes, clip_length)

    packed_shape = shape_of(rel_shape, LOW)
    flat_shape = shape_of((count, width), LOW)
    sums_shape = shape_of((8, width), WIDE)
    frames_flat = frames_in.reshape(rel_shape)

    order = Order()
    send, take, do = order.send, order.take, order.do
    grad_shapes = [shape_of((3, width // BLOCKS, inner), WIDE), shape_of((inner, width // BLOCKS), WIDE)]
    whole_shape = shape_of(rel_shape, WIDE)

    def kernel(body, outs, first, *others, stored=()):
        smem = [ONE_SMEM if a.ndim == 1 else ONE_VMEM for a in (first, *others)]
        return do(lambda *args: run(body, outs, args, smem, stored=stored), first, *others)

    def stacked(*parts):
        shape = (sum(part.shape[0] for part in parts), *parts[0].shape[1:])
        return kernel(stack_body, shape_of(shape, parts[0].dtype), *parts)

    def summed(*parts):
        return kernel(sum_body, shape_of(parts[0].shape, parts[0].dtype), *parts)

    def halves(first, second):
        shape = shape_of((first.shape[0] // 2, *first.shape[1:]), first.dtype)
        keep, left = kernel(add_split_body, [shape, shape], first, second)
        order.last = left
        return keep, left

    def added(first, second):
        return kernel(add_split_body, [shape_of(first.shape, first.dtype)], first, second)[0]

    def attention_rows_of(enter, leave):
        out = shape_of((enter.shape[0], 4 * inner), LOW)
        return kernel(pack_attention_body, out, jnp.transpose(enter, (1, 0, 2)), leave, stored=(0, 1))

    def split_columns(rows, far):
        outs = [shape_of((2 * rows.shape[0], rows.shape[1] // 2), LOW)] * 2
        a, b = kernel(stack_split_body, outs, rows, far)
        order.last = b
        return a, b

    def crossed(first, second):
        out = shape_of((2 * first.shape[0], first.shape[1]), LOW)
        return kernel(stack_cross_body, out, first, second)

    def joined(a, b):
        outs = [shape_of((a[0].shape[0] // 2, 2 * a[0].shape[1]), LOW)] * 2
        keep, left = kernel(add_join_body, outs, *a, *b)
        order.last = left
        return keep, left

    space_rows = attention_rows_of(spatialin, spatialout)
    got = send(space_rows, "space", 4)
    packed = kernel(pack_frames_body, packed_shape, frames_flat, stored=(0,))
    small_shape = (16, width // BLOCKS)
    block = kernel(
        small_mine_body,
        shape_of((1, *small_shape), WIDE),
        norm_gain,
        norm_bias,
        action_table,
        stored=(0, 1, 2),
    )
    got_small = take(send(block, "space", 1))
    pair = stacked(block, got_small)
    got_small = [send(pair, "space", mask) for mask in ORDER[1:4]]
    got = take(got)
    got_small = [take(part) for part in got_small]
    space_a, space_b = split_columns(space_rows, got)
    got_a, got_b = send(space_a, "space", 2), send(space_b, "space", 1)
    frame_blocks = order.exchange(packed)
    small = kernel(small_rows_body, shape_of((16, width), WIDE), pair, *got_small)
    small = summed(small, take(send(small, "head", 1)))
    got_small = send(small, "head", 2)
    time_rows = attention_rows_of(temporalin, temporalout)
    hidden_rows = kernel(pack_hidden_body, shape_of((expand.shape[0], 2 * hidden), LOW), expand, shrink)
    small = summed(small, take(got_small))
    space_b = stacked(space_b, take(got_b))
    space_a = stacked(space_a, take(got_a))
    got_a, got_b = send(space_a, "space", 1), send(space_b, "space", 2)
    frame_blocks = take(frame_blocks)
    normed, start = kernel(
        frame_norm_body, [flat_shape, shape_of((count, width), WIDE)], *scalars, small, frame_blocks
    )
    normed_far = send(normed, "head", 2)
    got_a, got_b = take(got_a), take(got_b)
    got_time = send(time_rows, "space", 4)
    space_a = stacked(space_a, got_a)
    space_b = crossed(space_b, got_b)
    normed_far = take(normed_far)
    beside_a, beside_b = send(space_a, "head", 1), send(space_b, "head", 1)
    space_weights = [space_a, space_b, take(beside_a), take(beside_b)]
    got_hidden = send(hidden_rows, "space", 4)
    far_kept = do(space_forward, normed_far, space_weights)
    order.last = far_kept[3]
    far_part = send(far_kept[3], "head", 2)
    time_a, time_b = split_columns(time_rows, take(got_time))
    got_a, got_b = send(time_a, "space", 2), send(time_b, "space", 1)
    own_kept = do(space_forward, normed, space_weights)
    order.last = own_kept[3]
    time_a = stacked(time_a, take(got_a))
    time_b = stacked(time_b, take(got_b))
    got_a, got_b = send(time_a, "space", 1), send(time_b, "space", 2)
    far_part = take(far_part)
    packed = kernel(spread_body, packed_shape, own_kept[3], far_part)
    spread = order.exchange(packed)
    hidden_a, hidden_b = split_columns(hidden_rows, take(got_hidden))
    frames_rel, grad_low = kernel(
        order_inputs_body, [packed_shape] * 2, clip_length, frames_flat, out_grad.reshape(rel_shape)
    )
    order.last = grad_low
    grad_far = send(grad_low.reshape(count, width), "head", 2)
    hidden_got = send(hidden_a, "space", 2), send(hidden_b, "space", 1)
    grad_far = take(grad_far)
    spread = take(spread)
    first, normed_two = kernel(
        join_norm_body, [whole_shape, packed_shape], *scalars, small, frames_rel, spread
    )
    order.last = normed_two
    normed_two = normed_two.reshape(local)
    far = send(normed_two, "head", 2)
    near = send(normed_two, "head", 1)
    hidden_b = stacked(hidden_b, take(hidden_got[1]))
    hidden_a = stacked(hidden_a, take(hidden_got[0]))
    hidden_got = send(hidden_a, "space", 1), send(hidden_b, "space", 2)
    time_a = stacked(time_a, take(got_a))
    time_b = crossed(time_b, take(got_b))
    far = take(far)
    diagonal = send(far, "head", 1)
    near = take(near)
    normed_two = [normed_two, near, far, take(diagonal)]
    time_projected, time_output, time_totals, time_parts = do(
        lambda first, *others: time_call(
            time_forward_body,
            clip_length,
            [time_a, time_b],
            [[first, *others]],
            [(3 * inner, LOW), (inner, LOW), (128, WIDE), (width, LOW)],
        ),
        *normed_two,
    )
    order.last = time_parts[3]
    diagonal = send(time_parts[3], "head", 1)
    near = send(time_parts[1], "head", 1)
    far = added(time_parts[2], take(diagonal))
    far = send(far, "head", 2)
    hidden_got = [take(got) for got in hidden_got]
    near = take(near)
    hidden_a = stacked(hidden_a, hidden_got[0])
    hidden_b = crossed(hidden_b, hidden_got[1])
    parts = [part.reshape(rel_shape) for part in (time_parts[0], near, take(far))]
    second, normed_three = kernel(add_norm_body, [whole_shape, packed_shape], small, first, *parts)
    order.last = normed_three
    normed_three = normed_three.reshape(count, width)
    grad_low_flat = grad_low.reshape(count, width)
    far = send(normed_three, "head", 2)
    beside_a, beside_b = send(hidden_a, "head", 1), send(hidden_b, "head", 1)
    hidden_weights = [hidden_a, hidden_b, take(beside_a), take(beside_b)]
    normed_three = [normed_three, take(far)]
    grad_third = [grad_low_flat, grad_far]
    far_kept_three = do(hidden_call, normed_three[1], grad_third[1], hidden_weights)
    order.last = far_kept_three[2]
    far_part = send(far_kept_three[2], "head", 2)
    own_kept_three = do(hidden_call, normed_three[0], grad_third[0], hidden_weights)
    hidden_kept = [own_kept_three, far_kept_three]
    def hidden_part(side, leave):
        lefts = grad_third if leave else normed_three
        rights = [kept[0 if leave else 1][side] for kept in hidden_kept]
        return do(lambda *left: weight_grad([(left, rights)], near_first=leave), *lefts)
    beside_a = hidden_part(1, False)
    beside_b = hidden_part(1, True)
    far_part = take(far_part)
    beside_a, beside_b = send(beside_a, "head", 1), send(beside_b, "head", 1)
    parts = [part.reshape(rel_shape) for part in (own_kept_three[2], far_part)]
    total_second, low_second, sums_third = kernel(
        back_third_body, [whole_shape, packed_shape, sums_shape], small, grad_low, second, *parts
    )
    order.last = low_second
    low_second = low_second.reshape(local)
    far = send(low_second, "head", 2)
    near = send(low_second, "head", 1)
    hidden_a = hidden_part(0, False)
    hidden_b = hidden_part(0, True)
    near = take(near)
    far = take(far)
    diagonal = send(far, "head", 1)
    hidden_a, send_a = halves(hidden_a, take(beside_a))
    got_a = send(send_a, "space", 1)
    hidden_b, send_b = halves(hidden_b, take(beside_b))
    got_b = send(send_b, "space", 2)
    grad_two = [low_second, near, far, take(diagonal)]
    time_grads, time_parts = do(
        lambda first, *others: time_call(
            time_back_body,
            clip_length,
            [time_a, time_b],
            [[first, *others], time_projected, time_totals],
            [(3 * inner, LOW), (width, LOW)],
        ),
        *grad_two,
    )
    order.last = time_parts[3]
    diagonal = send(time_parts[3], "head", 1)
    near = send(time_parts[1], "head", 1)
    flat = lambda arrays: [a.reshape(count, a.shape[-1]) for a in arrays]
    far = added(time_parts[2], take(diagonal))
    far = send(far, "head", 2)
    near = take(near)
    def attention_part(side, lefts, grads, backs, outputs):
        step = inner // 2
        return do(
            lambda *left: weight_grad(
                [(left, grads), (backs, outputs)],
                near_first=side % 2 == 1,
                ranges=[side_columns(side, 3 * step), side_columns(side, step)],
            ),
            *lefts,
        )
    time_args = flat(normed_two), flat(time_grads), flat(grad_two), flat(time_output)
    time_a = attention_part(0, *time_args)
    time_b = attention_part(1, *time_args)
    hidden_a, send_a = halves(hidden_a, take(got_a))
    hidden_b, send_b = halves(hidden_b, take(got_b))
    hidden_got = send(send_a, "space", 2), send(send_b, "space", 1)
    parts = [part.reshape(rel_shape) for part in (time_parts[0], near, take(far))]
    total_first, sums_second, table_first, packed = kernel(
        back_second_body,
        [whole_shape, sums_shape, sums_shape, packed_shape],
        *scalars,
        small,
        total_second,
        first,
        *parts,
    )
    order.last = packed
    grad_blocks = order.exchange(packed)
    hidden_keep, hidden_send = joined((hidden_a, take(hidden_got[0])), (hidden_b, take(hidden_got[1])))
    (time_a, send_a), (time_b, send_b) = [jnp.split(part, 2) for part in (time_a, time_b)]
    got_a, got_b = send(send_a, "space", 1), send(send_b, "space", 2)
    got_hidden = send(hidden_send, "space", 4)
    far_out = take(send(far_kept_three[3], "head", 2))
    grad_blocks = take(grad_blocks)
    grad_one = kernel(collect_body, flat_shape, grad_blocks)
    far = send(grad_one, "head", 2)
    own_result = do(space_back, grad_one, space_weights, own_kept[0], own_kept[2])
    order.last = own_result[1]
    got_a, got_b = take(got_a), take(got_b)
    grad_one = [grad_one, take(far)]
    far_result = do(space_back, grad_one[1], space_weights, far_kept[0], far_kept[2])
    order.last = far_result[1]
    far_part = send(far_result[1], "head", 2)
    time_a, send_a = halves(time_a, got_a)
    time_b, send_b = halves(time_b, got_b)
    got_hidden = take(got_hidden)
    got_a, got_b = send(send_a, "space", 2), send(send_b, "space", 1)
    space_args = [normed, normed_far], [own_result[0], far_result[0]], grad_one, [own_kept[1], far_kept[1]]
    beside_a = attention_part(2, *space_args)
    beside_b = attention_part(3, *space_args)
    time_keep, time_send = joined((time_a, take(got_a)), (time_b, take(got_b)))
    got_time = send(time_send, "space", 4)
    space_a = attention_part(0, *space_args)
    space_b = attention_part(1, *space_args)
    far_part = take(far_part)
    beside_a, beside_b = send(beside_a, "head", 1), send(beside_b, "head", 1)
    sums_first, table_second, packed = kernel(
        back_first_body,
        [sums_shape, sums_shape, packed_shape],
        *scalars,
        small,
        start,
        own_result[1],
        far_part,
    )
    order.last = packed
    last = order.exchange(packed)
    space_a, send_a = halves(space_a, take(beside_a))
    space_b, send_b = halves(space_b, take(beside_b))
    got_a, got_b = send(send_a, "space", 1), send(send_b, "space", 2)
    half_shape = shape_of((BLOCKS // 2, *small_shape), WIDE)
    sums, small_send = kernel(
        small_blocks_body, [half_shape] * 2, sums_first, sums_second, sums_third, table_first, table_second
    )
    order.last = small_send
    got_small = send(small_send, "space", 1)
    sums, small_send = halves(sums, take(got_small))
    got_small = send(small_send, "space", 2)
    parts = [part.reshape(rel_shape) for part in (own_kept_three[3], far_out)]
    frames_out = kernel(finish_forward_body, packed_shape, clip_length, second, *parts)
    hidden_grads = kernel(
        unpack_hidden_body,
        [shape_of((width // BLOCKS, hidden), WIDE), shape_of((hidden, width // BLOCKS), WIDE)],
        hidden_keep,
        got_hidden,
    )
    sums, small_send = halves(sums, take(got_small))
    got_small = send(small_send, "space", 4)
    space_a, send_a = halves(space_a, take(got_a))
    space_b, send_b = halves(space_b, take(got_b))
    got_a, got_b = send(send_a, "space", 2), send(send_b, "space", 1)
    space_keep, space_send = joined((space_a, take(got_a)), (space_b, take(got_b)))
    sums = summed(sums, take(got_small))
    got = send(space_send, "space", 4)
    got_small = send(sums, "head", 1)
    last = take(last)
    frames_grad = kernel(finish_back_body, whole_shape, clip_length, total_first, last)
    sums = summed(sums, take(got_small))
    got_small = send(sums, "head", 2)
    sums = summed(sums, take(got_small))[0]
    step = sums.shape[1] // ROUND
    sums = lax.dynamic_slice(sums, (0, lax.axis_index("head") * step), (sums.shape[0], step))
    time_grads = kernel(unpack_attention_body, grad_shapes, time_keep, take(got_time))
    space_grads = kernel(unpack_attention_body, grad_shapes, space_keep, take(got))
    return (
        frames_out.reshape(local),
        frames_grad.reshape(local),
        sums[0:3],
        sums[3:6],
        sums[6:14],
        jnp.transpose(space_grads[0], (1, 0, 2)),
        space_grads[1],
        jnp.transpose(time_grads[0], (1, 0, 2)),
        time_grads[1],
        *hidden_grads,
    )


def solution(mesh):
    placed = (
        P("head", None, "space", None),
        P("head", None),
        P(),
        P(None, ("space", "head")),
        P(None, ("space", "head")),
        P(None, ("space", "head")),
        P("space", None, "head"),
        P("head", "space"),
        P("space", None, "head"),
        P("head", "space"),
        P("space", "head"),
        P("head", "space"),
        P("head", None, "space", None),
    )
    eight = mesh.shape["space"] == BLOCKS and mesh.shape["head"] == ROUND
    return jax.shard_map(
        shards if eight else general_shards,
        mesh=mesh,
        in_specs=placed,
        out_specs=(
            P("head", None, "space", None),
            P("head", None, "space", None),
            P(None, ("space", "head")),
            P(None, ("space", "head")),
            P(None, ("space", "head")),
            P("space", None, "head"),
            P("head", "space"),
            P("space", None, "head"),
            P("head", "space"),
            P("space", "head"),
            P("head", "space"),
        ),
        check_vma=False,
    )
```

```python
import functools

import jax
import jax.numpy as jnp
from jax import lax
from jax.experimental import pallas as pl
from jax.experimental.pallas import tpu as pltpu
from jax.sharding import PartitionSpec as P

HEAD_DIM = 64


EPSILON = 1e-05
SCORE_SCALE = 0.125
MASKED_SCORE = -1e30
PRECISE = lax.Precision.HIGHEST
GELU_COEFF = 0.7978845608028654


def layer_norm(values, gain_row, bias_row):
    row_mean = jnp.mean(values, axis=-1, keepdims=True)
    centred = values - row_mean
    row_var = jnp.mean(centred * centred, axis=-1, keepdims=True)
    return centred * lax.rsqrt(row_var + EPSILON) * gain_row + bias_row


def gelu_tanh(inputs):
    return (
        0.5 * inputs * (1.0 + jnp.tanh(GELU_COEFF * (inputs + 0.044715 * inputs * inputs * inputs)))
    )


def gather_weights(small, large):
    small_full = (
        lax.all_gather(small[0], ("space", "head"), axis=1, tiled=True),
        lax.all_gather(small[1], ("space", "head"), axis=1, tiled=True),
        lax.all_gather(small[2], ("space", "head"), axis=1, tiled=True),
    )
    large_full = (
        lax.all_gather(large[0], "space", axis=0, tiled=True),
        lax.all_gather(large[1], "space", axis=1, tiled=True),
        lax.all_gather(large[2], "space", axis=0, tiled=True),
        lax.all_gather(large[3], "space", axis=1, tiled=True),
        lax.all_gather(large[4], "space", axis=0, tiled=True),
        lax.all_gather(large[5], "space", axis=1, tiled=True),
    )
    return (small_full, large_full)


def norm_step(inputs, gain_row, bias_row):
    normed, pullback = jax.vjp(layer_norm, inputs, gain_row, bias_row)
    whole = lax.all_gather(normed.astype(jnp.bfloat16), "head", axis=0, tiled=True)
    return (whole, pullback)


def cot_whole(grad_rows):
    return lax.all_gather(grad_rows.astype(jnp.bfloat16), "head", axis=0, tiled=True)


def input_total(partial_value):
    return lax.psum_scatter(
        partial_value.astype(jnp.bfloat16), "head", scatter_dimension=0, tiled=True
    ).astype(jnp.float32)


def heads_total(left, weight):
    return lax.psum_scatter(
        jnp.einsum("fcpe,ed->fcpd", left, weight, preferred_element_type=jnp.float32).astype(
            jnp.bfloat16
        ),
        "head",
        scatter_dimension=0,
        tiled=True,
    ).astype(jnp.float32)


def project_in(whole, weight):
    stacked = jnp.einsum(
        "fcpd,dke->kfcpe", whole, weight, preferred_element_type=jnp.float32
    ).astype(jnp.bfloat16)
    return (stacked[0], stacked[1], stacked[2])


def raw_scores(queries, keyset, form, allowed):
    key_form = form.replace("q", "k")
    scores = (
        jnp.einsum(
            form + "," + key_form + "->bhqk", queries, keyset, preferred_element_type=jnp.float32
        )
        * SCORE_SCALE
    )
    if allowed is not None:
        scores = jnp.where(allowed, scores, MASKED_SCORE)
    return scores


def attend(queries, keyset, values, form, allowed):
    key_form = form.replace("q", "k")
    scores = raw_scores(queries, keyset, form, allowed)
    row_max = jnp.max(scores, axis=-1, keepdims=True)
    log_total = row_max + jnp.log(jnp.sum(jnp.exp(scores - row_max), axis=-1, keepdims=True))
    shares = jnp.exp(scores - log_total).astype(jnp.bfloat16)
    output = jnp.einsum(
        "bhqk," + key_form + "->" + form, shares, values, preferred_element_type=jnp.float32
    )
    return (output.astype(jnp.bfloat16), log_total)


def attend_back(queries, keyset, values, log_total, output_grad, form, allowed):
    key_form = form.replace("q", "k")
    shares = jnp.exp(raw_scores(queries, keyset, form, allowed) - log_total)
    value_grad = jnp.einsum(
        "bhqk," + form + "->" + key_form,
        shares.astype(jnp.bfloat16),
        output_grad,
        preferred_element_type=jnp.float32,
    )
    share_grad = jnp.einsum(
        form + "," + key_form + "->bhqk", output_grad, values, preferred_element_type=jnp.float32
    )
    score_grad = (
        shares * (share_grad - jnp.sum(share_grad * shares, axis=-1, keepdims=True))
    ).astype(jnp.bfloat16)
    query_grad = (
        jnp.einsum(
            "bhqk," + key_form + "->" + form, score_grad, keyset, preferred_element_type=jnp.float32
        )
        * SCORE_SCALE
    )
    key_grad = (
        jnp.einsum(
            "bhqk," + form + "->" + key_form,
            score_grad,
            queries,
            preferred_element_type=jnp.float32,
        )
        * SCORE_SCALE
    )
    return (
        query_grad.astype(jnp.bfloat16),
        key_grad.astype(jnp.bfloat16),
        value_grad.astype(jnp.bfloat16),
    )


def general_shards(
    frames_in,
    action_codes,
    clip_length,
    norm_gain,
    norm_bias,
    action_table,
    spatialin,
    spatialout,
    temporalin,
    temporalout,
    expand,
    shrink,
    out_grad,
):
    head_count = lax.axis_size("head")
    frames_local, clip_count, pos_local, width = frames_in.shape
    frames_total = frames_local * head_count
    local_width = spatialin.shape[2]
    heads_local = local_width // HEAD_DIM
    frame_index = jnp.arange(frames_total)
    local_index = lax.axis_index("head") * frames_local + jnp.arange(frames_local)
    valid_local = (local_index[:, None] < clip_length[None, :]).astype(jnp.float32)[
        :, :, None, None
    ]
    allowed = (frame_index[None, :, None] >= frame_index[None, None, :]) & (
        frame_index[None, None, :] < clip_length[:, None, None]
    )
    allowed = jnp.broadcast_to(
        allowed[:, None, None], (clip_count, pos_local, 1, frames_total, frames_total)
    )
    allowed = allowed.reshape(clip_count * pos_local, 1, frames_total, frames_total)
    small_full, large_full = gather_weights(
        (norm_gain, norm_bias, action_table),
        (spatialin, spatialout, temporalin, temporalout, expand, shrink),
    )
    gain_full, bias_full, table_full = small_full
    space_in, space_out, time_in, time_out, expand_full, shrink_full = large_full
    code_hot = (action_codes[:, :, None] == jnp.arange(table_full.shape[0])[None, None, :]).astype(
        jnp.float32
    )
    embedded = jnp.einsum("fca,ad->fcd", code_hot, table_full, precision=PRECISE)
    start = valid_local * (frames_in.astype(jnp.float32) + embedded[:, :, None, :])
    whole_one, pull_one = norm_step(start, gain_full[0], bias_full[0])
    space_query, space_keys, space_values = project_in(whole_one, space_in)
    flat_shape = (frames_total * clip_count, pos_local, local_width)
    moved = (
        lax.all_to_all(
            space_query.reshape(flat_shape), "space", split_axis=0, concat_axis=1, tiled=True
        ),
        lax.all_to_all(
            space_keys.reshape(flat_shape), "space", split_axis=0, concat_axis=1, tiled=True
        ),
        lax.all_to_all(
            space_values.reshape(flat_shape), "space", split_axis=0, concat_axis=1, tiled=True
        ),
    )
    block_rows = moved[0].shape[0]
    block_cols = moved[0].shape[1]
    frame_shape = (block_rows, block_cols, heads_local, HEAD_DIM)
    frame_query = moved[0].reshape(frame_shape)
    frame_keys = moved[1].reshape(frame_shape)
    frame_values = moved[2].reshape(frame_shape)
    frame_out, frame_total = attend(frame_query, frame_keys, frame_values, "bqhe", None)
    returned = lax.all_to_all(
        frame_out.reshape(block_rows, block_cols, local_width),
        "space",
        split_axis=1,
        concat_axis=0,
        tiled=True,
    )
    space_attended = returned.reshape(frames_total, clip_count, pos_local, local_width)
    first = start + heads_total(space_attended, space_out)
    whole_two, pull_two = norm_step(first, gain_full[1], bias_full[1])
    time_query, time_keys, time_values = project_in(whole_two, time_in)
    time_shape = (frames_total, clip_count * pos_local, heads_local, HEAD_DIM)
    time_query = time_query.reshape(time_shape)
    time_keys = time_keys.reshape(time_shape)
    time_values = time_values.reshape(time_shape)
    time_out_rows, time_total = attend(time_query, time_keys, time_values, "qbhe", allowed)
    time_attended = time_out_rows.reshape(frames_total, clip_count, pos_local, local_width)
    second = first + heads_total(time_attended, time_out)
    whole_three, pull_three = norm_step(second, gain_full[2], bias_full[2])
    expanded = jnp.einsum(
        "fcpd,dh->fcph", whole_three, expand_full, preferred_element_type=jnp.float32
    )
    activated, gelu_pull = jax.vjp(gelu_tanh, expanded)
    activated_low = activated.astype(jnp.bfloat16)
    third = second + heads_total(activated_low, shrink_full)
    frames_out = (valid_local * third).astype(jnp.bfloat16)
    small_full, large_full = gather_weights(
        (norm_gain, norm_bias, action_table),
        (spatialin, spatialout, temporalin, temporalout, expand, shrink),
    )
    space_in, space_out, time_in, time_out, expand_full, shrink_full = large_full
    grad_third = valid_local * out_grad.astype(jnp.float32)
    cot_three = cot_whole(grad_third)
    shrink_part = jnp.einsum(
        "fcph,fcpd->hd", activated_low, cot_three, preferred_element_type=jnp.float32
    )
    act_grad = jnp.einsum(
        "fcpd,hd->fcph", cot_three, shrink_full, preferred_element_type=jnp.float32
    )
    pre_grad = gelu_pull(act_grad)[0].astype(jnp.bfloat16)
    expand_part = jnp.einsum(
        "fcpd,fcph->dh", whole_three, pre_grad, preferred_element_type=jnp.float32
    )
    normed_grad = input_total(
        jnp.einsum("fcph,dh->fcpd", pre_grad, expand_full, preferred_element_type=jnp.float32)
    )
    input_three, gain_three, bias_three = pull_three(normed_grad)
    grad_second = grad_third + input_three
    cot_two = cot_whole(grad_second)
    time_out_part = jnp.einsum(
        "fcpe,fcpd->ed", time_attended, cot_two, preferred_element_type=jnp.float32
    )
    time_grad = jnp.einsum(
        "fcpd,ed->fcpe", cot_two, time_out, preferred_element_type=jnp.float32
    ).astype(jnp.bfloat16)
    time_grads = attend_back(
        time_query,
        time_keys,
        time_values,
        time_total,
        time_grad.reshape(time_shape),
        "qbhe",
        allowed,
    )
    stacked_grad = jnp.stack(
        [member.reshape(frames_total, clip_count, pos_local, local_width) for member in time_grads]
    )
    time_in_part = jnp.einsum(
        "fcpd,kfcpe->dke", whole_two, stacked_grad, preferred_element_type=jnp.float32
    )
    normed_grad = input_total(
        jnp.einsum("kfcpe,dke->fcpd", stacked_grad, time_in, preferred_element_type=jnp.float32)
    )
    input_two, gain_two, bias_two = pull_two(normed_grad)
    grad_first = grad_second + input_two
    cot_one = cot_whole(grad_first)
    space_out_part = jnp.einsum(
        "fcpe,fcpd->ed", space_attended, cot_one, preferred_element_type=jnp.float32
    )
    space_grad = jnp.einsum(
        "fcpd,ed->fcpe", cot_one, space_out, preferred_element_type=jnp.float32
    ).astype(jnp.bfloat16)
    frame_grad = lax.all_to_all(
        space_grad.reshape(flat_shape), "space", split_axis=0, concat_axis=1, tiled=True
    ).reshape(frame_shape)
    query_grad, keys_grad, values_grad = attend_back(
        frame_query, frame_keys, frame_values, frame_total, frame_grad, "bqhe", None
    )
    block_shape = (block_rows, block_cols, local_width)
    back_grads = (
        lax.all_to_all(
            query_grad.reshape(block_shape), "space", split_axis=1, concat_axis=0, tiled=True
        ),
        lax.all_to_all(
            keys_grad.reshape(block_shape), "space", split_axis=1, concat_axis=0, tiled=True
        ),
        lax.all_to_all(
            values_grad.reshape(block_shape), "space", split_axis=1, concat_axis=0, tiled=True
        ),
    )
    stacked_grad = jnp.stack(
        [member.reshape(frames_total, clip_count, pos_local, local_width) for member in back_grads]
    )
    space_in_part = jnp.einsum(
        "fcpd,kfcpe->dke", whole_one, stacked_grad, preferred_element_type=jnp.float32
    )
    normed_grad = input_total(
        jnp.einsum("kfcpe,dke->fcpd", stacked_grad, space_in, preferred_element_type=jnp.float32)
    )
    input_one, gain_one, bias_one = pull_one(normed_grad)
    grad_start = grad_first + input_one
    frames_grad = valid_local * grad_start
    table_part = jnp.einsum(
        "fca,fcd->ad", code_hot, jnp.sum(frames_grad, axis=2), precision=PRECISE
    )
    gain_grad, bias_grad, table_grad = (
        lax.psum_scatter(
            jnp.stack([gain_one, gain_two, gain_three]),
            ("space", "head"),
            scatter_dimension=1,
            tiled=True,
        ),
        lax.psum_scatter(
            jnp.stack([bias_one, bias_two, bias_three]),
            ("space", "head"),
            scatter_dimension=1,
            tiled=True,
        ),
        lax.psum_scatter(table_part, ("space", "head"), scatter_dimension=1, tiled=True),
    )
    weight_grads = (
        lax.psum_scatter(space_in_part, "space", scatter_dimension=0, tiled=True),
        lax.psum_scatter(space_out_part, "space", scatter_dimension=1, tiled=True),
        lax.psum_scatter(time_in_part, "space", scatter_dimension=0, tiled=True),
        lax.psum_scatter(time_out_part, "space", scatter_dimension=1, tiled=True),
        lax.psum_scatter(expand_part, "space", scatter_dimension=0, tiled=True),
        lax.psum_scatter(shrink_part, "space", scatter_dimension=1, tiled=True),
    )
    return (
        frames_out,
        frames_grad,
        gain_grad,
        bias_grad,
        table_grad,
        weight_grads[0],
        weight_grads[1],
        weight_grads[2],
        weight_grads[3],
        weight_grads[4],
        weight_grads[5],
    )


ORDER = (0, 4, 2, 6, 1, 5, 3, 7)
BLOCKS = len(ORDER)
PLACE = tuple(ORDER.index(mask) for mask in range(BLOCKS))
ROUND = 4
ONE_VMEM = pl.BlockSpec(memory_space=pltpu.VMEM)
ONE_SMEM = pl.BlockSpec(memory_space=pltpu.SMEM)
MIB = 1024 * 1024
LOW = jnp.bfloat16
WIDE = jnp.float32


def swap(value, axis, mask):
    return lax.ppermute(value, axis, [(i, i ^ mask) for i in range(lax.axis_size(axis))])


class Order:
    def __init__(self):
        self.last = None

    def tied(self, value):
        if self.last is None:
            return value
        return lax.optimization_barrier((value, self.last))[0]

    def send(self, value, axis, mask):
        return swap(self.tied(value), axis, mask)

    def exchange(self, packed):
        return lax.all_to_all(self.tied(packed), "space", split_axis=0, concat_axis=0, tiled=True)

    def take(self, value):
        self.last = self.tied(value)
        return self.last

    def do(self, step, first, *others):
        result = step(self.tied(first), *others)
        self.last = jax.tree.leaves(result)[0]
        return result


def run(body, outs, args, specs, vmem=None, stored=()):
    single = not isinstance(outs, (list, tuple))
    name = getattr(body, "func", body).__name__.removesuffix("_body")
    args, specs, scratch, whole = list(args), list(specs), [], body
    if stored:
        for place in stored:
            args[place] = pltpu.with_memory_space_constraint(args[place], pltpu.HBM)
            specs[place] = pl.BlockSpec(memory_space=pltpu.HBM)
            scratch.append(pltpu.VMEM(args[place].shape, args[place].dtype))
        scratch.append(pltpu.SemaphoreType.DMA((len(stored),)))

        def whole(*refs):
            refs, held, sem = list(refs[: -len(scratch)]), refs[-len(scratch) : -1], refs[-1]
            copies = [
                pltpu.make_async_copy(refs[place], held[i], sem.at[i]) for i, place in enumerate(stored)
            ]
            for copy in copies:
                copy.start()
            for i, place in enumerate(stored):
                copies[i].wait()
                refs[place] = held[i]
            body(*refs)

    return pl.pallas_call(
        whole,
        out_shape=outs,
        in_specs=specs,
        out_specs=ONE_VMEM if single else [ONE_VMEM] * len(outs),
        scratch_shapes=scratch,
        cost_estimate=pl.CostEstimate(flops=0, bytes_accessed=1024, transcendentals=0),
        compiler_params=pltpu.CompilerParams(vmem_limit_bytes=vmem or 12 * MIB),
        name=name,
    )(*args)


def kept_of(dims, dtype):
    return pltpu.HBM(tuple(dims), dtype)


def shape_of(dims, dtype):
    return jax.ShapeDtypeStruct(tuple(dims), dtype)


def feature_block(place, step):
    return pl.ds(pl.multiple_of(place * step, step), step)


def partner(mask):
    return lax.axis_index("space") ^ mask


def frame_valid(lengths, frames, mask):
    clips = lengths.shape[0]
    frame = lax.axis_index("head") * (frames // clips) + partner(mask) // clips
    return jnp.where(frame < lengths[partner(mask) % clips], 1.0, 0.0).astype(WIDE)


def normed_parts(values):
    centred = values - jnp.mean(values, axis=-1, keepdims=True)
    scale = lax.rsqrt(jnp.mean(centred * centred, axis=-1, keepdims=True) + EPSILON)
    return centred * scale, scale


def norm_back(values, grad, gain_row):
    unit, scale = normed_parts(values)
    scaled = grad * gain_row
    out = scale * (
        scaled
        - jnp.mean(scaled, axis=-1, keepdims=True)
        - unit * jnp.mean(scaled * unit, axis=-1, keepdims=True)
    )
    return (
        out,
        jnp.sum(grad * unit, axis=0, keepdims=True),
        jnp.sum(grad, axis=0, keepdims=True),
    )


def store_for(ref, rows, mask):
    step = rows.shape[-1] // BLOCKS
    for i in range(BLOCKS):
        j = i ^ PLACE[mask]
        ref[partner(mask), :, i * step : (i + 1) * step] = rows[:, j * step : (j + 1) * step]


def pack_attention_body(enter, leave, out):
    step = leave.shape[0] // 2
    for i in range(2):
        place, column = slice(i * step, (i + 1) * step), 4 * i * step
        for j in range(3):
            out[:, column + j * step : column + (j + 1) * step] = enter[j, :, place]
        out[:, column + 3 * step : column + 4 * step] = jnp.transpose(leave[place, :])


def unpack_attention_body(mine, got, enter, leave):
    step = leave.shape[0] // 2
    for i in range(2):
        columns = side_columns(i, 4 * step)
        total = mine[:, columns].astype(WIDE) + got[:, columns].astype(WIDE)
        place = slice(i * step, (i + 1) * step)
        for j in range(3):
            enter[j, :, place] = total[:, j * step : (j + 1) * step]
        leave[place, :] = jnp.transpose(total[:, 3 * step :])


def pack_hidden_body(enter, leave, out):
    hidden = leave.shape[0]
    out[:, :hidden] = enter[...]
    out[:, hidden:] = jnp.transpose(leave[...])


def unpack_hidden_body(mine, got, enter, leave):
    hidden = leave.shape[0]
    total = mine[...].astype(WIDE) + got[...].astype(WIDE)
    enter[...] = total[:, :hidden]
    leave[...] = jnp.transpose(total[:, hidden:])


def stack_split_body(first, second, *outs):
    rows, column = first.shape[0], 0
    for out in outs:
        place = slice(column, column + out.shape[1])
        out[:rows, :] = first[:, place]
        out[rows:, :] = second[:, place]
        column += out.shape[1]


def stack_cross_body(first, second, out):
    tile = first.shape[0] // 2
    for i, (part, place) in enumerate(((first, 0), (second, 0), (first, 1), (second, 1))):
        out[i * tile : (i + 1) * tile, :] = part[place * tile : (place + 1) * tile, :]


def add_join_body(first_a, second_a, first_b, second_b, *outs):
    row, half = 0, first_a.shape[1]
    for out in outs:
        part = slice(row, row + out.shape[0])
        out[:, :half] = (first_a[part].astype(WIDE) + second_a[part].astype(WIDE)).astype(out.dtype)
        out[:, half:] = (first_b[part].astype(WIDE) + second_b[part].astype(WIDE)).astype(out.dtype)
        row += out.shape[0]


def pack_frames_body(frames, out):
    step = frames.shape[-1] // BLOCKS
    for mask in range(BLOCKS):
        for i in range(BLOCKS):
            source = partner(ORDER[i ^ PLACE[mask]])
            place = slice(i * step, (i + 1) * step)
            out[partner(mask), :, place] = frames[partner(mask), :, feature_block(source, step)]


def order_inputs_body(lengths, frames, grad, frames_out, grad_out):
    step = frames.shape[-1] // BLOCKS

    def one(mask, carry):
        valid = frame_valid(lengths, BLOCKS, mask)
        for i in range(BLOCKS):
            source = feature_block(partner(ORDER[i]), step)
            place = slice(i * step, (i + 1) * step)
            frames_out[mask, :, place] = frames[partner(mask), :, source]
            kept = grad[partner(mask), :, source].astype(WIDE) * valid
            grad_out[mask, :, place] = kept.astype(LOW)
        return carry

    lax.fori_loop(0, BLOCKS, one, 0)


def start_rows(rows, codes, lengths, small, mask):
    embedded = small[pl.ds(6 + codes[partner(mask)], 1), :]
    return frame_valid(lengths, BLOCKS, mask) * (rows.astype(WIDE) + embedded)


def frame_norm_body(codes, lengths, small, blocks, normed, start):
    rows = blocks.shape[1]
    for b in range(BLOCKS):
        values = start_rows(blocks[partner(b)], codes, lengths, small, 0)
        start[b * rows : (b + 1) * rows, :] = values
        unit, _ = normed_parts(values)
        normed[b * rows : (b + 1) * rows, :] = (unit * small[0:1, :] + small[3:4, :]).astype(LOW)


def spread_body(first, second, out):
    rows = out.shape[1]
    for mask in range(BLOCKS):
        part = slice(mask * rows, (mask + 1) * rows)
        total = first[part, :].astype(WIDE) + second[part, :].astype(WIDE)
        store_for(out, total.astype(LOW), mask)


def join_norm_body(codes, lengths, small, frames, blocks, whole, normed):
    for b in range(BLOCKS):
        values = start_rows(frames[b], codes, lengths, small, b) + blocks[partner(b)].astype(WIDE)
        whole[b] = values
        unit, _ = normed_parts(values)
        normed[b] = (unit * small[1:2, :] + small[4:5, :]).astype(LOW)


def add_norm_body(small, before, first, second, third, whole, normed):
    def one(b, carry):
        values = before[b] + (
            first[b].astype(WIDE) + second[b].astype(WIDE) + third[b].astype(WIDE)
        )
        whole[b] = values
        unit, _ = normed_parts(values)
        normed[b] = (unit * small[2:3, :] + small[5:6, :]).astype(LOW)
        return carry

    lax.fori_loop(0, BLOCKS, one, 0)


def finish_forward_body(lengths, before, first, second, out):
    step = out.shape[-1] // BLOCKS

    def one(b, carry):
        values = before[b] + (first[b].astype(WIDE) + second[b].astype(WIDE))
        values = (frame_valid(lengths, BLOCKS, b) * values).astype(LOW)
        for i in range(BLOCKS):
            place = feature_block(partner(ORDER[i]), step)
            out[partner(b), :, place] = values[:, i * step : (i + 1) * step]
        return carry

    lax.fori_loop(0, BLOCKS, one, 0)


def back_third_body(small, grad, values, first, second, total_out, low_out, sums):
    sums[...] = jnp.zeros_like(sums)

    def one(b, carry):
        normed_grad = first[b].astype(WIDE) + second[b].astype(WIDE)
        out, gain, bias = norm_back(values[b], normed_grad, small[2:3, :])
        total = grad[b].astype(WIDE) + out
        total_out[b] = total
        low_out[b] = total.astype(LOW)
        sums[0:1, :] += gain
        sums[1:2, :] += bias
        return carry

    lax.fori_loop(0, BLOCKS, one, 0)


def back_second_body(codes, lengths, small, grad, values, first, second, third, total_out, sums, table, packed):
    sums[...] = jnp.zeros_like(sums)
    table[...] = jnp.zeros_like(table)
    for b in range(BLOCKS):
        normed_grad = first[b].astype(WIDE) + second[b].astype(WIDE) + third[b].astype(WIDE)
        out, gain, bias = norm_back(values[b], normed_grad, small[1:2, :])
        total = grad[b] + out
        total_out[b] = total
        store_for(packed, total.astype(LOW), b)
        sums[0:1, :] += gain
        sums[1:2, :] += bias
        row = pl.ds(codes[partner(b)], 1)
        table[row, :] += frame_valid(lengths, BLOCKS, b) * jnp.sum(total, axis=0, keepdims=True)


def back_first_body(codes, lengths, small, values, first, second, sums, table, packed):
    sums[...] = jnp.zeros_like(sums)
    table[...] = jnp.zeros_like(table)
    rows = packed.shape[1]
    for b in range(BLOCKS):
        part = slice(b * rows, (b + 1) * rows)
        normed_grad = first[part, :].astype(WIDE) + second[part, :].astype(WIDE)
        out, gain, bias = norm_back(values[part, :], normed_grad, small[0:1, :])
        store_for(packed, out.astype(LOW), b)
        sums[0:1, :] += gain
        sums[1:2, :] += bias
        row = pl.ds(codes[partner(0)], 1)
        table[row, :] += frame_valid(lengths, BLOCKS, 0) * jnp.sum(out, axis=0, keepdims=True)


def collect_body(blocks, out):
    rows = blocks.shape[1]
    for b in range(BLOCKS):
        out[b * rows : (b + 1) * rows, :] = blocks[partner(b)]


def finish_back_body(lengths, grad, blocks, out):
    step = out.shape[-1] // BLOCKS
    for b in range(BLOCKS):
        values = frame_valid(lengths, BLOCKS, b) * (grad[b] + blocks[partner(b)].astype(WIDE))
        for i in range(BLOCKS):
            place = feature_block(partner(ORDER[i]), step)
            out[partner(b), :, place] = values[:, i * step : (i + 1) * step]


def matmul(left, right):
    return lax.dot_general(left, right, (((1,), (0,)), ((), ())), preferred_element_type=WIDE)


def matmul_t(left, right):
    return lax.dot_general(left, right, (((1,), (1,)), ((), ())), preferred_element_type=WIDE)


def matmul_tn(left, right):
    return lax.dot_general(left, right, (((0,), (0,)), ((), ())), preferred_element_type=WIDE)


def head_mask(width, head):
    lane = lax.broadcasted_iota(jnp.int32, (1, width), 1)
    return (lane // HEAD_DIM) == head


def pick(values, mask):
    return jnp.where(mask, values, jnp.zeros_like(values))


def attention_rows(projected, allowed, totals, first):
    width = projected.shape[1] // 3
    queries = projected[:, :width] * jnp.asarray(SCORE_SCALE, LOW)
    keyset = projected[:, width : 2 * width]
    values = projected[:, 2 * width :]
    lane = lax.broadcasted_iota(jnp.int32, (1, 128), 1)
    output = jnp.zeros((projected.shape[0], width), WIDE)
    for head in range(width // HEAD_DIM):
        mask = head_mask(width, head)
        scores = matmul_t(pick(queries, mask), keyset)
        if allowed is not None:
            scores = jnp.where(allowed, scores, MASKED_SCORE)
        row_max = jnp.max(scores, axis=-1, keepdims=True)
        raised = jnp.exp(scores - row_max)
        total = jnp.sum(raised, axis=-1, keepdims=True)
        shares = (raised * (1.0 / total)).astype(LOW)
        output = output + matmul(shares, pick(values, mask))
        totals = jnp.where(lane == first + head, row_max + jnp.log(total), totals)
    return output.astype(LOW), totals


def attention_rows_back(projected, totals, first, output_grad, allowed):
    width = projected.shape[1] // 3
    queries = projected[:, :width] * jnp.asarray(SCORE_SCALE, LOW)
    keyset = projected[:, width : 2 * width]
    values = projected[:, 2 * width :]
    scaled_keys = keyset * jnp.asarray(SCORE_SCALE, LOW)
    shape = (projected.shape[0], width)
    query_grad, key_grad, value_grad = (jnp.zeros(shape, WIDE) for _ in range(3))
    for head in range(width // HEAD_DIM):
        mask = head_mask(width, head)
        own_queries = pick(queries, mask)
        own_grad = pick(output_grad, mask)
        scores = matmul_t(own_queries, keyset)
        if allowed is not None:
            scores = jnp.where(allowed, scores, MASKED_SCORE)
        shares = jnp.exp(scores - totals[:, first + head : first + head + 1])
        value_grad = value_grad + matmul_tn(shares.astype(LOW), own_grad)
        share_grad = matmul_t(own_grad, values)
        score_grad = shares * (share_grad - jnp.sum(share_grad * shares, axis=-1, keepdims=True))
        score_grad = score_grad.astype(LOW)
        query_grad = query_grad + matmul(score_grad, pick(scaled_keys, mask))
        key_grad = key_grad + matmul_tn(score_grad, own_queries)
    return jnp.concatenate(
        [query_grad.astype(LOW), key_grad.astype(LOW), value_grad.astype(LOW)], axis=1
    )


def enter_rows(rows, parts, columns):
    depth = parts[0].shape[0]
    total = matmul(rows[:, :depth], parts[0][:, columns])
    for i, part in enumerate(parts[1:], 1):
        total = total + matmul(rows[:, i * depth : (i + 1) * depth], part[:, columns])
    return total


def leave_rows(sides, columns, store):
    depth = sides[0][1][0].shape[0]
    for i in range(len(sides[0][1])):
        total = matmul_t(sides[0][0], sides[0][1][i][:, columns])
        for values, parts in sides[1:]:
            total = total + matmul_t(values, parts[i][:, columns])
        store(slice(i * depth, (i + 1) * depth), total.astype(LOW))


def side_columns(side, width):
    return slice(side * width, (side + 1) * width)


def space_forward_body(count, rows, *refs):
    sides = [[ref] for ref in refs[:count]]
    projected_out, output_out, totals_out, part_out = refs[count:]
    width = output_out.shape[1] // count
    totals = jnp.zeros(totals_out.shape, WIDE)
    leaving = []
    for side, parts in enumerate(sides):
        projected = enter_rows(rows, parts, slice(0, 3 * width)).astype(LOW)
        projected_out[:, side_columns(side, 3 * width)] = projected
        output, totals = attention_rows(projected, None, totals, side * (width // HEAD_DIM))
        output_out[:, side_columns(side, width)] = output
        leaving.append((output, parts))
    totals_out[...] = totals

    def store(place, values):
        part_out[:, place] = values

    leave_rows(leaving, slice(3 * width, 4 * width), store)


def space_back_body(count, rows, *refs):
    sides = [[ref] for ref in refs[:count]]
    projected, totals, grads_out, part_out = refs[count:]
    width = projected.shape[1] // (3 * count)
    leaving = []
    for side, parts in enumerate(sides):
        output_grad = enter_rows(rows, parts, slice(3 * width, 4 * width)).astype(LOW)
        first, columns = side * (width // HEAD_DIM), side_columns(side, 3 * width)
        grads = attention_rows_back(projected[:, columns], totals[...], first, output_grad, None)
        grads_out[:, columns] = grads
        leaving.append((grads, parts))

    def store(place, values):
        part_out[:, place] = values

    leave_rows(leaving, slice(0, 3 * width), store)


def time_allowed(lengths, clip, frames_local, positions):
    clips = lengths.shape[0]
    count = ROUND * frames_local * positions
    head_at, frame_at = lax.axis_index("head"), partner(0) // clips

    def split(shape, axis):
        row = lax.broadcasted_iota(jnp.int32, shape, axis)
        group = row // (frames_local * positions)
        local = (row // positions) % frames_local
        return (group ^ head_at) * frames_local + (local ^ frame_at), row % positions

    query_frame, query_pos = split((count, 1), 0)
    key_frame, key_pos = split((1, count), 1)
    length = lengths[(partner(0) % clips) ^ clip]
    return (query_pos == key_pos) & (query_frame >= key_frame) & (key_frame < length)


PART = 16


def time_groups(ref):
    return [(c, p) for c in range(ref.shape[1]) for p in range(0, ref.shape[2], PART)]


def join_rows(refs, group):
    c, p = group
    return jnp.concatenate(
        [ref[:, c, p : p + PART, :].reshape(ref.shape[0] * PART, ref.shape[3]) for ref in refs], axis=0
    )


def split_rows(refs, group, values, place=slice(None)):
    c, p = group
    rows = values.shape[0] // len(refs)
    for i, ref in enumerate(refs):
        part = values[i * rows : (i + 1) * rows].reshape(ref.shape[0], PART, values.shape[1])
        ref[:, c, p : p + PART, place] = part


def time_forward_body(lengths, *refs):
    sides, refs = refs[:2], refs[2:]
    rows, projected_out, output_out, totals_out, part_out = (refs[i : i + 4] for i in range(0, 20, 4))
    frames_local, width = rows[0].shape[0], output_out[0].shape[3]
    side_width = width // len(sides)
    masks = [time_allowed(lengths, clip, frames_local, PART) for clip in range(rows[0].shape[1])]
    for group in time_groups(rows[0]):
        joined = join_rows(rows, group)
        allowed = masks[group[0]]
        totals = jnp.zeros((joined.shape[0], 128), WIDE)
        leaving = []
        for side, weights in enumerate(sides):
            projected = matmul(joined, weights[:, : 3 * side_width]).astype(LOW)
            split_rows(projected_out, group, projected, side_columns(side, 3 * side_width))
            output, totals = attention_rows(projected, allowed, totals, side * (side_width // HEAD_DIM))
            split_rows(output_out, group, output, side_columns(side, side_width))
            leaving.append((output, [weights]))
        split_rows(totals_out, group, totals)
        leave_rows(
            leaving,
            slice(3 * side_width, 4 * side_width),
            lambda place, values, group=group: split_rows(part_out, group, values, place),
        )


def time_back_body(lengths, *refs):
    sides, refs = refs[:2], refs[2:]
    rows, projected, totals, grads_out, part_out = (refs[i : i + 4] for i in range(0, 20, 4))
    frames_local, width = rows[0].shape[0], projected[0].shape[3] // 3
    side_width = width // len(sides)
    masks = [time_allowed(lengths, clip, frames_local, PART) for clip in range(rows[0].shape[1])]
    for group in time_groups(rows[0]):
        allowed = masks[group[0]]
        joined = join_rows(rows, group)
        kept, sums = join_rows(projected, group), join_rows(totals, group)
        leaving = []
        for side, weights in enumerate(sides):
            output_grad = matmul(joined, weights[:, 3 * side_width :]).astype(LOW)
            first, columns = side * (side_width // HEAD_DIM), side_columns(side, 3 * side_width)
            grads = attention_rows_back(kept[:, columns], sums, first, output_grad, allowed)
            split_rows(grads_out, group, grads, columns)
            leaving.append((grads, [weights]))
        leave_rows(
            leaving,
            slice(0, 3 * side_width),
            lambda place, values, group=group: split_rows(part_out, group, values, place),
        )


def space_forward(rows, weights):
    count, width = rows.shape
    sides, inner = len(weights), weights[0].shape[1] // 4
    outs = [
        kept_of((count, 3 * inner * sides), LOW),
        shape_of((count, inner * sides), LOW),
        kept_of((count, 128), WIDE),
        shape_of((count, width), LOW),
    ]
    body = functools.partial(space_forward_body, sides)
    return run(body, outs, (rows, *weights), [ONE_VMEM] * (1 + sides))


def space_back(rows, weights, projected, totals):
    count, width = rows.shape
    sides = len(weights)
    outs = [shape_of(projected.shape, LOW), shape_of((count, width), LOW)]
    args = (rows, *weights, projected, totals)
    body = functools.partial(space_back_body, sides)
    return run(body, outs, args, [ONE_VMEM] * len(args), stored=(sides + 1, sides + 2))


def time_call(body, lengths, weights, groups, out_widths):
    args, outs = [lengths, *weights], []
    for group in groups:
        args += group
    for features, dtype in out_widths:
        outs += [shape_of((*groups[0][0].shape[:3], features), dtype)] * ROUND
    results = run(body, outs, args, [ONE_SMEM] + [ONE_VMEM] * (len(args) - 1), vmem=16 * MIB)
    return [results[i : i + ROUND] for i in range(0, len(results), ROUND)]


def hidden_body(normed, grad, *refs):
    enters, leaves, acts, pres = (refs[0], refs[2]), (refs[1], refs[3]), refs[4:6], refs[6:8]
    in_part, out_part = refs[8:]
    hidden = acts[0].shape[1]
    tile = 256
    for side in range(2):
        for start in range(0, hidden, tile):
            place = slice(start, start + tile)
            value = matmul(normed[...], enters[side][:, place])
            square = value * value
            half = 0.5 + 0.5 * jnp.tanh(value * (GELU_COEFF + GELU_COEFF * 0.044715 * square))
            slope = half + value * (half - half * half) * (
                2.0 * GELU_COEFF + 6.0 * 0.044715 * GELU_COEFF * square
            )
            acts[side][:, place] = (value * half).astype(LOW)
            pres[side][:, place] = (matmul(grad[...], leaves[side][:, place]) * slope).astype(LOW)
    for values, part, weights in ((pres, in_part, enters), (acts, out_part, leaves)):
        total = matmul_t(values[0][...], weights[0][...]) + matmul_t(values[1][...], weights[1][...])
        part[...] = total.astype(LOW)


def hidden_call(normed, grad, weights):
    count, width = normed.shape
    hidden = weights[0].shape[1]
    outs = [shape_of((count, hidden), LOW)] * 4 + [shape_of((count, width), LOW)] * 2
    results = run(hidden_body, outs, (normed, grad, *weights), [ONE_VMEM] * 6)
    return results[0:2], results[2:4], results[4], results[5]


def weight_grad_tile(counts, ranges, refs, start, tile, store):
    at, column = 0, 0
    for count, columns in zip(counts, ranges):
        lefts, rights = refs[at : at + count], refs[at + count : at + 2 * count]
        at += 2 * count
        total = matmul_tn(lefts[0][:, start : start + tile], rights[0][:, columns])
        for left, right in zip(lefts[1:], rights[1:]):
            total = total + matmul_tn(left[:, start : start + tile], right[:, columns])
        store(column, total.astype(LOW))
        column += total.shape[1]


def weight_grad_body(counts, ranges, near_first, *refs):
    out = refs[-1]
    tile = out.shape[0] // 4
    for place, start in enumerate((0, 2, 1, 3) if near_first else range(4)):

        def store(column, values, place=place):
            out[place * tile : (place + 1) * tile, column : column + values.shape[1]] = values

        weight_grad_tile(counts, ranges, refs, start * tile, tile, store)


def weight_grad(pairs, near_first=False, ranges=None, stored=()):
    args, counts = [], []
    for lefts, rights in pairs:
        args += [*lefts, *rights]
        counts.append(len(lefts))
    width = pairs[0][0][0].shape[1]
    ranges = ranges or [slice(0, rights[0].shape[1]) for _, rights in pairs]
    columns = sum(part.stop - part.start for part in ranges)
    body = functools.partial(weight_grad_body, tuple(counts), ranges, near_first)
    return run(body, shape_of((width, columns), LOW), args, [ONE_VMEM] * len(args), stored=stored)


def small_mine_body(gain, bias, table, out):
    step = gain.shape[1]
    out[...] = jnp.zeros_like(out)
    row = 0
    for part in (gain, bias, table):
        values = jnp.concatenate([part[...]] * ROUND, axis=1)
        lane = lax.broadcasted_iota(jnp.int32, values.shape, 1)
        out[0, row : row + part.shape[0], :] = pick(values, lane // step == lax.axis_index("head"))
        row += part.shape[0]


def small_rows_body(*refs):
    pairs, out = refs[:-1], refs[-1]
    step = pairs[0].shape[2]
    for i, pair in enumerate(pairs):
        for half in range(2):
            place = (half * len(pairs) + i) * step
            out[:, place : place + step] = pair[half]


def small_blocks_body(first, second, third, table_a, table_b, *outs):
    step = outs[0].shape[2]
    for half, out in enumerate(outs):
        for i in range(out.shape[0]):
            place = slice((half * out.shape[0] + i) * step, (half * out.shape[0] + i + 1) * step)
            for row, part in enumerate((first, second, third)):
                out[i, row : row + 1, :] = part[0:1, place]
                out[i, row + 3 : row + 4, :] = part[1:2, place]
            out[i, 6:14, :] = table_a[:, place] + table_b[:, place]
            out[i, 14:16, :] = jnp.zeros((2, step), WIDE)


def stack_body(*refs):
    out, row = refs[-1], 0
    for part in refs[:-1]:
        out[row : row + part.shape[0], ...] = part[...]
        row += part.shape[0]


def sum_body(*refs):
    total = refs[0][...]
    for part in refs[1:-1]:
        total = total + part[...]
    refs[-1][...] = total


def add_split_body(first, second, *outs):
    row = 0
    for out in outs:
        part = slice(row, row + out.shape[0])
        out[...] = (first[part].astype(WIDE) + second[part].astype(WIDE)).astype(out.dtype)
        row += out.shape[0]


def shards(
    frames_in,
    action_codes,
    clip_length,
    norm_gain,
    norm_bias,
    action_table,
    spatialin,
    spatialout,
    temporalin,
    temporalout,
    expand,
    shrink,
    out_grad,
):
    frames_local, clips, pos_local, width = frames_in.shape
    local = (frames_local, clips, pos_local, width)
    rel_shape = (BLOCKS, pos_local, width)
    count = BLOCKS * pos_local
    inner = spatialin.shape[2]
    hidden = expand.shape[1]
    codes = action_codes.reshape(BLOCKS)
    scalars = (codes, clip_length)

    packed_shape = shape_of(rel_shape, LOW)
    flat_shape = shape_of((count, width), LOW)
    sums_shape = shape_of((8, width), WIDE)
    frames_flat = frames_in.reshape(rel_shape)

    order = Order()
    send, take, do = order.send, order.take, order.do
    grad_shapes = [shape_of((3, width // BLOCKS, inner), WIDE), shape_of((inner, width // BLOCKS), WIDE)]
    whole_shape = shape_of(rel_shape, WIDE)

    def kernel(body, outs, first, *others, stored=()):
        smem = [ONE_SMEM if a.ndim == 1 else ONE_VMEM for a in (first, *others)]
        return do(lambda *args: run(body, outs, args, smem, stored=stored), first, *others)

    def stacked(*parts):
        shape = (sum(part.shape[0] for part in parts), *parts[0].shape[1:])
        return kernel(stack_body, shape_of(shape, parts[0].dtype), *parts)

    def summed(*parts):
        return kernel(sum_body, shape_of(parts[0].shape, parts[0].dtype), *parts)

    def halves(first, second):
        shape = shape_of((first.shape[0] // 2, *first.shape[1:]), first.dtype)
        keep, left = kernel(add_split_body, [shape, shape], first, second)
        order.last = left
        return keep, left

    def added(first, second):
        return kernel(add_split_body, [shape_of(first.shape, first.dtype)], first, second)[0]

    def attention_rows_of(enter, leave):
        out = shape_of((enter.shape[0], 4 * inner), LOW)
        return kernel(pack_attention_body, out, jnp.transpose(enter, (1, 0, 2)), leave, stored=(0, 1))

    def split_columns(rows, far):
        outs = [shape_of((2 * rows.shape[0], rows.shape[1] // 2), LOW)] * 2
        a, b = kernel(stack_split_body, outs, rows, far)
        order.last = b
        return a, b

    def crossed(first, second):
        out = shape_of((2 * first.shape[0], first.shape[1]), LOW)
        return kernel(stack_cross_body, out, first, second)

    def joined(a, b):
        outs = [shape_of((a[0].shape[0] // 2, 2 * a[0].shape[1]), LOW)] * 2
        keep, left = kernel(add_join_body, outs, *a, *b)
        order.last = left
        return keep, left

    space_rows = attention_rows_of(spatialin, spatialout)
    got = send(space_rows, "space", 4)
    packed = kernel(pack_frames_body, packed_shape, frames_flat, stored=(0,))
    small_shape = (16, width // BLOCKS)
    block = kernel(
        small_mine_body,
        shape_of((1, *small_shape), WIDE),
        norm_gain,
        norm_bias,
        action_table,
        stored=(0, 1, 2),
    )
    got_small = take(send(block, "space", 1))
    pair = stacked(block, got_small)
    got_small = [send(pair, "space", mask) for mask in ORDER[1:4]]
    got = take(got)
    got_small = [take(part) for part in got_small]
    space_a, space_b = split_columns(space_rows, got)
    got_a, got_b = send(space_a, "space", 2), send(space_b, "space", 1)
    frame_blocks = order.exchange(packed)
    small = kernel(small_rows_body, shape_of((16, width), WIDE), pair, *got_small)
    small = summed(small, take(send(small, "head", 1)))
    got_small = send(small, "head", 2)
    time_rows = attention_rows_of(temporalin, temporalout)
    hidden_rows = kernel(pack_hidden_body, shape_of((expand.shape[0], 2 * hidden), LOW), expand, shrink)
    small = summed(small, take(got_small))
    space_b = stacked(space_b, take(got_b))
    space_a = stacked(space_a, take(got_a))
    got_a, got_b = send(space_a, "space", 1), send(space_b, "space", 2)
    frame_blocks = take(frame_blocks)
    normed, start = kernel(
        frame_norm_body, [flat_shape, shape_of((count, width), WIDE)], *scalars, small, frame_blocks
    )
    normed_far = send(normed, "head", 2)
    got_a, got_b = take(got_a), take(got_b)
    got_time = send(time_rows, "space", 4)
    space_a = stacked(space_a, got_a)
    space_b = crossed(space_b, got_b)
    normed_far = take(normed_far)
    beside_a, beside_b = send(space_a, "head", 1), send(space_b, "head", 1)
    space_weights = [space_a, space_b, take(beside_a), take(beside_b)]
    got_hidden = send(hidden_rows, "space", 4)
    far_kept = do(space_forward, normed_far, space_weights)
    order.last = far_kept[3]
    far_part = send(far_kept[3], "head", 2)
    time_a, time_b = split_columns(time_rows, take(got_time))
    got_a, got_b = send(time_a, "space", 2), send(time_b, "space", 1)
    own_kept = do(space_forward, normed, space_weights)
    order.last = own_kept[3]
    time_a = stacked(time_a, take(got_a))
    time_b = stacked(time_b, take(got_b))
    got_a, got_b = send(time_a, "space", 1), send(time_b, "space", 2)
    far_part = take(far_part)
    packed = kernel(spread_body, packed_shape, own_kept[3], far_part)
    spread = order.exchange(packed)
    hidden_a, hidden_b = split_columns(hidden_rows, take(got_hidden))
    frames_rel, grad_low = kernel(
        order_inputs_body, [packed_shape] * 2, clip_length, frames_flat, out_grad.reshape(rel_shape)
    )
    order.last = grad_low
    grad_far = send(grad_low.reshape(count, width), "head", 2)
    hidden_got = send(hidden_a, "space", 2), send(hidden_b, "space", 1)
    grad_far = take(grad_far)
    spread = take(spread)
    first, normed_two = kernel(
        join_norm_body, [whole_shape, packed_shape], *scalars, small, frames_rel, spread
    )
    order.last = normed_two
    normed_two = normed_two.reshape(local)
    far = send(normed_two, "head", 2)
    near = send(normed_two, "head", 1)
    hidden_b = stacked(hidden_b, take(hidden_got[1]))
    hidden_a = stacked(hidden_a, take(hidden_got[0]))
    hidden_got = send(hidden_a, "space", 1), send(hidden_b, "space", 2)
    time_a = stacked(time_a, take(got_a))
    time_b = crossed(time_b, take(got_b))
    far = take(far)
    diagonal = send(far, "head", 1)
    near = take(near)
    normed_two = [normed_two, near, far, take(diagonal)]
    time_projected, time_output, time_totals, time_parts = do(
        lambda first, *others: time_call(
            time_forward_body,
            clip_length,
            [time_a, time_b],
            [[first, *others]],
            [(3 * inner, LOW), (inner, LOW), (128, WIDE), (width, LOW)],
        ),
        *normed_two,
    )
    order.last = time_parts[3]
    diagonal = send(time_parts[3], "head", 1)
    near = send(time_parts[1], "head", 1)
    far = added(time_parts[2], take(diagonal))
    far = send(far, "head", 2)
    hidden_got = [take(got) for got in hidden_got]
    near = take(near)
    hidden_a = stacked(hidden_a, hidden_got[0])
    hidden_b = crossed(hidden_b, hidden_got[1])
    parts = [part.reshape(rel_shape) for part in (time_parts[0], near, take(far))]
    second, normed_three = kernel(add_norm_body, [whole_shape, packed_shape], small, first, *parts)
    order.last = normed_three
    normed_three = normed_three.reshape(count, width)
    grad_low_flat = grad_low.reshape(count, width)
    far = send(normed_three, "head", 2)
    beside_a, beside_b = send(hidden_a, "head", 1), send(hidden_b, "head", 1)
    hidden_weights = [hidden_a, hidden_b, take(beside_a), take(beside_b)]
    normed_three = [normed_three, take(far)]
    grad_third = [grad_low_flat, grad_far]
    far_kept_three = do(hidden_call, normed_three[1], grad_third[1], hidden_weights)
    order.last = far_kept_three[2]
    far_part = send(far_kept_three[2], "head", 2)
    own_kept_three = do(hidden_call, normed_three[0], grad_third[0], hidden_weights)
    hidden_kept = [own_kept_three, far_kept_three]
    def hidden_part(side, leave):
        lefts = grad_third if leave else normed_three
        rights = [kept[0 if leave else 1][side] for kept in hidden_kept]
        return do(lambda *left: weight_grad([(left, rights)], near_first=leave), *lefts)
    beside_a = hidden_part(1, False)
    beside_b = hidden_part(1, True)
    far_part = take(far_part)
    beside_a, beside_b = send(beside_a, "head", 1), send(beside_b, "head", 1)
    parts = [part.reshape(rel_shape) for part in (own_kept_three[2], far_part)]
    total_second, low_second, sums_third = kernel(
        back_third_body, [whole_shape, packed_shape, sums_shape], small, grad_low, second, *parts
    )
    order.last = low_second
    low_second = low_second.reshape(local)
    far = send(low_second, "head", 2)
    near = send(low_second, "head", 1)
    hidden_a = hidden_part(0, False)
    hidden_b = hidden_part(0, True)
    near = take(near)
    far = take(far)
    diagonal = send(far, "head", 1)
    hidden_a, send_a = halves(hidden_a, take(beside_a))
    got_a = send(send_a, "space", 1)
    hidden_b, send_b = halves(hidden_b, take(beside_b))
    got_b = send(send_b, "space", 2)
    grad_two = [low_second, near, far, take(diagonal)]
    time_grads, time_parts = do(
        lambda first, *others: time_call(
            time_back_body,
            clip_length,
            [time_a, time_b],
            [[first, *others], time_projected, time_totals],
            [(3 * inner, LOW), (width, LOW)],
        ),
        *grad_two,
    )
    order.last = time_parts[3]
    diagonal = send(time_parts[3], "head", 1)
    near = send(time_parts[1], "head", 1)
    flat = lambda arrays: [a.reshape(count, a.shape[-1]) for a in arrays]
    far = added(time_parts[2], take(diagonal))
    far = send(far, "head", 2)
    near = take(near)
    def attention_part(side, lefts, grads, backs, outputs):
        step = inner // 2
        return do(
            lambda *left: weight_grad(
                [(left, grads), (backs, outputs)],
                near_first=side % 2 == 1,
                ranges=[side_columns(side, 3 * step), side_columns(side, step)],
            ),
            *lefts,
        )
    time_args = flat(normed_two), flat(time_grads), flat(grad_two), flat(time_output)
    time_a = attention_part(0, *time_args)
    time_b = attention_part(1, *time_args)
    hidden_a, send_a = halves(hidden_a, take(got_a))
    hidden_b, send_b = halves(hidden_b, take(got_b))
    hidden_got = send(send_a, "space", 2), send(send_b, "space", 1)
    parts = [part.reshape(rel_shape) for part in (time_parts[0], near, take(far))]
    total_first, sums_second, table_first, packed = kernel(
        back_second_body,
        [whole_shape, sums_shape, sums_shape, packed_shape],
        *scalars,
        small,
        total_second,
        first,
        *parts,
    )
    order.last = packed
    grad_blocks = order.exchange(packed)
    hidden_keep, hidden_send = joined((hidden_a, take(hidden_got[0])), (hidden_b, take(hidden_got[1])))
    (time_a, send_a), (time_b, send_b) = [jnp.split(part, 2) for part in (time_a, time_b)]
    got_a, got_b = send(send_a, "space", 1), send(send_b, "space", 2)
    got_hidden = send(hidden_send, "space", 4)
    far_out = take(send(far_kept_three[3], "head", 2))
    grad_blocks = take(grad_blocks)
    grad_one = kernel(collect_body, flat_shape, grad_blocks)
    far = send(grad_one, "head", 2)
    own_result = do(space_back, grad_one, space_weights, own_kept[0], own_kept[2])
    order.last = own_result[1]
    got_hidden = take(got_hidden)
    got_a, got_b = take(got_a), take(got_b)
    grad_one = [grad_one, take(far)]
    far_result = do(space_back, grad_one[1], space_weights, far_kept[0], far_kept[2])
    order.last = far_result[1]
    time_a, send_a = halves(time_a, got_a)
    far_part = send(far_result[1], "head", 2)
    time_b, send_b = halves(time_b, got_b)
    got_a, got_b = send(send_a, "space", 2), send(send_b, "space", 1)
    space_args = [normed, normed_far], [own_result[0], far_result[0]], grad_one, [own_kept[1], far_kept[1]]
    beside_a = attention_part(2, *space_args)
    beside_b = attention_part(3, *space_args)
    time_keep, time_send = joined((time_a, take(got_a)), (time_b, take(got_b)))
    got_time = send(time_send, "space", 4)
    space_a = attention_part(0, *space_args)
    space_b = attention_part(1, *space_args)
    far_part = take(far_part)
    beside_a, beside_b = send(beside_a, "head", 1), send(beside_b, "head", 1)
    sums_first, table_second, packed = kernel(
        back_first_body,
        [sums_shape, sums_shape, packed_shape],
        *scalars,
        small,
        start,
        own_result[1],
        far_part,
    )
    order.last = packed
    last = order.exchange(packed)
    half_shape = shape_of((BLOCKS // 2, *small_shape), WIDE)
    sums, small_send = kernel(
        small_blocks_body, [half_shape] * 2, sums_first, sums_second, sums_third, table_first, table_second
    )
    order.last = small_send
    got_small = send(small_send, "space", 1)
    space_a, send_a = halves(space_a, take(beside_a))
    space_b, send_b = halves(space_b, take(beside_b))
    sums, small_send = halves(sums, take(got_small))
    got_small = send(small_send, "space", 2)
    got_a, got_b = send(send_a, "space", 1), send(send_b, "space", 2)
    parts = [part.reshape(rel_shape) for part in (own_kept_three[3], far_out)]
    frames_out = kernel(finish_forward_body, packed_shape, clip_length, second, *parts)
    hidden_grads = kernel(
        unpack_hidden_body,
        [shape_of((width // BLOCKS, hidden), WIDE), shape_of((hidden, width // BLOCKS), WIDE)],
        hidden_keep,
        got_hidden,
    )
    sums, small_send = halves(sums, take(got_small))
    got_small = send(small_send, "space", 4)
    space_a, send_a = halves(space_a, take(got_a))
    space_b, send_b = halves(space_b, take(got_b))
    got_a, got_b = send(send_a, "space", 2), send(send_b, "space", 1)
    space_keep, space_send = joined((space_a, take(got_a)), (space_b, take(got_b)))
    sums = summed(sums, take(got_small))
    got = send(space_send, "space", 4)
    got_small = send(sums, "head", 1)
    last = take(last)
    frames_grad = kernel(finish_back_body, whole_shape, clip_length, total_first, last)
    sums = summed(sums, take(got_small))
    got_small = send(sums, "head", 2)
    sums = summed(sums, take(got_small))[0]
    step = sums.shape[1] // ROUND
    sums = lax.dynamic_slice(sums, (0, lax.axis_index("head") * step), (sums.shape[0], step))
    time_grads = kernel(unpack_attention_body, grad_shapes, time_keep, take(got_time))
    space_grads = kernel(unpack_attention_body, grad_shapes, space_keep, take(got))
    return (
        frames_out.reshape(local),
        frames_grad.reshape(local),
        sums[0:3],
        sums[3:6],
        sums[6:14],
        jnp.transpose(space_grads[0], (1, 0, 2)),
        space_grads[1],
        jnp.transpose(time_grads[0], (1, 0, 2)),
        time_grads[1],
        *hidden_grads,
    )


def solution(mesh):
    placed = (
        P("head", None, "space", None),
        P("head", None),
        P(),
        P(None, ("space", "head")),
        P(None, ("space", "head")),
        P(None, ("space", "head")),
        P("space", None, "head"),
        P("head", "space"),
        P("space", None, "head"),
        P("head", "space"),
        P("space", "head"),
        P("head", "space"),
        P("head", None, "space", None),
    )
    eight = mesh.shape["space"] == BLOCKS and mesh.shape["head"] == ROUND
    return jax.shard_map(
        shards if eight else general_shards,
        mesh=mesh,
        in_specs=placed,
        out_specs=(
            P("head", None, "space", None),
            P("head", None, "space", None),
            P(None, ("space", "head")),
            P(None, ("space", "head")),
            P(None, ("space", "head")),
            P("space", None, "head"),
            P("head", "space"),
            P("space", None, "head"),
            P("head", "space"),
            P("space", "head"),
            P("head", "space"),
        ),
        check_vma=False,
    )
```
